32 devices in a mesh: dp: 8 (over y, x, core), mp: 4 (over z).
Axes of the slice: x: 2, y: 2, z: 4, core: 2. Of those that a mesh axis runs over, the one named last changes fastest.
Arguments:
- tokens: bfloat16 [10240, 1024], P('dp'), may hold values from -6 to 6
- text_states: bfloat16 [40, 128, 1024], P('dp'), may hold values from -6 to 6
- lengths: int32 [40], P('dp'), may hold values from 0 to 1024, as said below
- text_mask: int32 [40, 128], P('dp'), may hold values 0 or 1
- ln_gain: float32 [3, 1024], replicated, may hold values from 0.5 to 1.5
- ln_shift: float32 [3, 1024], replicated, may hold values from -2.5 to 2.5
- w_qkv: bfloat16 [1024, 3, 1024], P(None, None, 'mp'), may hold values from -0.1875 to 0.1875
- w_out: bfloat16 [1024, 1024], P('mp'), may hold values from -1 to 1
- w_cross_q: bfloat16 [1024, 1024], P(None, 'mp'), may hold values from -0.1875 to 0.1875
- w_cross_kv: bfloat16 [1024, 2, 1024], P(None, None, 'mp'), may hold values from -0.1875 to 0.1875
- w_cross_out: bfloat16 [1024, 1024], P('mp'), may hold values from -1 to 1
- w_up: bfloat16 [1024, 4096], P(None, 'mp'), may hold values from -0.1875 to 0.1875
- w_down: bfloat16 [4096, 1024], P('mp'), may hold values from -0.09375 to 0.09375
- cotangent: bfloat16 [10240, 1024], P('dp'), may hold values from -6 to 6
Outputs:
- output: bfloat16 [10240, 1024], P('dp')
- grad_tokens: float32 [10240, 1024], P('dp')
- grad_text: float32 [40, 128, 1024], P('dp')
- grad_gain: float32 [3, 1024], P(None, 'dp')
- grad_shift: float32 [3, 1024], P(None, 'dp')
- grad_qkv: float32 [1024, 3, 1024], P('dp', None, 'mp')
- grad_out: float32 [1024, 1024], P(('mp', 'dp'))
- grad_cross_q: float32 [1024, 1024], P('dp', 'mp')
- grad_cross_kv: float32 [1024, 2, 1024], P('dp', None, 'mp')
- grad_cross_out: float32 [1024, 1024], P(('mp', 'dp'))
- grad_up: float32 [1024, 4096], P('dp', 'mp')
- grad_down: float32 [4096, 1024], P(('mp', 'dp'))
The draws below stay inside these ranges and needn't reach their ends.
Inputs may be any that keep to these rules, and one draw needn't show every extreme that they name: `lengths`: each group of 5 entries (the slots of one index of dp) holds items of 256 or 1024 tokens followed by zeros, at most one of 1024, and sums to 1280.
All inputs are finite; a program needn't handle non-finite values. No bound on the sum of `text_mask` on one device may be relied on, other than what follows from the above.
Results may differ from the reference program's by a relative error of at most 0.019.
Values sent between devices are 32-bit elements; how exact they have to be, the bound alone decides.
No kernel may reach another device: no remote copies, remote signals or barrier semaphores. Data moves between devices by JAX's collectives and lax.ppermute only.
A program may use at most 192 MiB of HBM per device.

```python
import jax
import jax.numpy as jnp
from jax import lax

D = 1024
HEADS = 16
HEAD = 64
FF = 4096
TEXT = 128
LONG = 1024
SHORT = 256
TOK_DEV = 1280
SLOTS_DEV = 5
SLOTS = 40
TOKENS = 10240
N_DP = 8


def draw_lengths(key, part):
    key = jax.random.fold_in(key, 7)
    key_long, key_forced, key_place = jax.random.split(key, 3)
    has_long = jax.random.randint(key_long, (N_DP,), 0, 2)
    forced = jax.random.randint(key_forced, (), 0, N_DP)
    has_long = jnp.where(jnp.arange(N_DP) == forced, 1, has_long)
    long_span = LONG // SHORT
    placed = jax.random.randint(key_place, (N_DP,), 0, SLOTS_DEV - long_span + 1)
    slot_index = jnp.arange(SLOTS_DEV)[None, :]
    item_count = SLOTS_DEV - (long_span - 1) * has_long[:, None]
    lengths_out = jnp.where(slot_index < item_count, SHORT, 0)
    lengths_out = jnp.where((has_long[:, None] == 1) & (slot_index == placed[:, None]), LONG, lengths_out)
    return lengths_out.reshape(-1).astype(jnp.int32)


def place_ends(values, rng, smallest, high):
    extent = values.shape
    place = [jax.random.randint(jax.random.fold_in(rng, axis), (), 0, extent[axis]) for axis in range(len(extent))]
    values = values.at[tuple(place)].set(smallest)
    longest = extent.index(max(extent))
    place[longest] = (place[longest] + 1) % extent[longest]
    return values.at[tuple(place)].set(high)


def block_levels(rng, shape, cuts, low, largest):
    level, own = 1.0, jax.random.fold_in(rng, 6)
    for axis_at, parts in cuts:
        heights = jnp.exp(jax.random.uniform(jax.random.fold_in(own, axis_at), (parts,), jnp.float32, low / len(cuts), largest / len(cuts)))
        level = level * jnp.repeat(heights, shape[axis_at] // parts).reshape([-1 if axis == axis_at else 1 for axis in range(len(shape))])
    return level


def centred(own_key, extent, scale, reach, cuts=(), held_as=jnp.bfloat16):
    values = scale * jax.random.normal(own_key, extent, jnp.float32)
    if cuts:
        values = values * block_levels(own_key, extent, cuts, -0.22, 0.18)
    return jnp.clip(values, -reach, reach).astype(held_as)


def setup_inputs(seed: int = 0) -> dict:
    splits = jax.random.split(jax.random.key(seed), 15)
    tokens = centred(splits[0], (TOKENS, D), 1.0, 6.0, ((0, 8),))
    text_states = centred(splits[1], (SLOTS, TEXT, D), 1.0, 6.0, ((0, 8),))
    lengths = draw_lengths(jax.random.fold_in(splits[14], 71), 0)
    text_mask = place_ends((jax.random.randint(splits[3], (SLOTS, TEXT), 0, 4) < 3).astype(jnp.int32), jax.random.fold_in(splits[3], 1), 0, 1)
    ln_gain = jnp.clip(1.0 + 0.1 * jax.random.normal(splits[4], (3, D), jnp.float32), 0.5, 1.5)
    ln_shift = centred(splits[5], (3, D), 0.3, 2.5, (), jnp.float32)
    w_qkv = centred(splits[6], (D, 3, D), D ** -0.5, 0.1875, ((2, 4),))
    w_out = centred(splits[7], (D, D), (D // 32) ** -0.5, 1.0, ((0, 4),))
    w_cross_q = centred(splits[8], (D, D), D ** -0.5, 0.1875, ((1, 4),))
    w_cross_kv = centred(splits[9], (D, 2, D), D ** -0.5, 0.1875, ((2, 4),))
    w_cross_out = centred(splits[10], (D, D), (D // 32) ** -0.5, 1.0, ((0, 4),))
    w_up = centred(splits[11], (D, FF), D ** -0.5, 0.1875, ((1, 4),))
    w_down = centred(splits[12], (FF, D), FF ** -0.5, 0.09375, ((0, 4),))
    cotangent = centred(splits[13], (TOKENS, D), 1.0, 6.0, ((0, 8),))
    return dict(tokens=tokens, text_states=text_states, lengths=lengths, text_mask=text_mask, ln_gain=ln_gain, ln_shift=ln_shift, w_qkv=w_qkv, w_out=w_out, w_cross_q=w_cross_q, w_cross_kv=w_cross_kv, w_cross_out=w_cross_out, w_up=w_up, w_down=w_down, cotangent=cotangent)


highest = lax.Precision.HIGHEST
epsilon = 1e-05

@jax.custom_vjp
def low(v):
    return lax.optimization_barrier(v.astype(jnp.bfloat16)).astype(jnp.float32)

@jax.custom_vjp
def low_back(v):
    return v

def low_keep(v):
    return (low(v), None)

def low_pass(kept, grad):
    return (grad,)

def back_keep(v):
    return (v, None)

def back_low(kept, grad):
    return (low(grad),)
low.defvjp(low_keep, low_pass)
low_back.defvjp(back_keep, back_low)

def rounded(value):
    return low_back(low(value))

def normed(value, gain, shift):
    center = value - lax.optimization_barrier(jnp.mean(value, axis=-1, keepdims=True))
    spread = lax.optimization_barrier(jnp.mean(center * center, axis=-1, keepdims=True))
    return center * lax.rsqrt(spread + epsilon) * gain + shift

def attend(query, key_set, value_set, allowed):
    scale = HEAD ** (-0.5)
    scores = jnp.einsum('qhe,khe->hqk', query, key_set, precision=highest) * scale
    scores = low_back(scores)
    scores = jnp.where(allowed[None], scores, -1e+30)
    chances = jax.nn.softmax(scores, axis=-1)
    return jnp.einsum('hqk,khe->qhe', low(chances), value_set, precision=highest)

def split_heads(value):
    return value.reshape(value.shape[0], HEADS, HEAD)

def device_rows(weights, token_rows, text_rows, length_rows, mask_rows):
    gains, shifts, w_qkv, w_out, w_cross_q, w_cross_kv, w_cross_out, w_up, w_down = weights
    row_count = token_rows.shape[0]
    places = jnp.arange(row_count, dtype=jnp.int32)
    item_ends = jnp.cumsum(length_rows).astype(jnp.int32)
    item_of = lax.optimization_barrier(jnp.sum((places[:, None] >= item_ends[None, :]).astype(jnp.int32), axis=1))
    self_allowed = (item_of[:, None] == item_of[None, :]) & (places[None, :] <= places[:, None])
    text_places = jnp.arange(SLOTS_DEV * TEXT, dtype=jnp.int32)
    live_key = (mask_rows.reshape(-1) == 1) | (text_places % TEXT == 0)
    cross_allowed = (item_of[:, None] == (text_places // TEXT)[None, :]) & live_key[None, :]
    normed_first = low(normed(token_rows, gains[0], shifts[0]))
    triple = rounded(jnp.einsum('rd,dtc->rtc', normed_first, w_qkv, precision=highest))
    mixed = rounded(attend(split_heads(triple[:, 0]), split_heads(triple[:, 1]), split_heads(triple[:, 2]), self_allowed))
    after_self = token_rows + low_back(jnp.dot(mixed.reshape(row_count, D), w_out, precision=highest))
    normed_second = low(normed(after_self, gains[1], shifts[1]))
    cross_query = rounded(jnp.dot(normed_second, w_cross_q, precision=highest))
    text_flat = text_rows.reshape(SLOTS_DEV * TEXT, D)
    text_pair = rounded(jnp.einsum('sd,dtc->stc', text_flat, w_cross_kv, precision=highest))
    looked = rounded(attend(split_heads(cross_query), split_heads(text_pair[:, 0]), split_heads(text_pair[:, 1]), cross_allowed))
    after_cross = after_self + low_back(jnp.dot(looked.reshape(row_count, D), w_cross_out, precision=highest))
    normed_third = low(normed(after_cross, gains[2], shifts[2]))
    pre_act = low_back(jnp.dot(normed_third, w_up, precision=highest))
    hidden = low(jax.nn.gelu(pre_act, approximate=True))
    return after_cross + low_back(jnp.dot(hidden, w_down, precision=highest))

def reference(tokens, text_states, lengths, text_mask, ln_gain, ln_shift, w_qkv, w_out, w_cross_q, w_cross_kv, w_cross_out, w_up, w_down, cotangent):
    weights = tuple((array.astype(jnp.float32) for array in (ln_gain, ln_shift, w_qkv, w_out, w_cross_q, w_cross_kv, w_cross_out, w_up, w_down)))
    token_rows = tokens.astype(jnp.float32).reshape(N_DP, TOK_DEV, D)
    text_rows = text_states.astype(jnp.float32).reshape(N_DP, SLOTS_DEV, TEXT, D)
    length_rows = lengths.reshape(N_DP, SLOTS_DEV)
    mask_rows = text_mask.reshape(N_DP, SLOTS_DEV, TEXT)

    def forward(weight_set, token_set, text_set):

        def one_device(inputs):
            return device_rows(weight_set, *inputs)
        return lax.map(jax.checkpoint(one_device), (token_set, text_set, length_rows, mask_rows))
    result, pullback = jax.vjp(forward, weights, token_rows, text_rows)
    weight_grads, token_grads, text_grads = pullback(cotangent.astype(jnp.float32).reshape(N_DP, TOK_DEV, D))
    return (result.reshape(TOKENS, D).astype(jnp.bfloat16), token_grads.reshape(TOKENS, D), text_grads.reshape(SLOTS, TEXT, D), weight_grads[0], weight_grads[1], weight_grads[2], weight_grads[3], weight_grads[4], weight_grads[5], weight_grads[6], weight_grads[7], weight_grads[8])
```

```python
from functools import partial

import jax
import jax.numpy as jnp
from jax import lax
from jax.experimental import pallas as pl
from jax.experimental.pallas import tpu as pltpu
from jax.sharding import PartitionSpec as P

HEAD = 64
BLK = 256
SLOTS8 = 8
EPS = 1e-05
NEG = -1e30
F32 = jnp.float32
BF16 = jnp.bfloat16
MIB = 1024 * 1024

NN = (((1,), (0,)), ((), ()))
NT = (((1,), (1,)), ((), ()))
TN = (((0,), (0,)), ((), ()))


def dot(a, b, dims=NN):
    return lax.dot_general(a, b, dims, preferred_element_type=F32)


def params(mib=56, semantics=None):
    return pltpu.CompilerParams(vmem_limit_bytes=mib * MIB, dimension_semantics=semantics)


def shape(dims, dtype=F32):
    return jax.ShapeDtypeStruct(dims, dtype)


def smem():
    return pl.BlockSpec(memory_space=pltpu.SMEM)


def whole(dims):
    rank = len(dims)
    return pl.BlockSpec(dims, lambda *_: (0,) * rank)


def at(dims, index):
    return pl.BlockSpec(dims, lambda *_: index)


def rows_of(tile, width):
    return pl.BlockSpec((tile, width), lambda i, *_: (i, 0))


def norm_stats(value):
    center = value - jnp.mean(value, axis=-1, keepdims=True)
    spread = jnp.mean(center * center, axis=-1, keepdims=True)
    inverse = lax.rsqrt(spread + EPS)
    return center * inverse, inverse


def norm_forward(value, gain, shift):
    unit, _ = norm_stats(value)
    return (unit * gain + shift).astype(BF16)


def norm_backward(incoming, value, gain):
    unit, inverse = norm_stats(value)
    scaled = incoming * gain
    pushed = incoming * unit
    inner = (
        scaled
        - jnp.mean(scaled, axis=-1, keepdims=True)
        - unit * jnp.mean(scaled * unit, axis=-1, keepdims=True)
    )
    return (
        inner * inverse,
        jnp.sum(pushed, axis=0, keepdims=True),
        jnp.sum(incoming, axis=0, keepdims=True),
    )


def norm_kernel(tokens_ref, gain_ref, shift_ref, first_ref):
    first_ref[...] = norm_forward(tokens_ref[...].astype(F32), gain_ref[...], shift_ref[...])


def norm_first(tokens, gain, shift):
    rows, width = tokens.shape
    return pl.pallas_call(
        norm_kernel,
        grid=(rows // BLK,),
        in_specs=[rows_of(BLK, width), whole((1, width)), whole((1, width))],
        out_specs=rows_of(BLK, width),
        out_shape=shape((rows, width), BF16),
        name="norm_first",
    )(tokens, gain, shift)


def head_row(width, head, value):
    lane = lax.broadcasted_iota(jnp.int32, (1, width), 1)
    return jnp.where(lane // HEAD == head, value, 0.0)


def masked(block, row):
    return (block.astype(F32) * row).astype(BF16)


def item_at(lengths, place):
    item, start, end = 0, 0, 0
    for slot in range(lengths.shape[0]):
        end = end + lengths[slot]
        past = end <= place
        item = item + past.astype(jnp.int32)
        start = jnp.where(past, end, start)
    return item, start


def fill(target, slots, me, rows):
    for index, ref in enumerate(slots):
        place = pl.multiple_of((me ^ index) * rows, rows)
        for k in range(ref.shape[0]):
            target[k, pl.ds(place, rows), :] = ref[k].astype(BF16)


def causal():
    shape2 = (BLK, BLK)
    return lax.broadcasted_iota(jnp.int32, shape2, 0) <= lax.broadcasted_iota(
        jnp.int32, shape2, 1
    )


def lanes_of(head):
    return slice(head * HEAD, (head + 1) * HEAD)


def self_block(qb, count, qkv, turned, mixed, logs):
    q0 = pl.multiple_of(qb * BLK, BLK)
    k0 = pl.multiple_of((qb - (count - 1)) * BLK, BLK)
    width = qkv.shape[2]
    query = qkv[0, pl.ds(q0, BLK), :]
    diag = qkv[1, pl.ds(q0, BLK), :]
    pre_len = (count - 1) * BLK
    keep = causal()
    pieces = []
    for head in range(width // HEAD):
        part = masked(query, head_row(width, head, HEAD**-0.5))
        near = jnp.where(keep, dot(diag, part, NT), NEG)
        peak = jnp.max(near, axis=0, keepdims=True)
        if pre_len:
            far = dot(qkv[1, pl.ds(k0, pre_len), :], part, NT)
            peak = jnp.maximum(peak, jnp.max(far, axis=0, keepdims=True))
        near = jnp.exp(near - peak)
        total = jnp.sum(near, axis=0, keepdims=True)
        result = dot(turned[lanes_of(head), pl.ds(q0, BLK)], near.astype(BF16))
        if pre_len:
            far = jnp.exp(far - peak)
            total = total + jnp.sum(far, axis=0, keepdims=True)
            result = result + dot(
                turned[lanes_of(head), pl.ds(k0, pre_len)], far.astype(BF16)
            )
        pieces.append(result * (1.0 / total))
        logs[head : head + 1, pl.ds(q0, BLK)] = peak + jnp.log(total)
    mixed[pl.ds(q0, BLK), :] = jnp.concatenate(pieces, axis=0).T.astype(BF16)


def front_body(lengths, first, text, weights, cross, qkv, mixed, logs, pair, turned):
    rows = first.shape[0]
    for m in range(3):
        qkv[m] = dot(first[...], weights[m]).astype(BF16)
    for m in range(2):
        pair[m] = dot(text[...], cross[m + 1]).astype(BF16)
    turned[...] = qkv[2].T

    @pl.loop(0, rows // BLK)
    def _(qb):
        _, start = item_at(lengths, qb * BLK)
        count = qb - start // BLK + 1
        for n in range(1, 5):

            @pl.when(count == n)
            def _():
                self_block(qb, n, qkv, turned, mixed, logs)


def front_kernel(me, lengths, first, text, *refs):
    slots, (weights, cross, *rest) = refs[:16], refs[16:]
    rows = slots[0].shape[1]
    fill(weights, slots[:8], me[0], rows)
    fill(cross, slots[8:], me[0], rows)
    front_body(lengths, first, text, weights, cross, *rest)


def front_outs(rows, text_rows, width):
    return [
        shape((3, rows, width), BF16),
        shape((rows, width), BF16),
        shape((8, rows), F32),
        shape((2, text_rows, width), BF16),
    ]


def vmem():
    return pl.BlockSpec(memory_space=pltpu.VMEM)


def front_own(lengths, first, text, weights, cross):
    rows, _ = first.shape
    width = weights.shape[2]
    return pl.pallas_call(
        front_body,
        in_specs=[smem()] + [vmem()] * 4,
        out_specs=[vmem()] * 4,
        out_shape=front_outs(rows, text.shape[0], width),
        scratch_shapes=[pltpu.VMEM((width, rows), BF16)],
        compiler_params=params(),
        name="front_own",
    )(lengths, first, text, weights, cross)


def halves(slots):
    arrays, specs = [], []
    for half, group in enumerate(slots):
        for index, array in enumerate(group):
            size = group[6].shape
            arrays.append(array)
            specs.append(at(size, (half if index < 6 else 0, 0, 0)))
    return arrays, specs


def front(me, lengths, first, text, slots):
    rows, depth = first.shape
    arrays, specs = halves(slots)
    width = arrays[0].shape[2]
    outs = [shape((3, depth, width), BF16)] * 2 + front_outs(rows, text.shape[0], width)
    return pl.pallas_call(
        front_kernel,
        grid=(1,),
        in_specs=[smem(), smem(), vmem(), vmem()] + specs,
        out_specs=[vmem()] * 6,
        out_shape=outs,
        scratch_shapes=[pltpu.VMEM((width, rows), BF16)],
        compiler_params=params(),
        name="front",
    )(me, lengths, first, text, *arrays)


def middle_kernel(me, lengths, live, tokens, gain1, shift1, gain2, shift2, own_out, own_co, *refs):
    mixed, refs = refs[:4], refs[4:]
    queries, refs = refs[:4], refs[4:]
    pairs, refs = refs[:4], refs[4:]
    slots, refs = refs[:48], refs[48:]
    w_out, w_co, after_self, after_cross, second, third, cross_query, looked, logs, turned = refs
    step = pl.program_id(0)

    @pl.when(step == 0)
    def _():
        width = own_out.shape[0]
        w_out[:width, :] = own_out[...]
        w_co[:width, :] = own_co[...]
        for j in range(3):
            for half, target in enumerate((w_out, w_co)):
                for index in range(SLOTS8):
                    ref = slots[j * 16 + half * 8 + index]
                    rows = ref.shape[1]
                    place = pl.multiple_of((j + 1) * width + (me[0] ^ index) * rows, rows)
                    target[pl.ds(place, rows), :] = ref[0].astype(BF16)
        for j in range(4):
            turned[j] = pairs[j][1].T

    part = jnp.concatenate([ref[...] for ref in mixed], axis=1)
    residual = tokens[...].astype(F32) + dot(part, w_out[...])
    after_self[...] = residual
    normed = norm_forward(residual, gain1[...], shift1[...])
    second[...] = normed
    text = TEXT
    item, _ = item_at(lengths, step * BLK)
    t0 = pl.multiple_of(item * text, text)
    alive = live[pl.ds(t0, text), :] > 0.0
    for j in range(4):
        query = dot(normed, queries[j][0]).astype(BF16)
        width = query.shape[1]
        cols = slice(j * width, (j + 1) * width)
        cross_query[:, cols] = query
        keys = pairs[j][0, pl.ds(t0, text), :]
        pieces = []
        for head in range(width // HEAD):
            row = masked(query, head_row(width, head, HEAD**-0.5))
            score = jnp.where(alive, dot(keys, row, NT), NEG)
            peak = jnp.max(score, axis=0, keepdims=True)
            score = jnp.exp(score - peak)
            total = jnp.sum(score, axis=0, keepdims=True)
            result = dot(turned[j, lanes_of(head), pl.ds(t0, text)], score.astype(BF16))
            pieces.append(result * (1.0 / total))
            index = j * (width // HEAD) + head
            logs[index : index + 1, :] = peak + jnp.log(total)
        looked[:, cols] = jnp.concatenate(pieces, axis=0).T.astype(BF16)
    residual = residual + dot(looked[...], w_co[...])
    after_cross[...] = residual
    third[...] = norm_forward(residual, gain2[...], shift2[...])


TEXT = 128


def middle(me, lengths, live, tokens, norms, own_out, own_co, mixed, crosses, pairs, slots):
    rows, depth = tokens.shape
    width = own_out.shape[0]
    text_rows = live.shape[0]
    inner = 4 * width
    row = whole((1, depth))
    arrays, specs = [], []
    for entry in slots:
        more, more_specs = halves(entry)
        arrays += more
        specs += more_specs
    return pl.pallas_call(
        middle_kernel,
        grid=(rows // BLK,),
        in_specs=[smem(), smem(), whole((text_rows, 1)), rows_of(BLK, depth)]
        + [row] * 4
        + [whole((width, depth))] * 2
        + [rows_of(BLK, width)] * 4
        + [at((1, depth, width), (0, 0, 0))] * 4
        + [whole((2, text_rows, width))] * 4
        + specs,
        out_specs=[whole((inner, depth))] * 2
        + [rows_of(BLK, depth)] * 4
        + [rows_of(BLK, inner)] * 2
        + [pl.BlockSpec((inner // HEAD, BLK), lambda i: (0, i))],
        out_shape=[shape((inner, depth), BF16)] * 2
        + [shape((rows, depth)), shape((rows, depth))]
        + [shape((rows, depth), BF16)] * 2
        + [shape((rows, inner), BF16)] * 2
        + [shape((inner // HEAD, rows))],
        scratch_shapes=[pltpu.VMEM((4, width, text_rows), BF16)],
        compiler_params=params(),
        name="middle",
    )(me, lengths, live, tokens, *norms, own_out, own_co, *mixed, *crosses, *pairs, *arrays)


ROOT = 0.7978845608028654
CUBE = 0.044715


def gelu_both(value):
    square = value * value
    bend = jnp.tanh(value * (ROOT + (ROOT * CUBE) * square))
    half = 0.5 + 0.5 * bend
    slope = half + (0.5 * value) * (1.0 - bend * bend) * (ROOT + (3.0 * ROOT * CUBE) * square)
    return value * half, slope


def feed_rows(third, cot, up, down):
    pre_act = dot(third, up)
    hidden, slope = gelu_both(pre_act)
    hidden = hidden.astype(BF16)
    pre_grad = (dot(cot, down, NT) * slope).astype(BF16)
    return hidden, pre_grad, dot(hidden, down), dot(pre_grad, up, NT)


def feed_own_kernel(third, cot, after, up, down, out, grad, up_grad, down_grad):
    hidden, pre_grad, result, pushed = feed_rows(third[...], cot[...], up[...], down[...])
    out[...] = after[...] + result
    grad[...] = pushed
    first = pl.program_id(0) == 0
    more_up = dot(third[...], pre_grad, TN)
    more_down = dot(hidden, cot[...], TN)

    @pl.when(first)
    def _():
        up_grad[...] = more_up
        down_grad[...] = more_down

    @pl.when(jnp.logical_not(first))
    def _():
        up_grad[...] += more_up
        down_grad[...] += more_down


FEED = 320


def feed_own(third, cot, after, up, down):
    rows, depth = third.shape
    inner = up.shape[1]
    tile = rows_of(FEED, depth)
    return pl.pallas_call(
        feed_own_kernel,
        grid=(rows // FEED,),
        in_specs=[tile, tile, tile, whole((depth, inner)), whole((inner, depth))],
        out_specs=[tile, tile, whole((depth, inner)), whole((inner, depth))],
        out_shape=[
            shape((rows, depth)),
            shape((rows, depth)),
            shape((depth, inner)),
            shape((inner, depth)),
        ],
        compiler_params=params(),
        name="feed_own",
    )(third, cot, after, up, down)


def feed_kernel(me, third, cot, out_in, grad_in, *refs):
    slots, (out, grad, up, down) = refs[:16], refs[16:]

    @pl.when(pl.program_id(0) == 0)
    def _():
        rows = slots[0].shape[1]
        fill(up, slots[:8], me[0], rows)
        fill(down, slots[8:], me[0], rows)

    _, _, result, pushed = feed_rows(third[...], cot[...], up[0], down[0])
    out[...] = (out_in[...] + result).astype(out.dtype)
    grad[...] = grad_in[...] + pushed


def feed(me, third, cot, out, grad, slots, dtype):
    rows, depth = third.shape
    arrays, specs = halves(slots)
    inner = arrays[0].shape[2]
    tile = rows_of(FEED, depth)
    return pl.pallas_call(
        feed_kernel,
        grid=(rows // FEED,),
        in_specs=[smem(), tile, tile, tile, tile] + specs,
        out_specs=[tile, tile],
        out_shape=[shape((rows, depth), dtype), shape((rows, depth))],
        scratch_shapes=[
            pltpu.VMEM((1, depth, inner), BF16),
            pltpu.VMEM((1, 8 * arrays[8].shape[1], depth), BF16),
        ],
        compiler_params=params(),
        name="feed",
    )(me, third, cot, out, grad, *arrays)


def back_kernel(
    lengths, live, third_grad, cot, after_cross, after_self, second, cross_query, looked0, mixed0,
    logs, gain1, gain2, w_out, w_co, *refs,
):
    queries, refs = refs[:4], refs[4:]
    pairs, refs = refs[:4], refs[4:]
    up_grad, mixed_grad, pair_grad, co_grad, cq_grad, out_grad, sums, total, turned = refs
    step = pl.program_id(0)
    text = TEXT

    @pl.when(step == 0)
    def _():
        total[...] = jnp.zeros_like(total)
        co_grad[...] = jnp.zeros_like(co_grad)
        cq_grad[...] = jnp.zeros_like(cq_grad)
        out_grad[...] = jnp.zeros_like(out_grad)
        sums[...] = jnp.zeros_like(sums)
        for j in range(4):
            turned[j] = pairs[j][0].T

    pulled, gain_sum, shift_sum = norm_backward(third_grad[...], after_cross[...], gain2[...])
    sums[0:1, :] += gain_sum
    sums[1:2, :] += shift_sum
    upstream = cot[...].astype(F32) + pulled
    low = upstream.astype(BF16)
    co_grad[...] += dot(looked0[...], low, TN)
    looked_grad = dot(low, w_co[...], NT).astype(BF16)
    item, _ = item_at(lengths, step * BLK)
    t0 = pl.multiple_of(item * text, text)
    alive = live[pl.ds(t0, text), :] > 0.0
    second_grad = jnp.zeros(upstream.shape, F32)
    for j in range(4):
        width = queries[j].shape[2]
        cols = slice(j * width, (j + 1) * width)
        query = cross_query[:, cols]
        grads = looked_grad[:, cols]
        keys = pairs[j][0, pl.ds(t0, text), :]
        values = pairs[j][1, pl.ds(t0, text), :]
        pieces = []
        key_sum = jnp.zeros((text, width), F32)
        value_sum = jnp.zeros((text, width), F32)
        for head in range(width // HEAD):
            row = masked(query, head_row(width, head, HEAD**-0.5))
            grad = masked(grads, head_row(width, head, 1.0))
            index = j * (width // HEAD) + head
            score = jnp.where(alive, dot(keys, row, NT), NEG)
            chance = jnp.exp(score - logs[index : index + 1, :])
            pushed = dot(values, grad, NT)
            weighted = chance * pushed
            mean = jnp.sum(weighted, axis=0, keepdims=True)
            score_grad = (weighted - chance * mean).astype(BF16)
            pieces.append(dot(turned[j, lanes_of(head), pl.ds(t0, text)], score_grad))
            key_sum = key_sum + dot(score_grad, row)
            value_sum = value_sum + dot(chance.astype(BF16), grad)
        total[j, 0, pl.ds(t0, text), :] += key_sum
        total[j, 1, pl.ds(t0, text), :] += value_sum
        query_grad = (jnp.concatenate(pieces, axis=0).T * HEAD**-0.5).astype(BF16)
        if j == 0:
            cq_grad[...] += dot(second[...], query_grad, TN)
        second_grad = second_grad + dot(query_grad, queries[j][0], NT)

    pulled, gain_sum, shift_sum = norm_backward(second_grad, after_self[...], gain1[...])
    sums[2:3, :] += gain_sum
    sums[3:4, :] += shift_sum
    upstream = upstream + pulled
    up_grad[...] = upstream
    low = upstream.astype(BF16)
    out_grad[...] += dot(mixed0[...], low, TN)
    mixed_grad[...] = dot(low, w_out[...], NT).astype(BF16)

    @pl.when(step == pl.num_programs(0) - 1)
    def _():
        pair_grad[...] = total[...].astype(BF16)


def back(
    lengths, live, third_grad, cot, after_cross, after_self, second, cross_query, looked, mixed0,
    logs, gain1, gain2, w_out, w_co, crosses, pairs,
):
    rows, depth = cot.shape
    text_rows = live.shape[0]
    width = mixed0.shape[1]
    inner = 4 * width
    tile = rows_of(BLK, depth)
    row = whole((1, depth))
    return pl.pallas_call(
        back_kernel,
        grid=(rows // BLK,),
        in_specs=[smem(), whole((text_rows, 1))]
        + [tile] * 5
        + [rows_of(BLK, inner), rows_of(BLK, width), rows_of(BLK, width)]
        + [pl.BlockSpec((inner // HEAD, BLK), lambda i: (0, i)), row, row]
        + [whole((inner, depth))] * 2
        + [at((1, depth, width), (0, 0, 0))] * 4
        + [whole((2, text_rows, width))] * 4,
        out_specs=[tile, rows_of(BLK, inner), whole((4, 2, text_rows, width))]
        + [whole((width, depth)), whole((depth, width)), whole((width, depth)), whole((8, depth))],
        out_shape=[
            shape((rows, depth)),
            shape((rows, inner), BF16),
            shape((4, 2, text_rows, width), BF16),
            shape((width, depth)),
            shape((depth, width)),
            shape((width, depth)),
            shape((8, depth)),
        ],
        scratch_shapes=[
            pltpu.VMEM((4, 2, text_rows, width), F32),
            pltpu.VMEM((4, width, text_rows), BF16),
        ],
        compiler_params=params(),
        name="back",
    )(
        lengths, live, third_grad, cot, after_cross, after_self, second, cross_query, looked,
        mixed0, logs, gain1, gain2, w_out, w_co, *crosses, *pairs,
    )


def text_kernel(text, pair_grad, *refs):
    crosses, (text_grad, kv_grad) = refs[:4], refs[4:]
    total = jnp.zeros(text_grad.shape, F32)
    for j in range(4):
        for m in range(2):
            total = total + dot(pair_grad[j, m], crosses[j][m + 1], NT)
    text_grad[...] = total
    for m in range(2):
        kv_grad[m] = dot(text[...], pair_grad[0, m], TN)


def text_back(text, pair_grad, crosses):
    text_rows, depth = text.shape
    width = pair_grad.shape[3]
    return pl.pallas_call(
        text_kernel,
        in_specs=[vmem()] * 6,
        out_specs=[vmem()] * 2,
        out_shape=[shape((text_rows, depth)), shape((2, depth, width))],
        compiler_params=params(),
        name="text_back",
    )(text, pair_grad, *crosses)


def self_back_pair(qb, kb, diag, qkv, rows, grads, logs, means, turned, query_sum, key_sum, value_sum):
    q0 = pl.multiple_of(qb * BLK, BLK)
    k0 = pl.multiple_of(kb * BLK, BLK)
    keys = qkv[1, pl.ds(k0, BLK), :]
    values = qkv[2, pl.ds(k0, BLK), :]
    more_keys = 0.0
    more_values = 0.0
    for head in range(rows.shape[0]):
        score = dot(keys, rows[head], NT)
        if diag:
            score = jnp.where(causal(), score, NEG)
        chance = jnp.exp(score - logs[head : head + 1, pl.ds(q0, BLK)])
        pushed = dot(values, grads[head], NT)
        score_grad = (chance * (pushed - means[head : head + 1, :])).astype(BF16)
        query_sum[lanes_of(head), :] += dot(turned[lanes_of(head), pl.ds(k0, BLK)], score_grad)
        more_keys = more_keys + dot(score_grad, rows[head])
        more_values = more_values + dot(chance.astype(BF16), grads[head])
    key_sum[pl.ds(k0, BLK), :] += more_keys
    value_sum[pl.ds(k0, BLK), :] += more_values


def self_back_body(
    lengths, qkv, mixed, out_grad, logs, weights, triple, turned, rows, grads, means, query_sum,
    key_sum, value_sum,
):
    row_count, width = mixed.shape
    turned[...] = qkv[1].T
    key_sum[...] = jnp.zeros_like(key_sum)
    value_sum[...] = jnp.zeros_like(value_sum)

    @pl.loop(0, row_count // BLK)
    def _(qb):
        q0 = pl.multiple_of(qb * BLK, BLK)
        _, start = item_at(lengths, q0)
        query = qkv[0, pl.ds(q0, BLK), :]
        grad = out_grad[pl.ds(q0, BLK), :]
        flat = (grad.astype(F32) * mixed[pl.ds(q0, BLK), :].astype(F32)).T
        for head in range(width // HEAD):
            rows[head] = masked(query, head_row(width, head, HEAD**-0.5))
            grads[head] = masked(grad, head_row(width, head, 1.0))
            means[head : head + 1, :] = jnp.sum(flat[lanes_of(head), :], axis=0, keepdims=True)
        query_sum[...] = jnp.zeros_like(query_sum)
        rest = (qkv, rows, grads, logs, means, turned, query_sum, key_sum, value_sum)

        @pl.loop(start // BLK, qb)
        def _(kb):
            self_back_pair(qb, kb, False, *rest)

        self_back_pair(qb, qb, True, *rest)
        triple[0, pl.ds(q0, BLK), :] = (query_sum[...].T * HEAD**-0.5).astype(BF16)

    triple[1] = key_sum[...].astype(BF16)
    triple[2] = value_sum[...].astype(BF16)


def self_scratch(rows, width):
    heads = width // HEAD
    return [
        pltpu.VMEM((3, rows, width), BF16),
        pltpu.VMEM((width, rows), BF16),
        pltpu.VMEM((heads, BLK, width), BF16),
        pltpu.VMEM((heads, BLK, width), BF16),
        pltpu.VMEM((8, BLK), F32),
        pltpu.VMEM((width, BLK), F32),
        pltpu.VMEM((rows, width), F32),
        pltpu.VMEM((rows, width), F32),
    ]


def self_own_kernel(lengths, qkv, mixed, out_grad, logs, weights, first, total, qkv_grad, *scratch):
    self_back_body(lengths, qkv, mixed, out_grad, logs, weights, *scratch)
    triple = scratch[0]
    for m in range(3):
        qkv_grad[m] = dot(first[...], triple[m], TN)
    total[...] = sum(dot(triple[m], weights[m], NT) for m in range(3))


def self_own(lengths, qkv, mixed, out_grad, logs, weights, first):
    rows, depth = first.shape
    width = mixed.shape[1]
    return pl.pallas_call(
        self_own_kernel,
        grid=(1,),
        in_specs=[smem()]
        + [whole((3, rows, width)), whole((rows, width)), at((rows, width), (0, 0))]
        + [whole((8, rows)), whole((3, depth, width)), whole((rows, depth))],
        out_specs=[whole((rows, depth)), whole((3, depth, width))],
        out_shape=[shape((rows, depth)), shape((3, depth, width))],
        scratch_shapes=self_scratch(rows, width),
        compiler_params=params(),
        name="self_own",
    )(lengths, qkv, mixed, out_grad, logs, weights, first)


def self_kernel(lengths, qkv, mixed, out_grad, logs, weights, before, total, *scratch):
    self_back_body(lengths, qkv, mixed, out_grad, logs, weights, *scratch)
    triple = scratch[0]
    total[...] = before[...] + sum(dot(triple[m], weights[m], NT) for m in range(3))


def self_back(lengths, qkv, mixed, out_grad, logs, weights, before, j):
    rows, depth = before.shape
    width = mixed.shape[1]
    return pl.pallas_call(
        self_kernel,
        grid=(1,),
        in_specs=[smem()]
        + [whole((3, rows, width)), whole((rows, width)), at((rows, width), (0, j))]
        + [whole((8, rows)), whole((3, depth, width)), whole((rows, depth))],
        out_specs=whole((rows, depth)),
        out_shape=shape((rows, depth)),
        scratch_shapes=self_scratch(rows, width),
        compiler_params=params(),
        name="self_back",
    )(lengths, qkv, mixed, out_grad, logs, weights, before)


def last_kernel(first_grad, tokens, upstream, gain, token_grad, sums):
    @pl.when(pl.program_id(0) == 0)
    def _():
        sums[...] = jnp.zeros_like(sums)

    pulled, gain_sum, shift_sum = norm_backward(
        first_grad[...], tokens[...].astype(F32), gain[...]
    )
    token_grad[...] = upstream[...] + pulled
    sums[0:1, :] += gain_sum
    sums[1:2, :] += shift_sum


def last(first_grad, tokens, upstream, gain):
    rows, depth = tokens.shape
    tile = rows_of(BLK, depth)
    return pl.pallas_call(
        last_kernel,
        grid=(rows // BLK,),
        in_specs=[tile, tile, tile, whole((1, depth))],
        out_specs=[tile, whole((8, depth))],
        out_shape=[shape((rows, depth)), shape((8, depth))],
        compiler_params=params(),
        name="last",
    )(first_grad, tokens, upstream, gain)


UP = [(i, (i + 1) % 4) for i in range(4)]
DOWN = [(i, (i - 1) % 4) for i in range(4)]


def across(value, bit):
    return lax.ppermute(value, "dp", [(i, i ^ bit) for i in range(8)])


def spread(piece):
    half = piece.shape[0] // 2
    by_x = across(piece, 2)
    by_y = across(piece, 4)
    far_one = across(by_y[:half], 2)
    far_two = across(by_x[half:], 4)
    held = [piece, by_x, by_y, far_one, far_two]
    other = [across(value, 1) for value in held]
    common = [held[0], other[0], held[1], other[1], held[2], other[2]]
    return common + [held[3], other[3]], common + [held[4], other[4]]


def sliced(shard):
    rows = shard.shape[1] // SLOTS8
    half = shard.shape[0] // 2
    parts = [shard[:, s * rows : (s + 1) * rows] for s in range(SLOTS8)]
    return (
        parts[:6] + [part[:half] for part in parts[6:]],
        parts[:6] + [part[half:] for part in parts[6:]],
    )


def gather(shard, me, planar):
    if planar:
        rows = shard.shape[1] // SLOTS8
        shard = lax.dynamic_slice_in_dim(shard, me * rows, rows, 1)
    piece = shard.astype(F32)
    one = lax.ppermute(piece, "mp", UP)
    three = lax.ppermute(piece, "mp", DOWN)
    two = lax.ppermute(one, "mp", UP)
    return [spread(value) if planar else sliced(value) for value in (one, two, three)]


def scattered(value, axis):
    return lax.psum_scatter(value, "dp", scatter_dimension=axis, tiled=True)


def local(
    planar, tokens, text_states, lengths, text_mask, ln_gain, ln_shift, w_qkv, w_out, w_cross_q,
    w_cross_kv, w_cross_out, w_up, w_down, cotangent,
):
    slot_count, text_length = text_mask.shape
    place = lax.axis_index("dp") if planar else jnp.int32(0)
    me = jnp.reshape(place, (1,)).astype(jnp.int32)
    gains = [ln_gain[n : n + 1] for n in range(3)]
    shifts = [ln_shift[n : n + 1] for n in range(3)]
    text = text_states.reshape(slot_count * text_length, text_states.shape[2])
    position = lax.broadcasted_iota(jnp.int32, text_mask.shape, 1)
    live = ((text_mask == 1) | (position == 0)).astype(F32).reshape(-1, 1)
    own_qkv = jnp.transpose(w_qkv, (1, 0, 2))
    own_cross = jnp.concatenate([w_cross_q[None], jnp.transpose(w_cross_kv, (1, 0, 2))], axis=0)

    attention = gather(jnp.concatenate([own_qkv, own_cross], axis=0), place, planar)
    outer = gather(jnp.stack([w_out, w_cross_out]), place, planar)
    feeds = gather(jnp.stack([w_up, w_down]), place, planar)

    first = norm_first(tokens, gains[0], shifts[0])
    qkvs, mixeds, logs, pairs = ([None] * 4 for _ in range(4))
    weights, crosses = [own_qkv] + [None] * 3, [own_cross] + [None] * 3
    qkvs[0], mixeds[0], logs[0], pairs[0] = front_own(lengths, first, text, own_qkv, own_cross)
    for j in (1, 3, 2):
        weights[j], crosses[j], qkvs[j], mixeds[j], logs[j], pairs[j] = front(
            me, lengths, first, text, attention[j - 1]
        )
    full_out, full_co, after_self, after_cross, second, third, cross_query, looked, cross_logs = middle(
        me, lengths, live, tokens, (gains[1], shifts[1], gains[2], shifts[2]), w_out, w_cross_out,
        mixeds, crosses, pairs, outer,
    )
    out, grad, up_grad, down_grad = feed_own(third, cotangent, after_cross, w_up, w_down)
    for j in (1, 3, 2):
        out, grad = feed(
            me, third, cotangent, out, grad, feeds[j - 1], BF16 if j == 2 else F32
        )
    upstream, mixed_grad, pair_grad, co_grad, cq_grad, out_grad, sums = back(
        lengths, live, grad, cotangent, after_cross, after_self, second, cross_query, looked,
        mixeds[0], cross_logs, gains[1], gains[2], full_out, full_co, crosses, pairs,
    )
    text_grad, kv_grad = text_back(text, pair_grad, crosses)
    first_grad, qkv_grad = self_own(
        lengths, qkvs[0], mixeds[0], mixed_grad, logs[0], weights[0], first
    )
    for j in (1, 2, 3):
        first_grad = self_back(
            lengths, qkvs[j], mixeds[j], mixed_grad, logs[j], weights[j], first_grad, j
        )
    token_grad, last_sums = last(first_grad, tokens, upstream, gains[0])
    gain_grad = jnp.concatenate([last_sums[0:1], sums[2:3], sums[0:1]], axis=0)
    shift_grad = jnp.concatenate([last_sums[1:2], sums[3:4], sums[1:2]], axis=0)
    return (
        out,
        token_grad,
        text_grad.reshape(text_states.shape),
        scattered(gain_grad, 1),
        scattered(shift_grad, 1),
        jnp.transpose(scattered(qkv_grad, 1), (1, 0, 2)),
        scattered(out_grad, 0),
        scattered(cq_grad, 0),
        jnp.transpose(scattered(kv_grad, 1), (1, 0, 2)),
        scattered(co_grad, 0),
        scattered(up_grad, 0),
        scattered(down_grad, 0),
    )


def solution(mesh):
    placed = (
        P("dp", None),
        P("dp", None, None),
        P("dp"),
        P("dp", None),
        P(),
        P(),
        P(None, None, "mp"),
        P("mp", None),
        P(None, "mp"),
        P(None, None, "mp"),
        P("mp", None),
        P(None, "mp"),
        P("mp", None),
        P("dp", None),
    )
    return jax.shard_map(
        partial(local, mesh.shape["dp"] == SLOTS8),
        mesh=mesh,
        in_specs=placed,
        out_specs=(
            P("dp", None),
            P("dp", None),
            P("dp", None, None),
            P(None, "dp"),
            P(None, "dp"),
            P("dp", None, "mp"),
            P(("mp", "dp"), None),
            P("dp", "mp"),
            P("dp", None, "mp"),
            P(("mp", "dp"), None),
            P("dp", "mp"),
            P(("mp", "dp"), None),
        ),
        check_vma=False,
    )
```

```python
from functools import partial

import jax
import jax.numpy as jnp
from jax import lax
from jax.experimental import pallas as pl
from jax.experimental.pallas import tpu as pltpu
from jax.sharding import PartitionSpec as P

HEAD = 64
BLK = 256
EPS = 1e-05
NEG = -1e30
F32 = jnp.float32
BF16 = jnp.bfloat16
MIB = 1024 * 1024

NN = (((1,), (0,)), ((), ()))
NT = (((1,), (1,)), ((), ()))
TN = (((0,), (0,)), ((), ()))


def dot(a, b, dims=NN):
    return lax.dot_general(a, b, dims, preferred_element_type=F32)


def params(mib=56, semantics=None):
    return pltpu.CompilerParams(vmem_limit_bytes=mib * MIB, dimension_semantics=semantics)


def cost(us):
    return pl.CostEstimate(
        flops=int(us * 1.15e9), transcendentals=0, bytes_accessed=int(us * 3.6e6)
    )


def shape(dims, dtype=F32):
    return jax.ShapeDtypeStruct(dims, dtype)


def smem():
    return pl.BlockSpec(memory_space=pltpu.SMEM)


def whole(dims):
    rank = len(dims)
    return pl.BlockSpec(dims, lambda *_: (0,) * rank)


def at(dims, index):
    return pl.BlockSpec(dims, lambda *_: index)


def rows_of(tile, width):
    return pl.BlockSpec((tile, width), lambda i, *_: (i, 0))


def norm_stats(value):
    center = value - jnp.mean(value, axis=-1, keepdims=True)
    spread = jnp.mean(center * center, axis=-1, keepdims=True)
    inverse = lax.rsqrt(spread + EPS)
    return center * inverse, inverse


def norm_forward(value, gain, shift):
    unit, _ = norm_stats(value)
    return (unit * gain + shift).astype(BF16)


def norm_backward(incoming, value, gain):
    unit, inverse = norm_stats(value)
    scaled = incoming * gain
    pushed = incoming * unit
    inner = (
        scaled
        - jnp.mean(scaled, axis=-1, keepdims=True)
        - unit * jnp.mean(scaled * unit, axis=-1, keepdims=True)
    )
    return (
        inner * inverse,
        jnp.sum(pushed, axis=0, keepdims=True),
        jnp.sum(incoming, axis=0, keepdims=True),
    )


def norm_kernel(tokens_ref, gain_ref, shift_ref, first_ref):
    first_ref[...] = norm_forward(tokens_ref[...].astype(F32), gain_ref[...], shift_ref[...])


def norm_first(tokens, gain, shift):
    rows, width = tokens.shape
    return pl.pallas_call(
        norm_kernel,
        grid=(rows // BLK,),
        in_specs=[rows_of(BLK, width), whole((1, width)), whole((1, width))],
        out_specs=rows_of(BLK, width),
        out_shape=shape((rows, width), BF16),
        name="norm_first",
        cost_estimate=cost(6),
    )(tokens, gain, shift)


def head_row(width, head, value):
    lane = lax.broadcasted_iota(jnp.int32, (1, width), 1)
    return jnp.where(lane // HEAD == head, value, 0.0)


def masked(block, row):
    return (block.astype(F32) * row).astype(BF16)


def item_at(lengths, place):
    item, start, end = 0, 0, 0
    for slot in range(lengths.shape[0]):
        end = end + lengths[slot]
        past = end <= place
        item = item + past.astype(jnp.int32)
        start = jnp.where(past, end, start)
    return item, start


def offsets(core):
    return (0, 1 + core, 2 - core, 3)


def fill(targets, refs, chip, core):
    for ref, offset in zip(refs, offsets(core)):
        rows = ref.shape[1]
        place = pl.multiple_of((chip ^ offset) * rows, rows)
        for k, target in enumerate(targets):
            target[pl.ds(place, rows), :] = ref[k].astype(BF16)


def fill_two(first, second, mine, other, me, flip=1):
    chip, core = me[0], me[1]

    @pl.when(core == 0)
    def _():
        fill(first, mine, chip, 0)
        fill(second, other, chip, 1)

    @pl.when(core == 1)
    def _():
        fill(second[::flip], mine, chip, 1)
        fill(first[::flip], other, chip, 0)


def planes(ref):
    return [ref.at[k] for k in range(ref.shape[0])]


def causal():
    shape2 = (BLK, BLK)
    return lax.broadcasted_iota(jnp.int32, shape2, 0) <= lax.broadcasted_iota(
        jnp.int32, shape2, 1
    )


def lanes_of(head):
    return slice(head * HEAD, (head + 1) * HEAD)


def self_block(qb, count, qkv, turned, mixed, logs):
    q0 = pl.multiple_of(qb * BLK, BLK)
    k0 = pl.multiple_of((qb - (count - 1)) * BLK, BLK)
    width = qkv.shape[2]
    query = qkv[0, pl.ds(q0, BLK), :]
    diag = qkv[1, pl.ds(q0, BLK), :]
    pre_len = (count - 1) * BLK
    keep = causal()
    pieces = []
    for head in range(width // HEAD):
        part = masked(query, head_row(width, head, HEAD**-0.5))
        near = jnp.where(keep, dot(diag, part, NT), NEG)
        peak = jnp.max(near, axis=0, keepdims=True)
        if pre_len:
            far = dot(qkv[1, pl.ds(k0, pre_len), :], part, NT)
            peak = jnp.maximum(peak, jnp.max(far, axis=0, keepdims=True))
        near = jnp.exp(near - peak)
        total = jnp.sum(near, axis=0, keepdims=True)
        result = dot(turned[lanes_of(head), pl.ds(q0, BLK)], near.astype(BF16))
        if pre_len:
            far = jnp.exp(far - peak)
            total = total + jnp.sum(far, axis=0, keepdims=True)
            result = result + dot(
                turned[lanes_of(head), pl.ds(k0, pre_len)], far.astype(BF16)
            )
        pieces.append(result * (1.0 / total))
        logs[head : head + 1, pl.ds(q0, BLK)] = peak + jnp.log(total)
    mixed[pl.ds(q0, BLK), :] = jnp.concatenate(pieces, axis=0).T.astype(BF16)


def front_body(lengths, first, weights, qkv, mixed, logs, turned):
    rows = first.shape[0]
    for m in range(3):
        qkv[m] = dot(first[...], weights[m]).astype(BF16)
    turned[...] = qkv[2].T

    @pl.loop(0, rows // BLK)
    def _(qb):
        _, start = item_at(lengths, qb * BLK)
        count = qb - start // BLK + 1
        for n in range(1, 5):

            @pl.when(count == n)
            def _():
                self_block(qb, n, qkv, turned, mixed, logs)


def front_kernel(own, me, lengths, first, *refs):
    slots, (weights, *rest) = refs[:4], refs[4:]
    core = me[1] if own else 1 - me[1]
    fill(planes(weights), slots, me[0], core)
    front_body(lengths, first, weights, *rest)


def front_two_kernel(me, lengths, first, *refs):
    mine, other, (weights, cross, *rest) = refs[:4], refs[4:8], refs[8:]
    fill_two(planes(weights), planes(cross), mine, other, me)
    front_body(lengths, first, weights, *rest)


def vmem():
    return pl.BlockSpec(memory_space=pltpu.VMEM)


def front_call(kernel, name, us, prefix, first, arrays, weight_count):
    rows, depth = first.shape
    width = arrays[0].shape[2]
    outs = [shape((3, depth, width), BF16)] * weight_count + [
        shape((3, rows, width), BF16),
        shape((rows, width), BF16),
        shape((8, rows), F32),
    ]
    return pl.pallas_call(
        kernel,
        in_specs=[smem()] * len(prefix) + [vmem()] * (1 + len(arrays)),
        out_specs=[vmem()] * len(outs),
        out_shape=outs,
        scratch_shapes=[pltpu.VMEM((width, rows), BF16)],
        compiler_params=params(),
        name=name,
        cost_estimate=cost(us),
    )(*prefix, first, *arrays)


def front_own(lengths, first, weights):
    return front_call(front_body, "front_own", 12, (lengths,), first, [weights], 0)


def front(own, me, lengths, first, arrays):
    kernel = partial(front_kernel, own)
    return front_call(kernel, "front", 14, (me, lengths), first, arrays, 1)


def front_two(me, lengths, first, arrays):
    return front_call(front_two_kernel, "front_two", 15, (me, lengths), first, arrays, 2)


def text_front_kernel(me, text, own, two, *refs):
    mine, other, (cross_a, cross_b, *pairs) = refs[:4], refs[4:8], refs[8:]
    fill(planes(cross_a), mine, me[0], me[1])
    fill(planes(cross_b), other, me[0], 1 - me[1])
    for pair, cross in zip(pairs, (own, cross_a, two, cross_b)):
        for m in range(2):
            pair[m] = dot(text[...], cross[m + 1]).astype(BF16)


def text_front(me, text, own, two, arrays):
    rows = text.shape[0]
    width = own.shape[2]
    outs = [shape(own.shape, BF16)] * 2 + [shape((2, rows, width), BF16)] * 4
    return pl.pallas_call(
        text_front_kernel,
        in_specs=[smem()] + [vmem()] * 11,
        out_specs=[vmem()] * 6,
        out_shape=outs,
        compiler_params=params(),
        name="text_front",
        cost_estimate=cost(8),
    )(me, text, own, two, *arrays)


def middle_kernel(me, lengths, live, tokens, gain1, shift1, gain2, shift2, own_out, own_co, *refs):
    mixed, refs = refs[:4], refs[4:]
    queries, refs = refs[:4], refs[4:]
    pairs, refs = refs[:4], refs[4:]
    mine, other, refs = refs[:4], refs[4:8], refs[8:]
    w_out, w_co, after_self, after_cross, second, third, cross_query, looked, logs, turned = refs
    step = pl.program_id(0)

    @pl.when(step == 0)
    def _():
        width = own_out.shape[0]
        w_out[:width, :] = own_out[...]
        w_co[:width, :] = own_co[...]
        parts = [
            [target.at[pl.ds((j + 1) * width, width)] for j in range(3)] for target in (w_out, w_co)
        ]
        fill_two(*parts, mine, other, me, flip=-1)
        for j in range(4):
            turned[j] = pairs[j][1].T

    part = jnp.concatenate([ref[...] for ref in mixed], axis=1)
    residual = tokens[...].astype(F32) + dot(part, w_out[...])
    after_self[...] = residual
    normed = norm_forward(residual, gain1[...], shift1[...])
    second[...] = normed
    text = TEXT
    item, _ = item_at(lengths, step * BLK)
    t0 = pl.multiple_of(item * text, text)
    alive = live[pl.ds(t0, text), :] > 0.0
    for j in range(4):
        query = dot(normed, queries[j][0]).astype(BF16)
        width = query.shape[1]
        cols = slice(j * width, (j + 1) * width)
        cross_query[:, cols] = query
        keys = pairs[j][0, pl.ds(t0, text), :]
        pieces = []
        for head in range(width // HEAD):
            row = masked(query, head_row(width, head, HEAD**-0.5))
            score = jnp.where(alive, dot(keys, row, NT), NEG)
            peak = jnp.max(score, axis=0, keepdims=True)
            score = jnp.exp(score - peak)
            total = jnp.sum(score, axis=0, keepdims=True)
            result = dot(turned[j, lanes_of(head), pl.ds(t0, text)], score.astype(BF16))
            pieces.append(result * (1.0 / total))
            index = j * (width // HEAD) + head
            logs[index : index + 1, :] = peak + jnp.log(total)
        looked[:, cols] = jnp.concatenate(pieces, axis=0).T.astype(BF16)
    residual = residual + dot(looked[...], w_co[...])
    after_cross[...] = residual
    third[...] = norm_forward(residual, gain2[...], shift2[...])


TEXT = 128


def middle(me, lengths, live, tokens, norms, own_out, own_co, mixed, crosses, pairs, arrays):
    rows, depth = tokens.shape
    width = own_out.shape[0]
    text_rows = live.shape[0]
    inner = 4 * width
    row = whole((1, depth))
    return pl.pallas_call(
        middle_kernel,
        grid=(rows // BLK,),
        in_specs=[smem(), smem(), whole((text_rows, 1)), rows_of(BLK, depth)]
        + [row] * 4
        + [whole((width, depth))] * 2
        + [rows_of(BLK, width)] * 4
        + [at((1, depth, width), (0, 0, 0))] * 4
        + [whole((2, text_rows, width))] * 4
        + [whole(arrays[0].shape)] * 8,
        out_specs=[whole((inner, depth))] * 2
        + [rows_of(BLK, depth)] * 4
        + [rows_of(BLK, inner)] * 2
        + [pl.BlockSpec((inner // HEAD, BLK), lambda i: (0, i))],
        out_shape=[shape((inner, depth), BF16)] * 2
        + [shape((rows, depth)), shape((rows, depth))]
        + [shape((rows, depth), BF16)] * 2
        + [shape((rows, inner), BF16)] * 2
        + [shape((inner // HEAD, rows))],
        scratch_shapes=[pltpu.VMEM((4, width, text_rows), BF16)],
        compiler_params=params(),
        name="middle",
        cost_estimate=cost(43),
    )(me, lengths, live, tokens, *norms, own_out, own_co, *mixed, *crosses, *pairs, *arrays)


ROOT = 0.7978845608028654
CUBE = 0.044715


def gelu_both(value):
    square = value * value
    bend = jnp.tanh(value * (ROOT + (ROOT * CUBE) * square))
    half = 0.5 + 0.5 * bend
    slope = half + (0.5 * value) * (1.0 - bend * bend) * (ROOT + (3.0 * ROOT * CUBE) * square)
    return value * half, slope


def feed_rows(third, cot, up, down):
    pre_act = dot(third, up)
    hidden, slope = gelu_both(pre_act)
    hidden = hidden.astype(BF16)
    pre_grad = (dot(cot, down, NT) * slope).astype(BF16)
    return hidden, pre_grad, dot(hidden, down), dot(pre_grad, up, NT)


def feed_own_kernel(third, cot, after, up, down, out, grad, both):
    hidden, pre_grad, result, pushed = feed_rows(third[...], cot[...], up[...], down[...])
    out[...] = after[...] + result
    grad[...] = pushed
    first = pl.program_id(0) == 0
    more_up = dot(third[...], pre_grad, TN)
    more_down = dot(hidden, cot[...], TN)

    @pl.when(first)
    def _():
        both[0] = more_up
        both[1] = more_down

    @pl.when(jnp.logical_not(first))
    def _():
        both[0] += more_up
        both[1] += more_down


FEED = 320


def feed_own(third, cot, after, up, down):
    rows, depth = third.shape
    inner = up.shape[1]
    tile = rows_of(FEED, depth)
    return pl.pallas_call(
        feed_own_kernel,
        grid=(rows // FEED,),
        in_specs=[tile, tile, tile, whole((depth, inner)), whole((inner, depth))],
        out_specs=[tile, tile, whole((2, depth, inner))],
        out_shape=[shape((rows, depth)), shape((rows, depth)), shape((2, depth, inner))],
        compiler_params=params(),
        name="feed_own",
        cost_estimate=cost(32),
    )(third, cot, after, up, down)


def feed_kernel(kind, me, third, cot, out_in, grad_in, *refs):
    slots, (out, grad, both) = refs[:-3], refs[-3:]

    @pl.when(pl.program_id(0) == 0)
    def _():
        up, down = planes(both)
        if kind == 2:
            fill_two([up], [down], slots[:4], slots[4:], me)
        else:
            fill([up, down], slots, me[0], me[1] if kind == 0 else 1 - me[1])

    _, _, result, pushed = feed_rows(third[...], cot[...], both[0], both[1])
    out[...] = (out_in[...] + result).astype(out.dtype)
    grad[...] = grad_in[...] + pushed


def feed(kind, me, third, cot, out, grad, arrays, dtype):
    rows, depth = third.shape
    inner = arrays[0].shape[2]
    tile = rows_of(FEED, depth)
    return pl.pallas_call(
        partial(feed_kernel, kind),
        grid=(rows // FEED,),
        in_specs=[smem(), tile, tile, tile, tile] + [whole(arrays[0].shape)] * len(arrays),
        out_specs=[tile, tile],
        out_shape=[shape((rows, depth), dtype), shape((rows, depth))],
        scratch_shapes=[pltpu.VMEM((2, depth, inner), BF16)],
        compiler_params=params(),
        name="feed",
        cost_estimate=cost(18),
    )(me, third, cot, out, grad, *arrays)


def back_kernel(
    lengths, live, third_grad, cot, after_cross, after_self, cross_query, looked0, mixed0, logs,
    gain1, gain2, w_out, w_co, *refs,
):
    queries, refs = refs[:4], refs[4:]
    pairs, refs = refs[:4], refs[4:]
    up_grad, mixed_grad, pair_grad, row_grads, query_grads, sums, total, turned = refs
    step = pl.program_id(0)
    text = TEXT

    @pl.when(step == 0)
    def _():
        total[...] = jnp.zeros_like(total)
        row_grads[...] = jnp.zeros_like(row_grads)
        sums[...] = jnp.zeros_like(sums)
        for j in range(4):
            turned[j] = pairs[j][0].T

    pulled, gain_sum, shift_sum = norm_backward(third_grad[...], after_cross[...], gain2[...])
    sums[0:1, :] += gain_sum
    sums[1:2, :] += shift_sum
    upstream = cot[...].astype(F32) + pulled
    low = upstream.astype(BF16)
    row_grads[1] += dot(looked0[...], low, TN)
    looked_grad = dot(low, w_co[...], NT).astype(BF16)
    item, _ = item_at(lengths, step * BLK)
    t0 = pl.multiple_of(item * text, text)
    alive = live[pl.ds(t0, text), :] > 0.0
    second_grad = jnp.zeros(upstream.shape, F32)
    for j in range(4):
        width = queries[j].shape[2]
        cols = slice(j * width, (j + 1) * width)
        query = cross_query[:, cols]
        grads = looked_grad[:, cols]
        keys = pairs[j][0, pl.ds(t0, text), :]
        values = pairs[j][1, pl.ds(t0, text), :]
        pieces = []
        key_sum = jnp.zeros((text, width), F32)
        value_sum = jnp.zeros((text, width), F32)
        for head in range(width // HEAD):
            row = masked(query, head_row(width, head, HEAD**-0.5))
            grad = masked(grads, head_row(width, head, 1.0))
            index = j * (width // HEAD) + head
            score = jnp.where(alive, dot(keys, row, NT), NEG)
            chance = jnp.exp(score - logs[index : index + 1, :])
            pushed = dot(values, grad, NT)
            weighted = chance * pushed
            mean = jnp.sum(weighted, axis=0, keepdims=True)
            score_grad = (weighted - chance * mean).astype(BF16)
            pieces.append(dot(turned[j, lanes_of(head), pl.ds(t0, text)], score_grad))
            key_sum = key_sum + dot(score_grad, row)
            value_sum = value_sum + dot(chance.astype(BF16), grad)
        total[j, 0, pl.ds(t0, text), :] += key_sum
        total[j, 1, pl.ds(t0, text), :] += value_sum
        query_grad = (jnp.concatenate(pieces, axis=0).T * HEAD**-0.5).astype(BF16)
        if j == 0:
            query_grads[...] = query_grad
        second_grad = second_grad + dot(query_grad, queries[j][0], NT)

    pulled, gain_sum, shift_sum = norm_backward(second_grad, after_self[...], gain1[...])
    sums[2:3, :] += gain_sum
    sums[3:4, :] += shift_sum
    upstream = upstream + pulled
    up_grad[...] = upstream
    low = upstream.astype(BF16)
    row_grads[0] += dot(mixed0[...], low, TN)
    mixed_grad[...] = dot(low, w_out[...], NT).astype(BF16)

    @pl.when(step == pl.num_programs(0) - 1)
    def _():
        pair_grad[...] = total[...].astype(BF16)


def back(
    lengths, live, third_grad, cot, after_cross, after_self, cross_query, looked, mixed0, logs,
    gain1, gain2, w_out, w_co, crosses, pairs,
):
    rows, depth = cot.shape
    text_rows = live.shape[0]
    width = mixed0.shape[1]
    inner = 4 * width
    tile = rows_of(BLK, depth)
    row = whole((1, depth))
    return pl.pallas_call(
        back_kernel,
        grid=(rows // BLK,),
        in_specs=[smem(), whole((text_rows, 1))]
        + [tile] * 4
        + [rows_of(BLK, inner), rows_of(BLK, width), rows_of(BLK, width)]
        + [pl.BlockSpec((inner // HEAD, BLK), lambda i: (0, i)), row, row]
        + [whole((inner, depth))] * 2
        + [at((1, depth, width), (0, 0, 0))] * 4
        + [whole((2, text_rows, width))] * 4,
        out_specs=[tile, rows_of(BLK, inner), whole((4, 2, text_rows, width))]
        + [whole((2, width, depth)), rows_of(BLK, width), whole((8, depth))],
        out_shape=[
            shape((rows, depth)),
            shape((rows, inner), BF16),
            shape((4, 2, text_rows, width), BF16),
            shape((2, width, depth)),
            shape((rows, width), BF16),
            shape((8, depth)),
        ],
        scratch_shapes=[
            pltpu.VMEM((4, 2, text_rows, width), F32),
            pltpu.VMEM((4, width, text_rows), BF16),
        ],
        compiler_params=params(),
        name="back",
        cost_estimate=cost(53),
    )(
        lengths, live, third_grad, cot, after_cross, after_self, cross_query, looked, mixed0, logs,
        gain1, gain2, w_out, w_co, *crosses, *pairs,
    )


def text_kernel(text, pair_grad, second, query_grad, *refs):
    crosses, (text_grad, cross_grad) = refs[:4], refs[4:]
    total = jnp.zeros(text_grad.shape, F32)
    for j in range(4):
        for m in range(2):
            total = total + dot(pair_grad[j, m], crosses[j][m + 1], NT)
    text_grad[...] = total
    cross_grad[0] = dot(second[...], query_grad[...], TN)
    for m in range(2):
        cross_grad[m + 1] = dot(text[...], pair_grad[0, m], TN)


def text_back(text, pair_grad, second, query_grad, crosses):
    text_rows, depth = text.shape
    width = pair_grad.shape[3]
    return pl.pallas_call(
        text_kernel,
        in_specs=[vmem()] * 8,
        out_specs=[vmem()] * 2,
        out_shape=[shape((text_rows, depth)), shape((3, depth, width))],
        compiler_params=params(),
        name="text_back",
        cost_estimate=cost(9),
    )(text, pair_grad, second, query_grad, *crosses)


def self_back_pair(qb, kb, diag, qkv, rows, grads, logs, means, turned, query_sum, key_sum, value_sum):
    q0 = pl.multiple_of(qb * BLK, BLK)
    k0 = pl.multiple_of(kb * BLK, BLK)
    keys = qkv[1, pl.ds(k0, BLK), :]
    values = qkv[2, pl.ds(k0, BLK), :]
    more_keys = 0.0
    more_values = 0.0
    for head in range(rows.shape[0]):
        score = dot(keys, rows[head], NT)
        if diag:
            score = jnp.where(causal(), score, NEG)
        chance = jnp.exp(score - logs[head : head + 1, pl.ds(q0, BLK)])
        pushed = dot(values, grads[head], NT)
        score_grad = (chance * (pushed - means[head : head + 1, :])).astype(BF16)
        query_sum[lanes_of(head), :] += dot(turned[lanes_of(head), pl.ds(k0, BLK)], score_grad)
        more_keys = more_keys + dot(score_grad, rows[head])
        more_values = more_values + dot(chance.astype(BF16), grads[head])
    key_sum[pl.ds(k0, BLK), :] += more_keys
    value_sum[pl.ds(k0, BLK), :] += more_values


def self_back_body(
    lengths, qkv, mixed, out_grad, logs, weights, triple, turned, rows, grads, means, query_sum,
    key_sum, value_sum,
):
    row_count, width = mixed.shape
    turned[...] = qkv[1].T
    key_sum[...] = jnp.zeros_like(key_sum)
    value_sum[...] = jnp.zeros_like(value_sum)

    @pl.loop(0, row_count // BLK)
    def _(qb):
        q0 = pl.multiple_of(qb * BLK, BLK)
        _, start = item_at(lengths, q0)
        query = qkv[0, pl.ds(q0, BLK), :]
        grad = out_grad[pl.ds(q0, BLK), :]
        flat = (grad.astype(F32) * mixed[pl.ds(q0, BLK), :].astype(F32)).T
        for head in range(width // HEAD):
            rows[head] = masked(query, head_row(width, head, HEAD**-0.5))
            grads[head] = masked(grad, head_row(width, head, 1.0))
            means[head : head + 1, :] = jnp.sum(flat[lanes_of(head), :], axis=0, keepdims=True)
        query_sum[...] = jnp.zeros_like(query_sum)
        rest = (qkv, rows, grads, logs, means, turned, query_sum, key_sum, value_sum)

        @pl.loop(start // BLK, qb)
        def _(kb):
            self_back_pair(qb, kb, False, *rest)

        self_back_pair(qb, qb, True, *rest)
        triple[0, pl.ds(q0, BLK), :] = (query_sum[...].T * HEAD**-0.5).astype(BF16)

    triple[1] = key_sum[...].astype(BF16)
    triple[2] = value_sum[...].astype(BF16)


def self_scratch(rows, width):
    heads = width // HEAD
    return [
        pltpu.VMEM((3, rows, width), BF16),
        pltpu.VMEM((width, rows), BF16),
        pltpu.VMEM((heads, BLK, width), BF16),
        pltpu.VMEM((heads, BLK, width), BF16),
        pltpu.VMEM((8, BLK), F32),
        pltpu.VMEM((width, BLK), F32),
        pltpu.VMEM((rows, width), F32),
        pltpu.VMEM((rows, width), F32),
    ]


def self_own_kernel(me, lengths, qkv, mixed, out_grad, logs, weights, first, total, keep, send, *scratch):
    self_back_body(lengths, qkv, mixed, out_grad, logs, weights, *scratch[:-1])
    triple, whole_grad = scratch[0], scratch[-1]
    for m in range(3):
        whole_grad[m] = dot(first[...], triple[m], TN)
    put_pieces(whole_grad, keep, send, me)
    total[...] = sum(dot(triple[m], weights[m], NT) for m in range(3))


def put_pieces(source, keep, send, me):
    chip, core = me[0], me[1]
    rows = keep.shape[2]
    for target, owner in ((keep, core), (send, 1 - core)):
        for index, offset in enumerate((0, 2 - owner, 1 + owner, 3)):
            place = pl.multiple_of(((chip ^ offset) * 2 + owner) * rows, rows)
            for k in range(keep.shape[1]):
                target[index, k] = source[k, pl.ds(place, rows), :]


def self_own(me, lengths, qkv, mixed, out_grad, logs, weights, first):
    rows, depth = first.shape
    width = mixed.shape[1]
    pieces = (4, 3, depth // 8, width)
    return pl.pallas_call(
        self_own_kernel,
        grid=(1,),
        in_specs=[smem(), smem()]
        + [whole((3, rows, width)), whole((rows, width)), at((rows, width), (0, 0))]
        + [whole((8, rows)), whole((3, depth, width)), whole((rows, depth))],
        out_specs=[whole((rows, depth)), whole(pieces), whole(pieces)],
        out_shape=[shape((rows, depth)), shape(pieces), shape(pieces)],
        scratch_shapes=self_scratch(rows, width) + [pltpu.VMEM((3, depth, width), F32)],
        compiler_params=params(),
        name="self_own",
        cost_estimate=cost(20),
    )(me, lengths, qkv, mixed, out_grad, logs, weights, first)


def self_kernel(lengths, qkv, mixed, out_grad, logs, weights, before, total, *scratch):
    self_back_body(lengths, qkv, mixed, out_grad, logs, weights, *scratch)
    triple = scratch[0]
    total[...] = before[...] + sum(dot(triple[m], weights[m], NT) for m in range(3))


def self_back(lengths, qkv, mixed, out_grad, logs, weights, before, j):
    rows, depth = before.shape
    width = mixed.shape[1]
    return pl.pallas_call(
        self_kernel,
        grid=(1,),
        in_specs=[smem()]
        + [whole((3, rows, width)), whole((rows, width)), at((rows, width), (0, j))]
        + [whole((8, rows)), whole((3, depth, width)), whole((rows, depth))],
        out_specs=whole((rows, depth)),
        out_shape=shape((rows, depth)),
        scratch_shapes=self_scratch(rows, width),
        compiler_params=params(),
        name="self_back",
        cost_estimate=cost(17.5),
    )(lengths, qkv, mixed, out_grad, logs, weights, before)


def last_kernel(first_grad, tokens, upstream, gain, token_grad, sums):
    @pl.when(pl.program_id(0) == 0)
    def _():
        sums[...] = jnp.zeros_like(sums)

    pulled, gain_sum, shift_sum = norm_backward(
        first_grad[...], tokens[...].astype(F32), gain[...]
    )
    token_grad[...] = upstream[...] + pulled
    sums[0:1, :] += gain_sum
    sums[1:2, :] += shift_sum


def last(first_grad, tokens, upstream, gain):
    rows, depth = tokens.shape
    tile = rows_of(BLK, depth)
    return pl.pallas_call(
        last_kernel,
        grid=(rows // BLK,),
        in_specs=[tile, tile, tile, whole((1, depth))],
        out_specs=[tile, whole((8, depth))],
        out_shape=[shape((rows, depth)), shape((8, depth))],
        compiler_params=params(),
        name="last",
        cost_estimate=cost(10),
    )(first_grad, tokens, upstream, gain)


DP = 8
MP = 4


def ring(step):
    pairs = []
    for i in range(DP):
        for z in range(MP):
            to = (z + (step if i % 2 == 0 else -step)) % MP
            pairs.append((i * MP + z, i * MP + to))
    return pairs


def straight(step):
    return [(z, (z + step) % MP) for z in range(MP)]


def beside(first):
    return [(i, i ^ (2 if (i % 2 == 0) == first else 4)) for i in range(DP)]


def swap(value):
    return lax.ppermute(value, "dp", [(i, i ^ 1) for i in range(DP)])


def spread(piece):
    near = lax.ppermute(piece, "dp", beside(True))
    side = lax.ppermute(piece, "dp", beside(False))
    far = lax.ppermute(side, "dp", beside(True))
    mine = [piece, near, side, far]
    return mine, [swap(value) for value in mine]


def cut(shard, chip):
    rows = shard.shape[1] // 4
    return lax.dynamic_slice_in_dim(shard, chip * rows, rows, 1).astype(F32)


def sets(shard, other):
    def parts(value, order):
        rows = value.shape[1] // 4
        return [value[:, k * rows : (k + 1) * rows] for k in order]

    return parts(shard, (0, 1, 2, 3)), parts(other, (0, 2, 1, 3))


def gather_whole(qkv, cross, outer, feeds):
    def along(value, step):
        return lax.ppermute(value.astype(F32), "mp", straight(step))

    def joined(value):
        return jnp.concatenate([along(value[None], step) for step in (1, 2, 3)], axis=0)

    return (
        sets(along(qkv, 1), along(qkv, 3)),
        sets(along(qkv, 2), along(cross, 2)),
        sets(along(cross, 1), along(cross, 3)),
        sets(joined(outer[0]), joined(outer[1])),
        sets(along(feeds, 1), along(feeds, 3)),
        sets(along(feeds[:1], 2), along(feeds[1:], 2)),
    )


def gather(qkv, cross, outer, feeds, chip, core):
    axes = ("dp", "mp")
    own_qkv, own_cross = cut(qkv, chip), cut(cross, chip)
    own_outer = cut(lax.dynamic_slice_in_dim(outer, core, 1, 0), chip)
    own_feeds = cut(feeds, chip)
    qkv_one = lax.ppermute(own_qkv, axes, ring(1))
    cross_one = lax.ppermute(own_cross, axes, ring(1))
    two = lax.ppermute(jnp.where(core == 0, qkv_one, cross_one), axes, ring(1))
    outer_one = lax.ppermute(own_outer, "mp", straight(1))
    outer_three = lax.ppermute(own_outer, "mp", straight(3))
    outer_two = lax.ppermute(outer_one, "mp", straight(1))
    feed_one = lax.ppermute(own_feeds, axes, ring(1))
    feed_two = lax.ppermute(lax.dynamic_slice_in_dim(feed_one, core, 1, 0), axes, ring(1))
    outers = jnp.concatenate([outer_one, outer_two, outer_three], axis=0)
    return [spread(piece) for piece in (qkv_one, two, cross_one, outers, feed_one, feed_two)]


def scattered(value, axis):
    return lax.psum_scatter(value, "dp", scatter_dimension=axis, tiled=True)


def pair_sum(keep, send):
    part = keep + swap(send)
    part = part[:2] + lax.ppermute(part[2:], "dp", beside(True))
    return part[0] + lax.ppermute(part[1], "dp", beside(False))


def plane_sum(value):
    for bit in (1, 2, 4):
        value = value + lax.ppermute(value, "dp", [(i, i ^ bit) for i in range(DP)])
    return value


def local(
    planar, tokens, text_states, lengths, text_mask, ln_gain, ln_shift, w_qkv, w_out, w_cross_q,
    w_cross_kv, w_cross_out, w_up, w_down, cotangent,
):
    slot_count, text_length = text_mask.shape
    place = lax.axis_index("dp") if planar else jnp.int32(0)
    chip, core = place // 2, place % 2
    me = jnp.stack([chip, core]).astype(jnp.int32)
    gains = [ln_gain[n : n + 1] for n in range(3)]
    shifts = [ln_shift[n : n + 1] for n in range(3)]
    text = text_states.reshape(slot_count * text_length, text_states.shape[2])
    position = lax.broadcasted_iota(jnp.int32, text_mask.shape, 1)
    live = ((text_mask == 1) | (position == 0)).astype(F32).reshape(-1, 1)
    own_qkv = jnp.transpose(w_qkv, (1, 0, 2))
    own_cross = jnp.concatenate([w_cross_q[None], jnp.transpose(w_cross_kv, (1, 0, 2))], axis=0)
    shards = (own_qkv, own_cross, jnp.stack([w_out, w_cross_out]), jnp.stack([w_up, w_down]))
    g_qkv, g_two, g_cross, g_outer, g_feed, g_feed_two = (
        gather(*shards, chip, core) if planar else gather_whole(*shards)
    )

    first = norm_first(tokens, gains[0], shifts[0])
    qkvs, mixeds, logs, weights = ([None] * 4 for _ in range(4))
    weights[0] = own_qkv
    qkvs[0], mixeds[0], logs[0] = front_own(lengths, first, own_qkv)
    weights[1], qkvs[1], mixeds[1], logs[1] = front(True, me, lengths, first, g_qkv[0])
    weights[3], qkvs[3], mixeds[3], logs[3] = front(False, me, lengths, first, g_qkv[1])
    weights[2], cross_two, qkvs[2], mixeds[2], logs[2] = front_two(
        me, lengths, first, g_two[0] + g_two[1]
    )
    cross_a, cross_b, *pairs = text_front(
        me, text, own_cross, cross_two, g_cross[0] + g_cross[1]
    )
    crosses = [own_cross, cross_a, cross_two, cross_b]
    full_out, full_co, after_self, after_cross, second, third, cross_query, looked, cross_logs = middle(
        me, lengths, live, tokens, (gains[1], shifts[1], gains[2], shifts[2]), w_out, w_cross_out,
        mixeds, crosses, pairs, g_outer[0] + g_outer[1],
    )
    out, grad, both_grad = feed_own(third, cotangent, after_cross, w_up, w_down)
    out, grad = feed(0, me, third, cotangent, out, grad, g_feed[0], F32)
    out, grad = feed(1, me, third, cotangent, out, grad, g_feed[1], F32)
    out, grad = feed(
        2, me, third, cotangent, out, grad, g_feed_two[0] + g_feed_two[1], BF16
    )
    upstream, mixed_grad, pair_grad, row_grads, query_grad, sums = back(
        lengths, live, grad, cotangent, after_cross, after_self, cross_query, looked, mixeds[0],
        cross_logs, gains[1], gains[2], full_out, full_co, crosses, pairs,
    )
    text_grad, cross_grad = text_back(text, pair_grad, second, query_grad, crosses)
    first_grad, keep, send = self_own(
        me, lengths, qkvs[0], mixeds[0], mixed_grad, logs[0], weights[0], first
    )
    for j in (1, 2, 3):
        first_grad = self_back(
            lengths, qkvs[j], mixeds[j], mixed_grad, logs[j], weights[j], first_grad, j
        )
    token_grad, last_sums = last(first_grad, tokens, upstream, gains[0])
    both_sum = scattered(both_grad, 1)
    row_sum = scattered(row_grads, 1)
    cross_sum = scattered(cross_grad, 1)
    norm_sums = jnp.concatenate(
        [last_sums[0:1], sums[2:3], sums[0:1], last_sums[1:2], sums[3:4], sums[1:2]], axis=0
    )
    if planar:
        qkv_sum = pair_sum(keep, send)
        width = norm_sums.shape[1] // DP
        norm_sum = lax.dynamic_slice_in_dim(plane_sum(norm_sums), place * width, width, 1)
    else:
        pieces = [part[k] for k in (0, 2, 1, 3) for part in (keep, send)]
        pieces = jnp.stack(pieces, axis=1)
        qkv_sum = scattered(jnp.reshape(pieces, own_qkv.shape), 1)
        norm_sum = scattered(norm_sums, 1)
    return (
        out,
        token_grad,
        text_grad.reshape(text_states.shape),
        norm_sum[:3],
        norm_sum[3:],
        jnp.transpose(qkv_sum, (1, 0, 2)),
        row_sum[0],
        cross_sum[0],
        jnp.transpose(cross_sum[1:], (1, 0, 2)),
        row_sum[1],
        both_sum[0],
        both_sum[1],
    )


def solution(mesh):
    placed = (
        P("dp", None),
        P("dp", None, None),
        P("dp"),
        P("dp", None),
        P(),
        P(),
        P(None, None, "mp"),
        P("mp", None),
        P(None, "mp"),
        P(None, None, "mp"),
        P("mp", None),
        P(None, "mp"),
        P("mp", None),
        P("dp", None),
    )
    return jax.shard_map(
        partial(local, mesh.shape["dp"] == DP),
        mesh=mesh,
        in_specs=placed,
        out_specs=(
            P("dp", None),
            P("dp", None),
            P("dp", None, None),
            P(None, "dp"),
            P(None, "dp"),
            P("dp", None, "mp"),
            P(("mp", "dp"), None),
            P("dp", "mp"),
            P("dp", None, "mp"),
            P(("mp", "dp"), None),
            P("dp", "mp"),
            P(("mp", "dp"), None),
        ),
        check_vma=False,
    )
```

```python
from functools import partial

import jax
import jax.numpy as jnp
from jax import lax
from jax.experimental import pallas as pl
from jax.experimental.pallas import tpu as pltpu
from jax.sharding import PartitionSpec as P

HEAD = 64
BLK = 256
EPS = 1e-05
NEG = -1e30
F32 = jnp.float32
BF16 = jnp.bfloat16
MIB = 1024 * 1024

NN = (((1,), (0,)), ((), ()))
NT = (((1,), (1,)), ((), ()))
TN = (((0,), (0,)), ((), ()))


def dot(a, b, dims=NN):
    return lax.dot_general(a, b, dims, preferred_element_type=F32)


def params(mib=56, semantics=None):
    return pltpu.CompilerParams(vmem_limit_bytes=mib * MIB, dimension_semantics=semantics)


def cost(us):
    return pl.CostEstimate(
        flops=int(us * 1.15e9), transcendentals=0, bytes_accessed=int(us * 3.6e6)
    )


def shape(dims, dtype=F32):
    return jax.ShapeDtypeStruct(dims, dtype)


def smem():
    return pl.BlockSpec(memory_space=pltpu.SMEM)


def whole(dims):
    rank = len(dims)
    return pl.BlockSpec(dims, lambda *_: (0,) * rank)


def at(dims, index):
    return pl.BlockSpec(dims, lambda *_: index)


def once(dims):
    rank = len(dims)
    return pl.BlockSpec(dims, lambda *_: (0,) * rank, pipeline_mode=pl.Buffered(1))


def anywhere():
    return pl.BlockSpec(memory_space=pl.ANY)


def launch(kernel, args, in_specs, out_specs, out_shape, scratch=(), wait=(), carry=(), **options):
    args, wait, carry = list(args), list(wait), list(carry)
    count, extra, outs = len(args), len(wait) + len(carry), len(out_shape)

    def body(*refs):
        results = refs[count + extra : count + extra + outs]
        kernel(*refs[:count], *results, *refs[count + extra + outs + len(carry) :])

    return pl.pallas_call(
        body,
        in_specs=list(in_specs) + [anywhere()] * extra,
        out_specs=list(out_specs) + [anywhere()] * len(carry),
        out_shape=list(out_shape) + [shape(value.shape, value.dtype) for value in carry],
        scratch_shapes=list(scratch),
        input_output_aliases={count + len(wait) + k: outs + k for k in range(len(carry))},
        **options,
    )(*args, *wait, *carry)


def gate(wait, carry):
    return launch(
        lambda: None, [], [], [], [], wait=wait, carry=[carry], name="gate", cost_estimate=cost(1)
    )[0]


def rows_of(tile, width):
    return pl.BlockSpec((tile, width), lambda i, *_: (i, 0))


def norm_stats(value):
    center = value - jnp.mean(value, axis=-1, keepdims=True)
    spread = jnp.mean(center * center, axis=-1, keepdims=True)
    inverse = lax.rsqrt(spread + EPS)
    return center * inverse, inverse


def norm_forward(value, gain, shift):
    unit, _ = norm_stats(value)
    return (unit * gain + shift).astype(BF16)


def norm_backward(incoming, value, gain):
    unit, inverse = norm_stats(value)
    scaled = incoming * gain
    pushed = incoming * unit
    inner = (
        scaled
        - jnp.mean(scaled, axis=-1, keepdims=True)
        - unit * jnp.mean(scaled * unit, axis=-1, keepdims=True)
    )
    return (
        inner * inverse,
        jnp.sum(pushed, axis=0, keepdims=True),
        jnp.sum(incoming, axis=0, keepdims=True),
    )


def norm_kernel(tokens_ref, gain_ref, shift_ref, first_ref):
    first_ref[...] = norm_forward(tokens_ref[...].astype(F32), gain_ref[...], shift_ref[...])


def norm_first(tokens, gain, shift):
    rows, width = tokens.shape
    return launch(
        norm_kernel,
        [tokens, gain, shift],
        [rows_of(BLK, width), whole((1, width)), whole((1, width))],
        [rows_of(BLK, width)],
        [shape((rows, width), BF16)],
        grid=(rows // BLK,),
        name="norm_first",
        cost_estimate=cost(6),
    )[0]


def head_row(width, head, value):
    lane = lax.broadcasted_iota(jnp.int32, (1, width), 1)
    return jnp.where(lane // HEAD == head, value, 0.0)


def masked(block, row):
    return (block.astype(F32) * row).astype(BF16)


def item_at(lengths, place):
    item, start, end = 0, 0, 0
    for slot in range(lengths.shape[0]):
        end = end + lengths[slot]
        past = end <= place
        item = item + past.astype(jnp.int32)
        start = jnp.where(past, end, start)
    return item, start


def offsets(core):
    return (0, 1 + core, 2 - core, 3)


def join_kernel(me, *refs):
    parts, (target, sems) = refs[:4], refs[4:]
    copies = []
    for index, (part, offset) in enumerate(zip(parts, offsets(me[1]))):
        rows = part.shape[1]
        place = pl.multiple_of((me[0] ^ offset) * rows, rows)
        for k in range(part.shape[0]):
            copies.append(
                pltpu.make_async_copy(
                    part.at[k], target.at[k, pl.ds(place, rows)], sems.at[index, k]
                )
            )
    for copy in copies:
        copy.start()
    for copy in copies:
        copy.wait()


def join(me, parts, wait):
    count, rows, width = parts[0].shape
    return launch(
        join_kernel,
        [me, *parts],
        [smem()] + [anywhere()] * 4,
        [vmem()],
        [shape((count, 4 * rows, width))],
        scratch=[pltpu.SemaphoreType.DMA((4, count))],
        wait=wait,
        compiler_params=params(24),
        name="join",
        cost_estimate=cost(2),
    )[0]


def take(targets, source, flip=1):
    for k, target in enumerate(targets[::flip]):
        target[...] = source[k].astype(BF16)


def take_two(first, second, mine, other, core, flip=1):
    @pl.when(core == 0)
    def _():
        take(first, mine)
        take(second, other)

    @pl.when(core == 1)
    def _():
        take(second, mine, flip)
        take(first, other, flip)


def planes(ref):
    return [ref.at[k] for k in range(ref.shape[0])]


def causal():
    shape2 = (BLK, BLK)
    return lax.broadcasted_iota(jnp.int32, shape2, 0) <= lax.broadcasted_iota(
        jnp.int32, shape2, 1
    )


def lanes_of(head):
    return slice(head * HEAD, (head + 1) * HEAD)


def self_block(qb, count, qkv, turned, mixed, logs):
    q0 = pl.multiple_of(qb * BLK, BLK)
    k0 = pl.multiple_of((qb - (count - 1)) * BLK, BLK)
    width = qkv.shape[2]
    query = qkv[0, pl.ds(q0, BLK), :]
    diag = qkv[1, pl.ds(q0, BLK), :]
    pre_len = (count - 1) * BLK
    keep = causal()
    pieces = []
    for head in range(width // HEAD):
        part = masked(query, head_row(width, head, HEAD**-0.5))
        near = jnp.where(keep, dot(diag, part, NT), NEG)
        peak = jnp.max(near, axis=0, keepdims=True)
        if pre_len:
            far = dot(qkv[1, pl.ds(k0, pre_len), :], part, NT)
            peak = jnp.maximum(peak, jnp.max(far, axis=0, keepdims=True))
        near = jnp.exp(near - peak)
        total = jnp.sum(near, axis=0, keepdims=True)
        result = dot(turned[lanes_of(head), pl.ds(q0, BLK)], near.astype(BF16))
        if pre_len:
            far = jnp.exp(far - peak)
            total = total + jnp.sum(far, axis=0, keepdims=True)
            result = result + dot(
                turned[lanes_of(head), pl.ds(k0, pre_len)], far.astype(BF16)
            )
        pieces.append(result * (1.0 / total))
        logs[head : head + 1, pl.ds(q0, BLK)] = peak + jnp.log(total)
    mixed[pl.ds(q0, BLK), :] = jnp.concatenate(pieces, axis=0).T.astype(BF16)


def front_body(lengths, first, weights, qkv, mixed, logs, turned):
    rows = first.shape[0]
    for m in range(3):
        qkv[m] = dot(first[...], weights[m]).astype(BF16)
    turned[...] = qkv[2].T

    @pl.loop(0, rows // BLK)
    def _(qb):
        _, start = item_at(lengths, qb * BLK)
        count = qb - start // BLK + 1
        for n in range(1, 5):

            @pl.when(count == n)
            def _():
                self_block(qb, n, qkv, turned, mixed, logs)


def front_kernel(lengths, first, shard, weights, *rest):
    take(planes(weights), shard)
    front_body(lengths, first, weights, *rest)


def front_two_kernel(me, lengths, first, mine, other, text, weights, cross, qkv, mixed, logs, pair, turned):
    take_two(planes(weights), planes(cross), mine, other, me[1])
    text_pair(pair, text, cross)
    front_body(lengths, first, weights, qkv, mixed, logs, turned)


def vmem():
    return pl.BlockSpec(memory_space=pltpu.VMEM)


def front_call(kernel, name, us, prefix, first, arrays, weight_count, more, wait, carry=()):
    rows, depth = first.shape
    width = arrays[0].shape[2]
    outs = [shape((3, depth, width), BF16)] * weight_count + [
        shape((3, rows, width), BF16),
        shape((rows, width), BF16),
        shape((8, rows), F32),
    ] + more
    return launch(
        kernel,
        [*prefix, first, *arrays],
        [smem()] * len(prefix) + [vmem()] * (1 + len(arrays)),
        [vmem()] * len(outs),
        outs,
        scratch=[pltpu.VMEM((width, rows), BF16)],
        wait=wait,
        carry=carry,
        compiler_params=params(),
        name=name,
        cost_estimate=cost(us),
    )


def front_own(lengths, first, weights, wait):
    return front_call(front_body, "front_own", 15, (lengths,), first, [weights], 0, [], wait)


def front(lengths, first, shard, wait, carry):
    return front_call(front_kernel, "front", 16, (lengths,), first, [shard], 1, [], wait, carry)


def front_two(me, lengths, first, arrays, text, wait):
    pair = shape((2, text.shape[0], arrays[0].shape[2]), BF16)
    return front_call(
        front_two_kernel, "front_two", 18, (me, lengths), first, [*arrays, text], 2, [pair], wait
    )


def text_pair(pair, text, cross):
    for m in range(2):
        pair[m] = dot(text[...], cross[m + 1]).astype(BF16)


def text_front_kernel(text, own, mine, other, cross_a, cross_b, *pairs):
    take(planes(cross_a), mine)
    take(planes(cross_b), other)
    for pair, cross in zip(pairs, (own, cross_a, cross_b)):
        text_pair(pair, text, cross)


def text_front(text, own, arrays, wait):
    rows = text.shape[0]
    width = own.shape[2]
    outs = [shape(own.shape, BF16)] * 2 + [shape((2, rows, width), BF16)] * 3
    return launch(
        text_front_kernel,
        [text, own, *arrays],
        [vmem()] * 4,
        [vmem()] * 5,
        outs,
        wait=wait,
        compiler_params=params(),
        name="text_front",
        cost_estimate=cost(7),
    )


def middle_kernel(me, lengths, live, tokens, gain1, shift1, gain2, shift2, own_out, own_co, *refs):
    mixed, refs = refs[:4], refs[4:]
    queries, refs = refs[:4], refs[4:]
    pairs, refs = refs[:4], refs[4:]
    mine, other, *refs = refs
    w_out, w_co, after_self, after_cross, second, third, cross_query, looked, logs, turned = refs
    step = pl.program_id(0)

    @pl.when(step == 0)
    def _():
        width = own_out.shape[0]
        w_out[:width, :] = own_out[...]
        w_co[:width, :] = own_co[...]
        parts = [
            [target.at[pl.ds((j + 1) * width, width)] for j in range(3)] for target in (w_out, w_co)
        ]
        take_two(*parts, mine, other, me[1], flip=-1)
        for j in range(4):
            turned[j] = pairs[j][1].T

    part = jnp.concatenate([ref[...] for ref in mixed], axis=1)
    residual = tokens[...].astype(F32) + dot(part, w_out[...])
    after_self[...] = residual
    normed = norm_forward(residual, gain1[...], shift1[...])
    second[...] = normed
    text = TEXT
    item, _ = item_at(lengths, step * BLK)
    t0 = pl.multiple_of(item * text, text)
    alive = live[pl.ds(t0, text), :] > 0.0
    for j in range(4):
        query = dot(normed, queries[j][0]).astype(BF16)
        width = query.shape[1]
        cols = slice(j * width, (j + 1) * width)
        cross_query[:, cols] = query
        keys = pairs[j][0, pl.ds(t0, text), :]
        pieces = []
        for head in range(width // HEAD):
            row = masked(query, head_row(width, head, HEAD**-0.5))
            score = jnp.where(alive, dot(keys, row, NT), NEG)
            peak = jnp.max(score, axis=0, keepdims=True)
            score = jnp.exp(score - peak)
            total = jnp.sum(score, axis=0, keepdims=True)
            result = dot(turned[j, lanes_of(head), pl.ds(t0, text)], score.astype(BF16))
            pieces.append(result * (1.0 / total))
            index = j * (width // HEAD) + head
            logs[index : index + 1, :] = peak + jnp.log(total)
        looked[:, cols] = jnp.concatenate(pieces, axis=0).T.astype(BF16)
    residual = residual + dot(looked[...], w_co[...])
    after_cross[...] = residual
    third[...] = norm_forward(residual, gain2[...], shift2[...])


TEXT = 128


def middle(me, lengths, live, tokens, norms, own_out, own_co, mixed, crosses, pairs, arrays, wait):
    rows, depth = tokens.shape
    width = own_out.shape[0]
    text_rows = live.shape[0]
    inner = 4 * width
    row = whole((1, depth))
    return launch(
        middle_kernel,
        [me, lengths, live, tokens, *norms, own_out, own_co, *mixed, *crosses, *pairs, *arrays],
        [smem(), smem(), whole((text_rows, 1)), rows_of(BLK, depth)]
        + [row] * 4
        + [once((width, depth))] * 2
        + [rows_of(BLK, width)] * 4
        + [at((1, depth, width), (0, 0, 0))] * 4
        + [whole((2, text_rows, width))] * 4
        + [once(arrays[0].shape)] * 2,
        [whole((inner, depth))] * 2
        + [rows_of(BLK, depth)] * 4
        + [rows_of(BLK, inner)] * 2
        + [pl.BlockSpec((inner // HEAD, BLK), lambda i: (0, i))],
        [shape((inner, depth), BF16)] * 2
        + [shape((rows, depth)), shape((rows, depth))]
        + [shape((rows, depth), BF16)] * 2
        + [shape((rows, inner), BF16)] * 2
        + [shape((inner // HEAD, rows))],
        scratch=[pltpu.VMEM((4, width, text_rows), BF16)],
        wait=wait,
        grid=(rows // BLK,),
        compiler_params=params(),
        name="middle",
        cost_estimate=cost(43),
    )


ROOT = 0.7978845608028654
CUBE = 0.044715


def gelu_both(value):
    square = value * value
    bend = jnp.tanh(value * (ROOT + (ROOT * CUBE) * square))
    half = 0.5 + 0.5 * bend
    slope = half + (0.5 * value) * (1.0 - bend * bend) * (ROOT + (3.0 * ROOT * CUBE) * square)
    return value * half, slope


def feed_rows(third, cot, up, down):
    pre_act = dot(third, up)
    hidden, slope = gelu_both(pre_act)
    hidden = hidden.astype(BF16)
    pre_grad = (dot(cot, down, NT) * slope).astype(BF16)
    return hidden, pre_grad, dot(hidden, down), dot(pre_grad, up, NT)


def feed_own_kernel(me, third, cot, after, up, down, out, grad, keep, send, both):
    hidden, pre_grad, result, pushed = feed_rows(third[...], cot[...], up[...], down[...])
    out[...] = after[...] + result
    grad[...] = pushed
    step = pl.program_id(0)
    more_up = dot(third[...], pre_grad, TN)
    more_down = dot(hidden, cot[...], TN)

    @pl.when(step == 0)
    def _():
        both[0] = more_up
        both[1] = more_down

    @pl.when(step > 0)
    def _():
        both[0] += more_up
        both[1] += more_down

    @pl.when(step == pl.num_programs(0) - 1)
    def _():
        put_pieces(both, keep, send, me)


def put_pieces(source, keep, send, me, first=0):
    chip, core = me[0], me[1]
    rows = source.shape[1] // 8
    for target, owner in ((keep, core), (send, 1 - core)):
        for index, offset in enumerate((0, 2 - owner, 1 + owner, 3)):
            place = pl.multiple_of(((chip ^ offset) * 2 + owner) * rows, rows)
            for k in range(source.shape[0]):
                target[index, first + k] = source[k, pl.ds(place, rows), :]


FEED = 320


def feed_own(me, third, cot, after, up, down, wait):
    rows, depth = third.shape
    inner = up.shape[1]
    tile = rows_of(FEED, depth)
    pieces = (4, 2, depth // 8, depth)
    return launch(
        feed_own_kernel,
        [me, third, cot, after, up, down],
        [smem(), tile, tile, tile, once((depth, inner)), once((inner, depth))],
        [tile, tile, once(pieces), once(pieces)],
        [shape((rows, depth)), shape((rows, depth)), shape(pieces), shape(pieces)],
        scratch=[pltpu.VMEM((2, depth, inner), F32)],
        wait=wait,
        grid=(rows // FEED,),
        compiler_params=params(),
        name="feed_own",
        cost_estimate=cost(32),
    )


def feed_pair_kernel(third, cot, out_in, grad_in, mine, other, out, grad, one, two):
    @pl.when(pl.program_id(0) == 0)
    def _():
        take(planes(one), mine)
        take(planes(two), other)

    _, _, result, pushed = feed_rows(third[...], cot[...], one[0], one[1])
    _, _, more_result, more_pushed = feed_rows(third[...], cot[...], two[0], two[1])
    out[...] = out_in[...] + (result + more_result)
    grad[...] = grad_in[...] + (pushed + more_pushed)


def feed_last_kernel(me, third, cot, out_in, grad_in, mine, other, out, grad, both):
    @pl.when(pl.program_id(0) == 0)
    def _():
        up, down = planes(both)
        take_two([up], [down], mine, other, me[1])

    _, _, result, pushed = feed_rows(third[...], cot[...], both[0], both[1])
    out[...] = (out_in[...] + result).astype(BF16)
    grad[...] = grad_in[...] + pushed


def feed_call(kernel, name, us, prefix, dtype, copies, third, cot, out, grad, arrays, wait, carry=()):
    rows, depth = third.shape
    tile = rows_of(FEED, depth)
    return launch(
        kernel,
        [*prefix, third, cot, out, grad, *arrays],
        [smem()] * len(prefix) + [tile] * 4 + [once(arrays[0].shape)] * 2,
        [tile, tile],
        [shape((rows, depth), dtype), shape((rows, depth))],
        scratch=[pltpu.VMEM((2,) + arrays[0].shape[1:], BF16)] * copies,
        wait=wait,
        carry=carry,
        grid=(rows // FEED,),
        compiler_params=params(),
        name=name,
        cost_estimate=cost(us),
    )


def feed_pair(*operands):
    return feed_call(feed_pair_kernel, "feed_pair", 30, (), F32, 2, *operands)


def feed_last(me, *operands):
    return feed_call(feed_last_kernel, "feed_last", 18, (me,), BF16, 1, *operands)


def back_kernel(
    lengths, live, third_grad, cot, after_cross, after_self, cross_query, looked0, mixed0, logs,
    gain1, gain2, w_out, w_co, *refs,
):
    queries, refs = refs[:4], refs[4:]
    pairs, refs = refs[:4], refs[4:]
    up_grad, mixed_grad, pair_grad, row_grads, query_grads, sums, total, turned = refs
    step = pl.program_id(0)
    text = TEXT

    @pl.when(step == 0)
    def _():
        total[...] = jnp.zeros_like(total)
        row_grads[...] = jnp.zeros_like(row_grads)
        sums[...] = jnp.zeros_like(sums)
        for j in range(4):
            turned[j] = pairs[j][0].T

    pulled, gain_sum, shift_sum = norm_backward(third_grad[...], after_cross[...], gain2[...])
    sums[0:1, :] += gain_sum
    sums[1:2, :] += shift_sum
    upstream = cot[...].astype(F32) + pulled
    low = upstream.astype(BF16)
    row_grads[1] += dot(looked0[...], low, TN)
    looked_grad = dot(low, w_co[...], NT).astype(BF16)
    item, _ = item_at(lengths, step * BLK)
    t0 = pl.multiple_of(item * text, text)
    alive = live[pl.ds(t0, text), :] > 0.0
    second_grad = jnp.zeros(upstream.shape, F32)
    for j in range(4):
        width = queries[j].shape[2]
        cols = slice(j * width, (j + 1) * width)
        query = cross_query[:, cols]
        grads = looked_grad[:, cols]
        keys = pairs[j][0, pl.ds(t0, text), :]
        values = pairs[j][1, pl.ds(t0, text), :]
        pieces = []
        key_sum = jnp.zeros((text, width), F32)
        value_sum = jnp.zeros((text, width), F32)
        for head in range(width // HEAD):
            row = masked(query, head_row(width, head, HEAD**-0.5))
            grad = masked(grads, head_row(width, head, 1.0))
            index = j * (width // HEAD) + head
            score = jnp.where(alive, dot(keys, row, NT), NEG)
            chance = jnp.exp(score - logs[index : index + 1, :])
            pushed = dot(values, grad, NT)
            weighted = chance * pushed
            mean = jnp.sum(weighted, axis=0, keepdims=True)
            score_grad = (weighted - chance * mean).astype(BF16)
            pieces.append(dot(turned[j, lanes_of(head), pl.ds(t0, text)], score_grad))
            key_sum = key_sum + dot(score_grad, row)
            value_sum = value_sum + dot(chance.astype(BF16), grad)
        total[j, 0, pl.ds(t0, text), :] += key_sum
        total[j, 1, pl.ds(t0, text), :] += value_sum
        query_grad = (jnp.concatenate(pieces, axis=0).T * HEAD**-0.5).astype(BF16)
        if j == 0:
            query_grads[...] = query_grad
        second_grad = second_grad + dot(query_grad, queries[j][0], NT)

    pulled, gain_sum, shift_sum = norm_backward(second_grad, after_self[...], gain1[...])
    sums[2:3, :] += gain_sum
    sums[3:4, :] += shift_sum
    upstream = upstream + pulled
    up_grad[...] = upstream
    low = upstream.astype(BF16)
    row_grads[0] += dot(mixed0[...], low, TN)
    mixed_grad[...] = dot(low, w_out[...], NT).astype(BF16)

    @pl.when(step == pl.num_programs(0) - 1)
    def _():
        pair_grad[...] = total[...].astype(BF16)


def back(
    lengths, live, third_grad, cot, after_cross, after_self, cross_query, looked, mixed0, logs,
    gain1, gain2, w_out, w_co, crosses, pairs, wait,
):
    rows, depth = cot.shape
    text_rows = live.shape[0]
    width = mixed0.shape[1]
    inner = 4 * width
    tile = rows_of(BLK, depth)
    row = whole((1, depth))
    return launch(
        back_kernel,
        [lengths, live, third_grad, cot, after_cross, after_self, cross_query, looked, mixed0]
        + [logs, gain1, gain2, w_out, w_co, *crosses, *pairs],
        [smem(), whole((text_rows, 1))]
        + [tile] * 4
        + [rows_of(BLK, inner), rows_of(BLK, width), rows_of(BLK, width)]
        + [pl.BlockSpec((inner // HEAD, BLK), lambda i: (0, i)), row, row]
        + [whole((inner, depth))] * 2
        + [at((1, depth, width), (0, 0, 0))] * 4
        + [whole((2, text_rows, width))] * 4,
        [tile, rows_of(BLK, inner), whole((4, 2, text_rows, width))]
        + [whole((2, width, depth)), rows_of(BLK, width), whole((8, depth))],
        [
            shape((rows, depth)),
            shape((rows, inner), BF16),
            shape((4, 2, text_rows, width), BF16),
            shape((2, width, depth)),
            shape((rows, width), BF16),
            shape((8, depth)),
        ],
        scratch=[
            pltpu.VMEM((4, 2, text_rows, width), F32),
            pltpu.VMEM((4, width, text_rows), BF16),
        ],
        wait=wait,
        grid=(rows // BLK,),
        compiler_params=params(),
        name="back",
        cost_estimate=cost(53),
    )


def text_kernel(me, text, pair_grad, second, query_grad, row_grads, qkv_grad, *refs):
    crosses, (text_grad, keep, send, cross_grad, folded) = refs[:4], refs[4:]
    total = jnp.zeros(text_grad.shape, F32)
    for j in range(4):
        for m in range(2):
            total = total + dot(pair_grad[j, m], crosses[j][m + 1], NT)
    text_grad[...] = total
    cross_grad[0] = dot(second[...], query_grad[...], TN)
    for m in range(2):
        cross_grad[m + 1] = dot(text[...], pair_grad[0, m], TN)
    put_pieces(cross_grad, keep, send, me)
    put_pieces(qkv_grad, keep, send, me, 3)
    width = folded.shape[2]
    rows = row_grads.shape[1] // 8
    for k in range(2):
        for piece in range(8):
            for part in range(4):
                folded[k, pl.ds((piece * 4 + part) * rows, rows), :] = row_grads[
                    k, pl.ds(piece * rows, rows), part * width : (part + 1) * width
                ]
    put_pieces(folded, keep, send, me, 6)


def unfold(piece):
    rows, width = piece.shape
    parts = [piece[k * rows // 4 : (k + 1) * rows // 4] for k in range(4)]
    return jnp.concatenate(parts, axis=1)


def text_back(me, text, pair_grad, second, query_grad, row_grads, qkv_grad, crosses, wait):
    text_rows, depth = text.shape
    width = pair_grad.shape[3]
    pieces = (4, 8, depth // 8, width)
    return launch(
        text_kernel,
        [me, text, pair_grad, second, query_grad, row_grads, qkv_grad, *crosses],
        [smem()] + [vmem()] * 10,
        [vmem()] * 3,
        [shape((text_rows, depth)), shape(pieces), shape(pieces)],
        scratch=[pltpu.VMEM((3, depth, width), F32), pltpu.VMEM((2, depth, width), F32)],
        wait=wait,
        compiler_params=params(),
        name="text_back",
        cost_estimate=cost(15),
    )


def self_back_pair(qb, kb, diag, qkv, rows, grads, logs, means, turned, query_sum, key_sum, value_sum):
    q0 = pl.multiple_of(qb * BLK, BLK)
    k0 = pl.multiple_of(kb * BLK, BLK)
    keys = qkv[1, pl.ds(k0, BLK), :]
    values = qkv[2, pl.ds(k0, BLK), :]
    more_keys = 0.0
    more_values = 0.0
    for head in range(rows.shape[0]):
        score = dot(keys, rows[head], NT)
        if diag:
            score = jnp.where(causal(), score, NEG)
        chance = jnp.exp(score - logs[head : head + 1, pl.ds(q0, BLK)])
        pushed = dot(values, grads[head], NT)
        score_grad = (chance * (pushed - means[head : head + 1, :])).astype(BF16)
        query_sum[lanes_of(head), :] += dot(turned[lanes_of(head), pl.ds(k0, BLK)], score_grad)
        more_keys = more_keys + dot(score_grad, rows[head])
        more_values = more_values + dot(chance.astype(BF16), grads[head])
    key_sum[pl.ds(k0, BLK), :] += more_keys
    value_sum[pl.ds(k0, BLK), :] += more_values


def self_back_body(
    lengths, qkv, mixed, out_grad, logs, weights, triple, turned, rows, grads, means, query_sum,
    key_sum, value_sum,
):
    row_count, width = mixed.shape
    turned[...] = qkv[1].T
    key_sum[...] = jnp.zeros_like(key_sum)
    value_sum[...] = jnp.zeros_like(value_sum)

    @pl.loop(0, row_count // BLK)
    def _(qb):
        q0 = pl.multiple_of(qb * BLK, BLK)
        _, start = item_at(lengths, q0)
        query = qkv[0, pl.ds(q0, BLK), :]
        grad = out_grad[pl.ds(q0, BLK), :]
        flat = (grad.astype(F32) * mixed[pl.ds(q0, BLK), :].astype(F32)).T
        for head in range(width // HEAD):
            rows[head] = masked(query, head_row(width, head, HEAD**-0.5))
            grads[head] = masked(grad, head_row(width, head, 1.0))
            means[head : head + 1, :] = jnp.sum(flat[lanes_of(head), :], axis=0, keepdims=True)
        query_sum[...] = jnp.zeros_like(query_sum)
        rest = (qkv, rows, grads, logs, means, turned, query_sum, key_sum, value_sum)

        @pl.loop(start // BLK, qb)
        def _(kb):
            self_back_pair(qb, kb, False, *rest)

        self_back_pair(qb, qb, True, *rest)
        triple[0, pl.ds(q0, BLK), :] = (query_sum[...].T * HEAD**-0.5).astype(BF16)

    triple[1] = key_sum[...].astype(BF16)
    triple[2] = value_sum[...].astype(BF16)


def self_scratch(rows, width):
    heads = width // HEAD
    return [
        pltpu.VMEM((3, rows, width), BF16),
        pltpu.VMEM((width, rows), BF16),
        pltpu.VMEM((heads, BLK, width), BF16),
        pltpu.VMEM((heads, BLK, width), BF16),
        pltpu.VMEM((8, BLK), F32),
        pltpu.VMEM((width, BLK), F32),
        pltpu.VMEM((rows, width), F32),
        pltpu.VMEM((rows, width), F32),
    ]


def self_own_kernel(lengths, qkv, mixed, out_grad, logs, weights, first, total, qkv_grad, *scratch):
    self_back_body(lengths, qkv, mixed, out_grad, logs, weights, *scratch)
    triple = scratch[0]
    for m in range(3):
        qkv_grad[m] = dot(first[...], triple[m], TN)
    total[...] = sum(dot(triple[m], weights[m], NT) for m in range(3))


def self_call(kernel, name, us, j, outs, operands, wait):
    lengths, qkv, mixed, out_grad, logs, weights, last_in = operands
    rows, width = mixed.shape
    return launch(
        kernel,
        operands,
        [smem()]
        + [whole(qkv.shape), whole(mixed.shape), at((rows, width), (0, j))]
        + [whole(logs.shape), whole(weights.shape), whole(last_in.shape)],
        [whole(out.shape) for out in outs],
        outs,
        scratch=self_scratch(rows, width),
        wait=wait,
        grid=(1,),
        compiler_params=params(),
        name=name,
        cost_estimate=cost(us),
    )


def self_own(lengths, qkv, mixed, out_grad, logs, weights, first, wait):
    outs = [shape(first.shape), shape(weights.shape)]
    operands = (lengths, qkv, mixed, out_grad, logs, weights, first)
    return self_call(self_own_kernel, "self_own", 28, 0, outs, operands, wait)


def self_kernel(lengths, qkv, mixed, out_grad, logs, weights, before, total, *scratch):
    self_back_body(lengths, qkv, mixed, out_grad, logs, weights, *scratch)
    triple = scratch[0]
    total[...] = before[...] + sum(dot(triple[m], weights[m], NT) for m in range(3))


def self_back(lengths, qkv, mixed, out_grad, logs, weights, before, j, wait):
    operands = (lengths, qkv, mixed, out_grad, logs, weights, before)
    return self_call(self_kernel, "self_back", 26, j, [shape(before.shape)], operands, wait)[0]


def last_kernel(first_grad, tokens, upstream, gain, token_grad, sums):
    @pl.when(pl.program_id(0) == 0)
    def _():
        sums[...] = jnp.zeros_like(sums)

    pulled, gain_sum, shift_sum = norm_backward(
        first_grad[...], tokens[...].astype(F32), gain[...]
    )
    token_grad[...] = upstream[...] + pulled
    sums[0:1, :] += gain_sum
    sums[1:2, :] += shift_sum


def last(first_grad, tokens, upstream, gain, wait):
    rows, depth = tokens.shape
    tile = rows_of(BLK, depth)
    return launch(
        last_kernel,
        [first_grad, tokens, upstream, gain],
        [tile, tile, tile, whole((1, depth))],
        [tile, whole((8, depth))],
        [shape((rows, depth)), shape((8, depth))],
        wait=wait,
        grid=(rows // BLK,),
        compiler_params=params(),
        name="last",
        cost_estimate=cost(10),
    )


DP = 8
MP = 4


def ring(step):
    pairs = []
    for i in range(DP):
        for z in range(MP):
            to = (z + (step if i % 2 == 0 else -step)) % MP
            pairs.append((i * MP + z, i * MP + to))
    return pairs


def straight(step):
    return [(z, (z + step) % MP) for z in range(MP)]


def beside(first):
    return [(i, i ^ (2 if (i % 2 == 0) == first else 4)) for i in range(DP)]


def swap(value):
    return lax.ppermute(value, "dp", [(i, i ^ 1) for i in range(DP)])


def cut(shard, chip):
    rows = shard.shape[1] // 4
    return lax.dynamic_slice_in_dim(shard, chip * rows, rows, 1).astype(F32)


def near_of(piece):
    return lax.ppermute(piece, "dp", beside(True))


def side_of(piece):
    return lax.ppermute(piece, "dp", beside(False))


def along(value, step):
    return lax.ppermute(value, "mp", straight(step))


def around(value):
    return lax.ppermute(value, ("dp", "mp"), ring(1))


def in_order(keep, send):
    pieces = [part[k] for k, m in ((0, 0), (2, 1), (1, 2), (3, 3)) for part, k in ((keep, k), (send, m))]
    return jnp.concatenate(pieces, axis=1)


def scattered(value, axis):
    return lax.psum_scatter(value, "dp", scatter_dimension=axis, tiled=True)


def sum_near(keep, sent):
    part = keep + sent
    return part[:2], lax.ppermute(part[2:], "dp", beside(True))


def sum_side(part, near):
    part = part + near
    return part[0], side_of(part[1])


def plane_sum(value):
    for bit in (1, 2, 4):
        value = value + lax.ppermute(value, "dp", [(i, i ^ bit) for i in range(DP)])
    return value


def local(
    planar, tokens, text_states, lengths, text_mask, ln_gain, ln_shift, w_qkv, w_out, w_cross_q,
    w_cross_kv, w_cross_out, w_up, w_down, cotangent,
):
    slot_count, text_length = text_mask.shape
    place = lax.axis_index("dp") if planar else jnp.int32(0)
    chip, core = place // 2, place % 2
    me = jnp.stack([chip, core]).astype(jnp.int32)
    gains = [ln_gain[n : n + 1] for n in range(3)]
    shifts = [ln_shift[n : n + 1] for n in range(3)]
    text = text_states.reshape(slot_count * text_length, text_states.shape[2])
    position = lax.broadcasted_iota(jnp.int32, text_mask.shape, 1)
    live = ((text_mask == 1) | (position == 0)).astype(F32).reshape(-1, 1)
    own_qkv = jnp.transpose(w_qkv, (1, 0, 2))
    own_cross = jnp.concatenate([w_cross_q[None], jnp.transpose(w_cross_kv, (1, 0, 2))], axis=0)
    outer, feeds = jnp.stack([w_out, w_cross_out]), jnp.stack([w_up, w_down])
    first = norm_first(tokens, gains[0], shifts[0])
    qkvs, mixeds, logs, weights = ([None] * 4 for _ in range(4))
    weights[0] = own_qkv

    def shards(value):
        return along(value.astype(F32), 1), along(value.astype(F32), 3)

    if planar:
        qkv_one = around(cut(own_qkv, chip))
        qkv_near, qkv_side = near_of(qkv_one), side_of(qkv_one)
        own_piece = gate([qkv_one], cut(own_cross, chip))
        cross_one = around(own_piece)
        wait = [qkv_one]
    else:
        wait = []
    qkvs[0], mixeds[0], logs[0] = front_own(lengths, first, own_qkv, wait)
    carry = []
    if planar:
        mine = join(me, [qkv_one, qkv_near, qkv_side, near_of(qkv_side)], [logs[0], cross_one])
        g_qkv = mine, swap(mine)
        cross_near, cross_side = near_of(cross_one), side_of(cross_one)
        two = around(jnp.where(core == 0, qkv_one, cross_one))
        wait = [cross_one]
        carry = [cut(lax.dynamic_slice_in_dim(outer, core, 1, 0), chip)]
    else:
        g_qkv = shards(own_qkv)
    weights[1], qkvs[1], mixeds[1], logs[1], *carried = front(
        lengths, first, g_qkv[0], wait, carry
    )
    if planar:
        cross_side, two = gate([logs[1]], cross_side), gate([logs[1]], two)
        cross_far = near_of(cross_side)
        two_near, two_side = near_of(two), side_of(two)
        outer_one, outer_three = along(carried[0], 1), along(carried[0], 3)
        wait = [two, cross_near, cross_side, logs[1]]
        carry = []
    weights[3], qkvs[3], mixeds[3], logs[3], *carried = front(
        lengths, first, g_qkv[1], wait, carry
    )
    if planar:
        mine = join(me, [cross_one, cross_near, cross_side, cross_far], [logs[3], outer_one, outer_three])
        g_cross = mine, swap(mine)
        mine = join(me, [two, two_near, two_side, near_of(two_side)], [mine])
        g_two = mine, swap(mine)
        outer_two = along(outer_one, 1)
        feed_one = around(gate([outer_two], cut(feeds, chip)))
        wait = [two_near, two_side, outer_two]
    else:
        g_cross = shards(own_cross)
        g_two = along(own_qkv.astype(F32), 2), along(own_cross.astype(F32), 2)
    cross_a, cross_b, *pairs = text_front(text, own_cross, g_cross, wait)
    if planar:
        outers = jnp.concatenate([outer_one, outer_two, outer_three], axis=0)
        outers = gate([cross_a], outers)
        outer_near, outer_side = near_of(outers), side_of(outers)
        wait = [outers, feed_one]
    weights[2], cross_two, qkvs[2], mixeds[2], logs[2], pair_two = front_two(
        me, lengths, first, g_two, text, wait
    )
    pairs = [pairs[0], pairs[1], pair_two, pairs[2]]
    crosses = [own_cross, cross_a, cross_two, cross_b]
    if planar:
        outer_side, feed_one = gate([logs[2]], outer_side), gate([logs[2]], feed_one)
        mine = join(me, [outers, outer_near, outer_side, near_of(outer_side)], [logs[2]])
        g_outer = mine, swap(mine)
        feed_near, feed_side = near_of(feed_one), side_of(feed_one)
        feed_two = around(lax.dynamic_slice_in_dim(feed_one, core, 1, 0))
        wait = [feed_one]
    else:
        g_outer = [
            jnp.stack([along(value.astype(F32), step) for step in (1, 2, 3)])
            for value in (w_out, w_cross_out)
        ]
    full_out, full_co, after_self, after_cross, second, third, cross_query, looked, cross_logs = middle(
        me, lengths, live, tokens, (gains[1], shifts[1], gains[2], shifts[2]), w_out, w_cross_out,
        mixeds, crosses, pairs, g_outer, wait,
    )
    if planar:
        feed_side, feed_two = gate([third], feed_side), gate([third], feed_two)
        feed_far = near_of(feed_side)
        last_near, last_side = near_of(feed_two), side_of(feed_two)
        wait = [feed_near, feed_side, feed_two]
    out, grad, both_keep, both_send = feed_own(
        me, third, cotangent, after_cross, w_up, w_down, wait
    )
    if planar:
        mine = join(me, [feed_one, feed_near, feed_side, feed_far], [out, last_near, last_side])
        g_feed = mine, swap(mine)
        last_side = gate([out], last_side)
        last_far = near_of(last_side)
        wait = [last_near, last_side]
    else:
        g_feed = shards(feeds)
    out, grad, both_send = feed_pair(
        third, cotangent, out, grad, g_feed, wait, [both_send]
    )
    if planar:
        mine = join(me, [feed_two, last_near, last_side, last_far], [out])
        g_last = mine, swap(mine)
    else:
        g_last = along(feeds[:1].astype(F32), 2), along(feeds[1:].astype(F32), 2)
        wait = []
    out, grad = feed_last(me, third, cotangent, out, grad, g_last, [])
    if planar:
        both_part, both_near = sum_near(both_keep, swap(both_send))
    upstream, mixed_grad, pair_grad, row_grads, query_grad, sums = back(
        lengths, live, grad, cotangent, after_cross, after_self, cross_query, looked, mixeds[0],
        cross_logs, gains[1], gains[2], full_out, full_co, crosses, pairs,
        [both_part] if planar else [],
    )
    if planar:
        both_part, both_side = sum_side(both_part, both_near)
        wait = [both_near]
    first_grad, qkv_grad = self_own(
        lengths, qkvs[0], mixeds[0], mixed_grad, logs[0], weights[0], first, wait
    )
    if planar:
        wait = [both_side]
    text_grad, keep, send = text_back(
        me, text, pair_grad, second, query_grad, row_grads, qkv_grad, crosses, wait
    )
    waits = [[], [], [], []]
    if planar:
        late_swap = swap(send)
        late_part, late_near = sum_near(keep, late_swap)
        late_one, late_side = sum_side(late_part, late_near)
        waits = [[], [late_swap], [late_near], [late_side]]
    for j in (1, 2, 3):
        first_grad = self_back(
            lengths, qkvs[j], mixeds[j], mixed_grad, logs[j], weights[j], first_grad, j,
            waits[j - 1],
        )
    token_grad, last_sums = last(first_grad, tokens, upstream, gains[0], waits[3])
    norm_sums = jnp.concatenate(
        [last_sums[0:1], sums[2:3], sums[0:1], last_sums[1:2], sums[3:4], sums[1:2]], axis=0
    )
    if planar:
        both_sum, late_sum = both_part + both_side, late_one + late_side
        row_sum = [unfold(late_sum[k]) for k in (6, 7)]
        width = norm_sums.shape[1] // DP
        norm_sum = lax.dynamic_slice_in_dim(plane_sum(norm_sums), place * width, width, 1)
    else:
        both_sum = scattered(in_order(both_keep, both_send), 1)
        late = in_order(keep, send)
        late_sum = scattered(late[:6], 1)
        row_sum = [
            scattered(jnp.concatenate([unfold(part) for part in jnp.split(late[k], 8)]), 0)
            for k in (6, 7)
        ]
        norm_sum = scattered(norm_sums, 1)
    return (
        out,
        token_grad,
        text_grad.reshape(text_states.shape),
        norm_sum[:3],
        norm_sum[3:],
        jnp.transpose(late_sum[3:6], (1, 0, 2)),
        row_sum[0],
        late_sum[0],
        jnp.transpose(late_sum[1:3], (1, 0, 2)),
        row_sum[1],
        both_sum[0],
        both_sum[1],
    )


def solution(mesh):
    placed = (
        P("dp", None),
        P("dp", None, None),
        P("dp"),
        P("dp", None),
        P(),
        P(),
        P(None, None, "mp"),
        P("mp", None),
        P(None, "mp"),
        P(None, None, "mp"),
        P("mp", None),
        P(None, "mp"),
        P("mp", None),
        P("dp", None),
    )
    return jax.shard_map(
        partial(local, mesh.shape["dp"] == DP),
        mesh=mesh,
        in_specs=placed,
        out_specs=(
            P("dp", None),
            P("dp", None),
            P("dp", None, None),
            P(None, "dp"),
            P(None, "dp"),
            P("dp", None, "mp"),
            P(("mp", "dp"), None),
            P("dp", "mp"),
            P("dp", None, "mp"),
            P(("mp", "dp"), None),
            P("dp", "mp"),
            P(("mp", "dp"), None),
        ),
        check_vma=False,
    )
```

```python
from functools import partial

import jax
import jax.numpy as jnp
from jax import lax
from jax.experimental import pallas as pl
from jax.experimental.pallas import tpu as pltpu
from jax.sharding import PartitionSpec as P

HEAD = 64
BLK = 256
EPS = 1e-05
NEG = -1e30
F32 = jnp.float32
BF16 = jnp.bfloat16
MIB = 1024 * 1024

NN = (((1,), (0,)), ((), ()))
NT = (((1,), (1,)), ((), ()))
TN = (((0,), (0,)), ((), ()))


def dot(a, b, dims=NN):
    return lax.dot_general(a, b, dims, preferred_element_type=F32)


def params(mib=56, semantics=None):
    return pltpu.CompilerParams(vmem_limit_bytes=mib * MIB, dimension_semantics=semantics)


def cost(us):
    return pl.CostEstimate(
        flops=int(us * 1.15e9), transcendentals=0, bytes_accessed=int(us * 3.6e6)
    )


def shape(dims, dtype=F32):
    return jax.ShapeDtypeStruct(dims, dtype)


def smem():
    return pl.BlockSpec(memory_space=pltpu.SMEM)


def whole(dims):
    rank = len(dims)
    return pl.BlockSpec(dims, lambda *_: (0,) * rank)


def at(dims, index):
    return pl.BlockSpec(dims, lambda *_: index)


def once(dims):
    rank = len(dims)
    return pl.BlockSpec(dims, lambda *_: (0,) * rank, pipeline_mode=pl.Buffered(1))


def anywhere():
    return pl.BlockSpec(memory_space=pl.ANY)


def launch(kernel, args, in_specs, out_specs, out_shape, scratch=(), wait=(), carry=(), **options):
    args, wait, carry = list(args), list(wait), list(carry)
    count, extra, outs = len(args), len(wait) + len(carry), len(out_shape)

    def body(*refs):
        results = refs[count + extra : count + extra + outs]
        kernel(*refs[:count], *results, *refs[count + extra + outs + len(carry) :])

    return pl.pallas_call(
        body,
        in_specs=list(in_specs) + [anywhere()] * extra,
        out_specs=list(out_specs) + [anywhere()] * len(carry),
        out_shape=list(out_shape) + [shape(value.shape, value.dtype) for value in carry],
        scratch_shapes=list(scratch),
        input_output_aliases={count + len(wait) + k: outs + k for k in range(len(carry))},
        **options,
    )(*args, *wait, *carry)


def gate(wait, carry):
    return launch(
        lambda: None, [], [], [], [], wait=wait, carry=[carry], name="gate", cost_estimate=cost(1)
    )[0]


def rows_of(tile, width):
    return pl.BlockSpec((tile, width), lambda i, *_: (i, 0))


def norm_stats(value):
    center = value - jnp.mean(value, axis=-1, keepdims=True)
    spread = jnp.mean(center * center, axis=-1, keepdims=True)
    inverse = lax.rsqrt(spread + EPS)
    return center * inverse, inverse


def norm_forward(value, gain, shift):
    unit, _ = norm_stats(value)
    return (unit * gain + shift).astype(BF16)


def norm_backward(incoming, value, gain):
    unit, inverse = norm_stats(value)
    scaled = incoming * gain
    pushed = incoming * unit
    inner = (
        scaled
        - jnp.mean(scaled, axis=-1, keepdims=True)
        - unit * jnp.mean(scaled * unit, axis=-1, keepdims=True)
    )
    return (
        inner * inverse,
        jnp.sum(pushed, axis=0, keepdims=True),
        jnp.sum(incoming, axis=0, keepdims=True),
    )


def norm_kernel(tokens_ref, gain_ref, shift_ref, first_ref):
    first_ref[...] = norm_forward(tokens_ref[...].astype(F32), gain_ref[...], shift_ref[...])


def norm_first(tokens, gain, shift):
    rows, width = tokens.shape
    return launch(
        norm_kernel,
        [tokens, gain, shift],
        [rows_of(BLK, width), whole((1, width)), whole((1, width))],
        [rows_of(BLK, width)],
        [shape((rows, width), BF16)],
        grid=(rows // BLK,),
        name="norm_first",
        cost_estimate=cost(6),
    )[0]


def head_row(width, head, value):
    lane = lax.broadcasted_iota(jnp.int32, (1, width), 1)
    return jnp.where(lane // HEAD == head, value, 0.0)


def masked(block, row):
    return (block.astype(F32) * row).astype(BF16)


def item_at(lengths, place):
    item, start, end = 0, 0, 0
    for slot in range(lengths.shape[0]):
        end = end + lengths[slot]
        past = end <= place
        item = item + past.astype(jnp.int32)
        start = jnp.where(past, end, start)
    return item, start


def offsets(core):
    return (0, 1 + core, 2 - core, 3)


def join_kernel(me, *refs):
    parts, (target, sems) = refs[:4], refs[4:]
    copies = []
    for index, (part, offset) in enumerate(zip(parts, offsets(me[1]))):
        rows = part.shape[1]
        place = pl.multiple_of((me[0] ^ offset) * rows, rows)
        for k in range(part.shape[0]):
            copies.append(
                pltpu.make_async_copy(
                    part.at[k], target.at[k, pl.ds(place, rows)], sems.at[index, k]
                )
            )
    for copy in copies:
        copy.start()
    for copy in copies:
        copy.wait()


def join(me, parts, wait):
    count, rows, width = parts[0].shape
    return launch(
        join_kernel,
        [me, *parts],
        [smem()] + [anywhere()] * 4,
        [vmem()],
        [shape((count, 4 * rows, width))],
        scratch=[pltpu.SemaphoreType.DMA((4, count))],
        wait=wait,
        compiler_params=params(24),
        name="join",
        cost_estimate=cost(2),
    )[0]


def take(targets, source, flip=1):
    for k, target in enumerate(targets[::flip]):
        target[...] = source[k].astype(BF16)


def take_two(first, second, mine, other, core, flip=1):
    @pl.when(core == 0)
    def _():
        take(first, mine)
        take(second, other)

    @pl.when(core == 1)
    def _():
        take(second, mine, flip)
        take(first, other, flip)


def planes(ref):
    return [ref.at[k] for k in range(ref.shape[0])]


def causal():
    shape2 = (BLK, BLK)
    return lax.broadcasted_iota(jnp.int32, shape2, 0) <= lax.broadcasted_iota(
        jnp.int32, shape2, 1
    )


def lanes_of(head):
    return slice(head * HEAD, (head + 1) * HEAD)


def self_block(qb, count, qkv, turned, mixed, logs):
    q0 = pl.multiple_of(qb * BLK, BLK)
    k0 = pl.multiple_of((qb - (count - 1)) * BLK, BLK)
    width = qkv.shape[2]
    query = qkv[0, pl.ds(q0, BLK), :]
    diag = qkv[1, pl.ds(q0, BLK), :]
    pre_len = (count - 1) * BLK
    keep = causal()
    pieces = []
    heads = range(width // HEAD)
    parts = [masked(query, head_row(width, head, HEAD**-0.5)) for head in heads]
    nears = [dot(diag, part, NT) for part in parts]
    fars = [dot(qkv[1, pl.ds(k0, pre_len), :], part, NT) for part in parts] if pre_len else []
    for head in heads:
        near = jnp.where(keep, nears[head], NEG)
        peak = jnp.max(near, axis=0, keepdims=True)
        if pre_len:
            far = fars[head]
            peak = jnp.maximum(peak, jnp.max(far, axis=0, keepdims=True))
        near = jnp.exp(near - peak)
        total = jnp.sum(near, axis=0, keepdims=True)
        result = dot(turned[lanes_of(head), pl.ds(q0, BLK)], near.astype(BF16))
        if pre_len:
            far = jnp.exp(far - peak)
            total = total + jnp.sum(far, axis=0, keepdims=True)
            result = result + dot(
                turned[lanes_of(head), pl.ds(k0, pre_len)], far.astype(BF16)
            )
        pieces.append(result * (1.0 / total))
        logs[head : head + 1, pl.ds(q0, BLK)] = peak + jnp.log(total)
    mixed[pl.ds(q0, BLK), :] = jnp.concatenate(pieces, axis=0).T.astype(BF16)


def front_body(lengths, first, weights, qkv, mixed, logs, turned):
    rows = first.shape[0]
    for m in range(3):
        qkv[m] = dot(first[...], weights[m]).astype(BF16)
    turned[...] = qkv[2].T

    @pl.loop(0, rows // BLK)
    def _(qb):
        _, start = item_at(lengths, qb * BLK)
        count = qb - start // BLK + 1
        for n in range(1, 5):

            @pl.when(count == n)
            def _():
                self_block(qb, n, qkv, turned, mixed, logs)


def front_kernel(lengths, first, shard, weights, *rest):
    take(planes(weights), shard)
    front_body(lengths, first, weights, *rest)


def front_two_kernel(me, lengths, first, mine, other, text, weights, cross, qkv, mixed, logs, pair, turned):
    take_two(planes(weights), planes(cross), mine, other, me[1])
    text_pair(pair, text, cross)
    front_body(lengths, first, weights, qkv, mixed, logs, turned)


def vmem():
    return pl.BlockSpec(memory_space=pltpu.VMEM)


def front_call(kernel, name, us, prefix, first, arrays, weight_count, more, wait, carry=()):
    rows, depth = first.shape
    width = arrays[0].shape[2]
    outs = [shape((3, depth, width), BF16)] * weight_count + [
        shape((3, rows, width), BF16),
        shape((rows, width), BF16),
        shape((8, rows), F32),
    ] + more
    return launch(
        kernel,
        [*prefix, first, *arrays],
        [smem()] * len(prefix) + [vmem()] * (1 + len(arrays)),
        [vmem()] * len(outs),
        outs,
        scratch=[pltpu.VMEM((width, rows), BF16)],
        wait=wait,
        carry=carry,
        compiler_params=params(),
        name=name,
        cost_estimate=cost(us),
    )


def front_own(lengths, first, weights, wait):
    return front_call(front_body, "front_own", 15, (lengths,), first, [weights], 0, [], wait)


def front(lengths, first, shard, wait, carry):
    return front_call(front_kernel, "front", 16, (lengths,), first, [shard], 1, [], wait, carry)


def front_two(me, lengths, first, arrays, text, wait):
    pair = shape((2, text.shape[0], arrays[0].shape[2]), BF16)
    return front_call(
        front_two_kernel, "front_two", 18, (me, lengths), first, [*arrays, text], 2, [pair], wait
    )


def text_pair(pair, text, cross):
    for m in range(2):
        pair[m] = dot(text[...], cross[m + 1]).astype(BF16)


def text_front_kernel(text, own, mine, other, cross_a, cross_b, *pairs):
    take(planes(cross_a), mine)
    take(planes(cross_b), other)
    for pair, cross in zip(pairs, (own, cross_a, cross_b)):
        text_pair(pair, text, cross)


def text_front(text, own, arrays, wait):
    rows = text.shape[0]
    width = own.shape[2]
    outs = [shape(own.shape, BF16)] * 2 + [shape((2, rows, width), BF16)] * 3
    return launch(
        text_front_kernel,
        [text, own, *arrays],
        [vmem()] * 4,
        [vmem()] * 5,
        outs,
        wait=wait,
        compiler_params=params(),
        name="text_front",
        cost_estimate=cost(7),
    )


def middle_kernel(me, lengths, live, tokens, gain1, shift1, gain2, shift2, own_out, own_co, *refs):
    mixed, refs = refs[:4], refs[4:]
    queries, refs = refs[:4], refs[4:]
    pairs, refs = refs[:4], refs[4:]
    mine, other, *refs = refs
    w_out, w_co, after_self, after_cross, second, third, cross_query, looked, logs, turned = refs
    step = pl.program_id(0)

    @pl.when(step == 0)
    def _():
        width = own_out.shape[0]
        w_out[:width, :] = own_out[...]
        w_co[:width, :] = own_co[...]
        parts = [
            [target.at[pl.ds((j + 1) * width, width)] for j in range(3)] for target in (w_out, w_co)
        ]
        take_two(*parts, mine, other, me[1], flip=-1)
        for j in range(4):
            turned[j] = pairs[j][1].T

    part = jnp.concatenate([ref[...] for ref in mixed], axis=1)
    residual = tokens[...].astype(F32) + dot(part, w_out[...])
    after_self[...] = residual
    normed = norm_forward(residual, gain1[...], shift1[...])
    second[...] = normed
    text = TEXT
    item, _ = item_at(lengths, step * BLK)
    t0 = pl.multiple_of(item * text, text)
    alive = live[pl.ds(t0, text), :] > 0.0
    width = own_out.shape[0]
    heads = range(width // HEAD)
    stages = []
    for j in range(4):
        query = dot(normed, queries[j][0]).astype(BF16)
        cross_query[:, j * width : (j + 1) * width] = query
        rows = [masked(query, head_row(width, head, HEAD**-0.5)) for head in heads]
        keys = pairs[j][0, pl.ds(t0, text), :]
        stages.append([dot(keys, row, NT) for row in rows])
    for j in range(4):
        pieces = []
        for head in heads:
            score = jnp.where(alive, stages[j][head], NEG)
            peak = jnp.max(score, axis=0, keepdims=True)
            score = jnp.exp(score - peak)
            total = jnp.sum(score, axis=0, keepdims=True)
            result = dot(turned[j, lanes_of(head), pl.ds(t0, text)], score.astype(BF16))
            pieces.append(result * (1.0 / total))
            index = j * (width // HEAD) + head
            logs[index : index + 1, :] = peak + jnp.log(total)
        looked[:, j * width : (j + 1) * width] = jnp.concatenate(pieces, axis=0).T.astype(BF16)
    residual = residual + dot(looked[...], w_co[...])
    after_cross[...] = residual
    third[...] = norm_forward(residual, gain2[...], shift2[...])


TEXT = 128


def middle(me, lengths, live, tokens, norms, own_out, own_co, mixed, crosses, pairs, arrays, wait):
    rows, depth = tokens.shape
    width = own_out.shape[0]
    text_rows = live.shape[0]
    inner = 4 * width
    row = whole((1, depth))
    return launch(
        middle_kernel,
        [me, lengths, live, tokens, *norms, own_out, own_co, *mixed, *crosses, *pairs, *arrays],
        [smem(), smem(), whole((text_rows, 1)), rows_of(BLK, depth)]
        + [row] * 4
        + [once((width, depth))] * 2
        + [rows_of(BLK, width)] * 4
        + [at((1, depth, width), (0, 0, 0))] * 4
        + [whole((2, text_rows, width))] * 4
        + [once(arrays[0].shape)] * 2,
        [whole((inner, depth))] * 2
        + [rows_of(BLK, depth)] * 4
        + [rows_of(BLK, inner)] * 2
        + [pl.BlockSpec((inner // HEAD, BLK), lambda i: (0, i))],
        [shape((inner, depth), BF16)] * 2
        + [shape((rows, depth)), shape((rows, depth))]
        + [shape((rows, depth), BF16)] * 2
        + [shape((rows, inner), BF16)] * 2
        + [shape((inner // HEAD, rows))],
        scratch=[pltpu.VMEM((4, width, text_rows), BF16)],
        wait=wait,
        grid=(rows // BLK,),
        compiler_params=params(),
        name="middle",
        cost_estimate=cost(43),
    )


ROOT = 0.7978845608028654
CUBE = 0.044715


def gelu_both(value):
    square = value * value
    bend = jnp.tanh(value * (ROOT + (ROOT * CUBE) * square))
    half = 0.5 + 0.5 * bend
    slope = half + (0.5 * value) * (1.0 - bend * bend) * (ROOT + (3.0 * ROOT * CUBE) * square)
    return value * half, slope


def feed_rows(third, cot, up, down):
    return feed_finish(dot(third, up), dot(cot, down, NT), up, down)


def feed_finish(pre_act, hidden_grad, up, down):
    hidden, slope = gelu_both(pre_act)
    hidden = hidden.astype(BF16)
    pre_grad = (hidden_grad * slope).astype(BF16)
    return hidden, pre_grad, dot(hidden, down), dot(pre_grad, up, NT)


def feed_own_kernel(me, third, cot, after, up, down, out, grad, keep, send, both):
    hidden, pre_grad, result, pushed = feed_rows(third[...], cot[...], up[...], down[...])
    out[...] = after[...] + result
    grad[...] = pushed
    step = pl.program_id(0)
    more_up = dot(third[...], pre_grad, TN)
    more_down = dot(hidden, cot[...], TN)

    @pl.when(step == 0)
    def _():
        both[0] = more_up
        both[1] = more_down

    @pl.when(step > 0)
    def _():
        both[0] += more_up
        both[1] += more_down

    @pl.when(step == pl.num_programs(0) - 1)
    def _():
        put_pieces(both, keep, send, me)


def put_pieces(source, keep, send, me, first=0):
    chip, core = me[0], me[1]
    rows = source.shape[1] // 8
    for target, owner in ((keep, core), (send, 1 - core)):
        for index, offset in enumerate((0, 2 - owner, 1 + owner, 3)):
            place = pl.multiple_of(((chip ^ offset) * 2 + owner) * rows, rows)
            for k in range(source.shape[0]):
                target[index, first + k] = source[k, pl.ds(place, rows), :]


FEED = 320


def feed_own(me, third, cot, after, up, down, wait):
    rows, depth = third.shape
    inner = up.shape[1]
    tile = rows_of(FEED, depth)
    pieces = (4, 2, depth // 8, depth)
    return launch(
        feed_own_kernel,
        [me, third, cot, after, up, down],
        [smem(), tile, tile, tile, once((depth, inner)), once((inner, depth))],
        [tile, tile, once(pieces), once(pieces)],
        [shape((rows, depth)), shape((rows, depth)), shape(pieces), shape(pieces)],
        scratch=[pltpu.VMEM((2, depth, inner), F32)],
        wait=wait,
        grid=(rows // FEED,),
        compiler_params=params(),
        name="feed_own",
        cost_estimate=cost(32),
    )


def feed_pair_kernel(third, cot, out_in, grad_in, mine, other, out, grad, one, two):
    @pl.when(pl.program_id(0) == 0)
    def _():
        take(planes(one), mine)
        take(planes(two), other)

    _, _, result, pushed = feed_rows(third[...], cot[...], one[0], one[1])
    _, _, more_result, more_pushed = feed_rows(third[...], cot[...], two[0], two[1])
    out[...] = out_in[...] + (result + more_result)
    grad[...] = grad_in[...] + (pushed + more_pushed)


def feed_last_kernel(me, third, cot, out_in, grad_in, mine, other, out, grad, both):
    @pl.when(pl.program_id(0) == 0)
    def _():
        up, down = planes(both)
        take_two([up], [down], mine, other, me[1])

    _, _, result, pushed = feed_rows(third[...], cot[...], both[0], both[1])
    out[...] = (out_in[...] + result).astype(BF16)
    grad[...] = grad_in[...] + pushed


def feed_call(kernel, name, us, prefix, dtype, copies, third, cot, out, grad, arrays, wait, carry=()):
    rows, depth = third.shape
    tile = rows_of(FEED, depth)
    return launch(
        kernel,
        [*prefix, third, cot, out, grad, *arrays],
        [smem()] * len(prefix) + [tile] * 4 + [once(arrays[0].shape)] * 2,
        [tile, tile],
        [shape((rows, depth), dtype), shape((rows, depth))],
        scratch=[pltpu.VMEM((2,) + arrays[0].shape[1:], BF16)] * copies,
        wait=wait,
        carry=carry,
        grid=(rows // FEED,),
        compiler_params=params(),
        name=name,
        cost_estimate=cost(us),
    )


def feed_pair(*operands):
    return feed_call(feed_pair_kernel, "feed_pair", 30, (), F32, 2, *operands)


def feed_last(me, *operands):
    return feed_call(feed_last_kernel, "feed_last", 18, (me,), BF16, 1, *operands)


def back_kernel(
    lengths, live, third_grad, cot, after_cross, after_self, cross_query, looked0, mixed0, logs,
    gain1, gain2, w_out, w_co, *refs,
):
    queries, refs = refs[:4], refs[4:]
    pairs, refs = refs[:4], refs[4:]
    up_grad, mixed_grad, pair_grad, row_grads, query_grads, sums, total, turned = refs
    step = pl.program_id(0)
    text = TEXT

    @pl.when(step == 0)
    def _():
        total[...] = jnp.zeros_like(total)
        row_grads[...] = jnp.zeros_like(row_grads)
        sums[...] = jnp.zeros_like(sums)
        for j in range(4):
            turned[j] = pairs[j][0].T

    pulled, gain_sum, shift_sum = norm_backward(third_grad[...], after_cross[...], gain2[...])
    sums[0:1, :] += gain_sum
    sums[1:2, :] += shift_sum
    upstream = cot[...].astype(F32) + pulled
    low = upstream.astype(BF16)
    row_grads[1] += dot(looked0[...], low, TN)
    looked_grad = dot(low, w_co[...], NT).astype(BF16)
    item, _ = item_at(lengths, step * BLK)
    t0 = pl.multiple_of(item * text, text)
    alive = live[pl.ds(t0, text), :] > 0.0
    second_grad = jnp.zeros(upstream.shape, F32)
    width = queries[0].shape[2]
    heads = range(width // HEAD)

    def scores(j):
        cols = slice(j * width, (j + 1) * width)
        rows = [masked(cross_query[:, cols], head_row(width, h, HEAD**-0.5)) for h in heads]
        grads = [masked(looked_grad[:, cols], head_row(width, h, 1.0)) for h in heads]
        keys = pairs[j][0, pl.ds(t0, text), :]
        values = pairs[j][1, pl.ds(t0, text), :]
        return rows, grads, [dot(keys, row, NT) for row in rows], [dot(values, g, NT) for g in grads]

    ahead = scores(0)
    for j in range(4):
        rows, grads, score_set, pushed_set = ahead
        if j < 3:
            ahead = scores(j + 1)
        pieces, chances, score_grads = [], [], []
        for head in heads:
            index = j * (width // HEAD) + head
            score = jnp.where(alive, score_set[head], NEG)
            chance = jnp.exp(score - logs[index : index + 1, :])
            weighted = chance * pushed_set[head]
            mean = jnp.sum(weighted, axis=0, keepdims=True)
            score_grads.append((weighted - chance * mean).astype(BF16))
            chances.append(chance.astype(BF16))
            pieces.append(dot(turned[j, lanes_of(head), pl.ds(t0, text)], score_grads[head]))
        total[j, 0, pl.ds(t0, text), :] += dot(
            jnp.concatenate(score_grads, axis=1), jnp.concatenate(rows, axis=0)
        )
        total[j, 1, pl.ds(t0, text), :] += dot(
            jnp.concatenate(chances, axis=1), jnp.concatenate(grads, axis=0)
        )
        query_grad = (jnp.concatenate(pieces, axis=0).T * HEAD**-0.5).astype(BF16)
        if j == 0:
            query_grads[...] = query_grad
        second_grad = second_grad + dot(query_grad, queries[j][0], NT)

    pulled, gain_sum, shift_sum = norm_backward(second_grad, after_self[...], gain1[...])
    sums[2:3, :] += gain_sum
    sums[3:4, :] += shift_sum
    upstream = upstream + pulled
    up_grad[...] = upstream
    low = upstream.astype(BF16)
    row_grads[0] += dot(mixed0[...], low, TN)
    mixed_grad[...] = dot(low, w_out[...], NT).astype(BF16)

    @pl.when(step == pl.num_programs(0) - 1)
    def _():
        pair_grad[...] = total[...].astype(BF16)


def back(
    lengths, live, third_grad, cot, after_cross, after_self, cross_query, looked, mixed0, logs,
    gain1, gain2, w_out, w_co, crosses, pairs, wait,
):
    rows, depth = cot.shape
    text_rows = live.shape[0]
    width = mixed0.shape[1]
    inner = 4 * width
    tile = rows_of(BLK, depth)
    row = whole((1, depth))
    return launch(
        back_kernel,
        [lengths, live, third_grad, cot, after_cross, after_self, cross_query, looked, mixed0]
        + [logs, gain1, gain2, w_out, w_co, *crosses, *pairs],
        [smem(), whole((text_rows, 1))]
        + [tile] * 4
        + [rows_of(BLK, inner), rows_of(BLK, width), rows_of(BLK, width)]
        + [pl.BlockSpec((inner // HEAD, BLK), lambda i: (0, i)), row, row]
        + [whole((inner, depth))] * 2
        + [at((1, depth, width), (0, 0, 0))] * 4
        + [whole((2, text_rows, width))] * 4,
        [tile, rows_of(BLK, inner), whole((4, 2, text_rows, width))]
        + [whole((2, width, depth)), rows_of(BLK, width), whole((8, depth))],
        [
            shape((rows, depth)),
            shape((rows, inner), BF16),
            shape((4, 2, text_rows, width), BF16),
            shape((2, width, depth)),
            shape((rows, width), BF16),
            shape((8, depth)),
        ],
        scratch=[
            pltpu.VMEM((4, 2, text_rows, width), F32),
            pltpu.VMEM((4, width, text_rows), BF16),
        ],
        wait=wait,
        grid=(rows // BLK,),
        compiler_params=params(),
        name="back",
        cost_estimate=cost(53),
    )


def text_kernel(me, text, pair_grad, second, query_grad, row_grads, *refs):
    crosses, (text_grad, keep, send, cross_grad, folded) = refs[:4], refs[4:]
    total = jnp.zeros(text_grad.shape, F32)
    for j in range(4):
        for m in range(2):
            total = total + dot(pair_grad[j, m], crosses[j][m + 1], NT)
    text_grad[...] = total
    cross_grad[0] = dot(second[...], query_grad[...], TN)
    for m in range(2):
        cross_grad[m + 1] = dot(text[...], pair_grad[0, m], TN)
    put_pieces(cross_grad, keep, send, me)
    width = folded.shape[2]
    rows = row_grads.shape[1] // 8
    for k in range(2):
        for piece in range(8):
            for part in range(4):
                folded[k, pl.ds((piece * 4 + part) * rows, rows), :] = row_grads[
                    k, pl.ds(piece * rows, rows), part * width : (part + 1) * width
                ]
    put_pieces(folded, keep, send, me, 3)


def unfold(piece):
    rows, width = piece.shape
    parts = [piece[k * rows // 4 : (k + 1) * rows // 4] for k in range(4)]
    return jnp.concatenate(parts, axis=1)


def text_back(me, text, pair_grad, second, query_grad, row_grads, crosses, wait):
    text_rows, depth = text.shape
    width = pair_grad.shape[3]
    pieces = (4, 5, depth // 8, width)
    return launch(
        text_kernel,
        [me, text, pair_grad, second, query_grad, row_grads, *crosses],
        [smem()] + [vmem()] * 9,
        [vmem()] * 3,
        [shape((text_rows, depth)), shape(pieces), shape(pieces)],
        scratch=[pltpu.VMEM((3, depth, width), F32), pltpu.VMEM((2, depth, width), F32)],
        wait=wait,
        compiler_params=params(),
        name="text_back",
        cost_estimate=cost(15),
    )


def self_back_pair(qb, kb, diag, qkv, rows, grads, logs, means, turned, query_sum, key_sum, value_sum):
    q0 = pl.multiple_of(qb * BLK, BLK)
    k0 = pl.multiple_of(kb * BLK, BLK)
    keys = qkv[1, pl.ds(k0, BLK), :]
    values = qkv[2, pl.ds(k0, BLK), :]
    more_keys = 0.0
    more_values = 0.0
    heads = range(rows.shape[0])
    stages = [(dot(keys, rows[h], NT), dot(values, grads[h], NT)) for h in heads]
    for head, (score, pushed) in zip(heads, stages):
        if diag:
            score = jnp.where(causal(), score, NEG)
        chance = jnp.exp(score - logs[head : head + 1, pl.ds(q0, BLK)])
        score_grad = (chance * (pushed - means[head : head + 1, :])).astype(BF16)
        query_sum[lanes_of(head), :] += dot(turned[lanes_of(head), pl.ds(k0, BLK)], score_grad)
        more_keys = more_keys + dot(score_grad, rows[head])
        more_values = more_values + dot(chance.astype(BF16), grads[head])
    key_sum[pl.ds(k0, BLK), :] += more_keys
    value_sum[pl.ds(k0, BLK), :] += more_values


def self_back_body(
    lengths, qkv, mixed, out_grad, logs, weights, triple, turned, rows, grads, means, query_sum,
    key_sum, value_sum,
):
    row_count, width = mixed.shape
    turned[...] = qkv[1].T
    key_sum[...] = jnp.zeros_like(key_sum)
    value_sum[...] = jnp.zeros_like(value_sum)

    @pl.loop(0, row_count // BLK)
    def _(qb):
        q0 = pl.multiple_of(qb * BLK, BLK)
        _, start = item_at(lengths, q0)
        query = qkv[0, pl.ds(q0, BLK), :]
        grad = out_grad[pl.ds(q0, BLK), :]
        flat = (grad.astype(F32) * mixed[pl.ds(q0, BLK), :].astype(F32)).T
        for head in range(width // HEAD):
            rows[head] = masked(query, head_row(width, head, HEAD**-0.5))
            grads[head] = masked(grad, head_row(width, head, 1.0))
            means[head : head + 1, :] = jnp.sum(flat[lanes_of(head), :], axis=0, keepdims=True)
        query_sum[...] = jnp.zeros_like(query_sum)
        rest = (qkv, rows, grads, logs, means, turned, query_sum, key_sum, value_sum)

        @pl.loop(start // BLK, qb)
        def _(kb):
            self_back_pair(qb, kb, False, *rest)

        self_back_pair(qb, qb, True, *rest)
        triple[0, pl.ds(q0, BLK), :] = (query_sum[...].T * HEAD**-0.5).astype(BF16)

    triple[1] = key_sum[...].astype(BF16)
    triple[2] = value_sum[...].astype(BF16)


def self_scratch(rows, width):
    heads = width // HEAD
    return [
        pltpu.VMEM((3, rows, width), BF16),
        pltpu.VMEM((width, rows), BF16),
        pltpu.VMEM((heads, BLK, width), BF16),
        pltpu.VMEM((heads, BLK, width), BF16),
        pltpu.VMEM((8, BLK), F32),
        pltpu.VMEM((width, BLK), F32),
        pltpu.VMEM((rows, width), F32),
        pltpu.VMEM((rows, width), F32),
    ]


def self_own_kernel(me, lengths, qkv, mixed, out_grad, logs, weights, first, total, keep, send, *scratch):
    self_back_body(lengths, qkv, mixed, out_grad, logs, weights, *scratch[:-1])
    triple, qkv_grad = scratch[0], scratch[-1]
    for m in range(3):
        qkv_grad[m] = dot(first[...], triple[m], TN)
    put_pieces(qkv_grad, keep, send, me)
    total[...] = sum(dot(triple[m], weights[m], NT) for m in range(3))


def self_call(kernel, name, us, j, outs, operands, wait, prefix=(), scratch=()):
    lengths, qkv, mixed, out_grad, logs, weights, last_in = operands
    rows, width = mixed.shape
    return launch(
        kernel,
        [*prefix, *operands],
        [smem()] * (len(prefix) + 1)
        + [whole(qkv.shape), whole(mixed.shape), at((rows, width), (0, j))]
        + [whole(logs.shape), whole(weights.shape), whole(last_in.shape)],
        [whole(out.shape) for out in outs],
        outs,
        scratch=self_scratch(rows, width) + list(scratch),
        wait=wait,
        grid=(1,),
        compiler_params=params(),
        name=name,
        cost_estimate=cost(us),
    )


def self_own(me, lengths, qkv, mixed, out_grad, logs, weights, first, wait):
    _, depth, width = weights.shape
    pieces = shape((4, 3, depth // 8, width))
    operands = (lengths, qkv, mixed, out_grad, logs, weights, first)
    scratch = [pltpu.VMEM(weights.shape, F32)]
    outs = [shape(first.shape), pieces, pieces]
    return self_call(self_own_kernel, "self_own", 22, 0, outs, operands, wait, (me,), scratch)


def self_kernel(lengths, qkv, mixed, out_grad, logs, weights, before, total, *scratch):
    self_back_body(lengths, qkv, mixed, out_grad, logs, weights, *scratch)
    triple = scratch[0]
    total[...] = before[...] + sum(dot(triple[m], weights[m], NT) for m in range(3))


def self_back(lengths, qkv, mixed, out_grad, logs, weights, before, j, wait):
    operands = (lengths, qkv, mixed, out_grad, logs, weights, before)
    return self_call(self_kernel, "self_back", 26, j, [shape(before.shape)], operands, wait)[0]


def self_rest_kernel(places, lengths, *refs):
    count = len(places)
    sets, refs = [refs[4 * k : 4 * k + 4] for k in range(count)], refs[4 * count :]
    out_grad, before, tokens, upstream, gain, token_grad, sums, *refs = refs
    held, (total, token_rows, up_rows, sems, out_sems, *scratch) = refs[:5], refs[5:]
    rows, width = held[1].shape[1:]
    waits = []
    for k, (arrays, place) in enumerate(zip(sets, places)):
        sources = [*arrays, out_grad.at[:, pl.ds(place * width, width)]]
        waits.append(
            [
                pltpu.make_async_copy(source, target.at[k], sems.at[k, m])
                for m, (source, target) in enumerate(zip(sources, held))
            ]
        )
    ends = [
        pltpu.make_async_copy(source, target, sems.at[count, m])
        for m, (source, target) in enumerate(
            ((before, total), (tokens, token_rows), (upstream, up_rows))
        )
    ]
    for copy in waits[0] + ends[:1] + sum(waits[1:], []) + ends[1:]:
        copy.start()
    triple = scratch[0]
    for k in range(count):
        for copy in waits[k]:
            copy.wait()
        qkv, mixed, logs, weights, grads = (ref.at[k] for ref in held)
        self_back_body(lengths, qkv, mixed, grads, logs, weights, *scratch)
        if k == 0:
            ends[0].wait()
        total[...] += sum(dot(triple[m], weights[m], NT) for m in range(3))
    ends[1].wait()
    ends[2].wait()
    sums[...] = jnp.zeros_like(sums)
    outs = []
    for k in range(rows // BLK):
        part = slice(k * BLK, (k + 1) * BLK)
        pulled, gain_sum, shift_sum = norm_backward(
            total[part, :], token_rows[part, :].astype(F32), gain[...]
        )
        sums[0:1, :] += gain_sum
        sums[1:2, :] += shift_sum
        up_rows[part, :] = up_rows[part, :] + pulled
        outs.append(
            pltpu.make_async_copy(
                up_rows.at[pl.ds(k * BLK, BLK)], token_grad.at[pl.ds(k * BLK, BLK)], out_sems.at[k]
            )
        )
        outs[-1].start()
    for copy in outs:
        copy.wait()


def self_rest(places, lengths, sets, out_grad, before, tokens, upstream, gain, wait):
    rows, depth = tokens.shape
    count = len(places)
    width = sets[0][1].shape[1]
    args = [lengths, *sum(sets, []), out_grad, before, tokens, upstream, gain]
    held = [
        pltpu.VMEM((count,) + array.shape, array.dtype) for array in sets[0] + [sets[0][1]]
    ]
    return launch(
        partial(self_rest_kernel, places),
        args,
        [smem()] + [anywhere()] * (len(args) - 2) + [vmem()],
        [anywhere(), vmem()],
        [shape((rows, depth)), shape((8, depth))],
        scratch=held
        + [pltpu.VMEM((rows, depth), dtype) for dtype in (F32, BF16, F32)]
        + [pltpu.SemaphoreType.DMA((count + 1, 5)), pltpu.SemaphoreType.DMA((rows // BLK,))]
        + self_scratch(rows, width),
        wait=wait,
        compiler_params=params(),
        name="self_rest",
        cost_estimate=cost(40),
    )


DP = 8
MP = 4


def ring(step):
    pairs = []
    for i in range(DP):
        for z in range(MP):
            to = (z + (step if i % 2 == 0 else -step)) % MP
            pairs.append((i * MP + z, i * MP + to))
    return pairs


def straight(step):
    return [(z, (z + step) % MP) for z in range(MP)]


def beside(first):
    return [(i, i ^ (2 if (i % 2 == 0) == first else 4)) for i in range(DP)]


def swap(value):
    return lax.ppermute(value, "dp", [(i, i ^ 1) for i in range(DP)])


def cut(shard, chip):
    rows = shard.shape[1] // 4
    return lax.dynamic_slice_in_dim(shard, chip * rows, rows, 1).astype(F32)


def near_of(piece):
    return lax.ppermute(piece, "dp", beside(True))


def side_of(piece):
    return lax.ppermute(piece, "dp", beside(False))


def along(value, step):
    return lax.ppermute(value, "mp", straight(step))


def around(value):
    return lax.ppermute(value, ("dp", "mp"), ring(1))


def in_order(keep, send):
    pieces = [part[k] for k, m in ((0, 0), (2, 1), (1, 2), (3, 3)) for part, k in ((keep, k), (send, m))]
    return jnp.concatenate(pieces, axis=1)


def scattered(value, axis):
    return lax.psum_scatter(value, "dp", scatter_dimension=axis, tiled=True)


def sum_near(keep, sent):
    part = keep + sent
    return part[:2], lax.ppermute(part[2:], "dp", beside(True))


def sum_side(part, near):
    part = part + near
    return part[0], side_of(part[1])


def plane_sum(value):
    for bit in (1, 2, 4):
        value = value + lax.ppermute(value, "dp", [(i, i ^ bit) for i in range(DP)])
    return value


def local(
    planar, tokens, text_states, lengths, text_mask, ln_gain, ln_shift, w_qkv, w_out, w_cross_q,
    w_cross_kv, w_cross_out, w_up, w_down, cotangent,
):
    slot_count, text_length = text_mask.shape
    place = lax.axis_index("dp") if planar else jnp.int32(0)
    chip, core = place // 2, place % 2
    me = jnp.stack([chip, core]).astype(jnp.int32)
    gains = [ln_gain[n : n + 1] for n in range(3)]
    shifts = [ln_shift[n : n + 1] for n in range(3)]
    text = text_states.reshape(slot_count * text_length, text_states.shape[2])
    position = lax.broadcasted_iota(jnp.int32, text_mask.shape, 1)
    live = ((text_mask == 1) | (position == 0)).astype(F32).reshape(-1, 1)
    own_qkv = jnp.transpose(w_qkv, (1, 0, 2))
    own_cross = jnp.concatenate([w_cross_q[None], jnp.transpose(w_cross_kv, (1, 0, 2))], axis=0)
    outer, feeds = jnp.stack([w_out, w_cross_out]), jnp.stack([w_up, w_down])
    first = norm_first(tokens, gains[0], shifts[0])
    qkvs, mixeds, logs, weights = ([None] * 4 for _ in range(4))
    weights[0] = own_qkv

    def shards(value):
        return along(value.astype(F32), 1), along(value.astype(F32), 3)

    if planar:
        qkv_one = around(cut(own_qkv, chip))
        qkv_near, qkv_side = near_of(qkv_one), side_of(qkv_one)
        own_piece = gate([qkv_one], cut(own_cross, chip))
        cross_one = around(own_piece)
        wait = [qkv_one]
    else:
        wait = []
    qkvs[0], mixeds[0], logs[0] = front_own(lengths, first, own_qkv, wait)
    carry = []
    if planar:
        mine = join(me, [qkv_one, qkv_near, qkv_side, near_of(qkv_side)], [logs[0], cross_one])
        g_qkv = mine, swap(mine)
        cross_near, cross_side = near_of(cross_one), side_of(cross_one)
        two = around(jnp.where(core == 0, qkv_one, cross_one))
        wait = [cross_one]
        carry = [cut(lax.dynamic_slice_in_dim(outer, core, 1, 0), chip)]
    else:
        g_qkv = shards(own_qkv)
    weights[1], qkvs[1], mixeds[1], logs[1], *carried = front(
        lengths, first, g_qkv[0], wait, carry
    )
    if planar:
        cross_side, two = gate([logs[1]], cross_side), gate([logs[1]], two)
        cross_far = near_of(cross_side)
        two_near, two_side = near_of(two), side_of(two)
        outer_one, outer_three = along(carried[0], 1), along(carried[0], 3)
        wait = [two, cross_near, cross_side, logs[1]]
        carry = [cut(feeds, chip)]
    weights[3], qkvs[3], mixeds[3], logs[3], *carried = front(
        lengths, first, g_qkv[1], wait, carry
    )
    if planar:
        mine = join(me, [cross_one, cross_near, cross_side, cross_far], [logs[3], outer_one, outer_three])
        g_cross = mine, swap(mine)
        mine = join(me, [two, two_near, two_side, near_of(two_side)], [mine])
        g_two = mine, swap(mine)
        outer_two = along(outer_one, 1)
        feed_one = around(carried[0])
        wait = [two_near, two_side]
    else:
        g_cross = shards(own_cross)
        g_two = along(own_qkv.astype(F32), 2), along(own_cross.astype(F32), 2)
    cross_a, cross_b, *pairs = text_front(text, own_cross, g_cross, wait)
    if planar:
        outers = jnp.concatenate([outer_one, outer_two, outer_three], axis=0)
        outers = gate([cross_a], outers)
        outer_near, outer_side = near_of(outers), side_of(outers)
        wait = [outers, feed_one]
    weights[2], cross_two, qkvs[2], mixeds[2], logs[2], pair_two = front_two(
        me, lengths, first, g_two, text, wait
    )
    pairs = [pairs[0], pairs[1], pair_two, pairs[2]]
    crosses = [own_cross, cross_a, cross_two, cross_b]
    if planar:
        outer_side, feed_one = gate([logs[2]], outer_side), gate([logs[2]], feed_one)
        mine = join(me, [outers, outer_near, outer_side, near_of(outer_side)], [logs[2]])
        g_outer = mine, swap(mine)
        feed_near, feed_side = near_of(feed_one), side_of(feed_one)
        feed_two = around(lax.dynamic_slice_in_dim(feed_one, core, 1, 0))
        wait = [feed_one]
    else:
        g_outer = [
            jnp.stack([along(value.astype(F32), step) for step in (1, 2, 3)])
            for value in (w_out, w_cross_out)
        ]
    full_out, full_co, after_self, after_cross, second, third, cross_query, looked, cross_logs = middle(
        me, lengths, live, tokens, (gains[1], shifts[1], gains[2], shifts[2]), w_out, w_cross_out,
        mixeds, crosses, pairs, g_outer, wait,
    )
    if planar:
        feed_side, feed_two = gate([third], feed_side), gate([third], feed_two)
        feed_far = near_of(feed_side)
        last_near, last_side = near_of(feed_two), side_of(feed_two)
        wait = [feed_near, feed_side, feed_two]
    out, grad, both_keep, both_send = feed_own(
        me, third, cotangent, after_cross, w_up, w_down, wait
    )
    if planar:
        mine = join(me, [feed_one, feed_near, feed_side, feed_far], [out, last_near, last_side])
        g_feed = mine, swap(mine)
        last_side = gate([out], last_side)
        last_far = near_of(last_side)
        wait = [last_near, last_side]
    else:
        g_feed = shards(feeds)
    out, grad, both_send = feed_pair(
        third, cotangent, out, grad, g_feed, wait, [both_send]
    )
    if planar:
        mine = join(me, [feed_two, last_near, last_side, last_far], [out])
        g_last = mine, swap(mine)
    else:
        g_last = along(feeds[:1].astype(F32), 2), along(feeds[1:].astype(F32), 2)
        wait = []
    out, grad = feed_last(me, third, cotangent, out, grad, g_last, [])
    if planar:
        both_part, both_near = sum_near(both_keep, swap(both_send))
    upstream, mixed_grad, pair_grad, row_grads, query_grad, sums = back(
        lengths, live, grad, cotangent, after_cross, after_self, cross_query, looked, mixeds[0],
        cross_logs, gains[1], gains[2], full_out, full_co, crosses, pairs,
        [both_part] if planar else [],
    )
    wait = []
    if planar:
        both_part, both_side = sum_side(both_part, gate([sums], both_near))
        wait = [both_near]
    text_grad, keep, send = text_back(
        me, text, pair_grad, second, query_grad, row_grads, crosses, wait
    )
    if planar:
        late_swap = swap(send)
        wait = []
    first_grad, qkv_keep, qkv_send = self_own(
        me, lengths, qkvs[0], mixeds[0], mixed_grad, logs[0], weights[0], first, wait
    )
    if planar:
        late_part, late_near = sum_near(keep, late_swap)
        qkv_swap = swap(qkv_send)
        wait = [late_part, both_side]
    first_grad = self_back(
        lengths, qkvs[1], mixeds[1], mixed_grad, logs[1], weights[1], first_grad, 1, wait
    )
    if planar:
        late_one, late_side = sum_side(late_part, gate([first_grad], late_near))
        qkv_part, qkv_near = sum_near(qkv_keep, gate([first_grad], qkv_swap))
        wait = [late_one, qkv_part]
    token_grad, last_sums = self_rest(
        (2, 3), lengths, [[qkvs[j], mixeds[j], logs[j], weights[j]] for j in (2, 3)],
        mixed_grad, first_grad, tokens, upstream, gains[0], wait,
    )
    if planar:
        qkv_one, qkv_side = sum_side(qkv_part, gate([last_sums], qkv_near))
    norm_sums = jnp.concatenate(
        [last_sums[0:1], sums[2:3], sums[0:1], last_sums[1:2], sums[3:4], sums[1:2]], axis=0
    )
    if planar:
        both_sum, late_sum = both_part + both_side, late_one + late_side
        qkv_sum = qkv_one + qkv_side
        row_sum = [unfold(late_sum[k]) for k in (3, 4)]
        width = norm_sums.shape[1] // DP
        norm_sum = lax.dynamic_slice_in_dim(plane_sum(norm_sums), place * width, width, 1)
    else:
        both_sum = scattered(in_order(both_keep, both_send), 1)
        late = in_order(keep, send)
        late_sum = scattered(late[:3], 1)
        qkv_sum = scattered(in_order(qkv_keep, qkv_send), 1)
        row_sum = [
            scattered(jnp.concatenate([unfold(part) for part in jnp.split(late[k], 8)]), 0)
            for k in (3, 4)
        ]
        norm_sum = scattered(norm_sums, 1)
    return (
        out,
        token_grad,
        text_grad.reshape(text_states.shape),
        norm_sum[:3],
        norm_sum[3:],
        jnp.transpose(qkv_sum, (1, 0, 2)),
        row_sum[0],
        late_sum[0],
        jnp.transpose(late_sum[1:3], (1, 0, 2)),
        row_sum[1],
        both_sum[0],
        both_sum[1],
    )


def solution(mesh):
    placed = (
        P("dp", None),
        P("dp", None, None),
        P("dp"),
        P("dp", None),
        P(),
        P(),
        P(None, None, "mp"),
        P("mp", None),
        P(None, "mp"),
        P(None, None, "mp"),
        P("mp", None),
        P(None, "mp"),
        P("mp", None),
        P("dp", None),
    )
    return jax.shard_map(
        partial(local, mesh.shape["dp"] == DP),
        mesh=mesh,
        in_specs=placed,
        out_specs=(
            P("dp", None),
            P("dp", None),
            P("dp", None, None),
            P(None, "dp"),
            P(None, "dp"),
            P("dp", None, "mp"),
            P(("mp", "dp"), None),
            P("dp", "mp"),
            P("dp", None, "mp"),
            P(("mp", "dp"), None),
            P("dp", "mp"),
            P(("mp", "dp"), None),
        ),
        check_vma=False,
    )
```

```python
from functools import partial

import jax
import jax.numpy as jnp
from jax import lax
from jax.experimental import pallas as pl
from jax.experimental.pallas import tpu as pltpu
from jax.sharding import PartitionSpec as P

HEAD = 64
BLK = 256
EPS = 1e-05
NEG = -1e30
F32 = jnp.float32
BF16 = jnp.bfloat16
MIB = 1024 * 1024

NN = (((1,), (0,)), ((), ()))
NT = (((1,), (1,)), ((), ()))
TN = (((0,), (0,)), ((), ()))


def dot(a, b, dims=NN):
    return lax.dot_general(a, b, dims, preferred_element_type=F32)


def params(mib=56, semantics=None):
    return pltpu.CompilerParams(vmem_limit_bytes=mib * MIB, dimension_semantics=semantics)


def cost(us):
    return pl.CostEstimate(
        flops=int(us * 4.6e8), transcendentals=0, bytes_accessed=int(us * 1.4e6)
    )


def shape(dims, dtype=F32):
    return jax.ShapeDtypeStruct(dims, dtype)


def smem():
    return pl.BlockSpec(memory_space=pltpu.SMEM)


def whole(dims):
    rank = len(dims)
    return pl.BlockSpec(dims, lambda *_: (0,) * rank)


def at(dims, index):
    return pl.BlockSpec(dims, lambda *_: index)


def once(dims):
    rank = len(dims)
    return pl.BlockSpec(dims, lambda *_: (0,) * rank, pipeline_mode=pl.Buffered(1))


def anywhere():
    return pl.BlockSpec(memory_space=pl.ANY)


def launch(kernel, args, in_specs, out_specs, out_shape, scratch=(), wait=(), carry=(), **options):
    args, wait, carry = list(args), list(wait), list(carry)
    count, extra, outs = len(args), len(wait) + len(carry), len(out_shape)

    def body(*refs):
        results = refs[count + extra : count + extra + outs]
        kernel(*refs[:count], *results, *refs[count + extra + outs + len(carry) :])

    return pl.pallas_call(
        body,
        in_specs=list(in_specs) + [anywhere()] * extra,
        out_specs=list(out_specs) + [anywhere()] * len(carry),
        out_shape=list(out_shape) + [shape(value.shape, value.dtype) for value in carry],
        scratch_shapes=list(scratch),
        input_output_aliases={count + len(wait) + k: outs + k for k in range(len(carry))},
        **options,
    )(*args, *wait, *carry)


def gate(wait, carry):
    return launch(
        lambda: None, [], [], [], [], wait=wait, carry=[carry], name="gate", cost_estimate=cost(1)
    )[0]


def rows_of(tile, width):
    return pl.BlockSpec((tile, width), lambda i, *_: (i, 0))


def norm_stats(value):
    center = value - jnp.mean(value, axis=-1, keepdims=True)
    spread = jnp.mean(center * center, axis=-1, keepdims=True)
    inverse = lax.rsqrt(spread + EPS)
    return center * inverse, inverse


def norm_forward(value, gain, shift):
    unit, _ = norm_stats(value)
    return (unit * gain + shift).astype(BF16)


def norm_backward(incoming, value, gain):
    unit, inverse = norm_stats(value)
    scaled = incoming * gain
    pushed = incoming * unit
    inner = (
        scaled
        - jnp.mean(scaled, axis=-1, keepdims=True)
        - unit * jnp.mean(scaled * unit, axis=-1, keepdims=True)
    )
    return (
        inner * inverse,
        jnp.sum(pushed, axis=0, keepdims=True),
        jnp.sum(incoming, axis=0, keepdims=True),
    )


def norm_kernel(tokens_ref, gain_ref, shift_ref, first_ref):
    first_ref[...] = norm_forward(tokens_ref[...].astype(F32), gain_ref[...], shift_ref[...])


def norm_first(tokens, gain, shift):
    rows, width = tokens.shape
    return launch(
        norm_kernel,
        [tokens, gain, shift],
        [rows_of(BLK, width), whole((1, width)), whole((1, width))],
        [rows_of(BLK, width)],
        [shape((rows, width), BF16)],
        grid=(rows // BLK,),
        name="norm_first",
        cost_estimate=cost(6),
    )[0]


def head_row(width, head, value):
    lane = lax.broadcasted_iota(jnp.int32, (1, width), 1)
    return jnp.where(lane // HEAD == head, value, 0.0)


def masked(block, row):
    return (block.astype(F32) * row).astype(BF16)


def item_at(lengths, place):
    item, start, end = 0, 0, 0
    for slot in range(lengths.shape[0]):
        end = end + lengths[slot]
        past = end <= place
        item = item + past.astype(jnp.int32)
        start = jnp.where(past, end, start)
    return item, start


def offsets(core):
    return (0, 1 + core, 2 - core, 3)


def join_kernel(me, *refs):
    parts, (target, sems) = refs[:4], refs[4:]
    copies = []
    for index, (part, offset) in enumerate(zip(parts, offsets(me[1]))):
        rows = part.shape[1]
        place = pl.multiple_of((me[0] ^ offset) * rows, rows)
        for k in range(part.shape[0]):
            copies.append(
                pltpu.make_async_copy(
                    part.at[k], target.at[k, pl.ds(place, rows)], sems.at[index, k]
                )
            )
    for copy in copies:
        copy.start()
    for copy in copies:
        copy.wait()


def join(me, parts, wait):
    count, rows, width = parts[0].shape
    return launch(
        join_kernel,
        [me, *parts],
        [smem()] + [anywhere()] * 4,
        [vmem()],
        [shape((count, 4 * rows, width))],
        scratch=[pltpu.SemaphoreType.DMA((4, count))],
        wait=wait,
        compiler_params=params(24),
        name="join",
        cost_estimate=cost(2),
    )[0]


def take(targets, source):
    for k, target in enumerate(targets):
        target[...] = source[k].astype(BF16)


def take_two(first, second, mine, other, core):
    @pl.when(core == 0)
    def _():
        take(first, mine)
        take(second, other)

    @pl.when(core == 1)
    def _():
        take(second, mine)
        take(first, other)


def planes(ref):
    return [ref.at[k] for k in range(ref.shape[0])]


def causal():
    shape2 = (BLK, BLK)
    return lax.broadcasted_iota(jnp.int32, shape2, 0) <= lax.broadcasted_iota(
        jnp.int32, shape2, 1
    )


def lanes_of(head):
    return slice(head * HEAD, (head + 1) * HEAD)


def self_block(qb, count, qkv, turned, mixed, logs):
    q0 = pl.multiple_of(qb * BLK, BLK)
    k0 = pl.multiple_of((qb - (count - 1)) * BLK, BLK)
    width = qkv.shape[2]
    query = qkv[0, pl.ds(q0, BLK), :]
    diag = qkv[1, pl.ds(q0, BLK), :]
    pre_len = (count - 1) * BLK
    keep = causal()
    pieces = []
    heads = range(width // HEAD)
    parts = [masked(query, head_row(width, head, HEAD**-0.5)) for head in heads]
    nears = [dot(diag, part, NT) for part in parts]
    fars = [dot(qkv[1, pl.ds(k0, pre_len), :], part, NT) for part in parts] if pre_len else []
    for head in heads:
        near = jnp.where(keep, nears[head], NEG)
        peak = jnp.max(near, axis=0, keepdims=True)
        if pre_len:
            far = fars[head]
            peak = jnp.maximum(peak, jnp.max(far, axis=0, keepdims=True))
        near = jnp.exp(near - peak)
        total = jnp.sum(near, axis=0, keepdims=True)
        result = dot(turned[lanes_of(head), pl.ds(q0, BLK)], near.astype(BF16))
        if pre_len:
            far = jnp.exp(far - peak)
            total = total + jnp.sum(far, axis=0, keepdims=True)
            result = result + dot(
                turned[lanes_of(head), pl.ds(k0, pre_len)], far.astype(BF16)
            )
        pieces.append(result * (1.0 / total))
        logs[head : head + 1, pl.ds(q0, BLK)] = peak + jnp.log(total)
    mixed[pl.ds(q0, BLK), :] = jnp.concatenate(pieces, axis=0).T.astype(BF16)


def front_body(lengths, first, weights, qkv, mixed, logs, turned):
    rows = first.shape[0]
    for m in range(3):
        qkv[m] = dot(first[...], weights[m]).astype(BF16)
    turned[...] = qkv[2].T

    @pl.loop(0, rows // BLK)
    def _(qb):
        _, start = item_at(lengths, qb * BLK)
        count = qb - start // BLK + 1
        for n in range(1, 5):

            @pl.when(count == n)
            def _():
                self_block(qb, n, qkv, turned, mixed, logs)


def front_kernel(lengths, first, shard, weights, *rest):
    take(planes(weights), shard)
    front_body(lengths, first, weights, *rest)


def front_two_kernel(me, lengths, first, mine, other, text, weights, cross, qkv, mixed, logs, pair, turned):
    take_two(planes(weights), planes(cross), mine, other, me[1])
    text_pair(pair, text, cross)
    front_body(lengths, first, weights, qkv, mixed, logs, turned)


def vmem():
    return pl.BlockSpec(memory_space=pltpu.VMEM)


def front_call(kernel, name, us, prefix, first, arrays, weight_count, more, wait, carry=()):
    rows, depth = first.shape
    width = arrays[0].shape[2]
    outs = [shape((3, depth, width), BF16)] * weight_count + [
        shape((3, rows, width), BF16),
        shape((rows, width), BF16),
        shape((8, rows), F32),
    ] + more
    return launch(
        kernel,
        [*prefix, first, *arrays],
        [smem()] * len(prefix) + [vmem()] * (1 + len(arrays)),
        [vmem()] * len(outs),
        outs,
        scratch=[pltpu.VMEM((width, rows), BF16)],
        wait=wait,
        carry=carry,
        compiler_params=params(),
        name=name,
        cost_estimate=cost(us),
    )


def front_own(lengths, first, weights, wait, carry):
    return front_call(front_body, "front_own", 15, (lengths,), first, [weights], 0, [], wait, carry)


def front(lengths, first, shard, wait, carry):
    return front_call(front_kernel, "front", 16, (lengths,), first, [shard], 1, [], wait, carry)


def front_two(me, lengths, first, arrays, text, wait):
    pair = shape((2, text.shape[0], arrays[0].shape[2]), BF16)
    return front_call(
        front_two_kernel, "front_two", 18, (me, lengths), first, [*arrays, text], 2, [pair], wait
    )


def text_pair(pair, text, cross):
    for m in range(2):
        pair[m] = dot(text[...], cross[m + 1]).astype(BF16)


def text_front_kernel(text, own, mine, other, cross_a, cross_b, *pairs):
    take(planes(cross_a), mine)
    take(planes(cross_b), other)
    for pair, cross in zip(pairs, (own, cross_a, cross_b)):
        text_pair(pair, text, cross)


def text_front(text, own, arrays, wait):
    rows = text.shape[0]
    width = own.shape[2]
    outs = [shape(own.shape, BF16)] * 2 + [shape((2, rows, width), BF16)] * 3
    return launch(
        text_front_kernel,
        [text, own, *arrays],
        [vmem()] * 4,
        [vmem()] * 5,
        outs,
        wait=wait,
        compiler_params=params(),
        name="text_front",
        cost_estimate=cost(7),
    )


def unfold_into(target, first, source):
    width = source.shape[2]
    rows = width // 4
    for piece in range(4):
        for part in range(4):
            target[pl.ds(first + piece * rows, rows), part * width : (part + 1) * width] = source[
                0, pl.ds(piece * width + part * rows, rows), :
            ].astype(BF16)


def middle_kernel(me, lengths, live, tokens, gain1, shift1, gain2, shift2, own_out, own_co, *refs):
    mixed, refs = refs[:4], refs[4:]
    queries, refs = refs[:4], refs[4:]
    pairs, refs = refs[:4], refs[4:]
    outs, cos, (out_two, co_two), refs = refs[:2], refs[2:4], refs[4:6], refs[6:]
    w_out, w_co, after_self, after_cross, second, third, cross_query, looked, logs, turned = refs
    step = pl.program_id(0)

    @pl.when(step == 0)
    def _():
        width = own_out.shape[0]
        w_out[:width, :] = own_out[...]
        w_co[:width, :] = own_co[...]
        for place, out_part, co_part in ((1, outs[0], cos[0]), (3, outs[1], cos[1])):
            unfold_into(w_out, place * width, out_part)
            unfold_into(w_co, place * width, co_part)

        @pl.when(me[1] == 0)
        def _():
            unfold_into(w_out, 2 * width, out_two)
            unfold_into(w_co, 2 * width, co_two)

        @pl.when(me[1] == 1)
        def _():
            unfold_into(w_co, 2 * width, out_two)
            unfold_into(w_out, 2 * width, co_two)

        for j in range(4):
            turned[j] = pairs[j][1].T

    part = jnp.concatenate([ref[...] for ref in mixed], axis=1)
    residual = tokens[...].astype(F32) + dot(part, w_out[...])
    after_self[...] = residual
    normed = norm_forward(residual, gain1[...], shift1[...])
    second[...] = normed
    text = TEXT
    item, _ = item_at(lengths, step * BLK)
    t0 = pl.multiple_of(item * text, text)
    alive = live[pl.ds(t0, text), :] > 0.0
    width = own_out.shape[0]
    heads = range(width // HEAD)
    stages = []
    for j in range(4):
        query = dot(normed, queries[j][0]).astype(BF16)
        cross_query[:, j * width : (j + 1) * width] = query
        rows = [masked(query, head_row(width, head, HEAD**-0.5)) for head in heads]
        keys = pairs[j][0, pl.ds(t0, text), :]
        stages.append([dot(keys, row, NT) for row in rows])
    for j in range(4):
        pieces = []
        for head in heads:
            score = jnp.where(alive, stages[j][head], NEG)
            peak = jnp.max(score, axis=0, keepdims=True)
            score = jnp.exp(score - peak)
            total = jnp.sum(score, axis=0, keepdims=True)
            result = dot(turned[j, lanes_of(head), pl.ds(t0, text)], score.astype(BF16))
            pieces.append(result * (1.0 / total))
            index = j * (width // HEAD) + head
            logs[index : index + 1, :] = peak + jnp.log(total)
        looked[:, j * width : (j + 1) * width] = jnp.concatenate(pieces, axis=0).T.astype(BF16)
    residual = residual + dot(looked[...], w_co[...])
    after_cross[...] = residual
    third[...] = norm_forward(residual, gain2[...], shift2[...])


TEXT = 128


def middle(me, lengths, live, tokens, norms, own_out, own_co, mixed, crosses, pairs, g_cross, g_two, wait):
    rows, depth = tokens.shape
    width = own_out.shape[0]
    text_rows = live.shape[0]
    inner = 4 * width
    row = whole((1, depth))

    def plane_at(k):
        dims = (1, depth, width)
        return pl.BlockSpec(dims, lambda *_: (k, 0, 0), pipeline_mode=pl.Buffered(1))

    return launch(
        middle_kernel,
        [me, lengths, live, tokens, *norms, own_out, own_co, *mixed, *crosses, *pairs]
        + [*g_cross, *g_cross, *g_two],
        [smem(), smem(), whole((text_rows, 1)), rows_of(BLK, depth)]
        + [row] * 4
        + [once((width, depth))] * 2
        + [rows_of(BLK, width)] * 4
        + [at((1, depth, width), (0, 0, 0))] * 4
        + [whole((2, text_rows, width))] * 4
        + [plane_at(k) for k in (3, 3, 4, 4, 3, 3)],
        [whole((inner, depth))] * 2
        + [rows_of(BLK, depth)] * 4
        + [rows_of(BLK, inner)] * 2
        + [pl.BlockSpec((inner // HEAD, BLK), lambda i: (0, i))],
        [shape((inner, depth), BF16)] * 2
        + [shape((rows, depth)), shape((rows, depth))]
        + [shape((rows, depth), BF16)] * 2
        + [shape((rows, inner), BF16)] * 2
        + [shape((inner // HEAD, rows))],
        scratch=[pltpu.VMEM((4, width, text_rows), BF16)],
        wait=wait,
        grid=(rows // BLK,),
        compiler_params=params(),
        name="middle",
        cost_estimate=cost(43),
    )


ROOT = 0.7978845608028654
CUBE = 0.044715


def gelu_both(value):
    square = value * value
    bend = jnp.tanh(value * (ROOT + (ROOT * CUBE) * square))
    half = 0.5 + 0.5 * bend
    slope = half + (0.5 * value) * (1.0 - bend * bend) * (ROOT + (3.0 * ROOT * CUBE) * square)
    return value * half, slope


def feed_rows(third, cot, up, down):
    return feed_finish(dot(third, up), dot(cot, down, NT), up, down)


def feed_finish(pre_act, hidden_grad, up, down):
    hidden, slope = gelu_both(pre_act)
    hidden = hidden.astype(BF16)
    pre_grad = (hidden_grad * slope).astype(BF16)
    return hidden, pre_grad, dot(hidden, down), dot(pre_grad, up, NT)


def feed_own_kernel(me, third, cot, after, up, down, out, grad, keep, send, both):
    hidden, pre_grad, result, pushed = feed_rows(third[...], cot[...], up[...], down[...])
    out[...] = after[...] + result
    grad[...] = pushed
    step = pl.program_id(0)
    more_up = dot(third[...], pre_grad, TN)
    more_down = dot(hidden, cot[...], TN)

    @pl.when(step == 0)
    def _():
        both[0] = more_up
        both[1] = more_down

    @pl.when(step > 0)
    def _():
        both[0] += more_up
        both[1] += more_down

    @pl.when(step == pl.num_programs(0) - 1)
    def _():
        put_pieces(both, keep, send, me)


def put_pieces(source, keep, send, me, first=0):
    chip, core = me[0], me[1]
    rows = source.shape[1] // 8
    for target, owner in ((keep, core), (send, 1 - core)):
        for index, offset in enumerate((0, 2 - owner, 1 + owner, 3)):
            place = pl.multiple_of(((chip ^ offset) * 2 + owner) * rows, rows)
            for k in range(source.shape[0]):
                target[index, first + k] = source[k, pl.ds(place, rows), :]


FEED = 320


def feed_own(me, third, cot, after, up, down, wait):
    rows, depth = third.shape
    inner = up.shape[1]
    tile = rows_of(FEED, depth)
    pieces = (4, 2, depth // 8, depth)
    return launch(
        feed_own_kernel,
        [me, third, cot, after, up, down],
        [smem(), tile, tile, tile, once((depth, inner)), once((inner, depth))],
        [tile, tile, once(pieces), once(pieces)],
        [shape((rows, depth)), shape((rows, depth)), shape(pieces), shape(pieces)],
        scratch=[pltpu.VMEM((2, depth, inner), F32)],
        wait=wait,
        grid=(rows // FEED,),
        compiler_params=params(),
        name="feed_own",
        cost_estimate=cost(32),
    )


def feed_pair_kernel(third, cot, out_in, grad_in, mine, other, out, grad, one, two):
    @pl.when(pl.program_id(0) == 0)
    def _():
        take(planes(one), mine)
        take(planes(two), other)

    _, _, result, pushed = feed_rows(third[...], cot[...], one[0], one[1])
    _, _, more_result, more_pushed = feed_rows(third[...], cot[...], two[0], two[1])
    out[...] = out_in[...] + (result + more_result)
    grad[...] = grad_in[...] + (pushed + more_pushed)


def feed_last_kernel(me, third, cot, out_in, grad_in, mine, other, out, grad, both):
    @pl.when(pl.program_id(0) == 0)
    def _():
        up, down = planes(both)
        take_two([up], [down], mine, other, me[1])

    _, _, result, pushed = feed_rows(third[...], cot[...], both[0], both[1])
    out[...] = (out_in[...] + result).astype(BF16)
    grad[...] = grad_in[...] + pushed


def feed_call(kernel, name, us, prefix, dtype, copies, third, cot, out, grad, arrays, wait, carry=()):
    rows, depth = third.shape
    tile = rows_of(FEED, depth)
    return launch(
        kernel,
        [*prefix, third, cot, out, grad, *arrays],
        [smem()] * len(prefix) + [tile] * 4 + [once(arrays[0].shape)] * 2,
        [tile, tile],
        [shape((rows, depth), dtype), shape((rows, depth))],
        scratch=[pltpu.VMEM((2,) + arrays[0].shape[1:], BF16)] * copies,
        wait=wait,
        carry=carry,
        grid=(rows // FEED,),
        compiler_params=params(),
        name=name,
        cost_estimate=cost(us),
    )


def feed_pair(*operands):
    return feed_call(feed_pair_kernel, "feed_pair", 30, (), F32, 2, *operands)


def feed_last(me, *operands):
    return feed_call(feed_last_kernel, "feed_last", 18, (me,), BF16, 1, *operands)


def back_kernel(
    lengths, live, third_grad, cot, after_cross, after_self, cross_query, looked0, mixed0, logs,
    gain1, gain2, w_out, w_co, *refs,
):
    queries, refs = refs[:4], refs[4:]
    pairs, refs = refs[:4], refs[4:]
    up_grad, mixed_grad, pair_grad, row_grads, query_grads, sums, total, turned = refs
    step = pl.program_id(0)
    text = TEXT

    @pl.when(step == 0)
    def _():
        total[...] = jnp.zeros_like(total)
        row_grads[...] = jnp.zeros_like(row_grads)
        sums[...] = jnp.zeros_like(sums)
        for j in range(4):
            turned[j] = pairs[j][0].T

    pulled, gain_sum, shift_sum = norm_backward(third_grad[...], after_cross[...], gain2[...])
    sums[0:1, :] += gain_sum
    sums[1:2, :] += shift_sum
    upstream = cot[...].astype(F32) + pulled
    low = upstream.astype(BF16)
    row_grads[1] += dot(looked0[...], low, TN)
    looked_grad = dot(low, w_co[...], NT).astype(BF16)
    item, _ = item_at(lengths, step * BLK)
    t0 = pl.multiple_of(item * text, text)
    alive = live[pl.ds(t0, text), :] > 0.0
    second_grad = jnp.zeros(upstream.shape, F32)
    width = queries[0].shape[2]
    heads = range(width // HEAD)

    def scores(j):
        cols = slice(j * width, (j + 1) * width)
        rows = [masked(cross_query[:, cols], head_row(width, h, HEAD**-0.5)) for h in heads]
        grads = [masked(looked_grad[:, cols], head_row(width, h, 1.0)) for h in heads]
        keys = pairs[j][0, pl.ds(t0, text), :]
        values = pairs[j][1, pl.ds(t0, text), :]
        return rows, grads, [dot(keys, row, NT) for row in rows], [dot(values, g, NT) for g in grads]

    ahead = scores(0)
    for j in range(4):
        rows, grads, score_set, pushed_set = ahead
        if j < 3:
            ahead = scores(j + 1)
        pieces, chances, score_grads = [], [], []
        for head in heads:
            index = j * (width // HEAD) + head
            score = jnp.where(alive, score_set[head], NEG)
            chance = jnp.exp(score - logs[index : index + 1, :])
            weighted = chance * pushed_set[head]
            mean = jnp.sum(weighted, axis=0, keepdims=True)
            score_grads.append((weighted - chance * mean).astype(BF16))
            chances.append(chance.astype(BF16))
            pieces.append(dot(turned[j, lanes_of(head), pl.ds(t0, text)], score_grads[head]))
        total[j, 0, pl.ds(t0, text), :] += dot(
            jnp.concatenate(score_grads, axis=1), jnp.concatenate(rows, axis=0)
        )
        total[j, 1, pl.ds(t0, text), :] += dot(
            jnp.concatenate(chances, axis=1), jnp.concatenate(grads, axis=0)
        )
        query_grad = (jnp.concatenate(pieces, axis=0).T * HEAD**-0.5).astype(BF16)
        if j == 0:
            query_grads[...] = query_grad
        second_grad = second_grad + dot(query_grad, queries[j][0], NT)

    pulled, gain_sum, shift_sum = norm_backward(second_grad, after_self[...], gain1[...])
    sums[2:3, :] += gain_sum
    sums[3:4, :] += shift_sum
    upstream = upstream + pulled
    up_grad[...] = upstream
    low = upstream.astype(BF16)
    row_grads[0] += dot(mixed0[...], low, TN)
    mixed_grad[...] = dot(low, w_out[...], NT).astype(BF16)

    @pl.when(step == pl.num_programs(0) - 1)
    def _():
        pair_grad[...] = total[...].astype(BF16)


def back(
    lengths, live, third_grad, cot, after_cross, after_self, cross_query, looked, mixed0, logs,
    gain1, gain2, w_out, w_co, crosses, pairs, wait,
):
    rows, depth = cot.shape
    text_rows = live.shape[0]
    width = mixed0.shape[1]
    inner = 4 * width
    tile = rows_of(BLK, depth)
    row = whole((1, depth))
    return launch(
        back_kernel,
        [lengths, live, third_grad, cot, after_cross, after_self, cross_query, looked, mixed0]
        + [logs, gain1, gain2, w_out, w_co, *crosses, *pairs],
        [smem(), whole((text_rows, 1))]
        + [tile] * 4
        + [rows_of(BLK, inner), rows_of(BLK, width), rows_of(BLK, width)]
        + [pl.BlockSpec((inner // HEAD, BLK), lambda i: (0, i)), row, row]
        + [whole((inner, depth))] * 2
        + [at((1, depth, width), (0, 0, 0))] * 4
        + [whole((2, text_rows, width))] * 4,
        [tile, rows_of(BLK, inner), whole((4, 2, text_rows, width))]
        + [whole((2, width, depth)), rows_of(BLK, width), whole((8, depth))],
        [
            shape((rows, depth)),
            shape((rows, inner), BF16),
            shape((4, 2, text_rows, width), BF16),
            shape((2, width, depth)),
            shape((rows, width), BF16),
            shape((8, depth)),
        ],
        scratch=[
            pltpu.VMEM((4, 2, text_rows, width), F32),
            pltpu.VMEM((4, width, text_rows), BF16),
        ],
        wait=wait,
        grid=(rows // BLK,),
        compiler_params=params(),
        name="back",
        cost_estimate=cost(53),
    )


def text_kernel(me, text, pair_grad, second, query_grad, row_grads, *refs):
    crosses, (text_grad, keep, send, cross_grad, folded) = refs[:4], refs[4:]
    total = jnp.zeros(text_grad.shape, F32)
    for j in range(4):
        for m in range(2):
            total = total + dot(pair_grad[j, m], crosses[j][m + 1], NT)
    text_grad[...] = total
    cross_grad[0] = dot(second[...], query_grad[...], TN)
    for m in range(2):
        cross_grad[m + 1] = dot(text[...], pair_grad[0, m], TN)
    put_pieces(cross_grad, keep, send, me)
    width = folded.shape[2]
    rows = row_grads.shape[1] // 8
    for k in range(2):
        for piece in range(8):
            for part in range(4):
                folded[k, pl.ds((piece * 4 + part) * rows, rows), :] = row_grads[
                    k, pl.ds(piece * rows, rows), part * width : (part + 1) * width
                ]
    put_pieces(folded, keep, send, me, 3)


def unfold(piece):
    rows, width = piece.shape
    parts = [piece[k * rows // 4 : (k + 1) * rows // 4] for k in range(4)]
    return jnp.concatenate(parts, axis=1)


def text_back(me, text, pair_grad, second, query_grad, row_grads, crosses, wait):
    text_rows, depth = text.shape
    width = pair_grad.shape[3]
    pieces = (4, 5, depth // 8, width)
    return launch(
        text_kernel,
        [me, text, pair_grad, second, query_grad, row_grads, *crosses],
        [smem()] + [vmem()] * 9,
        [vmem()] * 3,
        [shape((text_rows, depth)), shape(pieces), shape(pieces)],
        scratch=[pltpu.VMEM((3, depth, width), F32), pltpu.VMEM((2, depth, width), F32)],
        wait=wait,
        compiler_params=params(),
        name="text_back",
        cost_estimate=cost(15),
    )


def self_back_pair(qb, kb, diag, qkv, rows, grads, logs, means, turned, query_sum, key_sum, value_sum):
    q0 = pl.multiple_of(qb * BLK, BLK)
    k0 = pl.multiple_of(kb * BLK, BLK)
    keys = qkv[1, pl.ds(k0, BLK), :]
    values = qkv[2, pl.ds(k0, BLK), :]
    more_keys = 0.0
    more_values = 0.0
    heads = range(rows.shape[0])
    stages = [(dot(keys, rows[h], NT), dot(values, grads[h], NT)) for h in heads]
    for head, (score, pushed) in zip(heads, stages):
        if diag:
            score = jnp.where(causal(), score, NEG)
        chance = jnp.exp(score - logs[head : head + 1, pl.ds(q0, BLK)])
        score_grad = (chance * (pushed - means[head : head + 1, :])).astype(BF16)
        query_sum[lanes_of(head), :] += dot(turned[lanes_of(head), pl.ds(k0, BLK)], score_grad)
        more_keys = more_keys + dot(score_grad, rows[head])
        more_values = more_values + dot(chance.astype(BF16), grads[head])
    key_sum[pl.ds(k0, BLK), :] += more_keys
    value_sum[pl.ds(k0, BLK), :] += more_values


def self_back_body(
    lengths, qkv, mixed, out_grad, logs, weights, triple, turned, rows, grads, means, query_sum,
    key_sum, value_sum,
):
    row_count, width = mixed.shape
    turned[...] = qkv[1].T
    key_sum[...] = jnp.zeros_like(key_sum)
    value_sum[...] = jnp.zeros_like(value_sum)

    @pl.loop(0, row_count // BLK)
    def _(qb):
        q0 = pl.multiple_of(qb * BLK, BLK)
        _, start = item_at(lengths, q0)
        query = qkv[0, pl.ds(q0, BLK), :]
        grad = out_grad[pl.ds(q0, BLK), :]
        flat = (grad.astype(F32) * mixed[pl.ds(q0, BLK), :].astype(F32)).T
        for head in range(width // HEAD):
            rows[head] = masked(query, head_row(width, head, HEAD**-0.5))
            grads[head] = masked(grad, head_row(width, head, 1.0))
            means[head : head + 1, :] = jnp.sum(flat[lanes_of(head), :], axis=0, keepdims=True)
        query_sum[...] = jnp.zeros_like(query_sum)
        rest = (qkv, rows, grads, logs, means, turned, query_sum, key_sum, value_sum)

        @pl.loop(start // BLK, qb)
        def _(kb):
            self_back_pair(qb, kb, False, *rest)

        self_back_pair(qb, qb, True, *rest)
        triple[0, pl.ds(q0, BLK), :] = (query_sum[...].T * HEAD**-0.5).astype(BF16)

    triple[1] = key_sum[...].astype(BF16)
    triple[2] = value_sum[...].astype(BF16)


def self_scratch(rows, width):
    heads = width // HEAD
    return [
        pltpu.VMEM((3, rows, width), BF16),
        pltpu.VMEM((width, rows), BF16),
        pltpu.VMEM((heads, BLK, width), BF16),
        pltpu.VMEM((heads, BLK, width), BF16),
        pltpu.VMEM((8, BLK), F32),
        pltpu.VMEM((width, BLK), F32),
        pltpu.VMEM((rows, width), F32),
        pltpu.VMEM((rows, width), F32),
    ]


def self_own_kernel(me, lengths, qkv, mixed, out_grad, logs, weights, first, total, keep, send, *scratch):
    self_back_body(lengths, qkv, mixed, out_grad, logs, weights, *scratch[:-1])
    triple, qkv_grad = scratch[0], scratch[-1]
    for m in range(3):
        qkv_grad[m] = dot(first[...], triple[m], TN)
    put_pieces(qkv_grad, keep, send, me)
    total[...] = sum(dot(triple[m], weights[m], NT) for m in range(3))


def self_call(kernel, name, us, j, outs, operands, wait, prefix=(), scratch=()):
    lengths, qkv, mixed, out_grad, logs, weights, last_in = operands
    rows, width = mixed.shape
    return launch(
        kernel,
        [*prefix, *operands],
        [smem()] * (len(prefix) + 1)
        + [whole(qkv.shape), whole(mixed.shape), at((rows, width), (0, j))]
        + [whole(logs.shape), whole(weights.shape), whole(last_in.shape)],
        [whole(out.shape) for out in outs],
        outs,
        scratch=self_scratch(rows, width) + list(scratch),
        wait=wait,
        grid=(1,),
        compiler_params=params(),
        name=name,
        cost_estimate=cost(us),
    )


def self_own(me, lengths, qkv, mixed, out_grad, logs, weights, first, wait):
    _, depth, width = weights.shape
    pieces = shape((4, 3, depth // 8, width))
    operands = (lengths, qkv, mixed, out_grad, logs, weights, first)
    scratch = [pltpu.VMEM(weights.shape, F32)]
    outs = [shape(first.shape), pieces, pieces]
    return self_call(self_own_kernel, "self_own", 22, 0, outs, operands, wait, (me,), scratch)


def self_kernel(lengths, qkv, mixed, out_grad, logs, weights, before, total, *scratch):
    self_back_body(lengths, qkv, mixed, out_grad, logs, weights, *scratch)
    triple = scratch[0]
    total[...] = before[...] + sum(dot(triple[m], weights[m], NT) for m in range(3))


def self_back(lengths, qkv, mixed, out_grad, logs, weights, before, j, wait):
    operands = (lengths, qkv, mixed, out_grad, logs, weights, before)
    return self_call(self_kernel, "self_back", 26, j, [shape(before.shape)], operands, wait)[0]


def self_rest_kernel(places, lengths, *refs):
    count = len(places)
    sets, refs = [refs[4 * k : 4 * k + 4] for k in range(count)], refs[4 * count :]
    out_grad, before, tokens, upstream, gain, token_grad, sums, *refs = refs
    held, (total, token_rows, up_rows, sems, out_sems, *scratch) = refs[:5], refs[5:]
    rows, width = held[1].shape[1:]
    waits = []
    for k, (arrays, place) in enumerate(zip(sets, places)):
        sources = [*arrays, out_grad.at[:, pl.ds(place * width, width)]]
        waits.append(
            [
                pltpu.make_async_copy(source, target.at[k], sems.at[k, m])
                for m, (source, target) in enumerate(zip(sources, held))
            ]
        )
    ends = [
        pltpu.make_async_copy(source, target, sems.at[count, m])
        for m, (source, target) in enumerate(
            ((before, total), (tokens, token_rows), (upstream, up_rows))
        )
    ]
    for copy in waits[0] + ends[:1] + sum(waits[1:], []) + ends[1:]:
        copy.start()
    triple = scratch[0]
    for k in range(count):
        for copy in waits[k]:
            copy.wait()
        qkv, mixed, logs, weights, grads = (ref.at[k] for ref in held)
        self_back_body(lengths, qkv, mixed, grads, logs, weights, *scratch)
        if k == 0:
            ends[0].wait()
        total[...] += sum(dot(triple[m], weights[m], NT) for m in range(3))
    ends[1].wait()
    ends[2].wait()
    sums[...] = jnp.zeros_like(sums)
    outs = []
    for k in range(rows // BLK):
        part = slice(k * BLK, (k + 1) * BLK)
        pulled, gain_sum, shift_sum = norm_backward(
            total[part, :], token_rows[part, :].astype(F32), gain[...]
        )
        sums[0:1, :] += gain_sum
        sums[1:2, :] += shift_sum
        up_rows[part, :] = up_rows[part, :] + pulled
        outs.append(
            pltpu.make_async_copy(
                up_rows.at[pl.ds(k * BLK, BLK)], token_grad.at[pl.ds(k * BLK, BLK)], out_sems.at[k]
            )
        )
        outs[-1].start()
    for copy in outs:
        copy.wait()


def self_rest(places, lengths, sets, out_grad, before, tokens, upstream, gain, wait):
    rows, depth = tokens.shape
    count = len(places)
    width = sets[0][1].shape[1]
    args = [lengths, *sum(sets, []), out_grad, before, tokens, upstream, gain]
    held = [
        pltpu.VMEM((count,) + array.shape, array.dtype) for array in sets[0] + [sets[0][1]]
    ]
    return launch(
        partial(self_rest_kernel, places),
        args,
        [smem()] + [anywhere()] * (len(args) - 2) + [vmem()],
        [anywhere(), vmem()],
        [shape((rows, depth)), shape((8, depth))],
        scratch=held
        + [pltpu.VMEM((rows, depth), dtype) for dtype in (F32, BF16, F32)]
        + [pltpu.SemaphoreType.DMA((count + 1, 5)), pltpu.SemaphoreType.DMA((rows // BLK,))]
        + self_scratch(rows, width),
        wait=wait,
        compiler_params=params(),
        name="self_rest",
        cost_estimate=cost(40),
    )


DP = 8
MP = 4


def ring(step):
    pairs = []
    for i in range(DP):
        for z in range(MP):
            to = (z + (step if i % 2 == 0 else -step)) % MP
            pairs.append((i * MP + z, i * MP + to))
    return pairs


def straight(step):
    return [(z, (z + step) % MP) for z in range(MP)]


def beside(first):
    return [(i, i ^ (2 if (i % 2 == 0) == first else 4)) for i in range(DP)]


def swap(value):
    return lax.ppermute(value, "dp", [(i, i ^ 1) for i in range(DP)])


def fold(piece):
    width = piece.shape[1] // 4
    return jnp.concatenate([piece[:, k * width : (k + 1) * width] for k in range(4)], axis=0)


def fold_whole(shard):
    return jnp.concatenate([fold(piece) for piece in jnp.split(shard, 4)], axis=0)


def cut(shard, chip):
    rows = shard.shape[1] // 4
    return lax.dynamic_slice_in_dim(shard, chip * rows, rows, 1).astype(F32)


def near_of(piece):
    return lax.ppermute(piece, "dp", beside(True))


def side_of(piece):
    return lax.ppermute(piece, "dp", beside(False))


def along(value, step):
    return lax.ppermute(value, "mp", straight(step))


def around(value):
    return lax.ppermute(value, ("dp", "mp"), ring(1))


def in_order(keep, send):
    pieces = [part[k] for k, m in ((0, 0), (2, 1), (1, 2), (3, 3)) for part, k in ((keep, k), (send, m))]
    return jnp.concatenate(pieces, axis=1)


def scattered(value, axis):
    return lax.psum_scatter(value, "dp", scatter_dimension=axis, tiled=True)


def sum_near(keep, sent):
    part = keep + sent
    return part[:2], lax.ppermute(part[2:], "dp", beside(True))


def sum_side(part, near):
    part = part + near
    return part[0], side_of(part[1])


def plane_sum(value):
    for bit in (1, 2, 4):
        value = value + lax.ppermute(value, "dp", [(i, i ^ bit) for i in range(DP)])
    return value


def local(
    planar, tokens, text_states, lengths, text_mask, ln_gain, ln_shift, w_qkv, w_out, w_cross_q,
    w_cross_kv, w_cross_out, w_up, w_down, cotangent,
):
    slot_count, text_length = text_mask.shape
    place = lax.axis_index("dp") if planar else jnp.int32(0)
    chip, core = place // 2, place % 2
    me = jnp.stack([chip, core]).astype(jnp.int32)
    gains = [ln_gain[n : n + 1] for n in range(3)]
    shifts = [ln_shift[n : n + 1] for n in range(3)]
    text = text_states.reshape(slot_count * text_length, text_states.shape[2])
    position = lax.broadcasted_iota(jnp.int32, text_mask.shape, 1)
    live = ((text_mask == 1) | (position == 0)).astype(F32).reshape(-1, 1)
    own_qkv = jnp.transpose(w_qkv, (1, 0, 2))
    own_cross = jnp.concatenate([w_cross_q[None], jnp.transpose(w_cross_kv, (1, 0, 2))], axis=0)
    feeds = jnp.stack([w_up, w_down])
    first = norm_first(tokens, gains[0], shifts[0])
    qkvs, mixeds, logs, weights = ([None] * 4 for _ in range(4))
    weights[0] = own_qkv

    def shards(value):
        return along(value.astype(F32), 1), along(value.astype(F32), 3)

    wait, carry = [], []
    if planar:
        rows = w_out.shape[0] // 4
        outer = [
            fold(lax.dynamic_slice_in_dim(value, chip * rows, rows, 0))[None].astype(F32)
            for value in (w_out, w_cross_out)
        ]
        qkv_one = around(cut(own_qkv, chip))
        qkv_near, qkv_side = near_of(qkv_one), side_of(qkv_one)
        own_piece = gate([qkv_one], jnp.concatenate([cut(own_cross, chip), *outer], axis=0))
        cross_one = around(own_piece)
        wait = [qkv_one, own_piece]
    qkvs[0], mixeds[0], logs[0] = front_own(lengths, first, own_qkv, wait, [])
    if planar:
        mine = join(me, [qkv_one, qkv_near, qkv_side, near_of(qkv_side)], [logs[0]])
        g_qkv = mine, swap(mine)
        cross_near, cross_side = near_of(cross_one), side_of(cross_one)
        two = jnp.where(
            core == 0,
            jnp.concatenate([qkv_one, cross_one[3:4]], axis=0),
            jnp.concatenate([cross_one[:3], cross_one[4:5]], axis=0),
        )
        two = around(two)
        wait = [cross_one]
        carry = [cut(feeds, chip)]
    else:
        folded = [fold_whole(value)[None] for value in (w_out, w_cross_out)]
        g_qkv = shards(own_qkv)
        g_cross = shards(jnp.concatenate([own_cross, *folded], axis=0))
        g_two = [
            along(jnp.concatenate(parts, axis=0).astype(F32), 2)
            for parts in ((own_qkv, folded[0]), (own_cross, folded[1]))
        ]
        g_feed = shards(feeds)
        g_last = along(feeds[:1].astype(F32), 2), along(feeds[1:].astype(F32), 2)
    weights[1], qkvs[1], mixeds[1], logs[1], *carried = front(
        lengths, first, g_qkv[0], wait, carry
    )
    if planar:
        cross_side, two = gate([logs[1]], cross_side), gate([logs[1]], two)
        cross_far = near_of(cross_side)
        two_near, two_side = near_of(two), side_of(two)
        feed_one = around(carried[0])
        wait = [two, cross_near, cross_side, logs[1]]
    weights[3], qkvs[3], mixeds[3], logs[3] = front(lengths, first, g_qkv[1], wait, [])
    if planar:
        mine = join(me, [cross_one, cross_near, cross_side, cross_far], [logs[3], feed_one, two_near, two_side])
        g_cross = mine, swap(mine)
        two_far = near_of(two_side)
        feed_near, feed_side = near_of(feed_one), side_of(feed_one)
        feed_two = around(lax.dynamic_slice_in_dim(feed_one, core, 1, 0))
        wait = [two_near, two_side]
    cross_a, cross_b, *pairs = text_front(text, own_cross, g_cross, wait)
    if planar:
        mine = join(me, [two, two_near, two_side, two_far], [cross_a])
        g_two = mine, swap(mine)
        wait = []
    weights[2], cross_two, qkvs[2], mixeds[2], logs[2], pair_two = front_two(
        me, lengths, first, g_two, text, wait
    )
    pairs = [pairs[0], pairs[1], pair_two, pairs[2]]
    crosses = [own_cross, cross_a, cross_two, cross_b]
    if planar:
        feed_side, feed_two = gate([logs[2]], feed_side), gate([logs[2]], feed_two)
        feed_far = near_of(feed_side)
        last_near, last_side = near_of(feed_two), side_of(feed_two)
        wait = [feed_near, feed_side, feed_two]
    full_out, full_co, after_self, after_cross, second, third, cross_query, looked, cross_logs = middle(
        me, lengths, live, tokens, (gains[1], shifts[1], gains[2], shifts[2]), w_out, w_cross_out,
        mixeds, crosses, pairs, g_cross, g_two, wait,
    )
    if planar:
        mine = join(me, [feed_one, feed_near, feed_side, feed_far], [third, last_near, last_side])
        g_feed = mine, swap(mine)
        last_far = near_of(last_side)
        wait = [mine]
    out, grad, both_keep, both_send = feed_own(
        me, third, cotangent, after_cross, w_up, w_down, wait
    )
    if planar:
        mine = join(me, [feed_two, last_near, last_side, last_far], [out])
        g_last = mine, swap(mine)
        wait = [mine]
    out, grad, both_send = feed_pair(
        third, cotangent, out, grad, g_feed, wait, [both_send]
    )
    out, grad = feed_last(me, third, cotangent, out, grad, g_last, [])
    if planar:
        both_part, both_near = sum_near(both_keep, swap(both_send))
    upstream, mixed_grad, pair_grad, row_grads, query_grad, sums = back(
        lengths, live, grad, cotangent, after_cross, after_self, cross_query, looked, mixeds[0],
        cross_logs, gains[1], gains[2], full_out, full_co, crosses, pairs,
        [both_part] if planar else [],
    )
    wait = []
    if planar:
        both_part, both_side = sum_side(both_part, gate([sums], both_near))
        wait = [both_near]
    text_grad, keep, send = text_back(
        me, text, pair_grad, second, query_grad, row_grads, crosses, wait
    )
    if planar:
        late_swap = swap(send)
        wait = []
    first_grad, qkv_keep, qkv_send = self_own(
        me, lengths, qkvs[0], mixeds[0], mixed_grad, logs[0], weights[0], first, wait
    )
    if planar:
        late_part, late_near = sum_near(keep, late_swap)
        qkv_swap = swap(qkv_send)
        wait = [late_part, both_side]
    first_grad = self_back(
        lengths, qkvs[1], mixeds[1], mixed_grad, logs[1], weights[1], first_grad, 1, wait
    )
    if planar:
        late_one, late_side = sum_side(late_part, gate([first_grad], late_near))
        qkv_part, qkv_near = sum_near(qkv_keep, gate([first_grad], qkv_swap))
        wait = [late_one, qkv_part]
    token_grad, last_sums = self_rest(
        (2, 3), lengths, [[qkvs[j], mixeds[j], logs[j], weights[j]] for j in (2, 3)],
        mixed_grad, first_grad, tokens, upstream, gains[0], wait,
    )
    if planar:
        qkv_one, qkv_side = sum_side(qkv_part, gate([last_sums], qkv_near))
    norm_sums = jnp.concatenate(
        [last_sums[0:1], sums[2:3], sums[0:1], last_sums[1:2], sums[3:4], sums[1:2]], axis=0
    )
    if planar:
        both_sum, late_sum = both_part + both_side, late_one + late_side
        qkv_sum = qkv_one + qkv_side
        row_sum = [unfold(late_sum[k]) for k in (3, 4)]
        width = norm_sums.shape[1] // DP
        norm_sum = lax.dynamic_slice_in_dim(plane_sum(norm_sums), place * width, width, 1)
    else:
        both_sum = scattered(in_order(both_keep, both_send), 1)
        late = in_order(keep, send)
        late_sum = scattered(late[:3], 1)
        qkv_sum = scattered(in_order(qkv_keep, qkv_send), 1)
        row_sum = [
            scattered(jnp.concatenate([unfold(part) for part in jnp.split(late[k], 8)]), 0)
            for k in (3, 4)
        ]
        norm_sum = scattered(norm_sums, 1)
    return (
        out,
        token_grad,
        text_grad.reshape(text_states.shape),
        norm_sum[:3],
        norm_sum[3:],
        jnp.transpose(qkv_sum, (1, 0, 2)),
        row_sum[0],
        late_sum[0],
        jnp.transpose(late_sum[1:3], (1, 0, 2)),
        row_sum[1],
        both_sum[0],
        both_sum[1],
    )


def solution(mesh):
    placed = (
        P("dp", None),
        P("dp", None, None),
        P("dp"),
        P("dp", None),
        P(),
        P(),
        P(None, None, "mp"),
        P("mp", None),
        P(None, "mp"),
        P(None, None, "mp"),
        P("mp", None),
        P(None, "mp"),
        P("mp", None),
        P("dp", None),
    )
    return jax.shard_map(
        partial(local, mesh.shape["dp"] == DP),
        mesh=mesh,
        in_specs=placed,
        out_specs=(
            P("dp", None),
            P("dp", None),
            P("dp", None, None),
            P(None, "dp"),
            P(None, "dp"),
            P("dp", None, "mp"),
            P(("mp", "dp"), None),
            P("dp", "mp"),
            P("dp", None, "mp"),
            P(("mp", "dp"), None),
            P("dp", "mp"),
            P(("mp", "dp"), None),
        ),
        check_vma=False,
    )
```

```python
from functools import partial

import jax
import jax.numpy as jnp
from jax import lax
from jax.experimental import pallas as pl
from jax.experimental.pallas import tpu as pltpu
from jax.sharding import PartitionSpec as P

HEAD = 64
BLK = 256
EPS = 1e-05
NEG = -1e30
F32 = jnp.float32
BF16 = jnp.bfloat16
MIB = 1024 * 1024

NN = (((1,), (0,)), ((), ()))
NT = (((1,), (1,)), ((), ()))
TN = (((0,), (0,)), ((), ()))


def dot(a, b, dims=NN):
    return lax.dot_general(a, b, dims, preferred_element_type=F32)


def params(mib=56, semantics=None):
    return pltpu.CompilerParams(vmem_limit_bytes=mib * MIB, dimension_semantics=semantics)


def cost(us):
    return pl.CostEstimate(
        flops=int(us * 4.6e8), transcendentals=0, bytes_accessed=int(us * 1.4e6)
    )


def shape(dims, dtype=F32):
    return jax.ShapeDtypeStruct(dims, dtype)


def smem():
    return pl.BlockSpec(memory_space=pltpu.SMEM)


def whole(dims):
    rank = len(dims)
    return pl.BlockSpec(dims, lambda *_: (0,) * rank)


def at(dims, index):
    return pl.BlockSpec(dims, lambda *_: index)


def once(dims):
    rank = len(dims)
    return pl.BlockSpec(dims, lambda *_: (0,) * rank, pipeline_mode=pl.Buffered(1))


def anywhere():
    return pl.BlockSpec(memory_space=pl.ANY)


def launch(kernel, args, in_specs, out_specs, out_shape, scratch=(), wait=(), carry=(), **options):
    args, wait, carry = list(args), list(wait), list(carry)
    count, extra, outs = len(args), len(wait) + len(carry), len(out_shape)

    def body(*refs):
        results = refs[count + extra : count + extra + outs]
        kernel(*refs[:count], *results, *refs[count + extra + outs + len(carry) :])

    return pl.pallas_call(
        body,
        in_specs=list(in_specs) + [anywhere()] * extra,
        out_specs=list(out_specs) + [anywhere()] * len(carry),
        out_shape=list(out_shape) + [shape(value.shape, value.dtype) for value in carry],
        scratch_shapes=list(scratch),
        input_output_aliases={count + len(wait) + k: outs + k for k in range(len(carry))},
        **options,
    )(*args, *wait, *carry)


def gate(wait, carry):
    return launch(
        lambda: None, [], [], [], [], wait=wait, carry=[carry], name="gate", cost_estimate=cost(0.1)
    )[0]


def rows_of(tile, width):
    return pl.BlockSpec((tile, width), lambda i, *_: (i, 0))


def norm_stats(value):
    center = value - jnp.mean(value, axis=-1, keepdims=True)
    spread = jnp.mean(center * center, axis=-1, keepdims=True)
    inverse = lax.rsqrt(spread + EPS)
    return center * inverse, inverse


def norm_forward(value, gain, shift):
    unit, _ = norm_stats(value)
    return (unit * gain + shift).astype(BF16)


def norm_backward(incoming, value, gain):
    unit, inverse = norm_stats(value)
    scaled = incoming * gain
    pushed = incoming * unit
    inner = (
        scaled
        - jnp.mean(scaled, axis=-1, keepdims=True)
        - unit * jnp.mean(scaled * unit, axis=-1, keepdims=True)
    )
    return (
        inner * inverse,
        jnp.sum(pushed, axis=0, keepdims=True),
        jnp.sum(incoming, axis=0, keepdims=True),
    )


def norm_kernel(tokens_ref, gain_ref, shift_ref, first_ref):
    first_ref[...] = norm_forward(tokens_ref[...].astype(F32), gain_ref[...], shift_ref[...])


def norm_first(tokens, gain, shift):
    rows, width = tokens.shape
    return launch(
        norm_kernel,
        [tokens, gain, shift],
        [rows_of(BLK, width), whole((1, width)), whole((1, width))],
        [rows_of(BLK, width)],
        [shape((rows, width), BF16)],
        grid=(rows // BLK,),
        name="norm_first",
        cost_estimate=cost(6),
    )[0]


def head_row(width, head, value):
    lane = lax.broadcasted_iota(jnp.int32, (1, width), 1)
    return jnp.where(lane // HEAD == head, value, 0.0)


def masked(block, row):
    return (block.astype(F32) * row).astype(BF16)


def item_at(lengths, place):
    item, start, end = 0, 0, 0
    for slot in range(lengths.shape[0]):
        end = end + lengths[slot]
        past = end <= place
        item = item + past.astype(jnp.int32)
        start = jnp.where(past, end, start)
    return item, start


def offsets(core):
    return (0, 1 + core, 2 - core, 3)


def join_kernel(me, *refs):
    parts, (target, sems) = refs[:4], refs[4:]
    copies = []
    for index, (part, offset) in enumerate(zip(parts, offsets(me[1]))):
        rows = part.shape[1]
        place = pl.multiple_of((me[0] ^ offset) * rows, rows)
        for k in range(part.shape[0]):
            copies.append(
                pltpu.make_async_copy(
                    part.at[k], target.at[k, pl.ds(place, rows)], sems.at[index, k]
                )
            )
    for copy in copies:
        copy.start()
    for copy in copies:
        copy.wait()


def join(me, parts, wait):
    count, rows, width = parts[0].shape
    return launch(
        join_kernel,
        [me, *parts],
        [smem()] + [anywhere()] * 4,
        [vmem()],
        [shape((count, 4 * rows, width))],
        scratch=[pltpu.SemaphoreType.DMA((4, count))],
        wait=wait,
        compiler_params=params(24),
        name="join",
        cost_estimate=cost(2),
    )[0]


def take(targets, source):
    for k, target in enumerate(targets):
        target[...] = source[k].astype(BF16)


def take_two(first, second, mine, other, core):
    @pl.when(core == 0)
    def _():
        take(first, mine)
        take(second, other)

    @pl.when(core == 1)
    def _():
        take(second, mine)
        take(first, other)


def fill(targets, parts, chip, core):
    for part, offset in zip(parts, offsets(core)):
        rows = part.shape[1]
        place = pl.multiple_of((chip ^ offset) * rows, rows)
        for k, target in enumerate(targets):
            target[pl.ds(place, rows), :] = part[k].astype(BF16)


def fill_two(first, second, mine, other, me):
    chip, core = me[0], me[1]

    @pl.when(core == 0)
    def _():
        fill(first, mine, chip, 0)
        fill(second, other, chip, 1)

    @pl.when(core == 1)
    def _():
        fill(second, mine, chip, 1)
        fill(first, other, chip, 0)


def planes(ref):
    return [ref.at[k] for k in range(ref.shape[0])]


def causal():
    shape2 = (BLK, BLK)
    return lax.broadcasted_iota(jnp.int32, shape2, 0) <= lax.broadcasted_iota(
        jnp.int32, shape2, 1
    )


def lanes_of(head):
    return slice(head * HEAD, (head + 1) * HEAD)


def self_block(qb, count, qkv, turned, mixed, logs):
    q0 = pl.multiple_of(qb * BLK, BLK)
    k0 = pl.multiple_of((qb - (count - 1)) * BLK, BLK)
    width = qkv.shape[2]
    query = qkv[0, pl.ds(q0, BLK), :]
    diag = qkv[1, pl.ds(q0, BLK), :]
    pre_len = (count - 1) * BLK
    keep = causal()
    pieces = []
    heads = range(width // HEAD)
    parts = [masked(query, head_row(width, head, HEAD**-0.5)) for head in heads]
    nears = [dot(diag, part, NT) for part in parts]
    fars = [dot(qkv[1, pl.ds(k0, pre_len), :], part, NT) for part in parts] if pre_len else []
    for head in heads:
        near = jnp.where(keep, nears[head], NEG)
        peak = jnp.max(near, axis=0, keepdims=True)
        if pre_len:
            far = fars[head]
            peak = jnp.maximum(peak, jnp.max(far, axis=0, keepdims=True))
        near = jnp.exp(near - peak)
        total = jnp.sum(near, axis=0, keepdims=True)
        result = dot(turned[lanes_of(head), pl.ds(q0, BLK)], near.astype(BF16))
        if pre_len:
            far = jnp.exp(far - peak)
            total = total + jnp.sum(far, axis=0, keepdims=True)
            result = result + dot(
                turned[lanes_of(head), pl.ds(k0, pre_len)], far.astype(BF16)
            )
        pieces.append(result * (1.0 / total))
        logs[head : head + 1, pl.ds(q0, BLK)] = peak + jnp.log(total)
    mixed[pl.ds(q0, BLK), :] = jnp.concatenate(pieces, axis=0).T.astype(BF16)


def front_body(lengths, first, weights, qkv, mixed, logs, turned):
    rows = first.shape[0]
    for m in range(3):
        qkv[m] = dot(first[...], weights[m]).astype(BF16)
    turned[...] = qkv[2].T

    @pl.loop(0, rows // BLK)
    def _(qb):
        _, start = item_at(lengths, qb * BLK)
        count = qb - start // BLK + 1
        for n in range(1, 5):

            @pl.when(count == n)
            def _():
                self_block(qb, n, qkv, turned, mixed, logs)


def front_kernel(lengths, first, shard, weights, *rest):
    take(planes(weights), shard)
    front_body(lengths, first, weights, *rest)


def front_two_kernel(me, lengths, first, mine, other, text, weights, cross, qkv, mixed, logs, pair, turned):
    take_two(planes(weights), planes(cross), mine, other, me[1])
    text_pair(pair, text, cross)
    front_body(lengths, first, weights, qkv, mixed, logs, turned)


def vmem():
    return pl.BlockSpec(memory_space=pltpu.VMEM)


def front_call(kernel, name, us, prefix, first, arrays, weight_count, more, wait, carry=()):
    rows, depth = first.shape
    width = arrays[0].shape[2]
    outs = [shape((3, depth, width), BF16)] * weight_count + [
        shape((3, rows, width), BF16),
        shape((rows, width), BF16),
        shape((8, rows), F32),
    ] + more
    return launch(
        kernel,
        [*prefix, first, *arrays],
        [smem()] * len(prefix) + [vmem()] * (1 + len(arrays)),
        [vmem()] * len(outs),
        outs,
        scratch=[pltpu.VMEM((width, rows), BF16)],
        wait=wait,
        carry=carry,
        compiler_params=params(),
        name=name,
        cost_estimate=cost(us),
    )


def front_own(lengths, first, weights, wait, carry):
    return front_call(front_body, "front_own", 15, (lengths,), first, [weights], 0, [], wait, carry)


def front(lengths, first, shard, wait, carry):
    return front_call(front_kernel, "front", 16, (lengths,), first, [shard], 1, [], wait, carry)


def front_two(me, lengths, first, arrays, text, wait):
    pair = shape((2, text.shape[0], arrays[0].shape[2]), BF16)
    return front_call(
        front_two_kernel, "front_two", 18, (me, lengths), first, [*arrays, text], 2, [pair], wait
    )


def text_pair(pair, text, cross):
    for m in range(2):
        pair[m] = dot(text[...], cross[m + 1]).astype(BF16)


def text_front_kernel(text, own, mine, other, cross_a, cross_b, *pairs):
    take(planes(cross_a), mine)
    take(planes(cross_b), other)
    for pair, cross in zip(pairs, (own, cross_a, cross_b)):
        text_pair(pair, text, cross)


def text_front(text, own, arrays, wait):
    rows = text.shape[0]
    width = own.shape[2]
    outs = [shape(own.shape, BF16)] * 2 + [shape((2, rows, width), BF16)] * 3
    return launch(
        text_front_kernel,
        [text, own, *arrays],
        [vmem()] * 4,
        [vmem()] * 5,
        outs,
        wait=wait,
        compiler_params=params(),
        name="text_front",
        cost_estimate=cost(7),
    )


def unfold_into(target, first, source):
    width = source.shape[2]
    rows = width // 4
    for piece in range(4):
        for part in range(4):
            target[pl.ds(first + piece * rows, rows), part * width : (part + 1) * width] = source[
                0, pl.ds(piece * width + part * rows, rows), :
            ].astype(BF16)


def middle_kernel(me, lengths, live, tokens, gain1, shift1, gain2, shift2, own_out, own_co, *refs):
    mixed, refs = refs[:4], refs[4:]
    queries, refs = refs[:4], refs[4:]
    pairs, refs = refs[:4], refs[4:]
    outs, cos, (out_two, co_two), refs = refs[:2], refs[2:4], refs[4:6], refs[6:]
    w_out, w_co, after_self, after_cross, second, third, cross_query, looked, logs, turned = refs
    step = pl.program_id(0)

    @pl.when(step == 0)
    def _():
        width = own_out.shape[0]
        w_out[:width, :] = own_out[...]
        w_co[:width, :] = own_co[...]
        for place, out_part, co_part in ((1, outs[0], cos[0]), (3, outs[1], cos[1])):
            unfold_into(w_out, place * width, out_part)
            unfold_into(w_co, place * width, co_part)

        @pl.when(me[1] == 0)
        def _():
            unfold_into(w_out, 2 * width, out_two)
            unfold_into(w_co, 2 * width, co_two)

        @pl.when(me[1] == 1)
        def _():
            unfold_into(w_co, 2 * width, out_two)
            unfold_into(w_out, 2 * width, co_two)

        for j in range(4):
            turned[j] = pairs[j][1].T

    part = jnp.concatenate([ref[...] for ref in mixed], axis=1)
    residual = tokens[...].astype(F32) + dot(part, w_out[...])
    after_self[...] = residual
    normed = norm_forward(residual, gain1[...], shift1[...])
    second[...] = normed
    text = TEXT
    item, _ = item_at(lengths, step * BLK)
    t0 = pl.multiple_of(item * text, text)
    alive = live[pl.ds(t0, text), :] > 0.0
    width = own_out.shape[0]
    heads = range(width // HEAD)
    stages = []
    for j in range(4):
        query = dot(normed, queries[j][0]).astype(BF16)
        cross_query[:, j * width : (j + 1) * width] = query
        rows = [masked(query, head_row(width, head, HEAD**-0.5)) for head in heads]
        keys = pairs[j][0, pl.ds(t0, text), :]
        stages.append([dot(keys, row, NT) for row in rows])
    for j in range(4):
        pieces = []
        for head in heads:
            score = jnp.where(alive, stages[j][head], NEG)
            peak = jnp.max(score, axis=0, keepdims=True)
            score = jnp.exp(score - peak)
            total = jnp.sum(score, axis=0, keepdims=True)
            result = dot(turned[j, lanes_of(head), pl.ds(t0, text)], score.astype(BF16))
            pieces.append(result * (1.0 / total))
            index = j * (width // HEAD) + head
            logs[index : index + 1, :] = peak + jnp.log(total)
        looked[:, j * width : (j + 1) * width] = jnp.concatenate(pieces, axis=0).T.astype(BF16)
    residual = residual + dot(looked[...], w_co[...])
    after_cross[...] = residual
    third[...] = norm_forward(residual, gain2[...], shift2[...])


TEXT = 128


def middle(me, lengths, live, tokens, norms, own_out, own_co, mixed, crosses, pairs, g_cross, g_two, wait):
    rows, depth = tokens.shape
    width = own_out.shape[0]
    text_rows = live.shape[0]
    inner = 4 * width
    row = whole((1, depth))

    def plane_at(k):
        dims = (1, depth, width)
        return pl.BlockSpec(dims, lambda *_: (k, 0, 0), pipeline_mode=pl.Buffered(1))

    return launch(
        middle_kernel,
        [me, lengths, live, tokens, *norms, own_out, own_co, *mixed, *crosses, *pairs]
        + [*g_cross, *g_cross, *g_two],
        [smem(), smem(), whole((text_rows, 1)), rows_of(BLK, depth)]
        + [row] * 4
        + [once((width, depth))] * 2
        + [rows_of(BLK, width)] * 4
        + [at((1, depth, width), (0, 0, 0))] * 4
        + [whole((2, text_rows, width))] * 4
        + [plane_at(k) for k in (3, 3, 4, 4, 3, 3)],
        [whole((inner, depth))] * 2
        + [rows_of(BLK, depth)] * 4
        + [rows_of(BLK, inner)] * 2
        + [pl.BlockSpec((inner // HEAD, BLK), lambda i: (0, i))],
        [shape((inner, depth), BF16)] * 2
        + [shape((rows, depth)), shape((rows, depth))]
        + [shape((rows, depth), BF16)] * 2
        + [shape((rows, inner), BF16)] * 2
        + [shape((inner // HEAD, rows))],
        scratch=[pltpu.VMEM((4, width, text_rows), BF16)],
        wait=wait,
        grid=(rows // BLK,),
        compiler_params=params(),
        name="middle",
        cost_estimate=cost(43),
    )


ROOT = 0.7978845608028654
CUBE = 0.044715


def gelu_both(value):
    square = value * value
    bend = jnp.tanh(value * (ROOT + (ROOT * CUBE) * square))
    half = 0.5 + 0.5 * bend
    slope = half + (0.5 * value) * (1.0 - bend * bend) * (ROOT + (3.0 * ROOT * CUBE) * square)
    return value * half, slope


def feed_rows(third, cot, up, down):
    return feed_finish(dot(third, up), dot(cot, down, NT), up, down)


def feed_finish(pre_act, hidden_grad, up, down):
    hidden, slope = gelu_both(pre_act)
    hidden = hidden.astype(BF16)
    pre_grad = (hidden_grad * slope).astype(BF16)
    return hidden, pre_grad, dot(hidden, down), dot(pre_grad, up, NT)


def feed_own_kernel(
    me, third, cot, after, up, down, out, grad, keep, send, hidden_rows, grad_rows, both
):
    step = pl.program_id(0)
    part = pl.ds(pl.multiple_of(step * FEED, FEED), FEED)
    hidden, pre_grad, result, pushed = feed_rows(third[part, :], cot[part, :], up[...], down[...])
    out[...] = after[...] + result
    grad[...] = pushed
    hidden_rows[part, :] = hidden
    grad_rows[part, :] = pre_grad

    @pl.when(step == pl.num_programs(0) - 1)
    def _():
        both[0] = dot(third[...], grad_rows[...], TN)
        both[1] = dot(hidden_rows[...], cot[...], TN)
        put_pieces(both, keep, send, me)


def put_pieces(source, keep, send, me, first=0):
    chip, core = me[0], me[1]
    rows = source.shape[1] // 8
    for target, owner in ((keep, core), (send, 1 - core)):
        for index, offset in enumerate((0, 2 - owner, 1 + owner, 3)):
            place = pl.multiple_of(((chip ^ offset) * 2 + owner) * rows, rows)
            for k in range(source.shape[0]):
                target[index, first + k] = source[k, pl.ds(place, rows), :]


FEED = 320


def feed_own(me, third, cot, after, up, down, wait):
    rows, depth = third.shape
    inner = up.shape[1]
    tile = rows_of(FEED, depth)
    pieces = (4, 2, depth // 8, depth)
    return launch(
        feed_own_kernel,
        [me, third, cot, after, up, down],
        [smem(), once(third.shape), once(cot.shape), tile]
        + [once((depth, inner)), once((inner, depth))],
        [tile, tile, once(pieces), once(pieces)],
        [shape((rows, depth)), shape((rows, depth)), shape(pieces), shape(pieces)],
        scratch=[pltpu.VMEM((rows, inner), BF16)] * 2 + [pltpu.VMEM((2, depth, inner), F32)],
        wait=wait,
        grid=(rows // FEED,),
        compiler_params=params(),
        name="feed_own",
        cost_estimate=cost(32),
    )


def feed_pair_kernel(me, third, cot, out_in, grad_in, *refs):
    mine, other, (out, grad, one, two) = refs[:4], refs[4:8], refs[8:]

    @pl.when(pl.program_id(0) == 0)
    def _():
        fill(planes(one), mine, me[0], me[1])
        fill(planes(two), other, me[0], 1 - me[1])

    _, _, result, pushed = feed_rows(third[...], cot[...], one[0], one[1])
    _, _, more_result, more_pushed = feed_rows(third[...], cot[...], two[0], two[1])
    out[...] = out_in[...] + (result + more_result)
    grad[...] = grad_in[...] + (pushed + more_pushed)


def feed_last_kernel(me, third, cot, out_in, grad_in, *refs):
    mine, other, (out, grad, both) = refs[:4], refs[4:8], refs[8:]

    @pl.when(pl.program_id(0) == 0)
    def _():
        up, down = planes(both)
        fill_two([up], [down], mine, other, me)

    _, _, result, pushed = feed_rows(third[...], cot[...], both[0], both[1])
    out[...] = (out_in[...] + result).astype(BF16)
    grad[...] = grad_in[...] + pushed


def feed_call(kernel, name, us, prefix, dtype, copies, third, cot, out, grad, arrays, wait, carry=()):
    rows, depth = third.shape
    tile = rows_of(FEED, depth)
    inner = arrays[0].shape[2]
    return launch(
        kernel,
        [*prefix, third, cot, out, grad, *arrays],
        [smem()] * len(prefix) + [tile] * 4 + [once(arrays[0].shape)] * 8,
        [tile, tile],
        [shape((rows, depth), dtype), shape((rows, depth))],
        scratch=[pltpu.VMEM((2, inner, depth), BF16)] * copies,
        wait=wait,
        carry=carry,
        grid=(rows // FEED,),
        compiler_params=params(),
        name=name,
        cost_estimate=cost(us),
    )


def feed_pair(me, *operands):
    return feed_call(feed_pair_kernel, "feed_pair", 33, (me,), F32, 2, *operands)


def feed_last(me, *operands):
    return feed_call(feed_last_kernel, "feed_last", 18, (me,), BF16, 1, *operands)


def back_kernel(
    lengths, live, third_grad, cot, after_cross, after_self, cross_query, looked0, mixed0, logs,
    gain1, gain2, w_out, w_co, *refs,
):
    queries, refs = refs[:4], refs[4:]
    pairs, refs = refs[:4], refs[4:]
    up_grad, mixed_grad, pair_grad, row_grads, query_grads, sums, total, turned = refs
    step = pl.program_id(0)
    text = TEXT

    @pl.when(step == 0)
    def _():
        total[...] = jnp.zeros_like(total)
        row_grads[...] = jnp.zeros_like(row_grads)
        sums[...] = jnp.zeros_like(sums)
        for j in range(4):
            turned[j] = pairs[j][0].T

    pulled, gain_sum, shift_sum = norm_backward(third_grad[...], after_cross[...], gain2[...])
    sums[0:1, :] += gain_sum
    sums[1:2, :] += shift_sum
    upstream = cot[...].astype(F32) + pulled
    low = upstream.astype(BF16)
    row_grads[1] += dot(looked0[...], low, TN)
    looked_grad = dot(low, w_co[...], NT).astype(BF16)
    item, _ = item_at(lengths, step * BLK)
    t0 = pl.multiple_of(item * text, text)
    alive = live[pl.ds(t0, text), :] > 0.0
    second_grad = jnp.zeros(upstream.shape, F32)
    width = queries[0].shape[2]
    heads = range(width // HEAD)

    def scores(j):
        cols = slice(j * width, (j + 1) * width)
        rows = [masked(cross_query[:, cols], head_row(width, h, HEAD**-0.5)) for h in heads]
        grads = [masked(looked_grad[:, cols], head_row(width, h, 1.0)) for h in heads]
        keys = pairs[j][0, pl.ds(t0, text), :]
        values = pairs[j][1, pl.ds(t0, text), :]
        return rows, grads, [dot(keys, row, NT) for row in rows], [dot(values, g, NT) for g in grads]

    ahead = scores(0)
    for j in range(4):
        rows, grads, score_set, pushed_set = ahead
        if j < 3:
            ahead = scores(j + 1)
        pieces, chances, score_grads = [], [], []
        for head in heads:
            index = j * (width // HEAD) + head
            score = jnp.where(alive, score_set[head], NEG)
            chance = jnp.exp(score - logs[index : index + 1, :])
            weighted = chance * pushed_set[head]
            mean = jnp.sum(weighted, axis=0, keepdims=True)
            score_grads.append((weighted - chance * mean).astype(BF16))
            chances.append(chance.astype(BF16))
            pieces.append(dot(turned[j, lanes_of(head), pl.ds(t0, text)], score_grads[head]))
        total[j, 0, pl.ds(t0, text), :] += dot(
            jnp.concatenate(score_grads, axis=1), jnp.concatenate(rows, axis=0)
        )
        total[j, 1, pl.ds(t0, text), :] += dot(
            jnp.concatenate(chances, axis=1), jnp.concatenate(grads, axis=0)
        )
        query_grad = (jnp.concatenate(pieces, axis=0).T * HEAD**-0.5).astype(BF16)
        if j == 0:
            query_grads[...] = query_grad
        second_grad = second_grad + dot(query_grad, queries[j][0], NT)

    pulled, gain_sum, shift_sum = norm_backward(second_grad, after_self[...], gain1[...])
    sums[2:3, :] += gain_sum
    sums[3:4, :] += shift_sum
    upstream = upstream + pulled
    up_grad[...] = upstream
    low = upstream.astype(BF16)
    row_grads[0] += dot(mixed0[...], low, TN)
    mixed_grad[...] = dot(low, w_out[...], NT).astype(BF16)

    @pl.when(step == pl.num_programs(0) - 1)
    def _():
        pair_grad[...] = total[...].astype(BF16)


def back(
    lengths, live, third_grad, cot, after_cross, after_self, cross_query, looked, mixed0, logs,
    gain1, gain2, w_out, w_co, crosses, pairs, wait,
):
    rows, depth = cot.shape
    text_rows = live.shape[0]
    width = mixed0.shape[1]
    inner = 4 * width
    tile = rows_of(BLK, depth)
    row = whole((1, depth))
    return launch(
        back_kernel,
        [lengths, live, third_grad, cot, after_cross, after_self, cross_query, looked, mixed0]
        + [logs, gain1, gain2, w_out, w_co, *crosses, *pairs],
        [smem(), whole((text_rows, 1))]
        + [tile] * 4
        + [rows_of(BLK, inner), rows_of(BLK, width), rows_of(BLK, width)]
        + [pl.BlockSpec((inner // HEAD, BLK), lambda i: (0, i)), row, row]
        + [whole((inner, depth))] * 2
        + [at((1, depth, width), (0, 0, 0))] * 4
        + [whole((2, text_rows, width))] * 4,
        [tile, rows_of(BLK, inner), whole((4, 2, text_rows, width))]
        + [whole((2, width, depth)), rows_of(BLK, width), whole((8, depth))],
        [
            shape((rows, depth)),
            shape((rows, inner), BF16),
            shape((4, 2, text_rows, width), BF16),
            shape((2, width, depth)),
            shape((rows, width), BF16),
            shape((8, depth)),
        ],
        scratch=[
            pltpu.VMEM((4, 2, text_rows, width), F32),
            pltpu.VMEM((4, width, text_rows), BF16),
        ],
        wait=wait,
        grid=(rows // BLK,),
        compiler_params=params(),
        name="back",
        cost_estimate=cost(53),
    )


def text_kernel(me, text, pair_grad, second, query_grad, row_grads, *refs):
    crosses, (text_grad, keep, send, cross_grad, folded) = refs[:4], refs[4:]
    total = jnp.zeros(text_grad.shape, F32)
    for j in range(4):
        for m in range(2):
            total = total + dot(pair_grad[j, m], crosses[j][m + 1], NT)
    text_grad[...] = total
    cross_grad[0] = dot(second[...], query_grad[...], TN)
    for m in range(2):
        cross_grad[m + 1] = dot(text[...], pair_grad[0, m], TN)
    put_pieces(cross_grad, keep, send, me)
    width = folded.shape[2]
    rows = row_grads.shape[1] // 8
    for k in range(2):
        for piece in range(8):
            for part in range(4):
                folded[k, pl.ds((piece * 4 + part) * rows, rows), :] = row_grads[
                    k, pl.ds(piece * rows, rows), part * width : (part + 1) * width
                ]
    put_pieces(folded, keep, send, me, 3)


def unfold(piece):
    rows, width = piece.shape
    parts = [piece[k * rows // 4 : (k + 1) * rows // 4] for k in range(4)]
    return jnp.concatenate(parts, axis=1)


def text_back(me, text, pair_grad, second, query_grad, row_grads, crosses, wait):
    text_rows, depth = text.shape
    width = pair_grad.shape[3]
    pieces = (4, 5, depth // 8, width)
    return launch(
        text_kernel,
        [me, text, pair_grad, second, query_grad, row_grads, *crosses],
        [smem()] + [vmem()] * 9,
        [vmem()] * 3,
        [shape((text_rows, depth)), shape(pieces), shape(pieces)],
        scratch=[pltpu.VMEM((3, depth, width), F32), pltpu.VMEM((2, depth, width), F32)],
        wait=wait,
        compiler_params=params(),
        name="text_back",
        cost_estimate=cost(15),
    )


def self_back_pair(qb, kb, diag, qkv, rows, grads, logs, means, turned, query_sum, key_sum, value_sum):
    q0 = pl.multiple_of(qb * BLK, BLK)
    k0 = pl.multiple_of(kb * BLK, BLK)
    keys = qkv[1, pl.ds(k0, BLK), :]
    values = qkv[2, pl.ds(k0, BLK), :]
    more_keys = 0.0
    more_values = 0.0
    heads = range(rows.shape[0])
    stages = [(dot(keys, rows[h], NT), dot(values, grads[h], NT)) for h in heads]
    for head, (score, pushed) in zip(heads, stages):
        if diag:
            score = jnp.where(causal(), score, NEG)
        chance = jnp.exp(score - logs[head : head + 1, pl.ds(q0, BLK)])
        score_grad = (chance * (pushed - means[head : head + 1, :])).astype(BF16)
        query_sum[lanes_of(head), :] += dot(turned[lanes_of(head), pl.ds(k0, BLK)], score_grad)
        more_keys = more_keys + dot(score_grad, rows[head])
        more_values = more_values + dot(chance.astype(BF16), grads[head])
    key_sum[pl.ds(k0, BLK), :] += more_keys
    value_sum[pl.ds(k0, BLK), :] += more_values


def self_back_body(
    lengths, qkv, mixed, out_grad, logs, weights, triple, turned, rows, grads, means, query_sum,
    key_sum, value_sum,
):
    row_count, width = mixed.shape
    turned[...] = qkv[1].T
    key_sum[...] = jnp.zeros_like(key_sum)
    value_sum[...] = jnp.zeros_like(value_sum)

    @pl.loop(0, row_count // BLK)
    def _(qb):
        q0 = pl.multiple_of(qb * BLK, BLK)
        _, start = item_at(lengths, q0)
        query = qkv[0, pl.ds(q0, BLK), :]
        grad = out_grad[pl.ds(q0, BLK), :]
        flat = (grad.astype(F32) * mixed[pl.ds(q0, BLK), :].astype(F32)).T
        for head in range(width // HEAD):
            rows[head] = masked(query, head_row(width, head, HEAD**-0.5))
            grads[head] = masked(grad, head_row(width, head, 1.0))
            means[head : head + 1, :] = jnp.sum(flat[lanes_of(head), :], axis=0, keepdims=True)
        query_sum[...] = jnp.zeros_like(query_sum)
        rest = (qkv, rows, grads, logs, means, turned, query_sum, key_sum, value_sum)

        @pl.loop(start // BLK, qb)
        def _(kb):
            self_back_pair(qb, kb, False, *rest)

        self_back_pair(qb, qb, True, *rest)
        triple[0, pl.ds(q0, BLK), :] = (query_sum[...].T * HEAD**-0.5).astype(BF16)

    triple[1] = key_sum[...].astype(BF16)
    triple[2] = value_sum[...].astype(BF16)


def self_scratch(rows, width):
    heads = width // HEAD
    return [
        pltpu.VMEM((3, rows, width), BF16),
        pltpu.VMEM((width, rows), BF16),
        pltpu.VMEM((heads, BLK, width), BF16),
        pltpu.VMEM((heads, BLK, width), BF16),
        pltpu.VMEM((8, BLK), F32),
        pltpu.VMEM((width, BLK), F32),
        pltpu.VMEM((rows, width), F32),
        pltpu.VMEM((rows, width), F32),
    ]


def self_own_kernel(me, lengths, qkv, mixed, out_grad, logs, weights, first, total, keep, send, *scratch):
    self_back_body(lengths, qkv, mixed, out_grad, logs, weights, *scratch[:-1])
    triple, qkv_grad = scratch[0], scratch[-1]
    for m in range(3):
        qkv_grad[m] = dot(first[...], triple[m], TN)
    put_pieces(qkv_grad, keep, send, me)
    total[...] = sum(dot(triple[m], weights[m], NT) for m in range(3))


def self_call(kernel, name, us, j, outs, operands, wait, prefix=(), scratch=()):
    lengths, qkv, mixed, out_grad, logs, weights, last_in = operands
    rows, width = mixed.shape
    return launch(
        kernel,
        [*prefix, *operands],
        [smem()] * (len(prefix) + 1)
        + [whole(qkv.shape), whole(mixed.shape), at((rows, width), (0, j))]
        + [whole(logs.shape), whole(weights.shape), whole(last_in.shape)],
        [whole(out.shape) for out in outs],
        outs,
        scratch=self_scratch(rows, width) + list(scratch),
        wait=wait,
        grid=(1,),
        compiler_params=params(),
        name=name,
        cost_estimate=cost(us),
    )


def self_own(me, lengths, qkv, mixed, out_grad, logs, weights, first, wait):
    _, depth, width = weights.shape
    pieces = shape((4, 3, depth // 8, width))
    operands = (lengths, qkv, mixed, out_grad, logs, weights, first)
    scratch = [pltpu.VMEM(weights.shape, F32)]
    outs = [shape(first.shape), pieces, pieces]
    return self_call(self_own_kernel, "self_own", 22, 0, outs, operands, wait, (me,), scratch)


def self_kernel(lengths, qkv, mixed, out_grad, logs, weights, before, total, *scratch):
    self_back_body(lengths, qkv, mixed, out_grad, logs, weights, *scratch)
    triple = scratch[0]
    total[...] = before[...] + sum(dot(triple[m], weights[m], NT) for m in range(3))


def self_back(lengths, qkv, mixed, out_grad, logs, weights, before, j, wait):
    operands = (lengths, qkv, mixed, out_grad, logs, weights, before)
    return self_call(self_kernel, "self_back", 26, j, [shape(before.shape)], operands, wait)[0]


def self_rest_kernel(places, lengths, *refs):
    count = len(places)
    sets, refs = [refs[4 * k : 4 * k + 4] for k in range(count)], refs[4 * count :]
    out_grad, before, tokens, upstream, gain, token_grad, sums, *refs = refs
    held, (total, token_rows, up_rows, sems, out_sems, *scratch) = refs[:5], refs[5:]
    rows, width = held[1].shape[1:]
    waits = []
    for k, (arrays, place) in enumerate(zip(sets, places)):
        sources = [*arrays, out_grad.at[:, pl.ds(place * width, width)]]
        waits.append(
            [
                pltpu.make_async_copy(source, target.at[k], sems.at[k, m])
                for m, (source, target) in enumerate(zip(sources, held))
            ]
        )
    ends = [
        pltpu.make_async_copy(source, target, sems.at[count, m])
        for m, (source, target) in enumerate(
            ((before, total), (tokens, token_rows), (upstream, up_rows))
        )
    ]
    for copy in waits[0] + ends[:1] + sum(waits[1:], []) + ends[1:]:
        copy.start()
    triple = scratch[0]
    for k in range(count):
        for copy in waits[k]:
            copy.wait()
        qkv, mixed, logs, weights, grads = (ref.at[k] for ref in held)
        self_back_body(lengths, qkv, mixed, grads, logs, weights, *scratch)
        if k == 0:
            ends[0].wait()
        total[...] += sum(dot(triple[m], weights[m], NT) for m in range(3))
    ends[1].wait()
    ends[2].wait()
    sums[...] = jnp.zeros_like(sums)
    outs = []
    for k in range(rows // BLK):
        part = slice(k * BLK, (k + 1) * BLK)
        pulled, gain_sum, shift_sum = norm_backward(
            total[part, :], token_rows[part, :].astype(F32), gain[...]
        )
        sums[0:1, :] += gain_sum
        sums[1:2, :] += shift_sum
        up_rows[part, :] = up_rows[part, :] + pulled
        outs.append(
            pltpu.make_async_copy(
                up_rows.at[pl.ds(k * BLK, BLK)], token_grad.at[pl.ds(k * BLK, BLK)], out_sems.at[k]
            )
        )
        outs[-1].start()
    for copy in outs:
        copy.wait()


def self_rest(places, lengths, sets, out_grad, before, tokens, upstream, gain, wait):
    rows, depth = tokens.shape
    count = len(places)
    width = sets[0][1].shape[1]
    args = [lengths, *sum(sets, []), out_grad, before, tokens, upstream, gain]
    held = [
        pltpu.VMEM((count,) + array.shape, array.dtype) for array in sets[0] + [sets[0][1]]
    ]
    return launch(
        partial(self_rest_kernel, places),
        args,
        [smem()] + [anywhere()] * (len(args) - 2) + [vmem()],
        [anywhere(), vmem()],
        [shape((rows, depth)), shape((8, depth))],
        scratch=held
        + [pltpu.VMEM((rows, depth), dtype) for dtype in (F32, BF16, F32)]
        + [pltpu.SemaphoreType.DMA((count + 1, 5)), pltpu.SemaphoreType.DMA((rows // BLK,))]
        + self_scratch(rows, width),
        wait=wait,
        compiler_params=params(),
        name="self_rest",
        cost_estimate=cost(40),
    )


DP = 8
MP = 4


def ring(step):
    pairs = []
    for i in range(DP):
        for z in range(MP):
            to = (z + (step if i % 2 == 0 else -step)) % MP
            pairs.append((i * MP + z, i * MP + to))
    return pairs


def straight(step):
    return [(z, (z + step) % MP) for z in range(MP)]


def beside(first):
    return [(i, i ^ (2 if (i % 2 == 0) == first else 4)) for i in range(DP)]


def swap(value):
    return lax.ppermute(value, "dp", [(i, i ^ 1) for i in range(DP)])


def fold(piece):
    width = piece.shape[1] // 4
    return jnp.concatenate([piece[:, k * width : (k + 1) * width] for k in range(4)], axis=0)


def fold_whole(shard):
    return jnp.concatenate([fold(piece) for piece in jnp.split(shard, 4)], axis=0)


def cut(shard, chip):
    rows = shard.shape[1] // 4
    return lax.dynamic_slice_in_dim(shard, chip * rows, rows, 1).astype(F32)


def near_of(piece):
    return lax.ppermute(piece, "dp", beside(True))


def side_of(piece):
    return lax.ppermute(piece, "dp", beside(False))


def along(value, step):
    return lax.ppermute(value, "mp", straight(step))


def around(value):
    return lax.ppermute(value, ("dp", "mp"), ring(1))


def in_order(keep, send):
    pieces = [part[k] for k, m in ((0, 0), (2, 1), (1, 2), (3, 3)) for part, k in ((keep, k), (send, m))]
    return jnp.concatenate(pieces, axis=1)


def scattered(value, axis):
    return lax.psum_scatter(value, "dp", scatter_dimension=axis, tiled=True)


def pieces_of(mine, other):
    mine, other = jnp.split(mine, 4, axis=1), jnp.split(other, 4, axis=1)
    return mine + [other[k] for k in (0, 2, 1, 3)]


def sum_near(keep, sent):
    return lax.ppermute(keep[2:] + sent[2:], "dp", beside(True))


def sum_side(keep, sent, near):
    return side_of(keep[1] + sent[1] + near[1])


def sum_last(keep, sent, near, side):
    return keep[0] + sent[0] + near[0] + side


def plane_sum(value):
    for bit in (1, 2, 4):
        value = value + lax.ppermute(value, "dp", [(i, i ^ bit) for i in range(DP)])
    return value


def local(
    planar, tokens, text_states, lengths, text_mask, ln_gain, ln_shift, w_qkv, w_out, w_cross_q,
    w_cross_kv, w_cross_out, w_up, w_down, cotangent,
):
    slot_count, text_length = text_mask.shape
    place = lax.axis_index("dp") if planar else jnp.int32(0)
    chip, core = place // 2, place % 2
    me = jnp.stack([chip, core]).astype(jnp.int32)
    gains = [ln_gain[n : n + 1] for n in range(3)]
    shifts = [ln_shift[n : n + 1] for n in range(3)]
    text = text_states.reshape(slot_count * text_length, text_states.shape[2])
    position = lax.broadcasted_iota(jnp.int32, text_mask.shape, 1)
    live = ((text_mask == 1) | (position == 0)).astype(F32).reshape(-1, 1)
    own_qkv = jnp.transpose(w_qkv, (1, 0, 2))
    own_cross = jnp.concatenate([w_cross_q[None], jnp.transpose(w_cross_kv, (1, 0, 2))], axis=0)
    feeds = jnp.stack([w_up, w_down])
    first = norm_first(tokens, gains[0], shifts[0])
    qkvs, mixeds, logs, weights = ([None] * 4 for _ in range(4))
    weights[0] = own_qkv

    def shards(value):
        return along(value.astype(F32), 1), along(value.astype(F32), 3)

    wait, carry = [], []
    if planar:
        rows = w_out.shape[0] // 4
        outer = [
            fold(lax.dynamic_slice_in_dim(value, chip * rows, rows, 0))[None].astype(F32)
            for value in (w_out, w_cross_out)
        ]
        qkv_one = around(cut(own_qkv, chip))
        qkv_near, qkv_side = near_of(qkv_one), side_of(qkv_one)
        own_piece = gate([qkv_one], jnp.concatenate([cut(own_cross, chip), *outer], axis=0))
        cross_one = around(own_piece)
        wait = [qkv_one, own_piece]
    qkvs[0], mixeds[0], logs[0] = front_own(lengths, first, own_qkv, wait, [])
    if planar:
        mine = join(me, [qkv_one, qkv_near, qkv_side, near_of(qkv_side)], [logs[0]])
        g_qkv = mine, swap(mine)
        cross_near, cross_side = near_of(cross_one), side_of(cross_one)
        two = jnp.where(
            core == 0,
            jnp.concatenate([qkv_one, cross_one[3:4]], axis=0),
            jnp.concatenate([cross_one[:3], cross_one[4:5]], axis=0),
        )
        two = around(two)
        wait = [cross_one]
        carry = [cut(feeds, chip)]
    else:
        folded = [fold_whole(value)[None] for value in (w_out, w_cross_out)]
        g_qkv = shards(own_qkv)
        g_cross = shards(jnp.concatenate([own_cross, *folded], axis=0))
        g_two = [
            along(jnp.concatenate(parts, axis=0).astype(F32), 2)
            for parts in ((own_qkv, folded[0]), (own_cross, folded[1]))
        ]
        g_feed = pieces_of(*shards(feeds))
        g_last = pieces_of(*[along(feeds[k : k + 1].astype(F32), 2) for k in range(2)])
    weights[1], qkvs[1], mixeds[1], logs[1], *carried = front(
        lengths, first, g_qkv[0], wait, carry
    )
    if planar:
        cross_side, two = gate([logs[1]], cross_side), gate([logs[1]], two)
        cross_far = near_of(cross_side)
        two_near, two_side = near_of(two), side_of(two)
        feed_one = around(carried[0])
        wait = [two, cross_near, cross_side, logs[1]]
    weights[3], qkvs[3], mixeds[3], logs[3] = front(lengths, first, g_qkv[1], wait, [])
    if planar:
        mine = join(me, [cross_one, cross_near, cross_side, cross_far], [logs[3], feed_one, two_near, two_side])
        g_cross = mine, swap(mine)
        two_far = near_of(two_side)
        feed_near, feed_side = near_of(feed_one), side_of(feed_one)
        feed_two = around(lax.dynamic_slice_in_dim(feed_one, core, 1, 0))
        wait = [two_near, two_side]
    cross_a, cross_b, *pairs = text_front(text, own_cross, g_cross, wait)
    if planar:
        mine = join(me, [two, two_near, two_side, two_far], [cross_a])
        g_two = mine, swap(mine)
        wait = []
    weights[2], cross_two, qkvs[2], mixeds[2], logs[2], pair_two = front_two(
        me, lengths, first, g_two, text, wait
    )
    pairs = [pairs[0], pairs[1], pair_two, pairs[2]]
    crosses = [own_cross, cross_a, cross_two, cross_b]
    if planar:
        wait = [feed_one, feed_two]
    full_out, full_co, after_self, after_cross, second, third, cross_query, looked, cross_logs = middle(
        me, lengths, live, tokens, (gains[1], shifts[1], gains[2], shifts[2]), w_out, w_cross_out,
        mixeds, crosses, pairs, g_cross, g_two, wait,
    )
    if planar:
        feed_side, feed_two = gate([third], feed_side), gate([third], feed_two)
        feed_far = near_of(feed_side)
        last_near, last_side = near_of(feed_two), side_of(feed_two)
        wait = [feed_near, feed_side, feed_two]
    out, grad, both_keep, both_send = feed_own(
        me, third, cotangent, after_cross, w_up, w_down, wait
    )
    if planar:
        g_feed = [feed_one, feed_near, feed_side, gate([out], feed_far)]
        g_feed = g_feed + [swap(value) for value in g_feed]
        last_far = near_of(last_side)
        last_swaps = [swap(value) for value in (feed_two, last_near, last_side)]
        wait = last_swaps
    out, grad, both_send = feed_pair(
        me, third, cotangent, out, grad, g_feed, wait, [both_send]
    )
    if planar:
        last_far = gate([out], last_far)
        g_last = [feed_two, last_near, last_side, last_far, *last_swaps, swap(last_far)]
    out, grad = feed_last(me, third, cotangent, out, grad, g_last, [])
    if planar:
        both_swap = swap(both_send)
        both_near = sum_near(both_keep, both_swap)
    upstream, mixed_grad, pair_grad, row_grads, query_grad, sums = back(
        lengths, live, grad, cotangent, after_cross, after_self, cross_query, looked, mixeds[0],
        cross_logs, gains[1], gains[2], full_out, full_co, crosses, pairs,
        [both_swap] if planar else [],
    )
    wait = []
    if planar:
        both_near = gate([sums], both_near)
        both_side = sum_side(both_keep, both_swap, both_near)
        wait = [both_near]
    text_grad, keep, send = text_back(
        me, text, pair_grad, second, query_grad, row_grads, crosses, wait
    )
    if planar:
        late_swap = swap(send)
        wait = []
    first_grad, qkv_keep, qkv_send = self_own(
        me, lengths, qkvs[0], mixeds[0], mixed_grad, logs[0], weights[0], first, wait
    )
    if planar:
        late_near = sum_near(keep, late_swap)
        qkv_swap = swap(qkv_send)
        wait = [late_swap, both_side]
    first_grad = self_back(
        lengths, qkvs[1], mixeds[1], mixed_grad, logs[1], weights[1], first_grad, 1, wait
    )
    if planar:
        late_near, qkv_swap = gate([first_grad], late_near), gate([first_grad], qkv_swap)
        late_side = sum_side(keep, late_swap, late_near)
        qkv_near = sum_near(qkv_keep, qkv_swap)
        wait = [late_near, qkv_swap]
    token_grad, last_sums = self_rest(
        (2, 3), lengths, [[qkvs[j], mixeds[j], logs[j], weights[j]] for j in (2, 3)],
        mixed_grad, first_grad, tokens, upstream, gains[0], wait,
    )
    if planar:
        qkv_near = gate([last_sums], qkv_near)
        qkv_side = sum_side(qkv_keep, qkv_swap, qkv_near)
    norm_sums = jnp.concatenate(
        [last_sums[0:1], sums[2:3], sums[0:1], last_sums[1:2], sums[3:4], sums[1:2]], axis=0
    )
    if planar:
        both_sum = sum_last(both_keep, both_swap, both_near, both_side)
        late_sum = sum_last(keep, late_swap, late_near, late_side)
        qkv_sum = sum_last(qkv_keep, qkv_swap, qkv_near, qkv_side)
        row_sum = [unfold(late_sum[k]) for k in (3, 4)]
        width = norm_sums.shape[1] // DP
        norm_sum = lax.dynamic_slice_in_dim(plane_sum(norm_sums), place * width, width, 1)
    else:
        both_sum = scattered(in_order(both_keep, both_send), 1)
        late = in_order(keep, send)
        late_sum = scattered(late[:3], 1)
        qkv_sum = scattered(in_order(qkv_keep, qkv_send), 1)
        row_sum = [
            scattered(jnp.concatenate([unfold(part) for part in jnp.split(late[k], 8)]), 0)
            for k in (3, 4)
        ]
        norm_sum = scattered(norm_sums, 1)
    return (
        out,
        token_grad,
        text_grad.reshape(text_states.shape),
        norm_sum[:3],
        norm_sum[3:],
        jnp.transpose(qkv_sum, (1, 0, 2)),
        row_sum[0],
        late_sum[0],
        jnp.transpose(late_sum[1:3], (1, 0, 2)),
        row_sum[1],
        both_sum[0],
        both_sum[1],
    )


def solution(mesh):
    placed = (
        P("dp", None),
        P("dp", None, None),
        P("dp"),
        P("dp", None),
        P(),
        P(),
        P(None, None, "mp"),
        P("mp", None),
        P(None, "mp"),
        P(None, None, "mp"),
        P("mp", None),
        P(None, "mp"),
        P("mp", None),
        P("dp", None),
    )
    return jax.shard_map(
        partial(local, mesh.shape["dp"] == DP),
        mesh=mesh,
        in_specs=placed,
        out_specs=(
            P("dp", None),
            P("dp", None),
            P("dp", None, None),
            P(None, "dp"),
            P(None, "dp"),
            P("dp", None, "mp"),
            P(("mp", "dp"), None),
            P("dp", "mp"),
            P("dp", None, "mp"),
            P(("mp", "dp"), None),
            P("dp", "mp"),
            P(("mp", "dp"), None),
        ),
        check_vma=False,
    )
```

```python
from functools import partial

import jax
import jax.numpy as jnp
from jax import lax
from jax.experimental import pallas as pl
from jax.experimental.pallas import tpu as pltpu
from jax.sharding import PartitionSpec as P

HEAD = 64
BLK = 256
EPS = 1e-05
NEG = -1e30
F32 = jnp.float32
BF16 = jnp.bfloat16
MIB = 1024 * 1024

NN = (((1,), (0,)), ((), ()))
NT = (((1,), (1,)), ((), ()))
TN = (((0,), (0,)), ((), ()))


def dot(a, b, dims=NN):
    return lax.dot_general(a, b, dims, preferred_element_type=F32)


def params(mib=56, semantics=None):
    return pltpu.CompilerParams(vmem_limit_bytes=mib * MIB, dimension_semantics=semantics)


def cost(us):
    return pl.CostEstimate(
        flops=int(us * 4.6e8), transcendentals=0, bytes_accessed=int(us * 1.4e6)
    )


def shape(dims, dtype=F32):
    return jax.ShapeDtypeStruct(dims, dtype)


def smem():
    return pl.BlockSpec(memory_space=pltpu.SMEM)


def whole(dims):
    rank = len(dims)
    return pl.BlockSpec(dims, lambda *_: (0,) * rank)


def at(dims, index):
    return pl.BlockSpec(dims, lambda *_: index)


def once(dims):
    rank = len(dims)
    return pl.BlockSpec(dims, lambda *_: (0,) * rank, pipeline_mode=pl.Buffered(1))


def anywhere():
    return pl.BlockSpec(memory_space=pl.ANY)


def launch(kernel, args, in_specs, out_specs, out_shape, scratch=(), wait=(), carry=(), **options):
    args, wait, carry = list(args), list(wait), list(carry)
    count, extra, outs = len(args), len(wait) + len(carry), len(out_shape)

    def body(*refs):
        results = refs[count + extra : count + extra + outs]
        kernel(*refs[:count], *results, *refs[count + extra + outs + len(carry) :])

    return pl.pallas_call(
        body,
        in_specs=list(in_specs) + [anywhere()] * extra,
        out_specs=list(out_specs) + [anywhere()] * len(carry),
        out_shape=list(out_shape) + [shape(value.shape, value.dtype) for value in carry],
        scratch_shapes=list(scratch),
        input_output_aliases={count + len(wait) + k: outs + k for k in range(len(carry))},
        **options,
    )(*args, *wait, *carry)


def gate(wait, carry):
    return launch(
        lambda: None, [], [], [], [], wait=wait, carry=[carry], name="gate", cost_estimate=cost(0.1)
    )[0]


def rows_of(tile, width):
    return pl.BlockSpec((tile, width), lambda i, *_: (i, 0))


def norm_stats(value):
    center = value - jnp.mean(value, axis=-1, keepdims=True)
    spread = jnp.mean(center * center, axis=-1, keepdims=True)
    inverse = lax.rsqrt(spread + EPS)
    return center * inverse, inverse


def norm_forward(value, gain, shift):
    unit, _ = norm_stats(value)
    return (unit * gain + shift).astype(BF16)


def norm_backward(incoming, value, gain):
    unit, inverse = norm_stats(value)
    scaled = incoming * gain
    pushed = incoming * unit
    inner = (
        scaled
        - jnp.mean(scaled, axis=-1, keepdims=True)
        - unit * jnp.mean(scaled * unit, axis=-1, keepdims=True)
    )
    return (
        inner * inverse,
        jnp.sum(pushed, axis=0, keepdims=True),
        jnp.sum(incoming, axis=0, keepdims=True),
    )


def norm_kernel(tokens_ref, gain_ref, shift_ref, first_ref):
    first_ref[...] = norm_forward(tokens_ref[...].astype(F32), gain_ref[...], shift_ref[...])


def norm_first(tokens, gain, shift):
    rows, width = tokens.shape
    return launch(
        norm_kernel,
        [tokens, gain, shift],
        [rows_of(BLK, width), whole((1, width)), whole((1, width))],
        [rows_of(BLK, width)],
        [shape((rows, width), BF16)],
        grid=(rows // BLK,),
        name="norm_first",
        cost_estimate=cost(6),
    )[0]


def head_row(width, head, value):
    lane = lax.broadcasted_iota(jnp.int32, (1, width), 1)
    return jnp.where(lane // HEAD == head, value, 0.0)


def masked(block, row):
    return (block.astype(F32) * row).astype(BF16)


def item_at(lengths, place):
    item, start, end = 0, 0, 0
    for slot in range(lengths.shape[0]):
        end = end + lengths[slot]
        past = end <= place
        item = item + past.astype(jnp.int32)
        start = jnp.where(past, end, start)
    return item, start


def offsets(core):
    return (0, 1 + core, 2 - core, 3)


def join_kernel(me, *refs):
    parts, (target, sems) = refs[:4], refs[4:]
    copies = []
    for index, (part, offset) in enumerate(zip(parts, offsets(me[1]))):
        rows = part.shape[1]
        place = pl.multiple_of((me[0] ^ offset) * rows, rows)
        for k in range(part.shape[0]):
            copies.append(
                pltpu.make_async_copy(
                    part.at[k], target.at[k, pl.ds(place, rows)], sems.at[index, k]
                )
            )
    for copy in copies:
        copy.start()
    for copy in copies:
        copy.wait()


def join(me, parts, wait):
    count, rows, width = parts[0].shape
    return launch(
        join_kernel,
        [me, *parts],
        [smem()] + [anywhere()] * 4,
        [vmem()],
        [shape((count, 4 * rows, width))],
        scratch=[pltpu.SemaphoreType.DMA((4, count))],
        wait=wait,
        compiler_params=params(24),
        name="join",
        cost_estimate=cost(2),
    )[0]


def take(targets, source):
    for k, target in enumerate(targets):
        target[...] = source[k].astype(BF16)


def take_two(first, second, mine, other, core):
    @pl.when(core == 0)
    def _():
        take(first, mine)
        take(second, other)

    @pl.when(core == 1)
    def _():
        take(second, mine)
        take(first, other)


def fill(targets, parts, chip, core):
    for part, offset in zip(parts, offsets(core)):
        rows = part.shape[1]
        place = pl.multiple_of((chip ^ offset) * rows, rows)
        for k, target in enumerate(targets):
            target[pl.ds(place, rows), :] = part[k].astype(BF16)


def fill_two(first, second, mine, other, me):
    chip, core = me[0], me[1]

    @pl.when(core == 0)
    def _():
        fill(first, mine, chip, 0)
        fill(second, other, chip, 1)

    @pl.when(core == 1)
    def _():
        fill(second, mine, chip, 1)
        fill(first, other, chip, 0)


def planes(ref):
    return [ref.at[k] for k in range(ref.shape[0])]


def causal():
    shape2 = (BLK, BLK)
    return lax.broadcasted_iota(jnp.int32, shape2, 0) <= lax.broadcasted_iota(
        jnp.int32, shape2, 1
    )


def lanes_of(head):
    return slice(head * HEAD, (head + 1) * HEAD)


def self_block(qb, count, qkv, turned, mixed, logs):
    q0 = pl.multiple_of(qb * BLK, BLK)
    k0 = pl.multiple_of((qb - (count - 1)) * BLK, BLK)
    width = qkv.shape[2]
    query = qkv[0, pl.ds(q0, BLK), :]
    diag = qkv[1, pl.ds(q0, BLK), :]
    pre_len = (count - 1) * BLK
    keep = causal()
    pieces = []
    heads = range(width // HEAD)
    parts = [masked(query, head_row(width, head, HEAD**-0.5)) for head in heads]
    nears = [dot(diag, part, NT) for part in parts]
    fars = [dot(qkv[1, pl.ds(k0, pre_len), :], part, NT) for part in parts] if pre_len else []
    for head in heads:
        near = jnp.where(keep, nears[head], NEG)
        peak = jnp.max(near, axis=0, keepdims=True)
        if pre_len:
            far = fars[head]
            peak = jnp.maximum(peak, jnp.max(far, axis=0, keepdims=True))
        near = jnp.exp(near - peak)
        total = jnp.sum(near, axis=0, keepdims=True)
        result = dot(turned[lanes_of(head), pl.ds(q0, BLK)], near.astype(BF16))
        if pre_len:
            far = jnp.exp(far - peak)
            total = total + jnp.sum(far, axis=0, keepdims=True)
            result = result + dot(
                turned[lanes_of(head), pl.ds(k0, pre_len)], far.astype(BF16)
            )
        pieces.append(result * (1.0 / total))
        logs[head : head + 1, pl.ds(q0, BLK)] = peak + jnp.log(total)
    mixed[pl.ds(q0, BLK), :] = jnp.concatenate(pieces, axis=0).T.astype(BF16)


def front_body(lengths, first, weights, qkv, mixed, logs, turned):
    rows = first.shape[0]
    for m in range(3):
        qkv[m] = dot(first[...], weights[m]).astype(BF16)
    turned[...] = qkv[2].T

    @pl.loop(0, rows // BLK)
    def _(qb):
        _, start = item_at(lengths, qb * BLK)
        count = qb - start // BLK + 1
        for n in range(1, 5):

            @pl.when(count == n)
            def _():
                self_block(qb, n, qkv, turned, mixed, logs)


def front_kernel(lengths, first, shard, weights, *rest):
    take(planes(weights), shard)
    front_body(lengths, first, weights, *rest)


def front_two_kernel(me, lengths, first, mine, other, text, weights, cross, qkv, mixed, logs, pair, turned):
    take_two(planes(weights), planes(cross), mine, other, me[1])
    text_pair(pair, text, cross)
    front_body(lengths, first, weights, qkv, mixed, logs, turned)


def vmem():
    return pl.BlockSpec(memory_space=pltpu.VMEM)


def front_call(kernel, name, us, prefix, first, arrays, weight_count, more, wait, carry=()):
    rows, depth = first.shape
    width = arrays[0].shape[2]
    outs = [shape((3, depth, width), BF16)] * weight_count + [
        shape((3, rows, width), BF16),
        shape((rows, width), BF16),
        shape((8, rows), F32),
    ] + more
    return launch(
        kernel,
        [*prefix, first, *arrays],
        [smem()] * len(prefix) + [vmem()] * (1 + len(arrays)),
        [vmem()] * len(outs),
        outs,
        scratch=[pltpu.VMEM((width, rows), BF16)],
        wait=wait,
        carry=carry,
        compiler_params=params(),
        name=name,
        cost_estimate=cost(us),
    )


def front_own(lengths, first, weights, wait, carry):
    return front_call(front_body, "front_own", 15, (lengths,), first, [weights], 0, [], wait, carry)


def front(lengths, first, shard, wait, carry):
    return front_call(front_kernel, "front", 16, (lengths,), first, [shard], 1, [], wait, carry)


def front_two(me, lengths, first, arrays, text, wait):
    pair = shape((2, text.shape[0], arrays[0].shape[2]), BF16)
    return front_call(
        front_two_kernel, "front_two", 18, (me, lengths), first, [*arrays, text], 2, [pair], wait
    )


def text_pair(pair, text, cross):
    for m in range(2):
        pair[m] = dot(text[...], cross[m + 1]).astype(BF16)


def text_front_kernel(text, own, mine, other, cross_a, cross_b, *pairs):
    take(planes(cross_a), mine)
    take(planes(cross_b), other)
    for pair, cross in zip(pairs, (own, cross_a, cross_b)):
        text_pair(pair, text, cross)


def text_front(text, own, arrays, wait):
    rows = text.shape[0]
    width = own.shape[2]
    outs = [shape(own.shape, BF16)] * 2 + [shape((2, rows, width), BF16)] * 3
    return launch(
        text_front_kernel,
        [text, own, *arrays],
        [vmem()] * 4,
        [vmem()] * 5,
        outs,
        wait=wait,
        compiler_params=params(),
        name="text_front",
        cost_estimate=cost(7),
    )


def unfold_into(target, first, source):
    width = source.shape[2]
    rows = width // 4
    for piece in range(4):
        for part in range(4):
            target[pl.ds(first + piece * rows, rows), part * width : (part + 1) * width] = source[
                0, pl.ds(piece * width + part * rows, rows), :
            ].astype(BF16)


def middle_kernel(me, lengths, live, tokens, gain1, shift1, gain2, shift2, own_out, own_co, *refs):
    mixed, refs = refs[:4], refs[4:]
    queries, refs = refs[:4], refs[4:]
    pairs, refs = refs[:4], refs[4:]
    outs, cos, (out_two, co_two), refs = refs[:2], refs[2:4], refs[4:6], refs[6:]
    w_out, w_co, after_self, after_cross, second, third, cross_query, looked, logs, turned = refs
    step = pl.program_id(0)

    @pl.when(step == 0)
    def _():
        width = own_out.shape[0]
        w_out[:width, :] = own_out[...]
        w_co[:width, :] = own_co[...]
        for place, out_part, co_part in ((1, outs[0], cos[0]), (3, outs[1], cos[1])):
            unfold_into(w_out, place * width, out_part)
            unfold_into(w_co, place * width, co_part)

        @pl.when(me[1] == 0)
        def _():
            unfold_into(w_out, 2 * width, out_two)
            unfold_into(w_co, 2 * width, co_two)

        @pl.when(me[1] == 1)
        def _():
            unfold_into(w_co, 2 * width, out_two)
            unfold_into(w_out, 2 * width, co_two)

        for j in range(4):
            turned[j] = pairs[j][1].T

    part = jnp.concatenate([ref[...] for ref in mixed], axis=1)
    residual = tokens[...].astype(F32) + dot(part, w_out[...])
    after_self[...] = residual
    normed = norm_forward(residual, gain1[...], shift1[...])
    second[...] = normed
    text = TEXT
    item, _ = item_at(lengths, step * BLK)
    t0 = pl.multiple_of(item * text, text)
    alive = live[pl.ds(t0, text), :] > 0.0
    width = own_out.shape[0]
    heads = range(width // HEAD)
    stages = []
    for j in range(4):
        query = dot(normed, queries[j][0]).astype(BF16)
        cross_query[:, j * width : (j + 1) * width] = query
        rows = [masked(query, head_row(width, head, HEAD**-0.5)) for head in heads]
        keys = pairs[j][0, pl.ds(t0, text), :]
        stages.append([dot(keys, row, NT) for row in rows])
    for j in range(4):
        pieces = []
        for head in heads:
            score = jnp.where(alive, stages[j][head], NEG)
            peak = jnp.max(score, axis=0, keepdims=True)
            score = jnp.exp(score - peak)
            total = jnp.sum(score, axis=0, keepdims=True)
            result = dot(turned[j, lanes_of(head), pl.ds(t0, text)], score.astype(BF16))
            pieces.append(result * (1.0 / total))
            index = j * (width // HEAD) + head
            logs[index : index + 1, :] = peak + jnp.log(total)
        looked[:, j * width : (j + 1) * width] = jnp.concatenate(pieces, axis=0).T.astype(BF16)
    residual = residual + dot(looked[...], w_co[...])
    after_cross[...] = residual
    third[...] = norm_forward(residual, gain2[...], shift2[...])


TEXT = 128


def middle(me, lengths, live, tokens, norms, own_out, own_co, mixed, crosses, pairs, g_cross, g_two, wait):
    rows, depth = tokens.shape
    width = own_out.shape[0]
    text_rows = live.shape[0]
    inner = 4 * width
    row = whole((1, depth))

    def plane_at(k):
        dims = (1, depth, width)
        return pl.BlockSpec(dims, lambda *_: (k, 0, 0), pipeline_mode=pl.Buffered(1))

    return launch(
        middle_kernel,
        [me, lengths, live, tokens, *norms, own_out, own_co, *mixed, *crosses, *pairs]
        + [*g_cross, *g_cross, *g_two],
        [smem(), smem(), whole((text_rows, 1)), rows_of(BLK, depth)]
        + [row] * 4
        + [once((width, depth))] * 2
        + [rows_of(BLK, width)] * 4
        + [at((1, depth, width), (0, 0, 0))] * 4
        + [whole((2, text_rows, width))] * 4
        + [plane_at(k) for k in (3, 3, 4, 4, 3, 3)],
        [whole((inner, depth))] * 2
        + [rows_of(BLK, depth)] * 4
        + [rows_of(BLK, inner)] * 2
        + [pl.BlockSpec((inner // HEAD, BLK), lambda i: (0, i))],
        [shape((inner, depth), BF16)] * 2
        + [shape((rows, depth)), shape((rows, depth))]
        + [shape((rows, depth), BF16)] * 2
        + [shape((rows, inner), BF16)] * 2
        + [shape((inner // HEAD, rows))],
        scratch=[pltpu.VMEM((4, width, text_rows), BF16)],
        wait=wait,
        grid=(rows // BLK,),
        compiler_params=params(),
        name="middle",
        cost_estimate=cost(43),
    )


ROOT = 0.7978845608028654
CUBE = 0.044715


def gelu_both(value):
    square = value * value
    bend = jnp.tanh(value * (ROOT + (ROOT * CUBE) * square))
    half = 0.5 + 0.5 * bend
    slope = half + (0.5 * value) * (1.0 - bend * bend) * (ROOT + (3.0 * ROOT * CUBE) * square)
    return value * half, slope


def feed_rows(third, cot, up, down):
    return feed_finish(dot(third, up), dot(cot, down, NT), up, down)


def feed_finish(pre_act, hidden_grad, up, down):
    hidden, slope = gelu_both(pre_act)
    hidden = hidden.astype(BF16)
    pre_grad = (hidden_grad * slope).astype(BF16)
    return hidden, pre_grad, dot(hidden, down), dot(pre_grad, up, NT)


def feed_own_kernel(
    me, third, cot, after, up, down, out, grad, keep, send, hidden_rows, grad_rows, both
):
    step = pl.program_id(0)
    part = pl.ds(pl.multiple_of(step * FEED, FEED), FEED)
    hidden, pre_grad, result, pushed = feed_rows(third[part, :], cot[part, :], up[...], down[...])
    out[...] = after[...] + result
    grad[...] = pushed
    hidden_rows[part, :] = hidden
    grad_rows[part, :] = pre_grad

    @pl.when(step == pl.num_programs(0) - 1)
    def _():
        both[0] = dot(third[...], grad_rows[...], TN)
        both[1] = dot(hidden_rows[...], cot[...], TN)
        put_pieces(both, keep, send, me)


def put_pieces(source, keep, send, me, first=0):
    chip, core = me[0], me[1]
    rows = source.shape[1] // 8
    for target, owner in ((keep, core), (send, 1 - core)):
        for index, offset in enumerate((0, 2 - owner, 1 + owner, 3)):
            place = pl.multiple_of(((chip ^ offset) * 2 + owner) * rows, rows)
            for k in range(source.shape[0]):
                target[index, first + k] = source[k, pl.ds(place, rows), :]


FEED = 320


def feed_own(me, third, cot, after, up, down, wait):
    rows, depth = third.shape
    inner = up.shape[1]
    tile = rows_of(FEED, depth)
    pieces = (4, 2, depth // 8, depth)
    return launch(
        feed_own_kernel,
        [me, third, cot, after, up, down],
        [smem(), once(third.shape), once(cot.shape), tile]
        + [once((depth, inner)), once((inner, depth))],
        [tile, tile, once(pieces), once(pieces)],
        [shape((rows, depth)), shape((rows, depth)), shape(pieces), shape(pieces)],
        scratch=[pltpu.VMEM((rows, inner), BF16)] * 2 + [pltpu.VMEM((2, depth, inner), F32)],
        wait=wait,
        grid=(rows // FEED,),
        compiler_params=params(),
        name="feed_own",
        cost_estimate=cost(32),
    )


def feed_kernel(own, me, third, cot, out_in, grad_in, *refs):
    parts, (out, grad, both) = refs[:4], refs[4:]

    @pl.when(pl.program_id(0) == 0)
    def _():
        fill(planes(both), parts, me[0], me[1] if own else 1 - me[1])

    _, _, result, pushed = feed_rows(third[...], cot[...], both[0], both[1])
    out[...] = out_in[...] + result
    grad[...] = grad_in[...] + pushed


def feed_last_kernel(me, third, cot, out_in, grad_in, *refs):
    mine, other, (out, grad, both) = refs[:4], refs[4:8], refs[8:]

    @pl.when(pl.program_id(0) == 0)
    def _():
        up, down = planes(both)
        fill_two([up], [down], mine, other, me)

    _, _, result, pushed = feed_rows(third[...], cot[...], both[0], both[1])
    out[...] = (out_in[...] + result).astype(BF16)
    grad[...] = grad_in[...] + pushed


def feed_call(kernel, name, us, prefix, dtype, third, cot, out, grad, arrays, wait, carry=()):
    rows, depth = third.shape
    tile = rows_of(FEED, depth)
    inner = arrays[0].shape[2]
    return launch(
        kernel,
        [*prefix, third, cot, out, grad, *arrays],
        [smem()] * len(prefix) + [tile] * 4 + [once(arrays[0].shape)] * len(arrays),
        [tile, tile],
        [shape((rows, depth), dtype), shape((rows, depth))],
        scratch=[pltpu.VMEM((2, inner, depth), BF16)],
        wait=wait,
        carry=carry,
        grid=(rows // FEED,),
        compiler_params=params(),
        name=name,
        cost_estimate=cost(us),
    )


def feed(own, me, *operands):
    return feed_call(partial(feed_kernel, own), "feed", 18, (me,), F32, *operands)


def feed_last(me, *operands):
    return feed_call(feed_last_kernel, "feed_last", 18, (me,), BF16, *operands)


def back_kernel(
    lengths, live, third_grad, cot, after_cross, after_self, cross_query, looked0, mixed0, logs,
    gain1, gain2, w_out, w_co, *refs,
):
    queries, refs = refs[:4], refs[4:]
    pairs, refs = refs[:4], refs[4:]
    up_grad, mixed_grad, pair_grad, row_grads, query_grads, sums, total, turned = refs
    step = pl.program_id(0)
    text = TEXT

    @pl.when(step == 0)
    def _():
        total[...] = jnp.zeros_like(total)
        row_grads[...] = jnp.zeros_like(row_grads)
        sums[...] = jnp.zeros_like(sums)
        for j in range(4):
            turned[j] = pairs[j][0].T

    pulled, gain_sum, shift_sum = norm_backward(third_grad[...], after_cross[...], gain2[...])
    sums[0:1, :] += gain_sum
    sums[1:2, :] += shift_sum
    upstream = cot[...].astype(F32) + pulled
    low = upstream.astype(BF16)
    row_grads[1] += dot(looked0[...], low, TN)
    looked_grad = dot(low, w_co[...], NT).astype(BF16)
    item, _ = item_at(lengths, step * BLK)
    t0 = pl.multiple_of(item * text, text)
    alive = live[pl.ds(t0, text), :] > 0.0
    second_grad = jnp.zeros(upstream.shape, F32)
    width = queries[0].shape[2]
    heads = range(width // HEAD)

    def scores(j):
        cols = slice(j * width, (j + 1) * width)
        rows = [masked(cross_query[:, cols], head_row(width, h, HEAD**-0.5)) for h in heads]
        grads = [masked(looked_grad[:, cols], head_row(width, h, 1.0)) for h in heads]
        keys = pairs[j][0, pl.ds(t0, text), :]
        values = pairs[j][1, pl.ds(t0, text), :]
        return rows, grads, [dot(keys, row, NT) for row in rows], [dot(values, g, NT) for g in grads]

    ahead = scores(0)
    for j in range(4):
        rows, grads, score_set, pushed_set = ahead
        if j < 3:
            ahead = scores(j + 1)
        pieces, chances, score_grads = [], [], []
        for head in heads:
            index = j * (width // HEAD) + head
            score = jnp.where(alive, score_set[head], NEG)
            chance = jnp.exp(score - logs[index : index + 1, :])
            weighted = chance * pushed_set[head]
            mean = jnp.sum(weighted, axis=0, keepdims=True)
            score_grads.append((weighted - chance * mean).astype(BF16))
            chances.append(chance.astype(BF16))
            pieces.append(dot(turned[j, lanes_of(head), pl.ds(t0, text)], score_grads[head]))
        total[j, 0, pl.ds(t0, text), :] += dot(
            jnp.concatenate(score_grads, axis=1), jnp.concatenate(rows, axis=0)
        )
        total[j, 1, pl.ds(t0, text), :] += dot(
            jnp.concatenate(chances, axis=1), jnp.concatenate(grads, axis=0)
        )
        query_grad = (jnp.concatenate(pieces, axis=0).T * HEAD**-0.5).astype(BF16)
        if j == 0:
            query_grads[...] = query_grad
        second_grad = second_grad + dot(query_grad, queries[j][0], NT)

    pulled, gain_sum, shift_sum = norm_backward(second_grad, after_self[...], gain1[...])
    sums[2:3, :] += gain_sum
    sums[3:4, :] += shift_sum
    upstream = upstream + pulled
    up_grad[...] = upstream
    low = upstream.astype(BF16)
    row_grads[0] += dot(mixed0[...], low, TN)
    mixed_grad[...] = dot(low, w_out[...], NT).astype(BF16)

    @pl.when(step == pl.num_programs(0) - 1)
    def _():
        pair_grad[...] = total[...].astype(BF16)


def back(
    lengths, live, third_grad, cot, after_cross, after_self, cross_query, looked, mixed0, logs,
    gain1, gain2, w_out, w_co, crosses, pairs, wait,
):
    rows, depth = cot.shape
    text_rows = live.shape[0]
    width = mixed0.shape[1]
    inner = 4 * width
    tile = rows_of(BLK, depth)
    row = whole((1, depth))
    return launch(
        back_kernel,
        [lengths, live, third_grad, cot, after_cross, after_self, cross_query, looked, mixed0]
        + [logs, gain1, gain2, w_out, w_co, *crosses, *pairs],
        [smem(), whole((text_rows, 1))]
        + [tile] * 4
        + [rows_of(BLK, inner), rows_of(BLK, width), rows_of(BLK, width)]
        + [pl.BlockSpec((inner // HEAD, BLK), lambda i: (0, i)), row, row]
        + [whole((inner, depth))] * 2
        + [at((1, depth, width), (0, 0, 0))] * 4
        + [whole((2, text_rows, width))] * 4,
        [tile, rows_of(BLK, inner), whole((4, 2, text_rows, width))]
        + [whole((2, width, depth)), rows_of(BLK, width), whole((8, depth))],
        [
            shape((rows, depth)),
            shape((rows, inner), BF16),
            shape((4, 2, text_rows, width), BF16),
            shape((2, width, depth)),
            shape((rows, width), BF16),
            shape((8, depth)),
        ],
        scratch=[
            pltpu.VMEM((4, 2, text_rows, width), F32),
            pltpu.VMEM((4, width, text_rows), BF16),
        ],
        wait=wait,
        grid=(rows // BLK,),
        compiler_params=params(),
        name="back",
        cost_estimate=cost(53),
    )


def text_kernel(me, text, pair_grad, second, query_grad, row_grads, *refs):
    crosses, (text_grad, keep, send, cross_grad, folded) = refs[:4], refs[4:]
    total = jnp.zeros(text_grad.shape, F32)
    for j in range(4):
        for m in range(2):
            total = total + dot(pair_grad[j, m], crosses[j][m + 1], NT)
    text_grad[...] = total
    cross_grad[0] = dot(second[...], query_grad[...], TN)
    for m in range(2):
        cross_grad[m + 1] = dot(text[...], pair_grad[0, m], TN)
    put_pieces(cross_grad, keep, send, me)
    width = folded.shape[2]
    rows = row_grads.shape[1] // 8
    for k in range(2):
        for piece in range(8):
            for part in range(4):
                folded[k, pl.ds((piece * 4 + part) * rows, rows), :] = row_grads[
                    k, pl.ds(piece * rows, rows), part * width : (part + 1) * width
                ]
    put_pieces(folded, keep, send, me, 3)


def unfold(piece):
    rows, width = piece.shape
    parts = [piece[k * rows // 4 : (k + 1) * rows // 4] for k in range(4)]
    return jnp.concatenate(parts, axis=1)


def text_back(me, text, pair_grad, second, query_grad, row_grads, crosses, wait):
    text_rows, depth = text.shape
    width = pair_grad.shape[3]
    pieces = (4, 5, depth // 8, width)
    return launch(
        text_kernel,
        [me, text, pair_grad, second, query_grad, row_grads, *crosses],
        [smem()] + [vmem()] * 9,
        [vmem()] * 3,
        [shape((text_rows, depth)), shape(pieces), shape(pieces)],
        scratch=[pltpu.VMEM((3, depth, width), F32), pltpu.VMEM((2, depth, width), F32)],
        wait=wait,
        compiler_params=params(),
        name="text_back",
        cost_estimate=cost(15),
    )


def self_back_pair(qb, kb, diag, qkv, rows, grads, logs, means, turned, query_sum, key_sum, value_sum):
    q0 = pl.multiple_of(qb * BLK, BLK)
    k0 = pl.multiple_of(kb * BLK, BLK)
    keys = qkv[1, pl.ds(k0, BLK), :]
    values = qkv[2, pl.ds(k0, BLK), :]
    more_keys = 0.0
    more_values = 0.0
    heads = range(rows.shape[0])
    stages = [(dot(keys, rows[h], NT), dot(values, grads[h], NT)) for h in heads]
    for head, (score, pushed) in zip(heads, stages):
        if diag:
            score = jnp.where(causal(), score, NEG)
        chance = jnp.exp(score - logs[head : head + 1, pl.ds(q0, BLK)])
        score_grad = (chance * (pushed - means[head : head + 1, :])).astype(BF16)
        query_sum[lanes_of(head), :] += dot(turned[lanes_of(head), pl.ds(k0, BLK)], score_grad)
        more_keys = more_keys + dot(score_grad, rows[head])
        more_values = more_values + dot(chance.astype(BF16), grads[head])
    key_sum[pl.ds(k0, BLK), :] += more_keys
    value_sum[pl.ds(k0, BLK), :] += more_values


def self_back_body(
    lengths, qkv, mixed, out_grad, logs, weights, triple, turned, rows, grads, means, query_sum,
    key_sum, value_sum,
):
    row_count, width = mixed.shape
    turned[...] = qkv[1].T
    key_sum[...] = jnp.zeros_like(key_sum)
    value_sum[...] = jnp.zeros_like(value_sum)

    @pl.loop(0, row_count // BLK)
    def _(qb):
        q0 = pl.multiple_of(qb * BLK, BLK)
        _, start = item_at(lengths, q0)
        query = qkv[0, pl.ds(q0, BLK), :]
        grad = out_grad[pl.ds(q0, BLK), :]
        flat = (grad.astype(F32) * mixed[pl.ds(q0, BLK), :].astype(F32)).T
        for head in range(width // HEAD):
            rows[head] = masked(query, head_row(width, head, HEAD**-0.5))
            grads[head] = masked(grad, head_row(width, head, 1.0))
            means[head : head + 1, :] = jnp.sum(flat[lanes_of(head), :], axis=0, keepdims=True)
        query_sum[...] = jnp.zeros_like(query_sum)
        rest = (qkv, rows, grads, logs, means, turned, query_sum, key_sum, value_sum)

        @pl.loop(start // BLK, qb)
        def _(kb):
            self_back_pair(qb, kb, False, *rest)

        self_back_pair(qb, qb, True, *rest)
        triple[0, pl.ds(q0, BLK), :] = (query_sum[...].T * HEAD**-0.5).astype(BF16)

    triple[1] = key_sum[...].astype(BF16)
    triple[2] = value_sum[...].astype(BF16)


def self_scratch(rows, width):
    heads = width // HEAD
    return [
        pltpu.VMEM((3, rows, width), BF16),
        pltpu.VMEM((width, rows), BF16),
        pltpu.VMEM((heads, BLK, width), BF16),
        pltpu.VMEM((heads, BLK, width), BF16),
        pltpu.VMEM((8, BLK), F32),
        pltpu.VMEM((width, BLK), F32),
        pltpu.VMEM((rows, width), F32),
        pltpu.VMEM((rows, width), F32),
    ]


def self_own_kernel(me, lengths, qkv, mixed, out_grad, logs, weights, first, total, keep, send, *scratch):
    self_back_body(lengths, qkv, mixed, out_grad, logs, weights, *scratch[:-1])
    triple, qkv_grad = scratch[0], scratch[-1]
    for m in range(3):
        qkv_grad[m] = dot(first[...], triple[m], TN)
    put_pieces(qkv_grad, keep, send, me)
    total[...] = sum(dot(triple[m], weights[m], NT) for m in range(3))


def self_call(kernel, name, us, j, outs, operands, wait, prefix=(), scratch=()):
    lengths, qkv, mixed, out_grad, logs, weights, last_in = operands
    rows, width = mixed.shape
    return launch(
        kernel,
        [*prefix, *operands],
        [smem()] * (len(prefix) + 1)
        + [whole(qkv.shape), whole(mixed.shape), at((rows, width), (0, j))]
        + [whole(logs.shape), whole(weights.shape), whole(last_in.shape)],
        [whole(out.shape) for out in outs],
        outs,
        scratch=self_scratch(rows, width) + list(scratch),
        wait=wait,
        grid=(1,),
        compiler_params=params(),
        name=name,
        cost_estimate=cost(us),
    )


def self_own(me, lengths, qkv, mixed, out_grad, logs, weights, first, wait):
    _, depth, width = weights.shape
    pieces = shape((4, 3, depth // 8, width))
    operands = (lengths, qkv, mixed, out_grad, logs, weights, first)
    scratch = [pltpu.VMEM(weights.shape, F32)]
    outs = [shape(first.shape), pieces, pieces]
    return self_call(self_own_kernel, "self_own", 22, 0, outs, operands, wait, (me,), scratch)


def self_kernel(lengths, qkv, mixed, out_grad, logs, weights, before, total, *scratch):
    self_back_body(lengths, qkv, mixed, out_grad, logs, weights, *scratch)
    triple = scratch[0]
    total[...] = before[...] + sum(dot(triple[m], weights[m], NT) for m in range(3))


def self_back(lengths, qkv, mixed, out_grad, logs, weights, before, j, wait):
    operands = (lengths, qkv, mixed, out_grad, logs, weights, before)
    return self_call(self_kernel, "self_back", 26, j, [shape(before.shape)], operands, wait)[0]


def self_rest_kernel(places, lengths, *refs):
    count = len(places)
    sets, refs = [refs[4 * k : 4 * k + 4] for k in range(count)], refs[4 * count :]
    out_grad, before, tokens, upstream, gain, token_grad, sums, *refs = refs
    held, (total, token_rows, up_rows, sems, out_sems, *scratch) = refs[:5], refs[5:]
    rows, width = held[1].shape[1:]
    waits = []
    for k, (arrays, place) in enumerate(zip(sets, places)):
        sources = [*arrays, out_grad.at[:, pl.ds(place * width, width)]]
        waits.append(
            [
                pltpu.make_async_copy(source, target.at[k], sems.at[k, m])
                for m, (source, target) in enumerate(zip(sources, held))
            ]
        )
    ends = [
        pltpu.make_async_copy(source, target, sems.at[count, m])
        for m, (source, target) in enumerate(
            ((before, total), (tokens, token_rows), (upstream, up_rows))
        )
    ]
    for copy in waits[0] + ends[:1] + sum(waits[1:], []) + ends[1:]:
        copy.start()
    triple = scratch[0]
    for k in range(count):
        for copy in waits[k]:
            copy.wait()
        qkv, mixed, logs, weights, grads = (ref.at[k] for ref in held)
        self_back_body(lengths, qkv, mixed, grads, logs, weights, *scratch)
        if k == 0:
            ends[0].wait()
        total[...] += sum(dot(triple[m], weights[m], NT) for m in range(3))
    ends[1].wait()
    ends[2].wait()
    sums[...] = jnp.zeros_like(sums)
    outs = []
    for k in range(rows // BLK):
        part = slice(k * BLK, (k + 1) * BLK)
        pulled, gain_sum, shift_sum = norm_backward(
            total[part, :], token_rows[part, :].astype(F32), gain[...]
        )
        sums[0:1, :] += gain_sum
        sums[1:2, :] += shift_sum
        up_rows[part, :] = up_rows[part, :] + pulled
        outs.append(
            pltpu.make_async_copy(
                up_rows.at[pl.ds(k * BLK, BLK)], token_grad.at[pl.ds(k * BLK, BLK)], out_sems.at[k]
            )
        )
        outs[-1].start()
    for copy in outs:
        copy.wait()


def self_rest(places, lengths, sets, out_grad, before, tokens, upstream, gain, wait):
    rows, depth = tokens.shape
    count = len(places)
    width = sets[0][1].shape[1]
    args = [lengths, *sum(sets, []), out_grad, before, tokens, upstream, gain]
    held = [
        pltpu.VMEM((count,) + array.shape, array.dtype) for array in sets[0] + [sets[0][1]]
    ]
    return launch(
        partial(self_rest_kernel, places),
        args,
        [smem()] + [anywhere()] * (len(args) - 2) + [vmem()],
        [anywhere(), vmem()],
        [shape((rows, depth)), shape((8, depth))],
        scratch=held
        + [pltpu.VMEM((rows, depth), dtype) for dtype in (F32, BF16, F32)]
        + [pltpu.SemaphoreType.DMA((count + 1, 5)), pltpu.SemaphoreType.DMA((rows // BLK,))]
        + self_scratch(rows, width),
        wait=wait,
        compiler_params=params(),
        name="self_rest",
        cost_estimate=cost(40),
    )


DP = 8
MP = 4


def ring(step):
    pairs = []
    for i in range(DP):
        for z in range(MP):
            to = (z + (step if i % 2 == 0 else -step)) % MP
            pairs.append((i * MP + z, i * MP + to))
    return pairs


def straight(step):
    return [(z, (z + step) % MP) for z in range(MP)]


def beside(first):
    return [(i, i ^ (2 if (i % 2 == 0) == first else 4)) for i in range(DP)]


def swap(value):
    return lax.ppermute(value, "dp", [(i, i ^ 1) for i in range(DP)])


def fold(piece):
    width = piece.shape[1] // 4
    return jnp.concatenate([piece[:, k * width : (k + 1) * width] for k in range(4)], axis=0)


def fold_whole(shard):
    return jnp.concatenate([fold(piece) for piece in jnp.split(shard, 4)], axis=0)


def cut(shard, chip):
    rows = shard.shape[1] // 4
    return lax.dynamic_slice_in_dim(shard, chip * rows, rows, 1).astype(F32)


def near_of(piece):
    return lax.ppermute(piece, "dp", beside(True))


def side_of(piece):
    return lax.ppermute(piece, "dp", beside(False))


def along(value, step):
    return lax.ppermute(value, "mp", straight(step))


def around(value):
    return lax.ppermute(value, ("dp", "mp"), ring(1))


def in_order(keep, send):
    pieces = [part[k] for k, m in ((0, 0), (2, 1), (1, 2), (3, 3)) for part, k in ((keep, k), (send, m))]
    return jnp.concatenate(pieces, axis=1)


def scattered(value, axis):
    return lax.psum_scatter(value, "dp", scatter_dimension=axis, tiled=True)


def pieces_of(mine, other):
    mine, other = jnp.split(mine, 4, axis=1), jnp.split(other, 4, axis=1)
    return mine + [other[k] for k in (0, 2, 1, 3)]


def sum_near(keep, sent):
    return lax.ppermute(keep[2:] + sent[2:], "dp", beside(True))


def sum_side(keep, sent, near):
    return side_of(keep[1] + sent[1] + near[1])


def sum_last(keep, sent, near, side):
    return keep[0] + sent[0] + near[0] + side


def plane_sum(value):
    chips = [lax.ppermute(value, "dp", [(i, i ^ bit) for i in range(DP)]) for bit in (2, 4, 6)]
    value = value + chips[0] + (chips[1] + chips[2])
    return value + swap(value)


def local(
    planar, tokens, text_states, lengths, text_mask, ln_gain, ln_shift, w_qkv, w_out, w_cross_q,
    w_cross_kv, w_cross_out, w_up, w_down, cotangent,
):
    slot_count, text_length = text_mask.shape
    place = lax.axis_index("dp") if planar else jnp.int32(0)
    chip, core = place // 2, place % 2
    me = jnp.stack([chip, core]).astype(jnp.int32)
    gains = [ln_gain[n : n + 1] for n in range(3)]
    shifts = [ln_shift[n : n + 1] for n in range(3)]
    text = text_states.reshape(slot_count * text_length, text_states.shape[2])
    position = lax.broadcasted_iota(jnp.int32, text_mask.shape, 1)
    live = ((text_mask == 1) | (position == 0)).astype(F32).reshape(-1, 1)
    own_qkv = jnp.transpose(w_qkv, (1, 0, 2))
    own_cross = jnp.concatenate([w_cross_q[None], jnp.transpose(w_cross_kv, (1, 0, 2))], axis=0)
    feeds = jnp.stack([w_up, w_down])
    first = norm_first(tokens, gains[0], shifts[0])
    qkvs, mixeds, logs, weights = ([None] * 4 for _ in range(4))
    weights[0] = own_qkv

    def shards(value):
        return along(value.astype(F32), 1), along(value.astype(F32), 3)

    wait, carry = [], []
    if planar:
        rows = w_out.shape[0] // 4
        outer = [
            fold(lax.dynamic_slice_in_dim(value, chip * rows, rows, 0))[None].astype(F32)
            for value in (w_out, w_cross_out)
        ]
        qkv_one = around(cut(own_qkv, chip))
        qkv_near, qkv_side = near_of(qkv_one), side_of(qkv_one)
        own_piece = gate([qkv_one], jnp.concatenate([cut(own_cross, chip), *outer], axis=0))
        cross_one = around(own_piece)
        wait = [qkv_one, own_piece]
    qkvs[0], mixeds[0], logs[0] = front_own(lengths, first, own_qkv, wait, [])
    if planar:
        mine = join(me, [qkv_one, qkv_near, qkv_side, near_of(qkv_side)], [logs[0]])
        g_qkv = mine, swap(mine)
        cross_near, cross_side = near_of(cross_one), side_of(cross_one)
        two = jnp.where(
            core == 0,
            jnp.concatenate([qkv_one, cross_one[3:4]], axis=0),
            jnp.concatenate([cross_one[:3], cross_one[4:5]], axis=0),
        )
        two = around(two)
        wait = [cross_one]
        carry = [cut(feeds, chip)]
    else:
        folded = [fold_whole(value)[None] for value in (w_out, w_cross_out)]
        g_qkv = shards(own_qkv)
        g_cross = shards(jnp.concatenate([own_cross, *folded], axis=0))
        g_two = [
            along(jnp.concatenate(parts, axis=0).astype(F32), 2)
            for parts in ((own_qkv, folded[0]), (own_cross, folded[1]))
        ]
        g_feed = pieces_of(*shards(feeds))
        g_last = pieces_of(*[along(feeds[k : k + 1].astype(F32), 2) for k in range(2)])
    weights[1], qkvs[1], mixeds[1], logs[1], *carried = front(
        lengths, first, g_qkv[0], wait, carry
    )
    if planar:
        cross_side, two = gate([logs[1]], cross_side), gate([logs[1]], two)
        cross_far = near_of(cross_side)
        two_near, two_side = near_of(two), side_of(two)
        feed_one = around(carried[0])
        wait = [two, cross_near, cross_side, logs[1]]
    weights[3], qkvs[3], mixeds[3], logs[3] = front(lengths, first, g_qkv[1], wait, [])
    if planar:
        mine = join(me, [cross_one, cross_near, cross_side, cross_far], [logs[3], feed_one, two_near, two_side])
        g_cross = mine, swap(mine)
        two_far = near_of(two_side)
        feed_near, feed_side = near_of(feed_one), side_of(feed_one)
        feed_two = around(lax.dynamic_slice_in_dim(feed_one, core, 1, 0))
        wait = [two_near, two_side]
    cross_a, cross_b, *pairs = text_front(text, own_cross, g_cross, wait)
    if planar:
        mine = join(me, [two, two_near, two_side, two_far], [cross_a])
        g_two = mine, swap(mine)
        wait = []
    weights[2], cross_two, qkvs[2], mixeds[2], logs[2], pair_two = front_two(
        me, lengths, first, g_two, text, wait
    )
    pairs = [pairs[0], pairs[1], pair_two, pairs[2]]
    crosses = [own_cross, cross_a, cross_two, cross_b]
    if planar:
        wait = [feed_one, feed_two]
    full_out, full_co, after_self, after_cross, second, third, cross_query, looked, cross_logs = middle(
        me, lengths, live, tokens, (gains[1], shifts[1], gains[2], shifts[2]), w_out, w_cross_out,
        mixeds, crosses, pairs, g_cross, g_two, wait,
    )
    if planar:
        feed_side, feed_two = gate([third], feed_side), gate([third], feed_two)
        feed_far = near_of(feed_side)
        last_near, last_side = near_of(feed_two), side_of(feed_two)
        wait = [feed_near, feed_side, feed_two]
    out, grad, both_keep, both_send = feed_own(
        me, third, cotangent, after_cross, w_up, w_down, wait
    )
    wait, carry = [], [both_send]
    if planar:
        g_feed = [feed_one, feed_near, feed_side, gate([out], feed_far)]
        g_feed = g_feed + [swap(value) for value in g_feed]
        wait = g_feed[4:7]
    out, grad = feed(True, me, third, cotangent, out, grad, g_feed[:4], wait)
    if planar:
        last_far = near_of(gate([out], last_side))
    out, grad = feed(False, me, third, cotangent, out, grad, g_feed[4:], [])
    if planar:
        g_last = [feed_two, last_near, last_side, gate([out], last_far)]
        g_last = g_last + [swap(value) for value in g_last]
    out, grad, both_send = feed_last(
        me, third, cotangent, out, grad, g_last, [], [both_send]
    )
    if planar:
        both_swap = swap(both_send)
    upstream, mixed_grad, pair_grad, row_grads, query_grad, sums = back(
        lengths, live, grad, cotangent, after_cross, after_self, cross_query, looked, mixeds[0],
        cross_logs, gains[1], gains[2], full_out, full_co, crosses, pairs,
        [],
    )
    wait = []
    if planar:
        both_swap = gate([sums], both_swap)
        both_near = sum_near(both_keep, both_swap)
    text_grad, keep, send = text_back(
        me, text, pair_grad, second, query_grad, row_grads, crosses, wait
    )
    if planar:
        late_swap = swap(send)
        wait = []
    first_grad, qkv_keep, qkv_send = self_own(
        me, lengths, qkvs[0], mixeds[0], mixed_grad, logs[0], weights[0], first, wait
    )
    if planar:
        both_near = gate([first_grad], both_near)
        both_side = sum_side(both_keep, both_swap, both_near)
        late_near = sum_near(keep, late_swap)
        qkv_swap = swap(qkv_send)
        wait = [late_swap, both_near]
    first_grad = self_back(
        lengths, qkvs[1], mixeds[1], mixed_grad, logs[1], weights[1], first_grad, 1, wait
    )
    if planar:
        late_near, qkv_swap = gate([first_grad], late_near), gate([first_grad], qkv_swap)
        late_side = sum_side(keep, late_swap, late_near)
        qkv_near = sum_near(qkv_keep, qkv_swap)
        wait = [late_near, qkv_swap]
    token_grad, last_sums = self_rest(
        (2, 3), lengths, [[qkvs[j], mixeds[j], logs[j], weights[j]] for j in (2, 3)],
        mixed_grad, first_grad, tokens, upstream, gains[0], wait,
    )
    if planar:
        qkv_near = gate([last_sums], qkv_near)
        late_side = gate([last_sums], late_side)
        both_side = gate([last_sums], both_side)
        last_sums = gate([late_side, both_side, qkv_near], last_sums)
        qkv_side = sum_side(qkv_keep, qkv_swap, qkv_near)
    norm_sums = jnp.concatenate(
        [last_sums[0:1], sums[2:3], sums[0:1], last_sums[1:2], sums[3:4], sums[1:2]], axis=0
    )
    if planar:
        both_sum = sum_last(both_keep, both_swap, both_near, both_side)
        late_sum = sum_last(keep, late_swap, late_near, late_side)
        qkv_sum = sum_last(qkv_keep, qkv_swap, qkv_near, qkv_side)
        row_sum = [unfold(late_sum[k]) for k in (3, 4)]
        width = norm_sums.shape[1] // DP
        norm_sum = lax.dynamic_slice_in_dim(plane_sum(norm_sums), place * width, width, 1)
    else:
        both_sum = scattered(in_order(both_keep, both_send), 1)
        late = in_order(keep, send)
        late_sum = scattered(late[:3], 1)
        qkv_sum = scattered(in_order(qkv_keep, qkv_send), 1)
        row_sum = [
            scattered(jnp.concatenate([unfold(part) for part in jnp.split(late[k], 8)]), 0)
            for k in (3, 4)
        ]
        norm_sum = scattered(norm_sums, 1)
    return (
        out,
        token_grad,
        text_grad.reshape(text_states.shape),
        norm_sum[:3],
        norm_sum[3:],
        jnp.transpose(qkv_sum, (1, 0, 2)),
        row_sum[0],
        late_sum[0],
        jnp.transpose(late_sum[1:3], (1, 0, 2)),
        row_sum[1],
        both_sum[0],
        both_sum[1],
    )


def solution(mesh):
    placed = (
        P("dp", None),
        P("dp", None, None),
        P("dp"),
        P("dp", None),
        P(),
        P(),
        P(None, None, "mp"),
        P("mp", None),
        P(None, "mp"),
        P(None, None, "mp"),
        P("mp", None),
        P(None, "mp"),
        P("mp", None),
        P("dp", None),
    )
    return jax.shard_map(
        partial(local, mesh.shape["dp"] == DP),
        mesh=mesh,
        in_specs=placed,
        out_specs=(
            P("dp", None),
            P("dp", None),
            P("dp", None, None),
            P(None, "dp"),
            P(None, "dp"),
            P("dp", None, "mp"),
            P(("mp", "dp"), None),
            P("dp", "mp"),
            P("dp", None, "mp"),
            P(("mp", "dp"), None),
            P("dp", "mp"),
            P(("mp", "dp"), None),
        ),
        check_vma=False,
    )
```

```python
from functools import partial

import jax
import jax.numpy as jnp
from jax import lax
from jax.experimental import pallas as pl
from jax.experimental.pallas import tpu as pltpu
from jax.sharding import PartitionSpec as P

HEAD = 64
BLK = 256
EPS = 1e-05
NEG = -1e30
F32 = jnp.float32
BF16 = jnp.bfloat16
MIB = 1024 * 1024

NN = (((1,), (0,)), ((), ()))
NT = (((1,), (1,)), ((), ()))
TN = (((0,), (0,)), ((), ()))


def dot(a, b, dims=NN):
    return lax.dot_general(a, b, dims, preferred_element_type=F32)


def params(mib=56, semantics=None):
    return pltpu.CompilerParams(vmem_limit_bytes=mib * MIB, dimension_semantics=semantics)


def cost(us):
    return pl.CostEstimate(
        flops=int(us * 4.6e8), transcendentals=0, bytes_accessed=int(us * 1.4e6)
    )


def shape(dims, dtype=F32):
    return jax.ShapeDtypeStruct(dims, dtype)


def smem():
    return pl.BlockSpec(memory_space=pltpu.SMEM)


def whole(dims):
    rank = len(dims)
    return pl.BlockSpec(dims, lambda *_: (0,) * rank)


def at(dims, index):
    return pl.BlockSpec(dims, lambda *_: index)


def once(dims):
    rank = len(dims)
    return pl.BlockSpec(dims, lambda *_: (0,) * rank, pipeline_mode=pl.Buffered(1))


def anywhere():
    return pl.BlockSpec(memory_space=pl.ANY)


def launch(kernel, args, in_specs, out_specs, out_shape, scratch=(), wait=(), carry=(), **options):
    args, wait, carry = list(args), list(wait), list(carry)
    count, extra, outs = len(args), len(wait) + len(carry), len(out_shape)

    def body(*refs):
        results = refs[count + extra : count + extra + outs]
        kernel(*refs[:count], *results, *refs[count + extra + outs + len(carry) :])

    return pl.pallas_call(
        body,
        in_specs=list(in_specs) + [anywhere()] * extra,
        out_specs=list(out_specs) + [anywhere()] * len(carry),
        out_shape=list(out_shape) + [shape(value.shape, value.dtype) for value in carry],
        scratch_shapes=list(scratch),
        input_output_aliases={count + len(wait) + k: outs + k for k in range(len(carry))},
        **options,
    )(*args, *wait, *carry)


def gate(wait, carry):
    return launch(
        lambda: None, [], [], [], [], wait=wait, carry=[carry], name="gate", cost_estimate=cost(0.1)
    )[0]


def rows_of(tile, width):
    return pl.BlockSpec((tile, width), lambda i, *_: (i, 0))


def norm_stats(value):
    center = value - jnp.mean(value, axis=-1, keepdims=True)
    spread = jnp.mean(center * center, axis=-1, keepdims=True)
    inverse = lax.rsqrt(spread + EPS)
    return center * inverse, inverse


def norm_forward(value, gain, shift):
    unit, _ = norm_stats(value)
    return (unit * gain + shift).astype(BF16)


def norm_backward(incoming, value, gain):
    unit, inverse = norm_stats(value)
    scaled = incoming * gain
    pushed = incoming * unit
    inner = (
        scaled
        - jnp.mean(scaled, axis=-1, keepdims=True)
        - unit * jnp.mean(scaled * unit, axis=-1, keepdims=True)
    )
    return (
        inner * inverse,
        jnp.sum(pushed, axis=0, keepdims=True),
        jnp.sum(incoming, axis=0, keepdims=True),
    )


def norm_kernel(tokens_ref, gain_ref, shift_ref, first_ref):
    first_ref[...] = norm_forward(tokens_ref[...].astype(F32), gain_ref[...], shift_ref[...])


def norm_first(tokens, gain, shift, wait):
    rows, width = tokens.shape
    return launch(
        norm_kernel,
        [tokens, gain, shift],
        [rows_of(BLK, width), whole((1, width)), whole((1, width))],
        [rows_of(BLK, width)],
        [shape((rows, width), BF16)],
        wait=wait,
        grid=(rows // BLK,),
        name="norm_first",
        cost_estimate=cost(6),
    )[0]


def head_row(width, head, value):
    lane = lax.broadcasted_iota(jnp.int32, (1, width), 1)
    return jnp.where(lane // HEAD == head, value, 0.0)


def masked(block, row):
    return (block.astype(F32) * row).astype(BF16)


def item_at(lengths, place):
    item, start, end = 0, 0, 0
    for slot in range(lengths.shape[0]):
        end = end + lengths[slot]
        past = end <= place
        item = item + past.astype(jnp.int32)
        start = jnp.where(past, end, start)
    return item, start


def offsets(core):
    return (0, 1 + core, 2 - core, 3)


def join_kernel(me, *refs):
    parts, (target, sems) = refs[:4], refs[4:]
    copies = []
    for index, (part, offset) in enumerate(zip(parts, offsets(me[1]))):
        rows = part.shape[1]
        place = pl.multiple_of((me[0] ^ offset) * rows, rows)
        for k in range(part.shape[0]):
            copies.append(
                pltpu.make_async_copy(
                    part.at[k], target.at[k, pl.ds(place, rows)], sems.at[index, k]
                )
            )
    for copy in copies:
        copy.start()
    for copy in copies:
        copy.wait()


def join(me, parts, wait):
    count, rows, width = parts[0].shape
    return launch(
        join_kernel,
        [me, *parts],
        [smem()] + [anywhere()] * 4,
        [vmem()],
        [shape((count, 4 * rows, width))],
        scratch=[pltpu.SemaphoreType.DMA((4, count))],
        wait=wait,
        compiler_params=params(24),
        name="join",
        cost_estimate=cost(0.1),
    )[0]


def take(targets, source):
    for k, target in enumerate(targets):
        target[...] = source[k].astype(BF16)


def take_two(first, second, mine, other, core):
    @pl.when(core == 0)
    def _():
        take(first, mine)
        take(second, other)

    @pl.when(core == 1)
    def _():
        take(second, mine)
        take(first, other)


def fill(targets, parts, chip, core):
    for part, offset in zip(parts, offsets(core)):
        rows = part.shape[1]
        place = pl.multiple_of((chip ^ offset) * rows, rows)
        for k, target in enumerate(targets):
            target[pl.ds(place, rows), :] = part[k].astype(BF16)


def fill_two(first, second, mine, other, me):
    chip, core = me[0], me[1]

    @pl.when(core == 0)
    def _():
        fill(first, mine, chip, 0)
        fill(second, other, chip, 1)

    @pl.when(core == 1)
    def _():
        fill(second, mine, chip, 1)
        fill(first, other, chip, 0)


def planes(ref):
    return [ref.at[k] for k in range(ref.shape[0])]


def causal():
    shape2 = (BLK, BLK)
    return lax.broadcasted_iota(jnp.int32, shape2, 0) <= lax.broadcasted_iota(
        jnp.int32, shape2, 1
    )


def lanes_of(head):
    return slice(head * HEAD, (head + 1) * HEAD)


def self_block(qb, count, qkv, turned, mixed, logs):
    q0 = pl.multiple_of(qb * BLK, BLK)
    k0 = pl.multiple_of((qb - (count - 1)) * BLK, BLK)
    width = qkv.shape[2]
    query = qkv[0, pl.ds(q0, BLK), :]
    diag = qkv[1, pl.ds(q0, BLK), :]
    pre_len = (count - 1) * BLK
    keep = causal()
    pieces = []
    heads = range(width // HEAD)
    parts = [masked(query, head_row(width, head, HEAD**-0.5)) for head in heads]
    nears = [dot(diag, part, NT) for part in parts]
    fars = [dot(qkv[1, pl.ds(k0, pre_len), :], part, NT) for part in parts] if pre_len else []
    for head in heads:
        near = jnp.where(keep, nears[head], NEG)
        peak = jnp.max(near, axis=0, keepdims=True)
        if pre_len:
            far = fars[head]
            peak = jnp.maximum(peak, jnp.max(far, axis=0, keepdims=True))
        near = jnp.exp(near - peak)
        total = jnp.sum(near, axis=0, keepdims=True)
        result = dot(turned[lanes_of(head), pl.ds(q0, BLK)], near.astype(BF16))
        if pre_len:
            far = jnp.exp(far - peak)
            total = total + jnp.sum(far, axis=0, keepdims=True)
            result = result + dot(
                turned[lanes_of(head), pl.ds(k0, pre_len)], far.astype(BF16)
            )
        pieces.append(result * (1.0 / total))
        logs[head : head + 1, pl.ds(q0, BLK)] = peak + jnp.log(total)
    mixed[pl.ds(q0, BLK), :] = jnp.concatenate(pieces, axis=0).T.astype(BF16)


def front_body(lengths, first, weights, qkv, mixed, logs, turned):
    rows = first.shape[0]
    for m in range(3):
        qkv[m] = dot(first[...], weights[m]).astype(BF16)
    turned[...] = qkv[2].T

    @pl.loop(0, rows // BLK)
    def _(qb):
        _, start = item_at(lengths, qb * BLK)
        count = qb - start // BLK + 1
        for n in range(1, 5):

            @pl.when(count == n)
            def _():
                self_block(qb, n, qkv, turned, mixed, logs)


def front_kernel(lengths, first, shard, weights, *rest):
    take(planes(weights), shard)
    front_body(lengths, first, weights, *rest)


def front_two_kernel(me, lengths, first, mine, other, text, weights, cross, qkv, mixed, logs, pair, turned):
    take_two(planes(weights), planes(cross), mine, other, me[1])
    text_pair(pair, text, cross)
    front_body(lengths, first, weights, qkv, mixed, logs, turned)


def vmem():
    return pl.BlockSpec(memory_space=pltpu.VMEM)


def front_call(kernel, name, us, prefix, first, arrays, weight_count, more, wait, carry=()):
    rows, depth = first.shape
    width = arrays[0].shape[2]
    outs = [shape((3, depth, width), BF16)] * weight_count + [
        shape((3, rows, width), BF16),
        shape((rows, width), BF16),
        shape((8, rows), F32),
    ] + more
    return launch(
        kernel,
        [*prefix, first, *arrays],
        [smem()] * len(prefix) + [vmem()] * (1 + len(arrays)),
        [vmem()] * len(outs),
        outs,
        scratch=[pltpu.VMEM((width, rows), BF16)],
        wait=wait,
        carry=carry,
        compiler_params=params(),
        name=name,
        cost_estimate=cost(us),
    )


def front_own(lengths, first, weights, wait, carry):
    return front_call(front_body, "front_own", 15, (lengths,), first, [weights], 0, [], wait, carry)


def front(lengths, first, shard, wait, carry):
    return front_call(front_kernel, "front", 16, (lengths,), first, [shard], 1, [], wait, carry)


def front_two(me, lengths, first, arrays, text, wait):
    pair = shape((2, text.shape[0], arrays[0].shape[2]), BF16)
    return front_call(
        front_two_kernel, "front_two", 18, (me, lengths), first, [*arrays, text], 2, [pair], wait
    )


def text_pair(pair, text, cross):
    for m in range(2):
        pair[m] = dot(text[...], cross[m + 1]).astype(BF16)


def text_front_kernel(text, own, mine, other, cross_a, cross_b, *pairs):
    take(planes(cross_a), mine)
    take(planes(cross_b), other)
    for pair, cross in zip(pairs, (own, cross_a, cross_b)):
        text_pair(pair, text, cross)


def text_front(text, own, arrays, wait):
    rows = text.shape[0]
    width = own.shape[2]
    outs = [shape(own.shape, BF16)] * 2 + [shape((2, rows, width), BF16)] * 3
    return launch(
        text_front_kernel,
        [text, own, *arrays],
        [vmem()] * 4,
        [vmem()] * 5,
        outs,
        wait=wait,
        compiler_params=params(),
        name="text_front",
        cost_estimate=cost(7),
    )


def unfold_into(target, first, source):
    width = source.shape[2]
    rows = width // 4
    for piece in range(4):
        for part in range(4):
            target[pl.ds(first + piece * rows, rows), part * width : (part + 1) * width] = source[
                0, pl.ds(piece * width + part * rows, rows), :
            ].astype(BF16)


def middle_kernel(me, lengths, live, tokens, gain1, shift1, gain2, shift2, own_out, own_co, *refs):
    mixed, refs = refs[:4], refs[4:]
    queries, refs = refs[:4], refs[4:]
    pairs, refs = refs[:4], refs[4:]
    outs, cos, (out_two, co_two), refs = refs[:2], refs[2:4], refs[4:6], refs[6:]
    w_out, w_co, after_self, after_cross, second, third, cross_query, looked, logs, turned = refs
    step = pl.program_id(0)

    @pl.when(step == 0)
    def _():
        width = own_out.shape[0]
        w_out[:width, :] = own_out[...]
        w_co[:width, :] = own_co[...]
        for place, out_part, co_part in ((1, outs[0], cos[0]), (3, outs[1], cos[1])):
            unfold_into(w_out, place * width, out_part)
            unfold_into(w_co, place * width, co_part)

        @pl.when(me[1] == 0)
        def _():
            unfold_into(w_out, 2 * width, out_two)
            unfold_into(w_co, 2 * width, co_two)

        @pl.when(me[1] == 1)
        def _():
            unfold_into(w_co, 2 * width, out_two)
            unfold_into(w_out, 2 * width, co_two)

        for j in range(4):
            turned[j] = pairs[j][1].T

    part = jnp.concatenate([ref[...] for ref in mixed], axis=1)
    residual = tokens[...].astype(F32) + dot(part, w_out[...])
    after_self[...] = residual
    normed = norm_forward(residual, gain1[...], shift1[...])
    second[...] = normed
    text = TEXT
    item, _ = item_at(lengths, step * BLK)
    t0 = pl.multiple_of(item * text, text)
    alive = live[pl.ds(t0, text), :] > 0.0
    width = own_out.shape[0]
    heads = range(width // HEAD)
    stages = []
    for j in range(4):
        query = dot(normed, queries[j][0]).astype(BF16)
        cross_query[:, j * width : (j + 1) * width] = query
        rows = [masked(query, head_row(width, head, HEAD**-0.5)) for head in heads]
        keys = pairs[j][0, pl.ds(t0, text), :]
        stages.append([dot(keys, row, NT) for row in rows])
    for j in range(4):
        pieces = []
        for head in heads:
            score = jnp.where(alive, stages[j][head], NEG)
            peak = jnp.max(score, axis=0, keepdims=True)
            score = jnp.exp(score - peak)
            total = jnp.sum(score, axis=0, keepdims=True)
            result = dot(turned[j, lanes_of(head), pl.ds(t0, text)], score.astype(BF16))
            pieces.append(result * (1.0 / total))
            index = j * (width // HEAD) + head
            logs[index : index + 1, :] = peak + jnp.log(total)
        looked[:, j * width : (j + 1) * width] = jnp.concatenate(pieces, axis=0).T.astype(BF16)
    residual = residual + dot(looked[...], w_co[...])
    after_cross[...] = residual
    third[...] = norm_forward(residual, gain2[...], shift2[...])


TEXT = 128


def middle(me, lengths, live, tokens, norms, own_out, own_co, mixed, crosses, pairs, g_cross, g_two, wait):
    rows, depth = tokens.shape
    width = own_out.shape[0]
    text_rows = live.shape[0]
    inner = 4 * width
    row = whole((1, depth))

    def plane_at(k):
        dims = (1, depth, width)
        return pl.BlockSpec(dims, lambda *_: (k, 0, 0), pipeline_mode=pl.Buffered(1))

    return launch(
        middle_kernel,
        [me, lengths, live, tokens, *norms, own_out, own_co, *mixed, *crosses, *pairs]
        + [*g_cross, *g_cross, *g_two],
        [smem(), smem(), whole((text_rows, 1)), rows_of(BLK, depth)]
        + [row] * 4
        + [once((width, depth))] * 2
        + [rows_of(BLK, width)] * 4
        + [at((1, depth, width), (0, 0, 0))] * 4
        + [whole((2, text_rows, width))] * 4
        + [plane_at(k) for k in (3, 3, 4, 4, 3, 3)],
        [whole((inner, depth))] * 2
        + [rows_of(BLK, depth)] * 4
        + [rows_of(BLK, inner)] * 2
        + [pl.BlockSpec((inner // HEAD, BLK), lambda i: (0, i))],
        [shape((inner, depth), BF16)] * 2
        + [shape((rows, depth)), shape((rows, depth))]
        + [shape((rows, depth), BF16)] * 2
        + [shape((rows, inner), BF16)] * 2
        + [shape((inner // HEAD, rows))],
        scratch=[pltpu.VMEM((4, width, text_rows), BF16)],
        wait=wait,
        grid=(rows // BLK,),
        compiler_params=params(),
        name="middle",
        cost_estimate=cost(43),
    )


ROOT = 0.7978845608028654
CUBE = 0.044715


def gelu_both(value):
    square = value * value
    bend = jnp.tanh(value * (ROOT + (ROOT * CUBE) * square))
    half = 0.5 + 0.5 * bend
    slope = half + (0.5 * value) * (1.0 - bend * bend) * (ROOT + (3.0 * ROOT * CUBE) * square)
    return value * half, slope


def feed_rows(third, cot, up, down):
    return feed_finish(dot(third, up), dot(cot, down, NT), up, down)


def feed_finish(pre_act, hidden_grad, up, down):
    hidden, slope = gelu_both(pre_act)
    hidden = hidden.astype(BF16)
    pre_grad = (hidden_grad * slope).astype(BF16)
    return hidden, pre_grad, dot(hidden, down), dot(pre_grad, up, NT)


def feed_own_kernel(
    me, third, cot, after, up, down, out, grad, keep, send, hidden_rows, grad_rows, both
):
    step = pl.program_id(0)
    part = pl.ds(pl.multiple_of(step * FEED, FEED), FEED)
    hidden, pre_grad, result, pushed = feed_rows(third[part, :], cot[part, :], up[...], down[...])
    out[...] = after[...] + result
    grad[...] = pushed
    hidden_rows[part, :] = hidden
    grad_rows[part, :] = pre_grad

    @pl.when(step == pl.num_programs(0) - 1)
    def _():
        both[0] = dot(third[...], grad_rows[...], TN)
        both[1] = dot(hidden_rows[...], cot[...], TN)
        put_pieces(both, keep, send, me)


def put_pieces(source, keep, send, me, first=0):
    chip, core = me[0], me[1]
    rows = source.shape[1] // 8
    for target, owner in ((keep, core), (send, 1 - core)):
        for index, offset in enumerate((0, 2 - owner, 1 + owner, 3)):
            place = pl.multiple_of(((chip ^ offset) * 2 + owner) * rows, rows)
            for k in range(source.shape[0]):
                target[index, first + k] = source[k, pl.ds(place, rows), :]


FEED = 320


def feed_own(me, third, cot, after, up, down, wait):
    rows, depth = third.shape
    inner = up.shape[1]
    tile = rows_of(FEED, depth)
    pieces = (4, 2, depth // 8, depth)
    return launch(
        feed_own_kernel,
        [me, third, cot, after, up, down],
        [smem(), once(third.shape), once(cot.shape), tile]
        + [once((depth, inner)), once((inner, depth))],
        [tile, tile, once(pieces), once(pieces)],
        [shape((rows, depth)), shape((rows, depth)), shape(pieces), shape(pieces)],
        scratch=[pltpu.VMEM((rows, inner), BF16)] * 2 + [pltpu.VMEM((2, depth, inner), F32)],
        wait=wait,
        grid=(rows // FEED,),
        compiler_params=params(),
        name="feed_own",
        cost_estimate=cost(32),
    )


def feed_kernel(own, me, third, cot, out_in, grad_in, *refs):
    parts, (out, grad, both) = refs[:4], refs[4:]

    @pl.when(pl.program_id(0) == 0)
    def _():
        fill(planes(both), parts, me[0], me[1] if own else 1 - me[1])

    _, _, result, pushed = feed_rows(third[...], cot[...], both[0], both[1])
    out[...] = out_in[...] + result
    grad[...] = grad_in[...] + pushed


def feed_last_kernel(me, third, cot, out_in, grad_in, *refs):
    mine, other, (out, grad, both) = refs[:4], refs[4:8], refs[8:]

    @pl.when(pl.program_id(0) == 0)
    def _():
        up, down = planes(both)
        fill_two([up], [down], mine, other, me)

    _, _, result, pushed = feed_rows(third[...], cot[...], both[0], both[1])
    out[...] = (out_in[...] + result).astype(BF16)
    grad[...] = grad_in[...] + pushed


def feed_call(kernel, name, us, prefix, dtype, third, cot, out, grad, arrays, wait, carry=()):
    rows, depth = third.shape
    tile = rows_of(FEED, depth)
    inner = arrays[0].shape[2]
    return launch(
        kernel,
        [*prefix, third, cot, out, grad, *arrays],
        [smem()] * len(prefix) + [tile] * 4 + [once(arrays[0].shape)] * len(arrays),
        [tile, tile],
        [shape((rows, depth), dtype), shape((rows, depth))],
        scratch=[pltpu.VMEM((2, inner, depth), BF16)],
        wait=wait,
        carry=carry,
        grid=(rows // FEED,),
        compiler_params=params(),
        name=name,
        cost_estimate=cost(us),
    )


def feed(own, me, *operands):
    return feed_call(partial(feed_kernel, own), "feed", 18, (me,), F32, *operands)


def feed_last(me, *operands):
    return feed_call(feed_last_kernel, "feed_last", 18, (me,), BF16, *operands)


def back_kernel(
    lengths, live, third_grad, cot, after_cross, after_self, cross_query, looked0, mixed0, logs,
    gain1, gain2, w_out, w_co, *refs,
):
    queries, refs = refs[:4], refs[4:]
    pairs, refs = refs[:4], refs[4:]
    up_grad, mixed_grad, pair_grad, row_grads, query_grads, sums, total, turned = refs
    step = pl.program_id(0)
    text = TEXT

    @pl.when(step == 0)
    def _():
        total[...] = jnp.zeros_like(total)
        row_grads[...] = jnp.zeros_like(row_grads)
        sums[...] = jnp.zeros_like(sums)
        for j in range(4):
            turned[j] = pairs[j][0].T

    pulled, gain_sum, shift_sum = norm_backward(third_grad[...], after_cross[...], gain2[...])
    sums[0:1, :] += gain_sum
    sums[1:2, :] += shift_sum
    upstream = cot[...].astype(F32) + pulled
    low = upstream.astype(BF16)
    row_grads[1] += dot(looked0[...], low, TN)
    looked_grad = dot(low, w_co[...], NT).astype(BF16)
    item, _ = item_at(lengths, step * BLK)
    t0 = pl.multiple_of(item * text, text)
    alive = live[pl.ds(t0, text), :] > 0.0
    second_grad = jnp.zeros(upstream.shape, F32)
    width = queries[0].shape[2]
    heads = range(width // HEAD)

    def scores(j):
        cols = slice(j * width, (j + 1) * width)
        rows = [masked(cross_query[:, cols], head_row(width, h, HEAD**-0.5)) for h in heads]
        grads = [masked(looked_grad[:, cols], head_row(width, h, 1.0)) for h in heads]
        keys = pairs[j][0, pl.ds(t0, text), :]
        values = pairs[j][1, pl.ds(t0, text), :]
        return rows, grads, [dot(keys, row, NT) for row in rows], [dot(values, g, NT) for g in grads]

    ahead = scores(0)
    for j in range(4):
        rows, grads, score_set, pushed_set = ahead
        if j < 3:
            ahead = scores(j + 1)
        pieces, chances, score_grads = [], [], []
        for head in heads:
            index = j * (width // HEAD) + head
            score = jnp.where(alive, score_set[head], NEG)
            chance = jnp.exp(score - logs[index : index + 1, :])
            weighted = chance * pushed_set[head]
            mean = jnp.sum(weighted, axis=0, keepdims=True)
            score_grads.append((weighted - chance * mean).astype(BF16))
            chances.append(chance.astype(BF16))
            pieces.append(dot(turned[j, lanes_of(head), pl.ds(t0, text)], score_grads[head]))
        total[j, 0, pl.ds(t0, text), :] += dot(
            jnp.concatenate(score_grads, axis=1), jnp.concatenate(rows, axis=0)
        )
        total[j, 1, pl.ds(t0, text), :] += dot(
            jnp.concatenate(chances, axis=1), jnp.concatenate(grads, axis=0)
        )
        query_grad = (jnp.concatenate(pieces, axis=0).T * HEAD**-0.5).astype(BF16)
        if j == 0:
            query_grads[...] = query_grad
        second_grad = second_grad + dot(query_grad, queries[j][0], NT)

    pulled, gain_sum, shift_sum = norm_backward(second_grad, after_self[...], gain1[...])
    sums[2:3, :] += gain_sum
    sums[3:4, :] += shift_sum
    upstream = upstream + pulled
    up_grad[...] = upstream
    low = upstream.astype(BF16)
    row_grads[0] += dot(mixed0[...], low, TN)
    mixed_grad[...] = dot(low, w_out[...], NT).astype(BF16)

    @pl.when(step == pl.num_programs(0) - 1)
    def _():
        pair_grad[...] = total[...].astype(BF16)


def back(
    lengths, live, third_grad, cot, after_cross, after_self, cross_query, looked, mixed0, logs,
    gain1, gain2, w_out, w_co, crosses, pairs, wait,
):
    rows, depth = cot.shape
    text_rows = live.shape[0]
    width = mixed0.shape[1]
    inner = 4 * width
    tile = rows_of(BLK, depth)
    row = whole((1, depth))
    return launch(
        back_kernel,
        [lengths, live, third_grad, cot, after_cross, after_self, cross_query, looked, mixed0]
        + [logs, gain1, gain2, w_out, w_co, *crosses, *pairs],
        [smem(), whole((text_rows, 1))]
        + [tile] * 4
        + [rows_of(BLK, inner), rows_of(BLK, width), rows_of(BLK, width)]
        + [pl.BlockSpec((inner // HEAD, BLK), lambda i: (0, i)), row, row]
        + [whole((inner, depth))] * 2
        + [at((1, depth, width), (0, 0, 0))] * 4
        + [whole((2, text_rows, width))] * 4,
        [tile, rows_of(BLK, inner), whole((4, 2, text_rows, width))]
        + [whole((2, width, depth)), rows_of(BLK, width), whole((8, depth))],
        [
            shape((rows, depth)),
            shape((rows, inner), BF16),
            shape((4, 2, text_rows, width), BF16),
            shape((2, width, depth)),
            shape((rows, width), BF16),
            shape((8, depth)),
        ],
        scratch=[
            pltpu.VMEM((4, 2, text_rows, width), F32),
            pltpu.VMEM((4, width, text_rows), BF16),
        ],
        wait=wait,
        grid=(rows // BLK,),
        compiler_params=params(),
        name="back",
        cost_estimate=cost(53),
    )


def text_kernel(me, text, pair_grad, second, query_grad, row_grads, *refs):
    crosses, (text_grad, keep, send, cross_grad, folded) = refs[:4], refs[4:]
    total = jnp.zeros(text_grad.shape, F32)
    for j in range(4):
        for m in range(2):
            total = total + dot(pair_grad[j, m], crosses[j][m + 1], NT)
    text_grad[...] = total
    cross_grad[0] = dot(second[...], query_grad[...], TN)
    for m in range(2):
        cross_grad[m + 1] = dot(text[...], pair_grad[0, m], TN)
    put_pieces(cross_grad, keep, send, me)
    width = folded.shape[2]
    rows = row_grads.shape[1] // 8
    for k in range(2):
        for piece in range(8):
            for part in range(4):
                folded[k, pl.ds((piece * 4 + part) * rows, rows), :] = row_grads[
                    k, pl.ds(piece * rows, rows), part * width : (part + 1) * width
                ]
    put_pieces(folded, keep, send, me, 3)


def unfold(piece):
    rows, width = piece.shape
    parts = [piece[k * rows // 4 : (k + 1) * rows // 4] for k in range(4)]
    return jnp.concatenate(parts, axis=1)


def text_back(me, text, pair_grad, second, query_grad, row_grads, crosses, wait):
    text_rows, depth = text.shape
    width = pair_grad.shape[3]
    pieces = (4, 5, depth // 8, width)
    return launch(
        text_kernel,
        [me, text, pair_grad, second, query_grad, row_grads, *crosses],
        [smem()] + [vmem()] * 9,
        [vmem()] * 3,
        [shape((text_rows, depth)), shape(pieces), shape(pieces)],
        scratch=[pltpu.VMEM((3, depth, width), F32), pltpu.VMEM((2, depth, width), F32)],
        wait=wait,
        compiler_params=params(),
        name="text_back",
        cost_estimate=cost(15),
    )


def self_back_pair(qb, kb, diag, qkv, rows, grads, logs, means, turned, query_sum, key_sum, value_sum):
    q0 = pl.multiple_of(qb * BLK, BLK)
    k0 = pl.multiple_of(kb * BLK, BLK)
    keys = qkv[1, pl.ds(k0, BLK), :]
    values = qkv[2, pl.ds(k0, BLK), :]
    more_keys = 0.0
    more_values = 0.0
    heads = range(rows.shape[0])
    stages = [(dot(keys, rows[h], NT), dot(values, grads[h], NT)) for h in heads]
    for head, (score, pushed) in zip(heads, stages):
        if diag:
            score = jnp.where(causal(), score, NEG)
        chance = jnp.exp(score - logs[head : head + 1, pl.ds(q0, BLK)])
        score_grad = (chance * (pushed - means[head : head + 1, :])).astype(BF16)
        query_sum[lanes_of(head), :] += dot(turned[lanes_of(head), pl.ds(k0, BLK)], score_grad)
        more_keys = more_keys + dot(score_grad, rows[head])
        more_values = more_values + dot(chance.astype(BF16), grads[head])
    key_sum[pl.ds(k0, BLK), :] += more_keys
    value_sum[pl.ds(k0, BLK), :] += more_values


def self_back_body(
    lengths, qkv, mixed, out_grad, logs, weights, triple, turned, rows, grads, means, query_sum,
    key_sum, value_sum,
):
    row_count, width = mixed.shape
    turned[...] = qkv[1].T
    key_sum[...] = jnp.zeros_like(key_sum)
    value_sum[...] = jnp.zeros_like(value_sum)

    @pl.loop(0, row_count // BLK)
    def _(qb):
        q0 = pl.multiple_of(qb * BLK, BLK)
        _, start = item_at(lengths, q0)
        query = qkv[0, pl.ds(q0, BLK), :]
        grad = out_grad[pl.ds(q0, BLK), :]
        flat = (grad.astype(F32) * mixed[pl.ds(q0, BLK), :].astype(F32)).T
        for head in range(width // HEAD):
            rows[head] = masked(query, head_row(width, head, HEAD**-0.5))
            grads[head] = masked(grad, head_row(width, head, 1.0))
            means[head : head + 1, :] = jnp.sum(flat[lanes_of(head), :], axis=0, keepdims=True)
        query_sum[...] = jnp.zeros_like(query_sum)
        rest = (qkv, rows, grads, logs, means, turned, query_sum, key_sum, value_sum)

        @pl.loop(start // BLK, qb)
        def _(kb):
            self_back_pair(qb, kb, False, *rest)

        self_back_pair(qb, qb, True, *rest)
        triple[0, pl.ds(q0, BLK), :] = (query_sum[...].T * HEAD**-0.5).astype(BF16)

    triple[1] = key_sum[...].astype(BF16)
    triple[2] = value_sum[...].astype(BF16)


def self_scratch(rows, width):
    heads = width // HEAD
    return [
        pltpu.VMEM((3, rows, width), BF16),
        pltpu.VMEM((width, rows), BF16),
        pltpu.VMEM((heads, BLK, width), BF16),
        pltpu.VMEM((heads, BLK, width), BF16),
        pltpu.VMEM((8, BLK), F32),
        pltpu.VMEM((width, BLK), F32),
        pltpu.VMEM((rows, width), F32),
        pltpu.VMEM((rows, width), F32),
    ]


def self_own_kernel(me, lengths, qkv, mixed, out_grad, logs, weights, first, total, keep, send, *scratch):
    self_back_body(lengths, qkv, mixed, out_grad, logs, weights, *scratch[:-1])
    triple, qkv_grad = scratch[0], scratch[-1]
    for m in range(3):
        qkv_grad[m] = dot(first[...], triple[m], TN)
    put_pieces(qkv_grad, keep, send, me)
    total[...] = sum(dot(triple[m], weights[m], NT) for m in range(3))


def self_call(kernel, name, us, j, outs, operands, wait, prefix=(), scratch=()):
    lengths, qkv, mixed, out_grad, logs, weights, last_in = operands
    rows, width = mixed.shape
    return launch(
        kernel,
        [*prefix, *operands],
        [smem()] * (len(prefix) + 1)
        + [whole(qkv.shape), whole(mixed.shape), at((rows, width), (0, j))]
        + [whole(logs.shape), whole(weights.shape), whole(last_in.shape)],
        [whole(out.shape) for out in outs],
        outs,
        scratch=self_scratch(rows, width) + list(scratch),
        wait=wait,
        grid=(1,),
        compiler_params=params(),
        name=name,
        cost_estimate=cost(us),
    )


def self_own(me, lengths, qkv, mixed, out_grad, logs, weights, first, wait):
    _, depth, width = weights.shape
    pieces = shape((4, 3, depth // 8, width))
    operands = (lengths, qkv, mixed, out_grad, logs, weights, first)
    scratch = [pltpu.VMEM(weights.shape, F32)]
    outs = [shape(first.shape), pieces, pieces]
    return self_call(self_own_kernel, "self_own", 22, 0, outs, operands, wait, (me,), scratch)


def self_kernel(lengths, qkv, mixed, out_grad, logs, weights, before, total, *scratch):
    self_back_body(lengths, qkv, mixed, out_grad, logs, weights, *scratch)
    triple = scratch[0]
    total[...] = before[...] + sum(dot(triple[m], weights[m], NT) for m in range(3))


def self_back(lengths, qkv, mixed, out_grad, logs, weights, before, j, wait):
    operands = (lengths, qkv, mixed, out_grad, logs, weights, before)
    return self_call(self_kernel, "self_back", 26, j, [shape(before.shape)], operands, wait)[0]


def self_rest_kernel(places, lengths, *refs):
    count = len(places)
    sets, refs = [refs[4 * k : 4 * k + 4] for k in range(count)], refs[4 * count :]
    out_grad, before, tokens, upstream, gain, token_grad, sums, *refs = refs
    held, (total, token_rows, up_rows, sems, out_sems, *scratch) = refs[:5], refs[5:]
    rows, width = held[1].shape[1:]
    waits = []
    for k, (arrays, place) in enumerate(zip(sets, places)):
        sources = [*arrays, out_grad.at[:, pl.ds(place * width, width)]]
        waits.append(
            [
                pltpu.make_async_copy(source, target.at[k], sems.at[k, m])
                for m, (source, target) in enumerate(zip(sources, held))
            ]
        )
    ends = [
        pltpu.make_async_copy(source, target, sems.at[count, m])
        for m, (source, target) in enumerate(
            ((before, total), (tokens, token_rows), (upstream, up_rows))
        )
    ]
    for copy in waits[0] + ends[:1] + sum(waits[1:], []) + ends[1:]:
        copy.start()
    triple = scratch[0]
    for k in range(count):
        for copy in waits[k]:
            copy.wait()
        qkv, mixed, logs, weights, grads = (ref.at[k] for ref in held)
        self_back_body(lengths, qkv, mixed, grads, logs, weights, *scratch)
        if k == 0:
            ends[0].wait()
        total[...] += sum(dot(triple[m], weights[m], NT) for m in range(3))
    ends[1].wait()
    ends[2].wait()
    sums[...] = jnp.zeros_like(sums)
    outs = []
    for k in range(rows // BLK):
        part = slice(k * BLK, (k + 1) * BLK)
        pulled, gain_sum, shift_sum = norm_backward(
            total[part, :], token_rows[part, :].astype(F32), gain[...]
        )
        sums[0:1, :] += gain_sum
        sums[1:2, :] += shift_sum
        up_rows[part, :] = up_rows[part, :] + pulled
        outs.append(
            pltpu.make_async_copy(
                up_rows.at[pl.ds(k * BLK, BLK)], token_grad.at[pl.ds(k * BLK, BLK)], out_sems.at[k]
            )
        )
        outs[-1].start()
    for copy in outs:
        copy.wait()


def self_rest(places, lengths, sets, out_grad, before, tokens, upstream, gain, wait):
    rows, depth = tokens.shape
    count = len(places)
    width = sets[0][1].shape[1]
    args = [lengths, *sum(sets, []), out_grad, before, tokens, upstream, gain]
    held = [
        pltpu.VMEM((count,) + array.shape, array.dtype) for array in sets[0] + [sets[0][1]]
    ]
    return launch(
        partial(self_rest_kernel, places),
        args,
        [smem()] + [anywhere()] * (len(args) - 2) + [vmem()],
        [anywhere(), vmem()],
        [shape((rows, depth)), shape((8, depth))],
        scratch=held
        + [pltpu.VMEM((rows, depth), dtype) for dtype in (F32, BF16, F32)]
        + [pltpu.SemaphoreType.DMA((count + 1, 5)), pltpu.SemaphoreType.DMA((rows // BLK,))]
        + self_scratch(rows, width),
        wait=wait,
        compiler_params=params(),
        name="self_rest",
        cost_estimate=cost(40),
    )


DP = 8
MP = 4


def ring(step):
    pairs = []
    for i in range(DP):
        for z in range(MP):
            to = (z + (step if i % 2 == 0 else -step)) % MP
            pairs.append((i * MP + z, i * MP + to))
    return pairs


def straight(step):
    return [(z, (z + step) % MP) for z in range(MP)]


def beside(first):
    return [(i, i ^ (2 if (i % 2 == 0) == first else 4)) for i in range(DP)]


def swap(value):
    return lax.ppermute(value, "dp", [(i, i ^ 1) for i in range(DP)])


def fold(piece):
    width = piece.shape[1] // 4
    return jnp.concatenate([piece[:, k * width : (k + 1) * width] for k in range(4)], axis=0)


def fold_whole(shard):
    return jnp.concatenate([fold(piece) for piece in jnp.split(shard, 4)], axis=0)


def cut(shard, chip):
    rows = shard.shape[1] // 4
    return lax.dynamic_slice_in_dim(shard, chip * rows, rows, 1).astype(F32)


def near_of(piece):
    return lax.ppermute(piece, "dp", beside(True))


def side_of(piece):
    return lax.ppermute(piece, "dp", beside(False))


def along(value, step):
    return lax.ppermute(value, "mp", straight(step))


def around(value):
    return lax.ppermute(value, ("dp", "mp"), ring(1))


def in_order(keep, send):
    pieces = [part[k] for k, m in ((0, 0), (2, 1), (1, 2), (3, 3)) for part, k in ((keep, k), (send, m))]
    return jnp.concatenate(pieces, axis=1)


def scattered(value, axis):
    return lax.psum_scatter(value, "dp", scatter_dimension=axis, tiled=True)


def pieces_of(mine, other):
    mine, other = jnp.split(mine, 4, axis=1), jnp.split(other, 4, axis=1)
    return mine + [other[k] for k in (0, 2, 1, 3)]


def sum_near(keep, sent):
    return lax.ppermute(keep[2:] + sent[2:], "dp", beside(True))


def sum_side(keep, sent, near):
    return side_of(keep[1] + sent[1] + near[1])


def sum_last(keep, sent, near, side):
    return keep[0] + sent[0] + near[0] + side


def plane_sum(value):
    chips = [lax.ppermute(value, "dp", [(i, i ^ bit) for i in range(DP)]) for bit in (2, 4, 6)]
    value = value + chips[0] + (chips[1] + chips[2])
    return value + swap(value)


def local(
    planar, tokens, text_states, lengths, text_mask, ln_gain, ln_shift, w_qkv, w_out, w_cross_q,
    w_cross_kv, w_cross_out, w_up, w_down, cotangent,
):
    slot_count, text_length = text_mask.shape
    place = lax.axis_index("dp") if planar else jnp.int32(0)
    chip, core = place // 2, place % 2
    me = jnp.stack([chip, core]).astype(jnp.int32)
    gains = [ln_gain[n : n + 1] for n in range(3)]
    shifts = [ln_shift[n : n + 1] for n in range(3)]
    text = text_states.reshape(slot_count * text_length, text_states.shape[2])
    position = lax.broadcasted_iota(jnp.int32, text_mask.shape, 1)
    live = ((text_mask == 1) | (position == 0)).astype(F32).reshape(-1, 1)
    own_qkv = jnp.transpose(w_qkv, (1, 0, 2))
    own_cross = jnp.concatenate([w_cross_q[None], jnp.transpose(w_cross_kv, (1, 0, 2))], axis=0)
    feeds = jnp.stack([w_up, w_down])
    qkvs, mixeds, logs, weights = ([None] * 4 for _ in range(4))
    weights[0] = own_qkv

    def shards(value):
        return along(value.astype(F32), 1), along(value.astype(F32), 3)

    wait, carry = [], []
    first = None if planar else norm_first(tokens, gains[0], shifts[0], [])
    if planar:
        rows = w_out.shape[0] // 4
        outer = [
            fold(lax.dynamic_slice_in_dim(value, chip * rows, rows, 0))[None].astype(F32)
            for value in (w_out, w_cross_out)
        ]
        qkv_one = around(cut(own_qkv, chip))
        own_piece = gate([qkv_one], jnp.concatenate([cut(own_cross, chip), *outer], axis=0))
        cross_one = around(own_piece)
        first = norm_first(tokens, gains[0], shifts[0], [own_piece])
        qkv_near, qkv_side = near_of(qkv_one), gate([first], side_of(qkv_one))
        wait = [qkv_one, cross_one]
    qkvs[0], mixeds[0], logs[0] = front_own(lengths, first, own_qkv, wait, [])
    if planar:
        mine = join(me, [qkv_one, qkv_near, qkv_side, near_of(qkv_side)], [logs[0]])
        g_qkv = mine, swap(mine)
        cross_near, cross_side = near_of(cross_one), side_of(cross_one)
        two = jnp.where(
            core == 0,
            jnp.concatenate([qkv_one, cross_one[3:4]], axis=0),
            jnp.concatenate([cross_one[:3], cross_one[4:5]], axis=0),
        )
        two = around(two)
        wait = [cross_near, cross_side]
        carry = [cut(feeds, chip)]
    else:
        folded = [fold_whole(value)[None] for value in (w_out, w_cross_out)]
        g_qkv = shards(own_qkv)
        g_cross = shards(jnp.concatenate([own_cross, *folded], axis=0))
        g_two = [
            along(jnp.concatenate(parts, axis=0).astype(F32), 2)
            for parts in ((own_qkv, folded[0]), (own_cross, folded[1]))
        ]
        g_feed = pieces_of(*shards(feeds))
        g_last = pieces_of(*[along(feeds[k : k + 1].astype(F32), 2) for k in range(2)])
    weights[1], qkvs[1], mixeds[1], logs[1], *carried = front(
        lengths, first, g_qkv[0], wait, carry
    )
    if planar:
        two = gate([logs[1]], two)
        cross_far = near_of(cross_side)
        two_near, two_side = near_of(two), side_of(two)
        feed_one = around(carried[0])
        wait = [two, cross_near, cross_side, logs[1]]
    weights[3], qkvs[3], mixeds[3], logs[3] = front(lengths, first, g_qkv[1], wait, [])
    if planar:
        mine = join(me, [cross_one, cross_near, cross_side, cross_far], [logs[3], feed_one, two_near, two_side])
        g_cross = mine, swap(mine)
        two_far = near_of(two_side)
        feed_near, feed_side = near_of(feed_one), side_of(feed_one)
        feed_two = around(lax.dynamic_slice_in_dim(feed_one, core, 1, 0))
        wait = [two_near, two_side]
    cross_a, cross_b, *pairs = text_front(text, own_cross, g_cross, wait)
    if planar:
        mine = join(me, [two, two_near, two_side, two_far], [cross_a])
        g_two = mine, swap(mine)
        wait = []
    weights[2], cross_two, qkvs[2], mixeds[2], logs[2], pair_two = front_two(
        me, lengths, first, g_two, text, wait
    )
    pairs = [pairs[0], pairs[1], pair_two, pairs[2]]
    crosses = [own_cross, cross_a, cross_two, cross_b]
    if planar:
        wait = [feed_one, feed_two]
    full_out, full_co, after_self, after_cross, second, third, cross_query, looked, cross_logs = middle(
        me, lengths, live, tokens, (gains[1], shifts[1], gains[2], shifts[2]), w_out, w_cross_out,
        mixeds, crosses, pairs, g_cross, g_two, wait,
    )
    if planar:
        feed_side, feed_two = gate([third], feed_side), gate([third], feed_two)
        feed_far = near_of(feed_side)
        last_near, last_side = near_of(feed_two), side_of(feed_two)
        wait = [feed_near, feed_side, feed_two]
    out, grad, both_keep, both_send = feed_own(
        me, third, cotangent, after_cross, w_up, w_down, wait
    )
    wait, carry = [], [both_send]
    if planar:
        g_feed = [feed_one, feed_near, feed_side, gate([out], feed_far)]
        g_feed = g_feed + [swap(value) for value in g_feed]
        wait = g_feed[4:7]
    out, grad = feed(True, me, third, cotangent, out, grad, g_feed[:4], wait)
    if planar:
        last_far = near_of(gate([out], last_side))
    out, grad = feed(False, me, third, cotangent, out, grad, g_feed[4:], [])
    if planar:
        g_last = [feed_two, last_near, last_side, gate([out], last_far)]
        g_last = g_last + [swap(value) for value in g_last]
    out, grad, both_send = feed_last(
        me, third, cotangent, out, grad, g_last, [], [both_send]
    )
    if planar:
        both_swap = swap(both_send)
    upstream, mixed_grad, pair_grad, row_grads, query_grad, sums = back(
        lengths, live, grad, cotangent, after_cross, after_self, cross_query, looked, mixeds[0],
        cross_logs, gains[1], gains[2], full_out, full_co, crosses, pairs,
        [],
    )
    wait = []
    if planar:
        both_swap = gate([sums], both_swap)
        both_near = sum_near(both_keep, both_swap)
    text_grad, keep, send = text_back(
        me, text, pair_grad, second, query_grad, row_grads, crosses, wait
    )
    if planar:
        late_swap = swap(send)
        wait = []
    first_grad, qkv_keep, qkv_send = self_own(
        me, lengths, qkvs[0], mixeds[0], mixed_grad, logs[0], weights[0], first, wait
    )
    if planar:
        both_near = gate([first_grad], both_near)
        both_side = sum_side(both_keep, both_swap, both_near)
        late_near = sum_near(keep, late_swap)
        qkv_swap = swap(qkv_send)
        wait = [late_swap, both_near]
    first_grad = self_back(
        lengths, qkvs[1], mixeds[1], mixed_grad, logs[1], weights[1], first_grad, 1, wait
    )
    if planar:
        late_near, qkv_swap = gate([first_grad], late_near), gate([first_grad], qkv_swap)
        late_side = sum_side(keep, late_swap, late_near)
        qkv_near = sum_near(qkv_keep, qkv_swap)
        wait = [late_near, qkv_swap]
    token_grad, last_sums = self_rest(
        (2, 3), lengths, [[qkvs[j], mixeds[j], logs[j], weights[j]] for j in (2, 3)],
        mixed_grad, first_grad, tokens, upstream, gains[0], wait,
    )
    if planar:
        qkv_near = gate([last_sums], qkv_near)
        late_side = gate([last_sums], late_side)
        both_side = gate([last_sums], both_side)
        last_sums = gate([late_side, both_side, qkv_near], last_sums)
        qkv_side = sum_side(qkv_keep, qkv_swap, qkv_near)
    norm_sums = jnp.concatenate(
        [last_sums[0:1], sums[2:3], sums[0:1], last_sums[1:2], sums[3:4], sums[1:2]], axis=0
    )
    if planar:
        both_sum = sum_last(both_keep, both_swap, both_near, both_side)
        late_sum = sum_last(keep, late_swap, late_near, late_side)
        qkv_sum = sum_last(qkv_keep, qkv_swap, qkv_near, qkv_side)
        row_sum = [unfold(late_sum[k]) for k in (3, 4)]
        width = norm_sums.shape[1] // DP
        norm_sum = lax.dynamic_slice_in_dim(plane_sum(norm_sums), place * width, width, 1)
    else:
        both_sum = scattered(in_order(both_keep, both_send), 1)
        late = in_order(keep, send)
        late_sum = scattered(late[:3], 1)
        qkv_sum = scattered(in_order(qkv_keep, qkv_send), 1)
        row_sum = [
            scattered(jnp.concatenate([unfold(part) for part in jnp.split(late[k], 8)]), 0)
            for k in (3, 4)
        ]
        norm_sum = scattered(norm_sums, 1)
    return (
        out,
        token_grad,
        text_grad.reshape(text_states.shape),
        norm_sum[:3],
        norm_sum[3:],
        jnp.transpose(qkv_sum, (1, 0, 2)),
        row_sum[0],
        late_sum[0],
        jnp.transpose(late_sum[1:3], (1, 0, 2)),
        row_sum[1],
        both_sum[0],
        both_sum[1],
    )


def solution(mesh):
    placed = (
        P("dp", None),
        P("dp", None, None),
        P("dp"),
        P("dp", None),
        P(),
        P(),
        P(None, None, "mp"),
        P("mp", None),
        P(None, "mp"),
        P(None, None, "mp"),
        P("mp", None),
        P(None, "mp"),
        P("mp", None),
        P("dp", None),
    )
    return jax.shard_map(
        partial(local, mesh.shape["dp"] == DP),
        mesh=mesh,
        in_specs=placed,
        out_specs=(
            P("dp", None),
            P("dp", None),
            P("dp", None, None),
            P(None, "dp"),
            P(None, "dp"),
            P("dp", None, "mp"),
            P(("mp", "dp"), None),
            P("dp", "mp"),
            P("dp", None, "mp"),
            P(("mp", "dp"), None),
            P("dp", "mp"),
            P(("mp", "dp"), None),
        ),
        check_vma=False,
    )
```

```python
from functools import partial

import jax
import jax.numpy as jnp
from jax import lax
from jax.experimental import pallas as pl
from jax.experimental.pallas import tpu as pltpu
from jax.sharding import PartitionSpec as P

HEAD = 64
BLK = 256
EPS = 1e-05
NEG = -1e30
F32 = jnp.float32
BF16 = jnp.bfloat16
MIB = 1024 * 1024

NN = (((1,), (0,)), ((), ()))
NT = (((1,), (1,)), ((), ()))
TN = (((0,), (0,)), ((), ()))


def dot(a, b, dims=NN):
    return lax.dot_general(a, b, dims, preferred_element_type=F32)


def params(mib=56, semantics=None):
    return pltpu.CompilerParams(vmem_limit_bytes=mib * MIB, dimension_semantics=semantics)


def cost(us):
    return pl.CostEstimate(
        flops=int(us * 4.6e8), transcendentals=0, bytes_accessed=int(us * 1.4e6)
    )


def shape(dims, dtype=F32):
    return jax.ShapeDtypeStruct(dims, dtype)


def smem():
    return pl.BlockSpec(memory_space=pltpu.SMEM)


def whole(dims):
    rank = len(dims)
    return pl.BlockSpec(dims, lambda *_: (0,) * rank)


def at(dims, index):
    return pl.BlockSpec(dims, lambda *_: index)


def once(dims):
    rank = len(dims)
    return pl.BlockSpec(dims, lambda *_: (0,) * rank, pipeline_mode=pl.Buffered(1))


def anywhere():
    return pl.BlockSpec(memory_space=pl.ANY)


def launch(kernel, args, in_specs, out_specs, out_shape, scratch=(), wait=(), carry=(), **options):
    args, wait, carry = list(args), list(wait), list(carry)
    count, extra, outs = len(args), len(wait) + len(carry), len(out_shape)

    def body(*refs):
        results = refs[count + extra : count + extra + outs]
        kernel(*refs[:count], *results, *refs[count + extra + outs + len(carry) :])

    return pl.pallas_call(
        body,
        in_specs=list(in_specs) + [anywhere()] * extra,
        out_specs=list(out_specs) + [anywhere()] * len(carry),
        out_shape=list(out_shape) + [shape(value.shape, value.dtype) for value in carry],
        scratch_shapes=list(scratch),
        input_output_aliases={count + len(wait) + k: outs + k for k in range(len(carry))},
        **options,
    )(*args, *wait, *carry)


def gate(wait, carry):
    return launch(
        lambda: None, [], [], [], [], wait=wait, carry=[carry], name="gate", cost_estimate=cost(0.1)
    )[0]


def rows_of(tile, width):
    return pl.BlockSpec((tile, width), lambda i, *_: (i, 0))


def norm_stats(value):
    center = value - jnp.mean(value, axis=-1, keepdims=True)
    spread = jnp.mean(center * center, axis=-1, keepdims=True)
    inverse = lax.rsqrt(spread + EPS)
    return center * inverse, inverse


def norm_forward(value, gain, shift):
    unit, _ = norm_stats(value)
    return (unit * gain + shift).astype(BF16)


def norm_backward(incoming, value, gain):
    unit, inverse = norm_stats(value)
    scaled = incoming * gain
    pushed = incoming * unit
    inner = (
        scaled
        - jnp.mean(scaled, axis=-1, keepdims=True)
        - unit * jnp.mean(scaled * unit, axis=-1, keepdims=True)
    )
    return (
        inner * inverse,
        jnp.sum(pushed, axis=0, keepdims=True),
        jnp.sum(incoming, axis=0, keepdims=True),
    )


def norm_kernel(tokens_ref, gain_ref, shift_ref, first_ref):
    first_ref[...] = norm_forward(tokens_ref[...].astype(F32), gain_ref[...], shift_ref[...])


def norm_first(tokens, gain, shift, wait):
    rows, width = tokens.shape
    return launch(
        norm_kernel,
        [tokens, gain, shift],
        [rows_of(BLK, width), whole((1, width)), whole((1, width))],
        [rows_of(BLK, width)],
        [shape((rows, width), BF16)],
        wait=wait,
        grid=(rows // BLK,),
        name="norm_first",
        cost_estimate=cost(6),
    )[0]


def head_row(width, head, value):
    lane = lax.broadcasted_iota(jnp.int32, (1, width), 1)
    return jnp.where(lane // HEAD == head, value, 0.0)


def masked(block, row):
    return (block.astype(F32) * row).astype(BF16)


def item_at(lengths, place):
    item, start, end = 0, 0, 0
    for slot in range(lengths.shape[0]):
        end = end + lengths[slot]
        past = end <= place
        item = item + past.astype(jnp.int32)
        start = jnp.where(past, end, start)
    return item, start


def offsets(core):
    return (0, 1 + core, 2 - core, 3)


def join_kernel(me, *refs):
    parts, (target, sems) = refs[:4], refs[4:]
    copies = []
    for index, (part, offset) in enumerate(zip(parts, offsets(me[1]))):
        rows = part.shape[1]
        place = pl.multiple_of((me[0] ^ offset) * rows, rows)
        for k in range(part.shape[0]):
            copies.append(
                pltpu.make_async_copy(
                    part.at[k], target.at[k, pl.ds(place, rows)], sems.at[index, k]
                )
            )
    for copy in copies:
        copy.start()
    for copy in copies:
        copy.wait()


def join(me, parts, wait):
    count, rows, width = parts[0].shape
    return launch(
        join_kernel,
        [me, *parts],
        [smem()] + [anywhere()] * 4,
        [vmem()],
        [shape((count, 4 * rows, width))],
        scratch=[pltpu.SemaphoreType.DMA((4, count))],
        wait=wait,
        compiler_params=params(24),
        name="join",
        cost_estimate=cost(0.1),
    )[0]


def take(targets, source):
    for k, target in enumerate(targets):
        target[...] = source[k].astype(BF16)


def take_two(first, second, mine, other, core):
    @pl.when(core == 0)
    def _():
        take(first, mine)
        take(second, other)

    @pl.when(core == 1)
    def _():
        take(second, mine)
        take(first, other)


def fill(targets, parts, chip, core):
    for part, offset in zip(parts, offsets(core)):
        rows = part.shape[1]
        place = pl.multiple_of((chip ^ offset) * rows, rows)
        for k, target in enumerate(targets):
            target[pl.ds(place, rows), :] = part[k].astype(BF16)


def fill_two(first, second, mine, other, me):
    chip, core = me[0], me[1]

    @pl.when(core == 0)
    def _():
        fill(first, mine, chip, 0)
        fill(second, other, chip, 1)

    @pl.when(core == 1)
    def _():
        fill(second, mine, chip, 1)
        fill(first, other, chip, 0)


def planes(ref):
    return [ref.at[k] for k in range(ref.shape[0])]


def causal():
    shape2 = (BLK, BLK)
    return lax.broadcasted_iota(jnp.int32, shape2, 0) <= lax.broadcasted_iota(
        jnp.int32, shape2, 1
    )


def lanes_of(head):
    return slice(head * HEAD, (head + 1) * HEAD)


def self_block(qb, count, qkv, turned, mixed, logs):
    q0 = pl.multiple_of(qb * BLK, BLK)
    k0 = pl.multiple_of((qb - (count - 1)) * BLK, BLK)
    width = qkv.shape[2]
    query = qkv[0, pl.ds(q0, BLK), :]
    diag = qkv[1, pl.ds(q0, BLK), :]
    pre_len = (count - 1) * BLK
    keep = causal()
    pieces = []
    heads = range(width // HEAD)
    parts = [masked(query, head_row(width, head, HEAD**-0.5)) for head in heads]
    nears = [dot(diag, part, NT) for part in parts]
    fars = [dot(qkv[1, pl.ds(k0, pre_len), :], part, NT) for part in parts] if pre_len else []
    for head in heads:
        near = jnp.where(keep, nears[head], NEG)
        peak = jnp.max(near, axis=0, keepdims=True)
        if pre_len:
            far = fars[head]
            peak = jnp.maximum(peak, jnp.max(far, axis=0, keepdims=True))
        near = jnp.exp(near - peak)
        total = jnp.sum(near, axis=0, keepdims=True)
        result = dot(turned[lanes_of(head), pl.ds(q0, BLK)], near.astype(BF16))
        if pre_len:
            far = jnp.exp(far - peak)
            total = total + jnp.sum(far, axis=0, keepdims=True)
            result = result + dot(
                turned[lanes_of(head), pl.ds(k0, pre_len)], far.astype(BF16)
            )
        pieces.append(result * (1.0 / total))
        logs[head : head + 1, pl.ds(q0, BLK)] = peak + jnp.log(total)
    mixed[pl.ds(q0, BLK), :] = jnp.concatenate(pieces, axis=0).T.astype(BF16)


def front_body(lengths, first, weights, qkv, mixed, logs, turned):
    rows = first.shape[0]
    for m in range(3):
        qkv[m] = dot(first[...], weights[m]).astype(BF16)
    turned[...] = qkv[2].T

    @pl.loop(0, rows // BLK)
    def _(qb):
        _, start = item_at(lengths, qb * BLK)
        count = qb - start // BLK + 1
        for n in range(1, 5):

            @pl.when(count == n)
            def _():
                self_block(qb, n, qkv, turned, mixed, logs)


def front_kernel(lengths, first, shard, weights, *rest):
    take(planes(weights), shard)
    front_body(lengths, first, weights, *rest)


def front_two_kernel(me, lengths, first, mine, other, text, weights, cross, qkv, mixed, logs, pair, turned):
    take_two(planes(weights), planes(cross), mine, other, me[1])
    text_pair(pair, text, cross)
    front_body(lengths, first, weights, qkv, mixed, logs, turned)


def vmem():
    return pl.BlockSpec(memory_space=pltpu.VMEM)


def front_call(kernel, name, us, prefix, first, arrays, weight_count, more, wait, carry=()):
    rows, depth = first.shape
    width = arrays[0].shape[2]
    outs = [shape((3, depth, width), BF16)] * weight_count + [
        shape((3, rows, width), BF16),
        shape((rows, width), BF16),
        shape((8, rows), F32),
    ] + more
    return launch(
        kernel,
        [*prefix, first, *arrays],
        [smem()] * len(prefix) + [vmem()] * (1 + len(arrays)),
        [vmem()] * len(outs),
        outs,
        scratch=[pltpu.VMEM((width, rows), BF16)],
        wait=wait,
        carry=carry,
        compiler_params=params(),
        name=name,
        cost_estimate=cost(us),
    )


def front_own(lengths, first, weights, wait, carry):
    return front_call(front_body, "front_own", 15, (lengths,), first, [weights], 0, [], wait, carry)


def front(lengths, first, shard, wait, carry):
    return front_call(front_kernel, "front", 16, (lengths,), first, [shard], 1, [], wait, carry)


def front_two(me, lengths, first, arrays, text, wait):
    pair = shape((2, text.shape[0], arrays[0].shape[2]), BF16)
    return front_call(
        front_two_kernel, "front_two", 18, (me, lengths), first, [*arrays, text], 2, [pair], wait
    )


def text_pair(pair, text, cross):
    for m in range(2):
        pair[m] = dot(text[...], cross[m + 1]).astype(BF16)


def text_front_kernel(text, own, mine, other, cross_a, cross_b, *pairs):
    take(planes(cross_a), mine)
    take(planes(cross_b), other)
    for pair, cross in zip(pairs, (own, cross_a, cross_b)):
        text_pair(pair, text, cross)


def text_front(text, own, arrays, wait):
    rows = text.shape[0]
    width = own.shape[2]
    outs = [shape(own.shape, BF16)] * 2 + [shape((2, rows, width), BF16)] * 3
    return launch(
        text_front_kernel,
        [text, own, *arrays],
        [vmem()] * 4,
        [vmem()] * 5,
        outs,
        wait=wait,
        compiler_params=params(),
        name="text_front",
        cost_estimate=cost(7),
    )


def unfold_into(target, first, source):
    width = source.shape[2]
    rows = width // 4
    for piece in range(4):
        for part in range(4):
            target[pl.ds(first + piece * rows, rows), part * width : (part + 1) * width] = source[
                0, pl.ds(piece * width + part * rows, rows), :
            ].astype(BF16)


def middle_kernel(me, lengths, live, tokens, gain1, shift1, gain2, shift2, own_out, own_co, *refs):
    mixed, refs = refs[:4], refs[4:]
    queries, refs = refs[:4], refs[4:]
    pairs, refs = refs[:4], refs[4:]
    outs, cos, (out_two, co_two), refs = refs[:2], refs[2:4], refs[4:6], refs[6:]
    w_out, w_co, after_self, after_cross, second, third, cross_query, looked, logs, turned = refs
    step = pl.program_id(0)

    @pl.when(step == 0)
    def _():
        width = own_out.shape[0]
        w_out[:width, :] = own_out[...]
        w_co[:width, :] = own_co[...]
        for place, out_part, co_part in ((1, outs[0], cos[0]), (3, outs[1], cos[1])):
            unfold_into(w_out, place * width, out_part)
            unfold_into(w_co, place * width, co_part)

        @pl.when(me[1] == 0)
        def _():
            unfold_into(w_out, 2 * width, out_two)
            unfold_into(w_co, 2 * width, co_two)

        @pl.when(me[1] == 1)
        def _():
            unfold_into(w_co, 2 * width, out_two)
            unfold_into(w_out, 2 * width, co_two)

        for j in range(4):
            turned[j] = pairs[j][1].T

    part = jnp.concatenate([ref[...] for ref in mixed], axis=1)
    residual = tokens[...].astype(F32) + dot(part, w_out[...])
    after_self[...] = residual
    normed = norm_forward(residual, gain1[...], shift1[...])
    second[...] = normed
    text = TEXT
    item, _ = item_at(lengths, step * BLK)
    t0 = pl.multiple_of(item * text, text)
    alive = live[pl.ds(t0, text), :] > 0.0
    width = own_out.shape[0]
    heads = range(width // HEAD)
    stages = []
    for j in range(4):
        query = dot(normed, queries[j][0]).astype(BF16)
        cross_query[:, j * width : (j + 1) * width] = query
        rows = [masked(query, head_row(width, head, HEAD**-0.5)) for head in heads]
        keys = pairs[j][0, pl.ds(t0, text), :]
        stages.append([dot(keys, row, NT) for row in rows])
    for j in range(4):
        pieces = []
        for head in heads:
            score = jnp.where(alive, stages[j][head], NEG)
            peak = jnp.max(score, axis=0, keepdims=True)
            score = jnp.exp(score - peak)
            total = jnp.sum(score, axis=0, keepdims=True)
            result = dot(turned[j, lanes_of(head), pl.ds(t0, text)], score.astype(BF16))
            pieces.append(result * (1.0 / total))
            index = j * (width // HEAD) + head
            logs[index : index + 1, :] = peak + jnp.log(total)
        looked[:, j * width : (j + 1) * width] = jnp.concatenate(pieces, axis=0).T.astype(BF16)
    residual = residual + dot(looked[...], w_co[...])
    after_cross[...] = residual
    third[...] = norm_forward(residual, gain2[...], shift2[...])


TEXT = 128


def middle(me, lengths, live, tokens, norms, own_out, own_co, mixed, crosses, pairs, g_cross, g_two, wait):
    rows, depth = tokens.shape
    width = own_out.shape[0]
    text_rows = live.shape[0]
    inner = 4 * width
    row = whole((1, depth))

    def plane_at(k):
        dims = (1, depth, width)
        return pl.BlockSpec(dims, lambda *_: (k, 0, 0), pipeline_mode=pl.Buffered(1))

    return launch(
        middle_kernel,
        [me, lengths, live, tokens, *norms, own_out, own_co, *mixed, *crosses, *pairs]
        + [*g_cross, *g_cross, *g_two],
        [smem(), smem(), whole((text_rows, 1)), rows_of(BLK, depth)]
        + [row] * 4
        + [once((width, depth))] * 2
        + [rows_of(BLK, width)] * 4
        + [at((1, depth, width), (0, 0, 0))] * 4
        + [whole((2, text_rows, width))] * 4
        + [plane_at(k) for k in (3, 3, 4, 4, 3, 3)],
        [whole((inner, depth))] * 2
        + [rows_of(BLK, depth)] * 4
        + [rows_of(BLK, inner)] * 2
        + [pl.BlockSpec((inner // HEAD, BLK), lambda i: (0, i))],
        [shape((inner, depth), BF16)] * 2
        + [shape((rows, depth)), shape((rows, depth))]
        + [shape((rows, depth), BF16)] * 2
        + [shape((rows, inner), BF16)] * 2
        + [shape((inner // HEAD, rows))],
        scratch=[pltpu.VMEM((4, width, text_rows), BF16)],
        wait=wait,
        grid=(rows // BLK,),
        compiler_params=params(),
        name="middle",
        cost_estimate=cost(43),
    )


ROOT = 0.7978845608028654
CUBE = 0.044715


def gelu_both(value):
    square = value * value
    bend = jnp.tanh(value * (ROOT + (ROOT * CUBE) * square))
    half = 0.5 + 0.5 * bend
    slope = half + (0.5 * value) * (1.0 - bend * bend) * (ROOT + (3.0 * ROOT * CUBE) * square)
    return value * half, slope


def feed_rows(third, cot, up, down):
    return feed_finish(dot(third, up), dot(cot, down, NT), up, down)


def feed_finish(pre_act, hidden_grad, up, down):
    hidden, slope = gelu_both(pre_act)
    hidden = hidden.astype(BF16)
    pre_grad = (hidden_grad * slope).astype(BF16)
    return hidden, pre_grad, dot(hidden, down), dot(pre_grad, up, NT)


def feed_own_kernel(
    me, third, cot, after, up, down, out, grad, keep, send, hidden_rows, grad_rows, both
):
    step = pl.program_id(0)
    part = pl.ds(pl.multiple_of(step * FEED, FEED), FEED)
    hidden, pre_grad, result, pushed = feed_rows(third[part, :], cot[part, :], up[...], down[...])
    out[...] = after[...] + result
    grad[...] = pushed
    hidden_rows[part, :] = hidden
    grad_rows[part, :] = pre_grad

    @pl.when(step == pl.num_programs(0) - 1)
    def _():
        both[0] = dot(third[...], grad_rows[...], TN)
        both[1] = dot(hidden_rows[...], cot[...], TN)
        put_pieces(both, keep, send, me)


def put_pieces(source, keep, send, me, first=0):
    chip, core = me[0], me[1]
    rows = source.shape[1] // 8
    for target, owner in ((keep, core), (send, 1 - core)):
        for index, offset in enumerate((0, 2 - owner, 1 + owner, 3)):
            place = pl.multiple_of(((chip ^ offset) * 2 + owner) * rows, rows)
            for k in range(source.shape[0]):
                target[index, first + k] = source[k, pl.ds(place, rows), :]


FEED = 320


def feed_own(me, third, cot, after, up, down, wait):
    rows, depth = third.shape
    inner = up.shape[1]
    tile = rows_of(FEED, depth)
    pieces = (4, 2, depth // 8, depth)
    return launch(
        feed_own_kernel,
        [me, third, cot, after, up, down],
        [smem(), once(third.shape), once(cot.shape), tile]
        + [once((depth, inner)), once((inner, depth))],
        [tile, tile, once(pieces), once(pieces)],
        [shape((rows, depth)), shape((rows, depth)), shape(pieces), shape(pieces)],
        scratch=[pltpu.VMEM((rows, inner), BF16)] * 2 + [pltpu.VMEM((2, depth, inner), F32)],
        wait=wait,
        grid=(rows // FEED,),
        compiler_params=params(),
        name="feed_own",
        cost_estimate=cost(32),
    )


def feed_kernel(own, me, third, cot, out_in, grad_in, *refs):
    parts, (out, grad, both) = refs[:4], refs[4:]

    @pl.when(pl.program_id(0) == 0)
    def _():
        fill(planes(both), parts, me[0], me[1] if own else 1 - me[1])

    _, _, result, pushed = feed_rows(third[...], cot[...], both[0], both[1])
    out[...] = out_in[...] + result
    grad[...] = grad_in[...] + pushed


def feed_last_kernel(me, third, cot, out_in, grad_in, *refs):
    mine, other, (out, grad, both) = refs[:4], refs[4:8], refs[8:]

    @pl.when(pl.program_id(0) == 0)
    def _():
        up, down = planes(both)
        fill_two([up], [down], mine, other, me)

    _, _, result, pushed = feed_rows(third[...], cot[...], both[0], both[1])
    out[...] = (out_in[...] + result).astype(BF16)
    grad[...] = grad_in[...] + pushed


def feed_call(kernel, name, us, prefix, dtype, third, cot, out, grad, arrays, wait, carry=()):
    rows, depth = third.shape
    tile = rows_of(FEED, depth)
    inner = arrays[0].shape[2]
    return launch(
        kernel,
        [*prefix, third, cot, out, grad, *arrays],
        [smem()] * len(prefix) + [tile] * 4 + [once(arrays[0].shape)] * len(arrays),
        [tile, tile],
        [shape((rows, depth), dtype), shape((rows, depth))],
        scratch=[pltpu.VMEM((2, inner, depth), BF16)],
        wait=wait,
        carry=carry,
        grid=(rows // FEED,),
        compiler_params=params(),
        name=name,
        cost_estimate=cost(us),
    )


def feed(own, me, *operands):
    return feed_call(partial(feed_kernel, own), "feed", 18, (me,), F32, *operands)


def feed_last(me, *operands):
    return feed_call(feed_last_kernel, "feed_last", 18, (me,), BF16, *operands)


def back_kernel(
    lengths, live, third_grad, cot, after_cross, after_self, cross_query, looked0, mixed0, logs,
    gain1, gain2, w_out, w_co, *refs,
):
    queries, refs = refs[:4], refs[4:]
    pairs, refs = refs[:4], refs[4:]
    up_grad, mixed_grad, pair_grad, row_grads, query_grads, sums, total, turned = refs
    step = pl.program_id(0)
    text = TEXT

    @pl.when(step == 0)
    def _():
        total[...] = jnp.zeros_like(total)
        row_grads[...] = jnp.zeros_like(row_grads)
        sums[...] = jnp.zeros_like(sums)
        for j in range(4):
            turned[j] = pairs[j][0].T

    pulled, gain_sum, shift_sum = norm_backward(third_grad[...], after_cross[...], gain2[...])
    sums[0:1, :] += gain_sum
    sums[1:2, :] += shift_sum
    upstream = cot[...].astype(F32) + pulled
    low = upstream.astype(BF16)
    row_grads[1] += dot(looked0[...], low, TN)
    looked_grad = dot(low, w_co[...], NT).astype(BF16)
    item, _ = item_at(lengths, step * BLK)
    t0 = pl.multiple_of(item * text, text)
    alive = live[pl.ds(t0, text), :] > 0.0
    second_grad = jnp.zeros(upstream.shape, F32)
    width = queries[0].shape[2]
    heads = range(width // HEAD)

    def scores(j):
        cols = slice(j * width, (j + 1) * width)
        rows = [masked(cross_query[:, cols], head_row(width, h, HEAD**-0.5)) for h in heads]
        grads = [masked(looked_grad[:, cols], head_row(width, h, 1.0)) for h in heads]
        keys = pairs[j][0, pl.ds(t0, text), :]
        values = pairs[j][1, pl.ds(t0, text), :]
        return rows, grads, [dot(keys, row, NT) for row in rows], [dot(values, g, NT) for g in grads]

    ahead = scores(0)
    for j in range(4):
        rows, grads, score_set, pushed_set = ahead
        if j < 3:
            ahead = scores(j + 1)
        pieces, chances, score_grads = [], [], []
        for head in heads:
            index = j * (width // HEAD) + head
            score = jnp.where(alive, score_set[head], NEG)
            chance = jnp.exp(score - logs[index : index + 1, :])
            weighted = chance * pushed_set[head]
            mean = jnp.sum(weighted, axis=0, keepdims=True)
            score_grads.append((weighted - chance * mean).astype(BF16))
            chances.append(chance.astype(BF16))
            pieces.append(dot(turned[j, lanes_of(head), pl.ds(t0, text)], score_grads[head]))
        total[j, 0, pl.ds(t0, text), :] += dot(
            jnp.concatenate(score_grads, axis=1), jnp.concatenate(rows, axis=0)
        )
        total[j, 1, pl.ds(t0, text), :] += dot(
            jnp.concatenate(chances, axis=1), jnp.concatenate(grads, axis=0)
        )
        query_grad = (jnp.concatenate(pieces, axis=0).T * HEAD**-0.5).astype(BF16)
        if j == 0:
            query_grads[...] = query_grad
        second_grad = second_grad + dot(query_grad, queries[j][0], NT)

    pulled, gain_sum, shift_sum = norm_backward(second_grad, after_self[...], gain1[...])
    sums[2:3, :] += gain_sum
    sums[3:4, :] += shift_sum
    upstream = upstream + pulled
    up_grad[...] = upstream
    low = upstream.astype(BF16)
    row_grads[0] += dot(mixed0[...], low, TN)
    mixed_grad[...] = dot(low, w_out[...], NT).astype(BF16)

    @pl.when(step == pl.num_programs(0) - 1)
    def _():
        pair_grad[...] = total[...].astype(BF16)


def back(
    lengths, live, third_grad, cot, after_cross, after_self, cross_query, looked, mixed0, logs,
    gain1, gain2, w_out, w_co, crosses, pairs, wait,
):
    rows, depth = cot.shape
    text_rows = live.shape[0]
    width = mixed0.shape[1]
    inner = 4 * width
    tile = rows_of(BLK, depth)
    row = whole((1, depth))
    return launch(
        back_kernel,
        [lengths, live, third_grad, cot, after_cross, after_self, cross_query, looked, mixed0]
        + [logs, gain1, gain2, w_out, w_co, *crosses, *pairs],
        [smem(), whole((text_rows, 1))]
        + [tile] * 4
        + [rows_of(BLK, inner), rows_of(BLK, width), rows_of(BLK, width)]
        + [pl.BlockSpec((inner // HEAD, BLK), lambda i: (0, i)), row, row]
        + [whole((inner, depth))] * 2
        + [at((1, depth, width), (0, 0, 0))] * 4
        + [whole((2, text_rows, width))] * 4,
        [tile, rows_of(BLK, inner), whole((4, 2, text_rows, width))]
        + [whole((2, width, depth)), rows_of(BLK, width), whole((8, depth))],
        [
            shape((rows, depth)),
            shape((rows, inner), BF16),
            shape((4, 2, text_rows, width), BF16),
            shape((2, width, depth)),
            shape((rows, width), BF16),
            shape((8, depth)),
        ],
        scratch=[
            pltpu.VMEM((4, 2, text_rows, width), F32),
            pltpu.VMEM((4, width, text_rows), BF16),
        ],
        wait=wait,
        grid=(rows // BLK,),
        compiler_params=params(),
        name="back",
        cost_estimate=cost(53),
    )


def text_kernel(me, text, pair_grad, second, query_grad, row_grads, *refs):
    crosses, (text_grad, keep, send, cross_grad, folded) = refs[:4], refs[4:]
    total = jnp.zeros(text_grad.shape, F32)
    for j in range(4):
        for m in range(2):
            total = total + dot(pair_grad[j, m], crosses[j][m + 1], NT)
    text_grad[...] = total
    cross_grad[0] = dot(second[...], query_grad[...], TN)
    for m in range(2):
        cross_grad[m + 1] = dot(text[...], pair_grad[0, m], TN)
    put_pieces(cross_grad, keep, send, me)
    width = folded.shape[2]
    rows = row_grads.shape[1] // 8
    for k in range(2):
        for piece in range(8):
            for part in range(4):
                folded[k, pl.ds((piece * 4 + part) * rows, rows), :] = row_grads[
                    k, pl.ds(piece * rows, rows), part * width : (part + 1) * width
                ]
    put_pieces(folded, keep, send, me, 3)


def unfold(piece):
    rows, width = piece.shape
    parts = [piece[k * rows // 4 : (k + 1) * rows // 4] for k in range(4)]
    return jnp.concatenate(parts, axis=1)


def text_back(me, text, pair_grad, second, query_grad, row_grads, crosses, wait):
    text_rows, depth = text.shape
    width = pair_grad.shape[3]
    pieces = (4, 5, depth // 8, width)
    return launch(
        text_kernel,
        [me, text, pair_grad, second, query_grad, row_grads, *crosses],
        [smem()] + [vmem()] * 9,
        [vmem()] * 3,
        [shape((text_rows, depth)), shape(pieces), shape(pieces)],
        scratch=[pltpu.VMEM((3, depth, width), F32), pltpu.VMEM((2, depth, width), F32)],
        wait=wait,
        compiler_params=params(),
        name="text_back",
        cost_estimate=cost(15),
    )


def self_back_pair(qb, kb, diag, qkv, rows, grads, logs, means, turned, query_sum, key_sum, value_sum):
    q0 = pl.multiple_of(qb * BLK, BLK)
    k0 = pl.multiple_of(kb * BLK, BLK)
    keys = qkv[1, pl.ds(k0, BLK), :]
    values = qkv[2, pl.ds(k0, BLK), :]
    more_keys = 0.0
    more_values = 0.0
    heads = range(rows.shape[0])
    stages = [(dot(keys, rows[h], NT), dot(values, grads[h], NT)) for h in heads]
    for head, (score, pushed) in zip(heads, stages):
        if diag:
            score = jnp.where(causal(), score, NEG)
        chance = jnp.exp(score - logs[head : head + 1, pl.ds(q0, BLK)])
        score_grad = (chance * (pushed - means[head : head + 1, :])).astype(BF16)
        query_sum[lanes_of(head), :] += dot(turned[lanes_of(head), pl.ds(k0, BLK)], score_grad)
        more_keys = more_keys + dot(score_grad, rows[head])
        more_values = more_values + dot(chance.astype(BF16), grads[head])
    key_sum[pl.ds(k0, BLK), :] += more_keys
    value_sum[pl.ds(k0, BLK), :] += more_values


def self_back_body(
    lengths, qkv, mixed, out_grad, logs, weights, triple, turned, rows, grads, means, query_sum,
    key_sum, value_sum,
):
    row_count, width = mixed.shape
    turned[...] = qkv[1].T
    key_sum[...] = jnp.zeros_like(key_sum)
    value_sum[...] = jnp.zeros_like(value_sum)

    @pl.loop(0, row_count // BLK)
    def _(qb):
        q0 = pl.multiple_of(qb * BLK, BLK)
        _, start = item_at(lengths, q0)
        query = qkv[0, pl.ds(q0, BLK), :]
        grad = out_grad[pl.ds(q0, BLK), :]
        flat = (grad.astype(F32) * mixed[pl.ds(q0, BLK), :].astype(F32)).T
        for head in range(width // HEAD):
            rows[head] = masked(query, head_row(width, head, HEAD**-0.5))
            grads[head] = masked(grad, head_row(width, head, 1.0))
            means[head : head + 1, :] = jnp.sum(flat[lanes_of(head), :], axis=0, keepdims=True)
        query_sum[...] = jnp.zeros_like(query_sum)
        rest = (qkv, rows, grads, logs, means, turned, query_sum, key_sum, value_sum)

        @pl.loop(start // BLK, qb)
        def _(kb):
            self_back_pair(qb, kb, False, *rest)

        self_back_pair(qb, qb, True, *rest)
        triple[0, pl.ds(q0, BLK), :] = (query_sum[...].T * HEAD**-0.5).astype(BF16)

    triple[1] = key_sum[...].astype(BF16)
    triple[2] = value_sum[...].astype(BF16)


def self_scratch(rows, width):
    heads = width // HEAD
    return [
        pltpu.VMEM((3, rows, width), BF16),
        pltpu.VMEM((width, rows), BF16),
        pltpu.VMEM((heads, BLK, width), BF16),
        pltpu.VMEM((heads, BLK, width), BF16),
        pltpu.VMEM((8, BLK), F32),
        pltpu.VMEM((width, BLK), F32),
        pltpu.VMEM((rows, width), F32),
        pltpu.VMEM((rows, width), F32),
    ]


def self_own_kernel(me, lengths, qkv, mixed, out_grad, logs, weights, first, total, keep, send, *scratch):
    self_back_body(lengths, qkv, mixed, out_grad, logs, weights, *scratch[:-1])
    triple, qkv_grad = scratch[0], scratch[-1]
    for m in range(3):
        qkv_grad[m] = dot(first[...], triple[m], TN)
    put_pieces(qkv_grad, keep, send, me)
    total[...] = sum(dot(triple[m], weights[m], NT) for m in range(3))


def self_call(kernel, name, us, j, outs, operands, wait, prefix=(), scratch=()):
    lengths, qkv, mixed, out_grad, logs, weights, last_in = operands
    rows, width = mixed.shape
    return launch(
        kernel,
        [*prefix, *operands],
        [smem()] * (len(prefix) + 1)
        + [whole(qkv.shape), whole(mixed.shape), at((rows, width), (0, j))]
        + [whole(logs.shape), whole(weights.shape), whole(last_in.shape)],
        [whole(out.shape) for out in outs],
        outs,
        scratch=self_scratch(rows, width) + list(scratch),
        wait=wait,
        grid=(1,),
        compiler_params=params(),
        name=name,
        cost_estimate=cost(us),
    )


def self_own(me, lengths, qkv, mixed, out_grad, logs, weights, first, wait):
    _, depth, width = weights.shape
    pieces = shape((4, 3, depth // 8, width))
    operands = (lengths, qkv, mixed, out_grad, logs, weights, first)
    scratch = [pltpu.VMEM(weights.shape, F32)]
    outs = [shape(first.shape), pieces, pieces]
    return self_call(self_own_kernel, "self_own", 22, 0, outs, operands, wait, (me,), scratch)


def self_kernel(lengths, qkv, mixed, out_grad, logs, weights, before, total, *scratch):
    self_back_body(lengths, qkv, mixed, out_grad, logs, weights, *scratch)
    triple = scratch[0]
    total[...] = before[...] + sum(dot(triple[m], weights[m], NT) for m in range(3))


def self_back(lengths, qkv, mixed, out_grad, logs, weights, before, j, wait):
    operands = (lengths, qkv, mixed, out_grad, logs, weights, before)
    return self_call(self_kernel, "self_back", 26, j, [shape(before.shape)], operands, wait)[0]


def self_rest_kernel(places, lengths, *refs):
    count = len(places)
    sets, refs = [refs[4 * k : 4 * k + 4] for k in range(count)], refs[4 * count :]
    out_grad, before, tokens, upstream, gain, token_grad, sums, *refs = refs
    held, (total, token_rows, up_rows, sems, out_sems, *scratch) = refs[:5], refs[5:]
    rows, width = held[1].shape[1:]
    waits = []
    for k, (arrays, place) in enumerate(zip(sets, places)):
        sources = [*arrays, out_grad.at[:, pl.ds(place * width, width)]]
        waits.append(
            [
                pltpu.make_async_copy(source, target.at[k], sems.at[k, m])
                for m, (source, target) in enumerate(zip(sources, held))
            ]
        )
    ends = [
        pltpu.make_async_copy(source, target, sems.at[count, m])
        for m, (source, target) in enumerate(
            ((before, total), (tokens, token_rows), (upstream, up_rows))
        )
    ]
    for copy in waits[0] + ends[:1] + sum(waits[1:], []) + ends[1:]:
        copy.start()
    triple = scratch[0]
    for k in range(count):
        for copy in waits[k]:
            copy.wait()
        qkv, mixed, logs, weights, grads = (ref.at[k] for ref in held)
        self_back_body(lengths, qkv, mixed, grads, logs, weights, *scratch)
        if k == 0:
            ends[0].wait()
        total[...] += sum(dot(triple[m], weights[m], NT) for m in range(3))
    ends[1].wait()
    ends[2].wait()
    sums[...] = jnp.zeros_like(sums)
    outs = []
    for k in range(rows // BLK):
        part = slice(k * BLK, (k + 1) * BLK)
        pulled, gain_sum, shift_sum = norm_backward(
            total[part, :], token_rows[part, :].astype(F32), gain[...]
        )
        sums[0:1, :] += gain_sum
        sums[1:2, :] += shift_sum
        up_rows[part, :] = up_rows[part, :] + pulled
        outs.append(
            pltpu.make_async_copy(
                up_rows.at[pl.ds(k * BLK, BLK)], token_grad.at[pl.ds(k * BLK, BLK)], out_sems.at[k]
            )
        )
        outs[-1].start()
    for copy in outs:
        copy.wait()


def self_rest(places, lengths, sets, out_grad, before, tokens, upstream, gain, wait):
    rows, depth = tokens.shape
    count = len(places)
    width = sets[0][1].shape[1]
    args = [lengths, *sum(sets, []), out_grad, before, tokens, upstream, gain]
    held = [
        pltpu.VMEM((count,) + array.shape, array.dtype) for array in sets[0] + [sets[0][1]]
    ]
    return launch(
        partial(self_rest_kernel, places),
        args,
        [smem()] + [anywhere()] * (len(args) - 2) + [vmem()],
        [anywhere(), vmem()],
        [shape((rows, depth)), shape((8, depth))],
        scratch=held
        + [pltpu.VMEM((rows, depth), dtype) for dtype in (F32, BF16, F32)]
        + [pltpu.SemaphoreType.DMA((count + 1, 5)), pltpu.SemaphoreType.DMA((rows // BLK,))]
        + self_scratch(rows, width),
        wait=wait,
        compiler_params=params(),
        name="self_rest",
        cost_estimate=cost(40),
    )


DP = 8
MP = 4


def ring(step):
    pairs = []
    for i in range(DP):
        for z in range(MP):
            to = (z + (step if i % 2 == 0 else -step)) % MP
            pairs.append((i * MP + z, i * MP + to))
    return pairs


def straight(step):
    return [(z, (z + step) % MP) for z in range(MP)]


def beside(first):
    return [(i, i ^ (2 if (i % 2 == 0) == first else 4)) for i in range(DP)]


def swap(value):
    return lax.ppermute(value, "dp", [(i, i ^ 1) for i in range(DP)])


def fold(piece):
    width = piece.shape[1] // 4
    return jnp.concatenate([piece[:, k * width : (k + 1) * width] for k in range(4)], axis=0)


def fold_whole(shard):
    return jnp.concatenate([fold(piece) for piece in jnp.split(shard, 4)], axis=0)


def cut(shard, chip):
    rows = shard.shape[1] // 4
    return lax.dynamic_slice_in_dim(shard, chip * rows, rows, 1).astype(F32)


def near_of(piece):
    return lax.ppermute(piece, "dp", beside(True))


def side_of(piece):
    return lax.ppermute(piece, "dp", beside(False))


def along(value, step):
    return lax.ppermute(value, "mp", straight(step))


def around(value):
    return lax.ppermute(value, ("dp", "mp"), ring(1))


def in_order(keep, send):
    pieces = [part[k] for k, m in ((0, 0), (2, 1), (1, 2), (3, 3)) for part, k in ((keep, k), (send, m))]
    return jnp.concatenate(pieces, axis=1)


def scattered(value, axis):
    return lax.psum_scatter(value, "dp", scatter_dimension=axis, tiled=True)


def pieces_of(mine, other):
    mine, other = jnp.split(mine, 4, axis=1), jnp.split(other, 4, axis=1)
    return mine + [other[k] for k in (0, 2, 1, 3)]


def sum_near(keep, sent):
    return lax.ppermute(keep[2:] + sent[2:], "dp", beside(True))


def sum_side(keep, sent, near):
    return side_of(keep[1] + sent[1] + near[1])


def sum_last(keep, sent, near, side):
    return keep[0] + sent[0] + near[0] + side


def plane_sum(value):
    chips = [lax.ppermute(value, "dp", [(i, i ^ bit) for i in range(DP)]) for bit in (2, 4, 6)]
    value = value + chips[0] + (chips[1] + chips[2])
    return value + swap(value)


def local(
    planar, tokens, text_states, lengths, text_mask, ln_gain, ln_shift, w_qkv, w_out, w_cross_q,
    w_cross_kv, w_cross_out, w_up, w_down, cotangent,
):
    slot_count, text_length = text_mask.shape
    place = lax.axis_index("dp") if planar else jnp.int32(0)
    chip, core = place // 2, place % 2
    me = jnp.stack([chip, core]).astype(jnp.int32)
    gains = [ln_gain[n : n + 1] for n in range(3)]
    shifts = [ln_shift[n : n + 1] for n in range(3)]
    text = text_states.reshape(slot_count * text_length, text_states.shape[2])
    position = lax.broadcasted_iota(jnp.int32, text_mask.shape, 1)
    live = ((text_mask == 1) | (position == 0)).astype(F32).reshape(-1, 1)
    own_qkv = jnp.transpose(w_qkv, (1, 0, 2))
    own_cross = jnp.concatenate([w_cross_q[None], jnp.transpose(w_cross_kv, (1, 0, 2))], axis=0)
    feeds = jnp.stack([w_up, w_down])
    qkvs, mixeds, logs, weights = ([None] * 4 for _ in range(4))
    weights[0] = own_qkv

    def shards(value):
        return along(value.astype(F32), 1), along(value.astype(F32), 3)

    wait, carry = [], []
    first = None if planar else norm_first(tokens, gains[0], shifts[0], [])
    if planar:
        rows = w_out.shape[0] // 4
        outer = [
            fold(lax.dynamic_slice_in_dim(value, chip * rows, rows, 0))[None].astype(F32)
            for value in (w_out, w_cross_out)
        ]
        qkv_one = around(cut(own_qkv, chip))
        own_piece = gate([qkv_one], jnp.concatenate([cut(own_cross, chip), *outer], axis=0))
        cross_one = around(own_piece)
        first = norm_first(tokens, gains[0], shifts[0], [own_piece])
        qkv_near, qkv_side = near_of(qkv_one), gate([first], side_of(qkv_one))
        wait = [qkv_one, cross_one]
    qkvs[0], mixeds[0], logs[0] = front_own(lengths, first, own_qkv, wait, [])
    if planar:
        mine = join(me, [qkv_one, qkv_near, qkv_side, near_of(qkv_side)], [logs[0]])
        g_qkv = mine, swap(mine)
        cross_near, cross_side = near_of(cross_one), side_of(cross_one)
        two = jnp.where(
            core == 0,
            jnp.concatenate([qkv_one, cross_one[3:4]], axis=0),
            jnp.concatenate([cross_one[:3], cross_one[4:5]], axis=0),
        )
        two = around(two)
        wait = [cross_near, cross_side, two]
        carry = [cut(feeds, chip)]
    else:
        folded = [fold_whole(value)[None] for value in (w_out, w_cross_out)]
        g_qkv = shards(own_qkv)
        g_cross = shards(jnp.concatenate([own_cross, *folded], axis=0))
        g_two = [
            along(jnp.concatenate(parts, axis=0).astype(F32), 2)
            for parts in ((own_qkv, folded[0]), (own_cross, folded[1]))
        ]
        g_feed = pieces_of(*shards(feeds))
        g_last = pieces_of(*[along(feeds[k : k + 1].astype(F32), 2) for k in range(2)])
    weights[1], qkvs[1], mixeds[1], logs[1], *carried = front(
        lengths, first, g_qkv[0], wait, carry
    )
    if planar:
        two = gate([logs[1]], two)
        cross_far = near_of(cross_side)
        two_near, two_side = near_of(two), side_of(two)
        feed_one = around(carried[0])
        wait = [two, cross_near, cross_side, logs[1]]
    weights[3], qkvs[3], mixeds[3], logs[3] = front(lengths, first, g_qkv[1], wait, [])
    if planar:
        mine = join(me, [cross_one, cross_near, cross_side, cross_far], [logs[3], feed_one, two_near, two_side])
        g_cross = mine, swap(mine)
        two_far = near_of(two_side)
        feed_near, feed_side = near_of(feed_one), side_of(feed_one)
        feed_two = around(lax.dynamic_slice_in_dim(feed_one, core, 1, 0))
        wait = [two_near, two_side]
    cross_a, cross_b, *pairs = text_front(text, own_cross, g_cross, wait)
    if planar:
        mine = join(me, [two, two_near, two_side, two_far], [cross_a])
        g_two = mine, swap(mine)
        wait = []
    weights[2], cross_two, qkvs[2], mixeds[2], logs[2], pair_two = front_two(
        me, lengths, first, g_two, text, wait
    )
    pairs = [pairs[0], pairs[1], pair_two, pairs[2]]
    crosses = [own_cross, cross_a, cross_two, cross_b]
    if planar:
        wait = [feed_one, feed_two]
    full_out, full_co, after_self, after_cross, second, third, cross_query, looked, cross_logs = middle(
        me, lengths, live, tokens, (gains[1], shifts[1], gains[2], shifts[2]), w_out, w_cross_out,
        mixeds, crosses, pairs, g_cross, g_two, wait,
    )
    if planar:
        feed_side, feed_two = gate([third], feed_side), gate([third], feed_two)
        feed_far = near_of(feed_side)
        last_near, last_side = near_of(feed_two), side_of(feed_two)
        wait = [feed_near, feed_side, feed_two]
    out, grad, both_keep, both_send = feed_own(
        me, third, cotangent, after_cross, w_up, w_down, wait
    )
    wait, carry = [], [both_send]
    if planar:
        g_feed = [feed_one, feed_near, feed_side, gate([out], feed_far)]
        g_feed = g_feed + [swap(value) for value in g_feed]
        wait = g_feed[4:7]
    out, grad = feed(True, me, third, cotangent, out, grad, g_feed[:4], wait)
    if planar:
        last_far = near_of(gate([out], last_side))
    out, grad = feed(False, me, third, cotangent, out, grad, g_feed[4:], [])
    if planar:
        g_last = [feed_two, last_near, last_side, gate([out], last_far)]
        g_last = g_last + [swap(value) for value in g_last]
    out, grad, both_send = feed_last(
        me, third, cotangent, out, grad, g_last, [], [both_send]
    )
    if planar:
        both_swap = swap(both_send)
    upstream, mixed_grad, pair_grad, row_grads, query_grad, sums = back(
        lengths, live, grad, cotangent, after_cross, after_self, cross_query, looked, mixeds[0],
        cross_logs, gains[1], gains[2], full_out, full_co, crosses, pairs,
        [],
    )
    wait = []
    if planar:
        both_swap = gate([sums], both_swap)
        both_near = sum_near(both_keep, both_swap)
    text_grad, keep, send = text_back(
        me, text, pair_grad, second, query_grad, row_grads, crosses, wait
    )
    if planar:
        late_swap = swap(send)
        wait = []
    first_grad, qkv_keep, qkv_send = self_own(
        me, lengths, qkvs[0], mixeds[0], mixed_grad, logs[0], weights[0], first, wait
    )
    if planar:
        both_near = gate([first_grad], both_near)
        both_side = sum_side(both_keep, both_swap, both_near)
        late_near = sum_near(keep, late_swap)
        qkv_swap = swap(qkv_send)
        wait = [late_swap, both_near]
    first_grad = self_back(
        lengths, qkvs[1], mixeds[1], mixed_grad, logs[1], weights[1], first_grad, 1, wait
    )
    if planar:
        late_near, qkv_swap = gate([first_grad], late_near), gate([first_grad], qkv_swap)
        late_side = sum_side(keep, late_swap, late_near)
        qkv_near = sum_near(qkv_keep, qkv_swap)
        wait = [late_near, qkv_swap]
    token_grad, last_sums = self_rest(
        (2, 3), lengths, [[qkvs[j], mixeds[j], logs[j], weights[j]] for j in (2, 3)],
        mixed_grad, first_grad, tokens, upstream, gains[0], wait,
    )
    if planar:
        qkv_near = gate([last_sums], qkv_near)
        late_side = gate([last_sums], late_side)
        both_side = gate([last_sums], both_side)
        last_sums = gate([late_side, both_side, qkv_near], last_sums)
        qkv_side = sum_side(qkv_keep, qkv_swap, qkv_near)
    norm_sums = jnp.concatenate(
        [last_sums[0:1], sums[2:3], sums[0:1], last_sums[1:2], sums[3:4], sums[1:2]], axis=0
    )
    if planar:
        both_sum = sum_last(both_keep, both_swap, both_near, both_side)
        late_sum = sum_last(keep, late_swap, late_near, late_side)
        qkv_sum = sum_last(qkv_keep, qkv_swap, qkv_near, qkv_side)
        row_sum = [unfold(late_sum[k]) for k in (3, 4)]
        width = norm_sums.shape[1] // DP
        norm_sum = lax.dynamic_slice_in_dim(plane_sum(norm_sums), place * width, width, 1)
    else:
        both_sum = scattered(in_order(both_keep, both_send), 1)
        late = in_order(keep, send)
        late_sum = scattered(late[:3], 1)
        qkv_sum = scattered(in_order(qkv_keep, qkv_send), 1)
        row_sum = [
            scattered(jnp.concatenate([unfold(part) for part in jnp.split(late[k], 8)]), 0)
            for k in (3, 4)
        ]
        norm_sum = scattered(norm_sums, 1)
    return (
        out,
        token_grad,
        text_grad.reshape(text_states.shape),
        norm_sum[:3],
        norm_sum[3:],
        jnp.transpose(qkv_sum, (1, 0, 2)),
        row_sum[0],
        late_sum[0],
        jnp.transpose(late_sum[1:3], (1, 0, 2)),
        row_sum[1],
        both_sum[0],
        both_sum[1],
    )


def solution(mesh):
    placed = (
        P("dp", None),
        P("dp", None, None),
        P("dp"),
        P("dp", None),
        P(),
        P(),
        P(None, None, "mp"),
        P("mp", None),
        P(None, "mp"),
        P(None, None, "mp"),
        P("mp", None),
        P(None, "mp"),
        P("mp", None),
        P("dp", None),
    )
    return jax.shard_map(
        partial(local, mesh.shape["dp"] == DP),
        mesh=mesh,
        in_specs=placed,
        out_specs=(
            P("dp", None),
            P("dp", None),
            P("dp", None, None),
            P(None, "dp"),
            P(None, "dp"),
            P("dp", None, "mp"),
            P(("mp", "dp"), None),
            P("dp", "mp"),
            P("dp", None, "mp"),
            P(("mp", "dp"), None),
            P("dp", "mp"),
            P(("mp", "dp"), None),
        ),
        check_vma=False,
    )
```
